32 devices in a mesh: dp: 16 (over z, y, x), blk: 2 (over core).
Axes of the slice: x: 2, y: 2, z: 4, core: 2. Of those that a mesh axis runs over, the one named last changes fastest.
Arguments:
- tokens: bfloat16 [8192, 1024], P(('dp', 'blk')), may hold values from -6 to 6
- doc_lengths: int32 [16, 4], P('dp'), may hold values from 1 to 509, as said below
- w_query: bfloat16 [1024, 1024], replicated, may hold values from -0.1875 to 0.1875
- w_key: bfloat16 [1024, 1024], replicated, may hold values from -0.1875 to 0.1875
- w_value: bfloat16 [1024, 1024], replicated, may hold values from -0.1875 to 0.1875
- w_out: bfloat16 [1024, 1024], replicated, may hold values from -0.1875 to 0.1875
- w_up: bfloat16 [1024, 4096], replicated, may hold values from -0.1875 to 0.1875
- w_down: bfloat16 [4096, 1024], replicated, may hold values from -0.09375 to 0.09375
- bias_up: float32 [4096], replicated, may hold values from -1.75 to 1.75
- bias_down: float32 [1024], replicated, may hold values from -1.75 to 1.75
- gain_pre_attn: float32 [1024], replicated, may hold values from 0.5 to 1.5
- gain_post_attn: float32 [1024], replicated, may hold values from 0.5 to 1.5
- gain_pre_mlp: float32 [1024], replicated, may hold values from 0.5 to 1.5
- gain_post_mlp: float32 [1024], replicated, may hold values from 0.5 to 1.5
- cotangent: bfloat16 [8192, 1024], P(('dp', 'blk')), may hold values from -12 to 12
Outputs:
- output: bfloat16 [8192, 1024], P(('dp', 'blk'))
- grad_tokens: bfloat16 [8192, 1024], P(('dp', 'blk'))
- grad_query: float32 [1024, 1024], P(None, ('dp', 'blk'))
- grad_key: float32 [1024, 1024], P(None, ('dp', 'blk'))
- grad_value: float32 [1024, 1024], P(None, ('dp', 'blk'))
- grad_w_out: float32 [1024, 1024], P(None, ('dp', 'blk'))
- grad_up: float32 [1024, 4096], P(None, ('dp', 'blk'))
- grad_down: float32 [4096, 1024], P(None, ('dp', 'blk'))
- grad_bias_up: float32 [4096], P(('dp', 'blk'))
- grad_bias_down: float32 [1024], P(('dp', 'blk'))
- grad_gain_pre_attn: float32 [1024], P(('dp', 'blk'))
- grad_gain_post_attn: float32 [1024], P(('dp', 'blk'))
- grad_gain_pre_mlp: float32 [1024], P(('dp', 'blk'))
- grad_gain_post_mlp: float32 [1024], P(('dp', 'blk'))
- branch_rms: float32 [2, 8192], P(None, ('dp', 'blk'))
The draws below stay inside these ranges and needn't reach their ends.
Inputs may be any that keep to these rules, and one draw needn't show every extreme that they name: `doc_lengths`: each row holds four positive document lengths that sum to 512; the first two together and the last are each at most 128, so the third document runs from the pack's first block to its last. In one pack the first, second and last documents have one token each.
All inputs are finite; a program needn't handle non-finite values.
Results may differ from the reference program's by a relative error of at most 0.023.
Values may be sent and summed in bfloat16 or wider, within the bound.
A program may use at most 192 MiB of HBM per device.

```python
import math
import jax
import jax.numpy as jnp
from jax import lax

D = 1024
H = 16
HD = 64
FF = 4096
TOK_DEV = 256
GROUP_TOK = 512
GROUPS = 16
TOKENS = 8192


def draw_doc_lengths(key, part):
    key = jax.random.fold_in(key, 11)
    key_list = jax.random.split(key, 4)
    lead_one = jax.random.randint(key_list[0], (GROUPS, 1), 1, TOK_DEV // 4 + 1)
    lead_two = jax.random.randint(key_list[1], (GROUPS, 1), 1, TOK_DEV // 4 + 1)
    trailing = jax.random.randint(key_list[2], (GROUPS, 1), 1, TOK_DEV // 2 + 1)
    chosen = jax.random.randint(key_list[3], (), 0, GROUPS)
    picked = (jnp.arange(GROUPS, dtype=jnp.int32) == chosen)[:, None]
    lead_one = jnp.where(picked, 1, lead_one)
    lead_two = jnp.where(picked, 1, lead_two)
    trailing = jnp.where(picked, 1, trailing)
    middle = GROUP_TOK - lead_one - lead_two - trailing
    return jnp.concatenate([lead_one, lead_two, middle, trailing], axis=1).astype(jnp.int32)


def spiked(array, own_key, source, target, shards_of, factor):
    def block_of(axis_at):
        return (jnp.arange(array.shape[axis_at]) // (array.shape[axis_at] // shards_of)).reshape((-1,) + (1,) * (array.ndim - 1 - axis_at))

    near = jax.random.permutation(own_key, shards_of)[block_of(target)]
    other_side = (block_of(target) + shards_of // 2) % shards_of
    return jnp.where((block_of(source) == near) | (block_of(source) == other_side), factor * array, array)


def level_of(own_key, extent, shards, low, high):
    def one(dim, parts):
        draws = jax.random.uniform(jax.random.fold_in(jax.random.fold_in(own_key, 6), dim), (parts,), jnp.float32, low / len(shards), high / len(shards))
        return jnp.repeat(jnp.exp(draws), extent[dim] // parts).reshape((-1,) + (1,) * (len(extent) - dim - 1))

    level = one(*shards[0])
    for cut in shards[1:]:
        level = level * one(*cut)
    return level


def normal_values(own_key, extent, spread, bound, pieces=(), kind=jnp.bfloat16):
    gain = level_of(own_key, extent, pieces, -0.22, 0.18) if pieces else 1.0
    array = jax.random.normal(own_key, extent, jnp.float32) * spread * gain
    return jnp.minimum(jnp.maximum(array, -bound), bound).astype(kind)


def noise_with(stream_key, dims, spread, most, cuts, heavy, kind=jnp.bfloat16):
    entries = spread * jax.random.normal(stream_key, dims, jnp.float32)
    if cuts:
        entries = entries * level_of(stream_key, dims, cuts, -0.22, 0.18)
    return jnp.clip(spiked(entries, jax.random.fold_in(stream_key, 3), *heavy), -most, most).astype(kind)


def setup_inputs(seed: int = 0) -> dict:
    key_of = jax.random.split(jax.random.key(seed), 16)
    return {
        "tokens": normal_values(key_of[0], (TOKENS, D), 1.0, 6.0, ((0, 32),)),
        "doc_lengths": draw_doc_lengths(jax.random.fold_in(key_of[15], 71), 0),
        "w_query": normal_values(key_of[2], (D, D), D ** -0.5, 0.1875),
        "w_key": normal_values(key_of[3], (D, D), D ** -0.5, 0.1875),
        "w_value": normal_values(key_of[4], (D, D), D ** -0.5, 0.1875),
        "w_out": normal_values(key_of[5], (D, D), D ** -0.5, 0.1875),
        "w_up": normal_values(key_of[6], (D, FF), D ** -0.5, 0.1875),
        "w_down": normal_values(key_of[7], (FF, D), FF ** -0.5, 0.09375),
        "bias_up": normal_values(key_of[8], (FF,), 0.3, 1.75, (), jnp.float32),
        "bias_down": normal_values(key_of[9], (D,), 0.3, 1.75, (), jnp.float32),
        "gain_pre_attn": jnp.clip(1.0 + 0.1 * jax.random.normal(key_of[10], (D,), jnp.float32), 0.5, 1.5),
        "gain_post_attn": jnp.clip(1.0 + 0.1 * jax.random.normal(key_of[11], (D,), jnp.float32), 0.5, 1.5),
        "gain_pre_mlp": jnp.clip(1.0 + 0.1 * jax.random.normal(key_of[12], (D,), jnp.float32), 0.5, 1.5),
        "gain_post_mlp": jnp.clip(1.0 + 0.1 * jax.random.normal(key_of[13], (D,), jnp.float32), 0.5, 1.5),
        "cotangent": noise_with(key_of[14], (TOKENS, D), 1.0, 12.0, ((0, 32),), (0, 1, 32, 2.75)),
    }


eps = 1e-06
neg_big = -1e+30
exact_mode = lax.Precision.HIGHEST

@jax.custom_vjp
def low(v):
    return lax.optimization_barrier(v.astype(jnp.bfloat16)).astype(jnp.float32)

@jax.custom_vjp
def low_back(v):
    return v

def low_keep(v):
    return (low(v), None)

def low_pass(kept, grad):
    return (grad,)

def back_keep(v):
    return (v, None)

def back_low(kept, grad):
    return (low(grad),)
low.defvjp(low_keep, low_pass)
low_back.defvjp(back_keep, back_low)

def rms_norm(values, gain_row):
    return values * lax.rsqrt(lax.optimization_barrier(jnp.mean(values * values, axis=-1, keepdims=True)) + eps) * gain_row

def rotate(head_rows, position):
    half_size = head_rows.shape[-1] // 2
    frequency = 10000.0 ** (-2.0 * jnp.arange(half_size, dtype=jnp.float32) / head_rows.shape[-1])
    angles = position.astype(jnp.float32)[:, None] * frequency[None, :]
    cosine = jnp.cos(angles)[:, None, :]
    sine_part = jnp.sin(angles)[:, None, :]
    low_half = head_rows[..., :half_size]
    high_half = head_rows[..., half_size:]
    return jnp.concatenate([low_half * cosine - high_half * sine_part, low_half * sine_part + high_half * cosine], axis=-1)

def doc_layout(lengths, total_rows):
    index_row = jnp.arange(total_rows, dtype=jnp.int32)
    doc_ends = jnp.cumsum(lengths).astype(jnp.int32)
    segment = lax.optimization_barrier(jnp.sum((index_row[:, None] >= doc_ends[None, :3]).astype(jnp.int32), axis=1))
    starts = (doc_ends - lengths).astype(jnp.int32)
    matches = segment[:, None] == jnp.arange(4, dtype=jnp.int32)[None, :]
    return (index_row, lax.optimization_barrier(jnp.sum(jnp.where(matches, starts[None, :], 0), axis=1)).astype(jnp.int32))

def attend_group(arguments):
    queries, keys_rot, values, start_row = arguments
    total_rows = queries.shape[0]
    width = math.gcd(total_rows, 512)
    index_row = jnp.arange(total_rows, dtype=jnp.int32)
    blocks = (queries.reshape(-1, width, H, HD), index_row.reshape(-1, width), start_row.reshape(-1, width))

    def one_block(block):
        query_blk, query_index, query_start = block
        scores = jnp.einsum('qhd,khd->hqk', query_blk, keys_rot, precision=exact_mode) * HD ** (-0.5)
        allowed = (index_row[None, :] <= query_index[:, None]) & (index_row[None, :] >= query_start[:, None])
        scores = low_back(jnp.where(allowed[None], scores, neg_big))
        running = lax.optimization_barrier(jnp.max(scores, axis=-1, keepdims=True))
        expo_part = jnp.exp(scores - running)
        probs = expo_part / lax.optimization_barrier(jnp.sum(expo_part, axis=-1, keepdims=True))
        return jnp.einsum('hqk,khd->qhd', low(probs), values, precision=exact_mode)
    result = lax.map(jax.checkpoint(one_block), blocks)
    return result.reshape(total_rows, H, HD)

def reference(tokens, doc_lengths, w_query, w_key, w_value, w_out, w_up, w_down, bias_up, bias_down, gain_pre_attn, gain_post_attn, gain_pre_mlp, gain_post_mlp, cotangent):
    index_all, start_all = jax.vmap(lambda row: doc_layout(row, GROUP_TOK))(doc_lengths)
    position = (index_all - start_all).reshape(-1)

    def forward(tokens_f, query_w, key_w, value_w, out_w, up_w, down_w, up_bias, down_bias, gain_one, gain_two, gain_three, gain_four):
        attn_in = low(rms_norm(tokens_f, gain_one))
        query_pre = low_back(jnp.dot(attn_in, query_w, precision=exact_mode)).reshape(-1, H, HD)
        key_pre = low_back(jnp.dot(attn_in, key_w, precision=exact_mode)).reshape(-1, H, HD)
        values = low(low_back(jnp.dot(attn_in, value_w, precision=exact_mode))).reshape(-1, H, HD)
        queries = low(rotate(query_pre, position))
        keys_rot = low(rotate(key_pre, position))
        packed = lambda arr: arr.reshape(GROUPS, GROUP_TOK, H, HD)
        attn = lax.map(attend_group, (packed(queries), packed(keys_rot), packed(values), start_all))
        attn = low_back(low(attn.reshape(-1, D)))
        branch_attn = low_back(jnp.dot(attn, out_w, precision=exact_mode))
        hidden_res = tokens_f + rms_norm(branch_attn, gain_two)
        mlp_in = low(rms_norm(hidden_res, gain_three))
        pre_act = low_back(jnp.dot(mlp_in, up_w, precision=exact_mode) + up_bias)
        activated = low(jax.nn.gelu(pre_act, approximate=True))
        branch_mlp = low_back(jnp.dot(activated, down_w, precision=exact_mode) + down_bias)
        result = hidden_res + rms_norm(branch_mlp, gain_four)
        stats = jnp.stack([jnp.sqrt(lax.optimization_barrier(jnp.mean(branch_attn * branch_attn, axis=-1)) + eps), jnp.sqrt(lax.optimization_barrier(jnp.mean(branch_mlp * branch_mlp, axis=-1)) + eps)])
        return (result, stats)
    primals = (tokens.astype(jnp.float32), w_query.astype(jnp.float32), w_key.astype(jnp.float32), w_value.astype(jnp.float32), w_out.astype(jnp.float32), w_up.astype(jnp.float32), w_down.astype(jnp.float32), bias_up, bias_down, gain_pre_attn, gain_post_attn, gain_pre_mlp, gain_post_mlp)
    result, back_fn, stats = jax.vjp(forward, *primals, has_aux=True)
    grads = back_fn(cotangent.astype(jnp.float32))
    return (result.astype(jnp.bfloat16), grads[0].astype(jnp.bfloat16), grads[1], grads[2], grads[3], grads[4], grads[5], grads[6], grads[7], grads[8], grads[9], grads[10], grads[11], grads[12], stats)
```

```python
import math

import jax
import jax.numpy as jnp
from jax import lax
from jax.sharding import PartitionSpec as P

D = 1024
H = 16
HD = 64


eps = 1e-06
neg_big = -1e30


def rms_norm(values, gain_row):
    return values * lax.rsqrt(jnp.mean(values * values, axis=-1, keepdims=True) + eps) * gain_row


def rotate(head_rows, position):
    half_size = head_rows.shape[-1] // 2
    frequency = 10000.0 ** (-2.0 * jnp.arange(half_size, dtype=jnp.float32) / head_rows.shape[-1])
    angles = position.astype(jnp.float32)[:, None] * frequency[None, :]
    cosine = jnp.cos(angles)[:, None, :]
    sine_part = jnp.sin(angles)[:, None, :]
    low_half = head_rows[..., :half_size]
    high_half = head_rows[..., half_size:]
    return jnp.concatenate(
        [low_half * cosine - high_half * sine_part, low_half * sine_part + high_half * cosine],
        axis=-1,
    )


def doc_layout(lengths, total_rows):
    index_row = jnp.arange(total_rows, dtype=jnp.int32)
    doc_ends = jnp.stack(
        [
            lengths[0],
            lengths[0] + lengths[1],
            lengths[0] + lengths[1] + lengths[2],
            lengths[0] + lengths[1] + lengths[2] + lengths[3],
        ]
    )
    segment = jnp.sum((index_row[:, None] >= doc_ends[None, :3]).astype(jnp.int32), axis=1)
    starts = doc_ends - lengths
    matches = segment[:, None] == jnp.arange(4, dtype=jnp.int32)[None, :]
    return (index_row, jnp.sum(jnp.where(matches, starts[None, :], 0), axis=1))


def block_mask(query_index, query_start, key_first, width):
    key_index = key_first + jnp.arange(width, dtype=jnp.int32)
    return (key_index[None, :] <= query_index[:, None]) & (
        key_index[None, :] >= query_start[:, None]
    )


def on_device(
    tokens,
    doc_lengths,
    w_query,
    w_key,
    w_value,
    w_out,
    w_up,
    w_down,
    bias_up,
    bias_down,
    gain_pre_attn,
    gain_post_attn,
    gain_pre_mlp,
    gain_post_mlp,
    cotangent,
):
    row_count = tokens.shape[0]
    cycle_size = lax.axis_size("blk")
    group_rows = row_count * cycle_size
    first_row = lax.axis_index("blk") * row_count
    index_all, start_all = doc_layout(doc_lengths[0], group_rows)
    query_index = lax.dynamic_slice_in_dim(index_all, first_row, row_count)
    query_start = lax.dynamic_slice_in_dim(start_all, first_row, row_count)
    position = query_index - query_start
    query_last = first_row + row_count - 1
    start_least = jnp.min(query_start)
    scale = HD ** (-0.5)
    tokens_f = tokens.astype(jnp.float32)
    normed_in, back_pre_attn = jax.vjp(rms_norm, tokens_f, gain_pre_attn)
    attn_in = normed_in.astype(jnp.bfloat16)
    query_pre = jnp.dot(attn_in, w_query, preferred_element_type=jnp.float32)
    key_pre = jnp.dot(attn_in, w_key, preferred_element_type=jnp.float32)
    value_pre = jnp.dot(attn_in, w_value, preferred_element_type=jnp.float32)
    queries, back_rot_query = jax.vjp(
        lambda arr: rotate(arr, position), query_pre.reshape(row_count, H, HD)
    )
    keys_rot, back_rot_key = jax.vjp(
        lambda arr: rotate(arr, position), key_pre.reshape(row_count, H, HD)
    )
    queries_low = queries.astype(jnp.bfloat16)
    keys_low = keys_rot.reshape(row_count, D).astype(jnp.bfloat16)
    values_low = value_pre.astype(jnp.bfloat16)
    initial = (
        jnp.full((H, row_count), neg_big, jnp.float32),
        jnp.zeros((H, row_count), jnp.float32),
        jnp.zeros((row_count, H, HD), jnp.float32),
    )
    key_piece = lax.all_gather(keys_low, "blk", axis=0, tiled=True)
    value_piece = lax.all_gather(values_low, "blk", axis=0, tiled=True)
    piece_rows = key_piece.shape[0]
    fold_width = math.gcd(piece_rows, 512)

    def one_block(state, number):
        key_first = number * fold_width

        def one_compute(state):
            running_top, totals, accum = state
            keys_blk = lax.dynamic_slice_in_dim(
                key_piece, number * fold_width, fold_width, 0
            ).reshape(fold_width, H, HD)
            values_blk = lax.dynamic_slice_in_dim(
                value_piece, number * fold_width, fold_width, 0
            ).reshape(fold_width, H, HD)
            scores = (
                jnp.einsum(
                    "qhd,khd->hqk", queries_low, keys_blk, preferred_element_type=jnp.float32
                )
                * scale
            )
            allowed = block_mask(query_index, query_start, key_first, fold_width)[None]
            scores = jnp.where(allowed, scores, neg_big)
            new_top = jnp.maximum(running_top, jnp.max(scores, axis=-1))
            weights = jnp.where(allowed, jnp.exp(scores - new_top[..., None]), 0.0)
            factor = jnp.exp(running_top - new_top)
            totals = totals * factor + jnp.sum(weights, axis=-1)
            accum = accum * jnp.transpose(factor)[:, :, None] + jnp.einsum(
                "hqk,khd->qhd",
                weights.astype(jnp.bfloat16),
                values_blk,
                preferred_element_type=jnp.float32,
            )
            return (new_top, totals, accum)

        active = (key_first <= query_last) & (key_first + fold_width - 1 >= start_least)
        return (lax.cond(active, one_compute, lambda state: state, state), None)

    result, unused = lax.scan(
        one_block, initial, jnp.arange(piece_rows // fold_width, dtype=jnp.int32)
    )
    running_top, totals, accum = result
    attn_full = accum / jnp.transpose(totals)[:, :, None]
    log_total = running_top + jnp.log(totals)
    attn_low = attn_full.reshape(row_count, D).astype(jnp.bfloat16)
    branch_attn = jnp.dot(attn_low, w_out, preferred_element_type=jnp.float32)
    post_attn, back_post_attn = jax.vjp(rms_norm, branch_attn, gain_post_attn)
    hidden_res = tokens_f + post_attn
    normed_mlp, back_pre_mlp = jax.vjp(rms_norm, hidden_res, gain_pre_mlp)
    mlp_in = normed_mlp.astype(jnp.bfloat16)
    pre_act = jnp.dot(mlp_in, w_up, preferred_element_type=jnp.float32) + bias_up
    activated, back_gelu = jax.vjp(lambda arr: jax.nn.gelu(arr, approximate=True), pre_act)
    act_low = activated.astype(jnp.bfloat16)
    branch_mlp = jnp.dot(act_low, w_down, preferred_element_type=jnp.float32) + bias_down
    post_mlp, back_post_mlp = jax.vjp(rms_norm, branch_mlp, gain_post_mlp)
    output = (hidden_res + post_mlp).astype(jnp.bfloat16)
    branch_rms = jnp.stack(
        [
            jnp.sqrt(jnp.mean(branch_attn * branch_attn, axis=-1) + eps),
            jnp.sqrt(jnp.mean(branch_mlp * branch_mlp, axis=-1) + eps),
        ]
    )
    grad_out_f = cotangent.astype(jnp.float32)
    grad_branch_mlp, grad_gain_post_mlp = back_post_mlp(grad_out_f)
    grad_mlp_low = grad_branch_mlp.astype(jnp.bfloat16)
    grad_bias_down = jnp.sum(grad_mlp_low.astype(jnp.float32), axis=0)
    grad_down = jnp.einsum("tf,td->df", act_low, grad_mlp_low, preferred_element_type=jnp.float32)
    grad_act = jnp.einsum("td,fd->tf", grad_mlp_low, w_down, preferred_element_type=jnp.float32)
    (grad_pre_act,) = back_gelu(grad_act)
    grad_pre_low = grad_pre_act.astype(jnp.bfloat16)
    grad_bias_up = jnp.sum(grad_pre_low.astype(jnp.float32), axis=0)
    grad_up = jnp.einsum("td,tf->fd", mlp_in, grad_pre_low, preferred_element_type=jnp.float32)
    grad_normed_mlp = jnp.einsum(
        "tf,df->td", grad_pre_low, w_up, preferred_element_type=jnp.float32
    )
    grad_res_part, grad_gain_pre_mlp = back_pre_mlp(grad_normed_mlp)
    grad_hidden = grad_out_f + grad_res_part
    grad_branch_attn, grad_gain_post_attn = back_post_attn(grad_hidden)
    grad_branch_low = grad_branch_attn.astype(jnp.bfloat16)
    grad_w_out = jnp.einsum(
        "td,te->ed", attn_low, grad_branch_low, preferred_element_type=jnp.float32
    )
    grad_attn = jnp.einsum("te,de->td", grad_branch_low, w_out, preferred_element_type=jnp.float32)
    grad_attn_low = grad_attn.astype(jnp.bfloat16).reshape(row_count, H, HD)
    delta = jnp.einsum("qhd,qhd->hq", grad_attn_low.astype(jnp.float32), attn_full)
    key_source, value_source = key_piece, value_piece
    width = math.gcd(group_rows, 512)

    def back_block(grad_query_acc, number):
        key_first = number * width

        def back_compute(grad_query_acc):
            keys_blk = lax.dynamic_slice_in_dim(key_source, key_first, width, 0).reshape(
                width, H, HD
            )
            values_blk = lax.dynamic_slice_in_dim(value_source, key_first, width, 0).reshape(
                width, H, HD
            )
            scores = (
                jnp.einsum(
                    "qhd,khd->hqk", queries_low, keys_blk, preferred_element_type=jnp.float32
                )
                * scale
            )
            allowed = block_mask(query_index, query_start, key_first, width)[None]
            probs = jnp.where(allowed, jnp.exp(scores - log_total[..., None]), 0.0)
            grad_probs = jnp.einsum(
                "qhd,khd->hqk", grad_attn_low, values_blk, preferred_element_type=jnp.float32
            )
            grad_scores = (probs * (grad_probs - delta[..., None])).astype(jnp.bfloat16)
            grad_query_acc = (
                grad_query_acc
                + jnp.einsum(
                    "hqk,khd->qhd", grad_scores, keys_blk, preferred_element_type=jnp.float32
                )
                * scale
            )
            grad_keys_blk = (
                jnp.einsum(
                    "hqk,qhd->khd", grad_scores, queries_low, preferred_element_type=jnp.float32
                )
                * scale
            )
            grad_values_blk = jnp.einsum(
                "hqk,qhd->khd",
                probs.astype(jnp.bfloat16),
                grad_attn_low,
                preferred_element_type=jnp.float32,
            )
            return (
                grad_query_acc,
                (grad_keys_blk.reshape(width, D), grad_values_blk.reshape(width, D)),
            )

        def skipped(grad_query_acc):
            return (
                grad_query_acc,
                (jnp.zeros((width, D), jnp.float32), jnp.zeros((width, D), jnp.float32)),
            )

        active = (key_first <= query_last) & (key_first + width - 1 >= start_least)
        return lax.cond(active, back_compute, skipped, grad_query_acc)

    grad_query_acc, stacked = lax.scan(
        back_block,
        jnp.zeros((row_count, H, HD), jnp.float32),
        jnp.arange(group_rows // width, dtype=jnp.int32),
    )
    grad_keys_all = stacked[0].reshape(group_rows, D)
    grad_values_all = stacked[1].reshape(group_rows, D)
    grad_keys_mine, grad_values_mine = (
        lax.psum_scatter(
            grad_keys_all.astype(jnp.bfloat16), "blk", scatter_dimension=0, tiled=True
        ).astype(jnp.float32),
        lax.psum_scatter(
            grad_values_all.astype(jnp.bfloat16), "blk", scatter_dimension=0, tiled=True
        ).astype(jnp.float32),
    )
    (grad_key_pre,) = back_rot_key(grad_keys_mine.reshape(row_count, H, HD))
    (grad_query_pre,) = back_rot_query(grad_query_acc)
    grad_key_low = grad_key_pre.reshape(row_count, D).astype(jnp.bfloat16)
    grad_query_low = grad_query_pre.reshape(row_count, D).astype(jnp.bfloat16)
    grad_value_low = grad_values_mine.astype(jnp.bfloat16)
    grad_query = jnp.einsum(
        "td,te->ed", attn_in, grad_query_low, preferred_element_type=jnp.float32
    )
    grad_key = jnp.einsum("td,te->ed", attn_in, grad_key_low, preferred_element_type=jnp.float32)
    grad_value = jnp.einsum(
        "td,te->ed", attn_in, grad_value_low, preferred_element_type=jnp.float32
    )
    grad_normed_in = (
        jnp.einsum("te,de->td", grad_query_low, w_query, preferred_element_type=jnp.float32)
        + jnp.einsum("te,de->td", grad_key_low, w_key, preferred_element_type=jnp.float32)
        + jnp.einsum("te,de->td", grad_value_low, w_value, preferred_element_type=jnp.float32)
    )
    grad_tokens_part, grad_gain_pre_attn = back_pre_attn(grad_normed_in)
    grad_tokens = (grad_hidden + grad_tokens_part).astype(jnp.bfloat16)
    count = lax.axis_size(("dp", "blk"))
    low = jnp.bfloat16
    pieces = [
        part.astype(low).reshape(count, -1, D)
        for part in (grad_query, grad_key, grad_value, grad_w_out, grad_up, grad_down)
    ]
    small = [
        part.reshape(count, -1)
        for part in (
            grad_bias_up,
            grad_bias_down,
            grad_gain_pre_attn,
            grad_gain_post_attn,
            grad_gain_pre_mlp,
            grad_gain_post_mlp,
        )
    ]
    sizes = [part.shape[1] for part in pieces]
    summed = lax.psum_scatter(
        jnp.concatenate(pieces, axis=1), ("dp", "blk"), scatter_dimension=0
    ).astype(jnp.float32)
    small_sizes = [part.shape[1] for part in small]
    small_flat = jnp.concatenate(small, axis=1)
    padding = -small_flat.shape[1] % 128
    small_flat = jnp.pad(small_flat, ((0, 0), (0, padding)))
    small_summed = lax.psum_scatter(small_flat, ("dp", "blk"), scatter_dimension=0)
    cuts = [sum(sizes[: i + 1]) for i in range(len(sizes) - 1)]
    parts = jnp.split(summed, cuts, axis=0)
    parts[5] = parts[5].reshape(D // count, -1)
    small_cuts = [sum(small_sizes[: i + 1]) for i in range(len(small_sizes))]
    small_parts = jnp.split(small_summed, small_cuts, axis=0)[:6]
    return (output, grad_tokens, *[part.T for part in parts], *small_parts, branch_rms)


def solution(mesh):
    placed = (
        P(("dp", "blk"), None),
        P("dp", None),
        P(),
        P(),
        P(),
        P(),
        P(),
        P(),
        P(),
        P(),
        P(),
        P(),
        P(),
        P(),
        P(("dp", "blk"), None),
    )
    return jax.shard_map(
        on_device,
        mesh=mesh,
        in_specs=placed,
        out_specs=(
            P(("dp", "blk"), None),
            P(("dp", "blk"), None),
            P(None, ("dp", "blk")),
            P(None, ("dp", "blk")),
            P(None, ("dp", "blk")),
            P(None, ("dp", "blk")),
            P(None, ("dp", "blk")),
            P(None, ("dp", "blk")),
            P(("dp", "blk")),
            P(("dp", "blk")),
            P(("dp", "blk")),
            P(("dp", "blk")),
            P(("dp", "blk")),
            P(("dp", "blk")),
            P(None, ("dp", "blk")),
        ),
        check_vma=False,
    )
```

```python
import math

import jax
import jax.numpy as jnp
from jax import lax
from jax.experimental import pallas as pl
from jax.experimental.pallas import tpu as pltpu
from jax.sharding import PartitionSpec as P

D = 1024
H = 16
HD = 64


eps = 1e-06
neg_big = -1e30


def rms_norm(values, gain_row):
    return values * lax.rsqrt(jnp.mean(values * values, axis=-1, keepdims=True) + eps) * gain_row


def rotate(head_rows, position):
    half_size = head_rows.shape[-1] // 2
    frequency = 10000.0 ** (-2.0 * jnp.arange(half_size, dtype=jnp.float32) / head_rows.shape[-1])
    angles = position.astype(jnp.float32)[:, None] * frequency[None, :]
    cosine = jnp.cos(angles)[:, None, :]
    sine_part = jnp.sin(angles)[:, None, :]
    low_half = head_rows[..., :half_size]
    high_half = head_rows[..., half_size:]
    return jnp.concatenate(
        [low_half * cosine - high_half * sine_part, low_half * sine_part + high_half * cosine],
        axis=-1,
    )


def doc_layout(lengths, total_rows):
    index_row = jnp.arange(total_rows, dtype=jnp.int32)
    doc_ends = jnp.stack(
        [
            lengths[0],
            lengths[0] + lengths[1],
            lengths[0] + lengths[1] + lengths[2],
            lengths[0] + lengths[1] + lengths[2] + lengths[3],
        ]
    )
    segment = jnp.sum((index_row[:, None] >= doc_ends[None, :3]).astype(jnp.int32), axis=1)
    starts = doc_ends - lengths
    matches = segment[:, None] == jnp.arange(4, dtype=jnp.int32)[None, :]
    return (index_row, jnp.sum(jnp.where(matches, starts[None, :], 0), axis=1))


def block_mask(query_index, query_start, key_first, width):
    key_index = key_first + jnp.arange(width, dtype=jnp.int32)
    return (key_index[None, :] <= query_index[:, None]) & (
        key_index[None, :] >= query_start[:, None]
    )


def on_device(
    tokens,
    doc_lengths,
    w_query,
    w_key,
    w_value,
    w_out,
    w_up,
    w_down,
    bias_up,
    bias_down,
    gain_pre_attn,
    gain_post_attn,
    gain_pre_mlp,
    gain_post_mlp,
    cotangent,
):
    row_count = tokens.shape[0]
    cycle_size = lax.axis_size("blk")
    group_rows = row_count * cycle_size
    first_row = lax.axis_index("blk") * row_count
    index_all, start_all = doc_layout(doc_lengths[0], group_rows)
    query_index = lax.dynamic_slice_in_dim(index_all, first_row, row_count)
    query_start = lax.dynamic_slice_in_dim(start_all, first_row, row_count)
    position = query_index - query_start
    query_last = first_row + row_count - 1
    start_least = jnp.min(query_start)
    scale = HD ** (-0.5)
    tokens_f = tokens.astype(jnp.float32)
    normed_in, back_pre_attn = jax.vjp(rms_norm, tokens_f, gain_pre_attn)
    attn_in = normed_in.astype(jnp.bfloat16)
    query_pre = jnp.dot(attn_in, w_query, preferred_element_type=jnp.float32)
    key_pre = jnp.dot(attn_in, w_key, preferred_element_type=jnp.float32)
    value_pre = jnp.dot(attn_in, w_value, preferred_element_type=jnp.float32)
    queries, back_rot_query = jax.vjp(
        lambda arr: rotate(arr, position), query_pre.reshape(row_count, H, HD)
    )
    keys_rot, back_rot_key = jax.vjp(
        lambda arr: rotate(arr, position), key_pre.reshape(row_count, H, HD)
    )
    queries_low = queries.astype(jnp.bfloat16)
    keys_low = keys_rot.reshape(row_count, D).astype(jnp.bfloat16)
    values_low = value_pre.astype(jnp.bfloat16)
    initial = (
        jnp.full((H, row_count), neg_big, jnp.float32),
        jnp.zeros((H, row_count), jnp.float32),
        jnp.zeros((row_count, H, HD), jnp.float32),
    )
    key_piece = lax.all_gather(keys_low, "blk", axis=0, tiled=True)
    value_piece = lax.all_gather(values_low, "blk", axis=0, tiled=True)
    piece_rows = key_piece.shape[0]
    fold_width = math.gcd(piece_rows, 512)

    def one_block(state, number):
        key_first = number * fold_width

        def one_compute(state):
            running_top, totals, accum = state
            keys_blk = lax.dynamic_slice_in_dim(
                key_piece, number * fold_width, fold_width, 0
            ).reshape(fold_width, H, HD)
            values_blk = lax.dynamic_slice_in_dim(
                value_piece, number * fold_width, fold_width, 0
            ).reshape(fold_width, H, HD)
            scores = (
                jnp.einsum(
                    "qhd,khd->hqk", queries_low, keys_blk, preferred_element_type=jnp.float32
                )
                * scale
            )
            allowed = block_mask(query_index, query_start, key_first, fold_width)[None]
            scores = jnp.where(allowed, scores, neg_big)
            new_top = jnp.maximum(running_top, jnp.max(scores, axis=-1))
            weights = jnp.where(allowed, jnp.exp(scores - new_top[..., None]), 0.0)
            factor = jnp.exp(running_top - new_top)
            totals = totals * factor + jnp.sum(weights, axis=-1)
            accum = accum * jnp.transpose(factor)[:, :, None] + jnp.einsum(
                "hqk,khd->qhd",
                weights.astype(jnp.bfloat16),
                values_blk,
                preferred_element_type=jnp.float32,
            )
            return (new_top, totals, accum)

        active = (key_first <= query_last) & (key_first + fold_width - 1 >= start_least)
        return (lax.cond(active, one_compute, lambda state: state, state), None)

    result, unused = lax.scan(
        one_block, initial, jnp.arange(piece_rows // fold_width, dtype=jnp.int32)
    )
    running_top, totals, accum = result
    attn_full = accum / jnp.transpose(totals)[:, :, None]
    log_total = running_top + jnp.log(totals)
    attn_low = attn_full.reshape(row_count, D).astype(jnp.bfloat16)
    branch_attn = jnp.dot(attn_low, w_out, preferred_element_type=jnp.float32)
    post_attn, back_post_attn = jax.vjp(rms_norm, branch_attn, gain_post_attn)
    hidden_res = tokens_f + post_attn
    normed_mlp, back_pre_mlp = jax.vjp(rms_norm, hidden_res, gain_pre_mlp)
    mlp_in = normed_mlp.astype(jnp.bfloat16)
    pre_act = jnp.dot(mlp_in, w_up, preferred_element_type=jnp.float32) + bias_up
    activated, back_gelu = jax.vjp(lambda arr: jax.nn.gelu(arr, approximate=True), pre_act)
    act_low = activated.astype(jnp.bfloat16)
    branch_mlp = jnp.dot(act_low, w_down, preferred_element_type=jnp.float32) + bias_down
    post_mlp, back_post_mlp = jax.vjp(rms_norm, branch_mlp, gain_post_mlp)
    output = (hidden_res + post_mlp).astype(jnp.bfloat16)
    branch_rms = jnp.stack(
        [
            jnp.sqrt(jnp.mean(branch_attn * branch_attn, axis=-1) + eps),
            jnp.sqrt(jnp.mean(branch_mlp * branch_mlp, axis=-1) + eps),
        ]
    )
    grad_out_f = cotangent.astype(jnp.float32)
    grad_branch_mlp, grad_gain_post_mlp = back_post_mlp(grad_out_f)
    grad_mlp_low = grad_branch_mlp.astype(jnp.bfloat16)
    grad_bias_down = jnp.sum(grad_mlp_low.astype(jnp.float32), axis=0)
    grad_down = jnp.einsum("tf,td->df", act_low, grad_mlp_low, preferred_element_type=jnp.float32)
    grad_act = jnp.einsum("td,fd->tf", grad_mlp_low, w_down, preferred_element_type=jnp.float32)
    (grad_pre_act,) = back_gelu(grad_act)
    grad_pre_low = grad_pre_act.astype(jnp.bfloat16)
    grad_bias_up = jnp.sum(grad_pre_low.astype(jnp.float32), axis=0)
    grad_up = jnp.einsum("td,tf->fd", mlp_in, grad_pre_low, preferred_element_type=jnp.float32)
    grad_normed_mlp = jnp.einsum(
        "tf,df->td", grad_pre_low, w_up, preferred_element_type=jnp.float32
    )
    grad_res_part, grad_gain_pre_mlp = back_pre_mlp(grad_normed_mlp)
    grad_hidden = grad_out_f + grad_res_part
    grad_branch_attn, grad_gain_post_attn = back_post_attn(grad_hidden)
    grad_branch_low = grad_branch_attn.astype(jnp.bfloat16)
    grad_w_out = jnp.einsum(
        "td,te->ed", attn_low, grad_branch_low, preferred_element_type=jnp.float32
    )
    grad_attn = jnp.einsum("te,de->td", grad_branch_low, w_out, preferred_element_type=jnp.float32)
    grad_attn_low = grad_attn.astype(jnp.bfloat16).reshape(row_count, H, HD)
    delta = jnp.einsum("qhd,qhd->hq", grad_attn_low.astype(jnp.float32), attn_full)
    key_source, value_source = key_piece, value_piece
    width = math.gcd(group_rows, 512)

    def back_block(grad_query_acc, number):
        key_first = number * width

        def back_compute(grad_query_acc):
            keys_blk = lax.dynamic_slice_in_dim(key_source, key_first, width, 0).reshape(
                width, H, HD
            )
            values_blk = lax.dynamic_slice_in_dim(value_source, key_first, width, 0).reshape(
                width, H, HD
            )
            scores = (
                jnp.einsum(
                    "qhd,khd->hqk", queries_low, keys_blk, preferred_element_type=jnp.float32
                )
                * scale
            )
            allowed = block_mask(query_index, query_start, key_first, width)[None]
            probs = jnp.where(allowed, jnp.exp(scores - log_total[..., None]), 0.0)
            grad_probs = jnp.einsum(
                "qhd,khd->hqk", grad_attn_low, values_blk, preferred_element_type=jnp.float32
            )
            grad_scores = (probs * (grad_probs - delta[..., None])).astype(jnp.bfloat16)
            grad_query_acc = (
                grad_query_acc
                + jnp.einsum(
                    "hqk,khd->qhd", grad_scores, keys_blk, preferred_element_type=jnp.float32
                )
                * scale
            )
            grad_keys_blk = (
                jnp.einsum(
                    "hqk,qhd->khd", grad_scores, queries_low, preferred_element_type=jnp.float32
                )
                * scale
            )
            grad_values_blk = jnp.einsum(
                "hqk,qhd->khd",
                probs.astype(jnp.bfloat16),
                grad_attn_low,
                preferred_element_type=jnp.float32,
            )
            return (
                grad_query_acc,
                (grad_keys_blk.reshape(width, D), grad_values_blk.reshape(width, D)),
            )

        def skipped(grad_query_acc):
            return (
                grad_query_acc,
                (jnp.zeros((width, D), jnp.float32), jnp.zeros((width, D), jnp.float32)),
            )

        active = (key_first <= query_last) & (key_first + width - 1 >= start_least)
        return lax.cond(active, back_compute, skipped, grad_query_acc)

    grad_query_acc, stacked = lax.scan(
        back_block,
        jnp.zeros((row_count, H, HD), jnp.float32),
        jnp.arange(group_rows // width, dtype=jnp.int32),
    )
    grad_keys_all = stacked[0].reshape(group_rows, D)
    grad_values_all = stacked[1].reshape(group_rows, D)
    grad_keys_mine, grad_values_mine = (
        lax.psum_scatter(
            grad_keys_all.astype(jnp.bfloat16), "blk", scatter_dimension=0, tiled=True
        ).astype(jnp.float32),
        lax.psum_scatter(
            grad_values_all.astype(jnp.bfloat16), "blk", scatter_dimension=0, tiled=True
        ).astype(jnp.float32),
    )
    (grad_key_pre,) = back_rot_key(grad_keys_mine.reshape(row_count, H, HD))
    (grad_query_pre,) = back_rot_query(grad_query_acc)
    grad_key_low = grad_key_pre.reshape(row_count, D).astype(jnp.bfloat16)
    grad_query_low = grad_query_pre.reshape(row_count, D).astype(jnp.bfloat16)
    grad_value_low = grad_values_mine.astype(jnp.bfloat16)
    grad_query = jnp.einsum(
        "td,te->ed", attn_in, grad_query_low, preferred_element_type=jnp.float32
    )
    grad_key = jnp.einsum("td,te->ed", attn_in, grad_key_low, preferred_element_type=jnp.float32)
    grad_value = jnp.einsum(
        "td,te->ed", attn_in, grad_value_low, preferred_element_type=jnp.float32
    )
    grad_normed_in = (
        jnp.einsum("te,de->td", grad_query_low, w_query, preferred_element_type=jnp.float32)
        + jnp.einsum("te,de->td", grad_key_low, w_key, preferred_element_type=jnp.float32)
        + jnp.einsum("te,de->td", grad_value_low, w_value, preferred_element_type=jnp.float32)
    )
    grad_tokens_part, grad_gain_pre_attn = back_pre_attn(grad_normed_in)
    grad_tokens = (grad_hidden + grad_tokens_part).astype(jnp.bfloat16)
    count = lax.axis_size(("dp", "blk"))
    low = jnp.bfloat16
    pieces = [
        part.astype(low).reshape(count, -1, D)
        for part in (grad_query, grad_key, grad_value, grad_w_out, grad_up, grad_down)
    ]
    small = [
        part.reshape(count, -1)
        for part in (
            grad_bias_up,
            grad_bias_down,
            grad_gain_pre_attn,
            grad_gain_post_attn,
            grad_gain_pre_mlp,
            grad_gain_post_mlp,
        )
    ]
    sizes = [part.shape[1] for part in pieces]
    summed = lax.psum_scatter(
        jnp.concatenate(pieces, axis=1), ("dp", "blk"), scatter_dimension=0
    ).astype(jnp.float32)
    small_sizes = [part.shape[1] for part in small]
    small_flat = jnp.concatenate(small, axis=1)
    padding = -small_flat.shape[1] % 128
    small_flat = jnp.pad(small_flat, ((0, 0), (0, padding)))
    small_summed = lax.psum_scatter(small_flat, ("dp", "blk"), scatter_dimension=0)
    cuts = [sum(sizes[: i + 1]) for i in range(len(sizes) - 1)]
    parts = jnp.split(summed, cuts, axis=0)
    parts[5] = parts[5].reshape(D // count, -1)
    small_cuts = [sum(small_sizes[: i + 1]) for i in range(len(small_sizes))]
    small_parts = jnp.split(small_summed, small_cuts, axis=0)[:6]
    return (output, grad_tokens, *[part.T for part in parts], *small_parts, branch_rms)


MESH_ID = pl.DeviceIdType.MESH
F32 = jnp.float32
BF16 = jnp.bfloat16
TOK = 256
PACK = 512
FF = 4096
HALF_FF = 2048
HALF_D = 512
CHUNK = 32
VMEM_BYTES = 62 * 1024 * 1024


def mm(a, b):
    return jnp.dot(a, b, preferred_element_type=F32)


def mm_nt(a, b):
    return lax.dot_general(a, b, (((1,), (1,)), ((), ())), preferred_element_type=F32)


def al(offset, step):
    return pl.multiple_of(offset, step)


def norm_back(v, r, gain, grad):
    scaled = grad * gain
    inner = jnp.mean(v * scaled, axis=-1, keepdims=True)
    return r * scaled - v * (r * r * r * inner), jnp.sum(grad * v * r, axis=0, keepdims=True)


def inv_rms(v):
    return lax.rsqrt(jnp.mean(v * v, axis=-1, keepdims=True) + eps)


def layer_kernel(
    doc, tok, cot, gain_a, gain_b, gain_c, gain_d, bias_up, bias_down,
    wq_hbm, wk_hbm, wv_hbm, wo_hbm, wu_hbm, wd_hbm,
    out, grad_tok, rms, o_down, o_up, o_late, o_aux,
    wq, wk, wv, wo, wu, wd, xin, q_t, k_t, v_t, k_n, v_n, mask, attn_t, attn_nat, attn_oth,
    branch, hid, xm, act, g_t, part_send, part_recv, part_own, nat, gb_t, gba_t, ga_t,
    rope, lse, stat, s_down, r1_down, r2_down, r3_down, r1_up, r2_up, r3_up,
    r1_late, r2_late, r3_late, fin_down, fin_late, rec_down, rec_late, aux_s, aux_r,
    w_sem, c_send, c_recv, rs_send, rs_recv, a_send, a_recv,
):
    dp = lax.axis_index("dp")
    b = lax.axis_index("blk")
    x = lax.rem(dp, 2)
    y = lax.rem(dp // 2, 2)
    z = dp // 4
    other = 1 - b
    core_peer = (dp, other)
    x_peer = (dp + 1 - 2 * x, b)
    y_peer = (dp + 2 - 4 * y, b)

    def z_peer(step):
        return (lax.rem(z + step, 4) * 4 + y * 2 + x, b)

    barrier = pltpu.get_barrier_semaphore()
    for peer in (core_peer, x_peer, y_peer, z_peer(1), z_peer(2), z_peer(3)):
        pl.semaphore_signal(barrier, inc=1, device_id=peer, device_id_type=MESH_ID)

    own_cols = al(b * HALF_D, HALF_D)
    oth_cols = al(other * HALF_D, HALF_D)
    own_tok = al(b * TOK, TOK)
    oth_tok = al(other * TOK, TOK)

    w_copies = [
        pltpu.make_async_copy(src.at[:, pl.ds(own_cols, HALF_D)], dst, w_sem.at[i])
        for i, (src, dst) in enumerate(((wq_hbm, wq), (wk_hbm, wk), (wv_hbm, wv)))
    ]
    w_copies.append(pltpu.make_async_copy(wo_hbm, wo, w_sem.at[3]))
    for copy in w_copies:
        copy.start()

    def up_copy(j):
        return pltpu.make_async_copy(
            wu_hbm.at[:, pl.ds(al((2 * j + b) * 128, 128), 128)],
            wu.at[:, pl.ds(al(j * 128, 128), 128)],
            w_sem.at[4 + j],
        )

    def down_copy(j):
        return pltpu.make_async_copy(
            wd_hbm.at[pl.ds(al((2 * j + b) * 128, 128), 128)],
            wd.at[pl.ds(al(j * 128, 128), 128)],
            w_sem.at[20 + j],
        )

    lax.fori_loop(0, 16, lambda j, c: (up_copy(j).start(), c)[1], 0)
    lax.fori_loop(0, 16, lambda j, c: (down_copy(j).start(), c)[1], 0)

    def to_core(k, src, dst):
        return pltpu.make_async_remote_copy(
            src_ref=src, dst_ref=dst, send_sem=c_send.at[k], recv_sem=c_recv.at[k],
            device_id=core_peer, device_id_type=MESH_ID,
        )

    def pre_attn(i, carry):
        rows = pl.ds(al(i * CHUNK, CHUNK), CHUNK)
        v = tok[rows, :].astype(F32)
        xin[pl.ds(al(own_tok + i * CHUNK, CHUNK), CHUNK), :] = (
            v * inv_rms(v) * gain_a[...]
        ).astype(BF16)
        return carry

    lax.fori_loop(0, TOK // CHUNK, pre_attn, 0)
    pl.semaphore_wait(barrier, 6)
    own_rows = xin.at[pl.ds(own_tok, TOK)]
    xin_copy = to_core(0, own_rows, own_rows)
    xin_copy.start()

    end_a = doc[0, 0]
    end_b = end_a + doc[0, 1]
    end_c = end_b + doc[0, 2]
    index_row = lax.broadcasted_iota(jnp.int32, (1, PACK), 1)
    start_row = jnp.where(
        index_row >= end_c,
        end_c,
        jnp.where(index_row >= end_b, end_b, jnp.where(index_row >= end_a, end_a, 0)),
    )
    position = (index_row - start_row).astype(F32)
    freq = jnp.exp(
        lax.broadcasted_iota(jnp.int32, (32, PACK), 0).astype(F32) * (-math.log(10000.0) / 32.0)
    )
    angle = position * freq
    rope[0] = jnp.cos(angle)
    rope[1] = jnp.sin(angle)

    def fill_mask(i, carry):
        rows = pl.ds(al(i * 64, 64), 64)
        key_index = lax.broadcasted_iota(jnp.int32, (64, PACK), 0) + i * 64
        query_index = lax.broadcasted_iota(jnp.int32, (64, PACK), 1)
        allowed = (key_index <= query_index) & (key_index >= start_row)
        mask[rows, :] = jnp.where(allowed, 0.0, neg_big)
        return carry

    lax.fori_loop(0, 8, fill_mask, 0)

    def project(tok_at):
        rows = pl.ds(tok_at, TOK)
        cos = rope[0, :, rows]
        sin = rope[1, :, rows]
        x_rows = xin[rows, :]

        def turned(w, scale):
            flat = mm(x_rows, w[...]).T.reshape(8, 2, 32, TOK)
            low, high = flat[:, 0], flat[:, 1]
            both = jnp.stack([low * cos - high * sin, low * sin + high * cos], axis=1)
            return (both * scale).reshape(HALF_D, TOK).astype(BF16)

        q_t[:, rows] = turned(wq, 0.125)
        keys = turned(wk, 1.0)
        k_t[:, rows] = keys
        k_n[rows, :] = keys.T
        values = mm(x_rows, wv[...]).astype(BF16)
        v_n[rows, :] = values
        v_t[:, rows] = values.T

    for copy in w_copies[:3]:
        copy.wait()
    project(own_tok)
    xin_copy.wait()
    project(oth_tok)

    zeros = jnp.zeros((64, TOK), BF16)

    def slab(head_rows, which):
        return jnp.concatenate([head_rows, zeros] if which == 0 else [zeros, head_rows], axis=0)

    def attend(p, carry):
        slab_cols = pl.ds(al(p * 128, 128), 128)
        for which in range(2):
            rows = pl.ds(al(p * 128 + which * 64, 64), 64)
            for block in range(2):
                cols = slice(block * TOK, block * TOK + TOK)
                keys = (block + 1) * TOK
                scores = mm(k_n[:keys, slab_cols], slab(q_t[rows, cols], which)) + mask[:keys, cols]
                top = jnp.max(scores, axis=0, keepdims=True)
                weights = jnp.exp(scores - top)
                total = jnp.sum(weights, axis=0, keepdims=True)
                attn_t[rows, cols] = mm(v_t[rows, :keys], weights.astype(BF16)) * (1.0 / total)
                lse[pl.ds(p * 2 + which, 1), cols] = top + jnp.log(total)
        attn_nat[:, slab_cols] = attn_t[pl.ds(al(p * 128, 128), 128), :].T.astype(BF16)
        to_core(
            1 + p, attn_nat.at[pl.ds(oth_tok, TOK), slab_cols], attn_oth.at[:, slab_cols]
        ).start()
        return carry

    lax.fori_loop(0, 4, attend, 0)

    w_copies[3].wait()
    branch[...] = mm(attn_nat[pl.ds(own_tok, TOK), :], wo[pl.ds(own_cols, HALF_D), :])

    def attn_copy(p):
        cols = pl.ds(al(p * 128, 128), 128)
        return to_core(1 + p, attn_nat.at[pl.ds(oth_tok, TOK), cols], attn_oth.at[:, cols])

    lax.fori_loop(0, 4, lambda p, c: (attn_copy(p).wait(), c)[1], 0)
    branch[...] += mm(attn_oth[...], wo[pl.ds(oth_cols, HALF_D), :])

    def post_attn(i, carry):
        rows = pl.ds(al(i * CHUNK, CHUNK), CHUNK)
        v = branch[rows, :]
        square = jnp.mean(v * v, axis=-1, keepdims=True) + eps
        stat[0, rows, :] = jnp.broadcast_to(jnp.sqrt(square), (CHUNK, 128))
        h = tok[rows, :].astype(F32) + v * lax.rsqrt(square) * gain_b[...]
        hid[rows, :] = h
        xm[pl.ds(al(own_tok + i * CHUNK, CHUNK), CHUNK), :] = (
            h * inv_rms(h) * gain_c[...]
        ).astype(BF16)
        return carry

    lax.fori_loop(0, TOK // CHUNK, post_attn, 0)
    own_rows_m = xm.at[pl.ds(own_tok, TOK)]
    xm_copy = to_core(5, own_rows_m, own_rows_m)
    xm_copy.start()

    def up_step(tok_at, i):
        cols = pl.ds(al(i * 256, 256), 256)
        rows = pl.ds(tok_at, TOK)
        bias = jnp.concatenate(
            [bias_up[pl.ds(4 * i + b, 1), :], bias_up[pl.ds(4 * i + 2 + b, 1), :]], axis=1
        )
        pre = mm(xm[rows, :], wu[:, cols]) + bias
        square = pre * pre
        th = jnp.tanh(pre * (0.7978845608 + (0.7978845608 * 0.044715) * square))
        half = 0.5 + 0.5 * th
        act[rows, cols] = (pre * half).astype(BF16)
        slope = half + pre * (0.5 - 0.5 * th * th) * (
            0.7978845608 + (0.7978845608 * 0.134145) * square
        )
        g_t[cols, rows] = slope.astype(BF16).T

    lax.fori_loop(0, 16, lambda j, c: (up_copy(j).wait(), c)[1], 0)
    lax.fori_loop(0, 8, lambda i, c: (up_step(own_tok, i), c)[1], 0)
    xm_copy.wait()
    lax.fori_loop(0, 8, lambda i, c: (up_step(oth_tok, i), c)[1], 0)
    lax.fori_loop(0, 16, lambda j, c: (down_copy(j).wait(), c)[1], 0)

    def down_step(tok_at, dst, i):
        cols = pl.ds(al(i * 256, 256), 256)
        dst[:, cols] = mm(act[pl.ds(tok_at, TOK), :], wd[:, cols])

    lax.fori_loop(0, 4, lambda i, c: (down_step(oth_tok, part_send, i), c)[1], 0)
    mlp_copy = to_core(6, part_send, part_recv)
    mlp_copy.start()
    lax.fori_loop(0, 4, lambda i, c: (down_step(own_tok, part_own, i), c)[1], 0)
    mlp_copy.wait()

    def post_mlp(i, carry):
        sum_bias, sum_gain = carry
        rows = pl.ds(al(i * CHUNK, CHUNK), CHUNK)
        v = part_own[rows, :] + part_recv[rows, :] + bias_down[...]
        square = jnp.mean(v * v, axis=-1, keepdims=True) + eps
        stat[1, rows, :] = jnp.broadcast_to(jnp.sqrt(square), (CHUNK, 128))
        r = lax.rsqrt(square)
        out[rows, :] = (hid[rows, :] + v * r * gain_d[...]).astype(BF16)
        back, gain_part = norm_back(v, r, gain_d[...], cot[rows, :].astype(F32))
        back = back.astype(BF16)
        nat[rows, :] = back
        return (
            sum_bias + jnp.sum(back.astype(F32), axis=0, keepdims=True),
            sum_gain + gain_part,
        )

    zero_row = jnp.zeros((1, D), F32)
    sum_bias_down, sum_gain_d = lax.fori_loop(0, TOK // CHUNK, post_mlp, (zero_row, zero_row))
    aux_s[0] = jnp.zeros((16, D), F32)
    aux_s[0, 0:1, :] = sum_bias_down
    aux_s[0, 4:5, :] = sum_gain_d
    for i in range(2):
        rms[i : i + 1, :] = stat[i].T[0:1, :]

    def turn_to(dst):
        def step(i, carry):
            cols = pl.ds(al(i * 256, 256), 256)
            dst[cols, pl.ds(own_tok, TOK)] = nat[:, cols].T
            return carry

        lax.fori_loop(0, 4, step, 0)

    turn_to(gb_t)
    own_gb = gb_t.at[:, pl.ds(own_tok, TOK)]
    gb_copy = to_core(7, own_gb, own_gb)
    gb_copy.start()
    gb_copy.wait()

    jobs = (
        (0, s_down, r1_down, r2_down, r3_down, 0, 1024, 64, "x"),
        (1, s_down, r1_down, r2_down, r3_down, 1024, 1024, 64, "y"),
        (2, wd, r1_up, r2_up, r3_up, 0, 512, 128, "x"),
        (3, wd, r1_up, r2_up, r3_up, 512, 512, 128, "y"),
        (4, wu, r1_late, r2_late, r3_late, 0, 512, 64, "x"),
        (5, wu, r1_late, r2_late, r3_late, 512, 512, 64, "y"),
        (6, wu, r1_late, r2_late, r3_late, 1024, 512, 64, "x"),
        (7, wu, r1_late, r2_late, r3_late, 1536, 512, 64, "y"),
    )

    def axes(job):
        return (x, y, x_peer, y_peer) if job[8] == "x" else (y, x, y_peer, x_peer)

    def remote(job, k, src, dst, peer):
        return pltpu.make_async_remote_copy(
            src_ref=src, dst_ref=dst, send_sem=rs_send.at[job[0], k],
            recv_sem=rs_recv.at[job[0], k], device_id=peer, device_id_type=MESH_ID,
        )

    def send_one(job, k):
        n, s, r1, _, _, c0, width, rows, _ = job
        one, two, peer, _ = axes(job)
        second = lax.rem(two + 1 + k, 2)
        cols = pl.ds(c0, width)
        return remote(
            job, k,
            s.at[pl.ds(al(((1 - one) * 2 + second) * 4 * rows, 4 * rows), 4 * rows), cols],
            r1.at[pl.ds(al(second * 4 * rows, 4 * rows), 4 * rows), cols],
            peer,
        )

    def send_two(job):
        n, s, _, r2, _, c0, width, rows, _ = job
        one, two, _, peer = axes(job)
        cols = pl.ds(c0, width)
        return remote(
            job, 2,
            s.at[pl.ds(al((one * 2 + 1 - two) * 4 * rows, 4 * rows), 4 * rows), cols],
            r2.at[:, cols],
            peer,
        )

    def send_three(job, step):
        n, s, _, _, r3, c0, width, rows, _ = job
        one, two, _, _ = axes(job)
        cols = pl.ds(c0, width)
        target = lax.rem(z + step, 4)
        return remote(
            job, 2 + step,
            s.at[pl.ds(al((one * 2 + two) * 4 * rows + target * rows, rows), rows), cols],
            r3.at[pl.ds((step - 1) * rows, rows), cols],
            z_peer(step),
        )

    def weight_grad(job, first, last, lhs, rhs, rhs_at):
        n, s, _, _, _, c0, width, rows, axis = job
        one, two, _, _ = axes(job)

        def group(g, carry):
            i = lax.rem(one + 1 + g // 2, 2)
            j = lax.rem(two + 1 + lax.rem(g, 2), 2)
            base = j * 2 + i if axis == "x" else i * 2 + j
            left = jnp.concatenate(
                [lhs[pl.ds(al((4 * k + base) * rows, rows), rows), :] for k in range(4)], axis=0
            )
            at = pl.ds(al((i * 2 + j) * 4 * rows, 4 * rows), 4 * rows)
            for c in range(0, width, 512):
                right = rhs[:, pl.ds(al(rhs_at + c, 512), 512)]
                s[at, pl.ds(c0 + c, 512)] = mm(left, right).astype(BF16)
            return carry

        for g in range(first, last):
            group(g, 0)
            if g < 2:
                send_one(job, g).start()

    def add_rows(dst, dst_at, src, src_at, count, c0, width):
        def step(i, carry):
            to = pl.ds(al(dst_at + i * 64, 64), 64)
            got = src[pl.ds(al(src_at + i * 64, 64), 64), pl.ds(c0, width)]
            dst[to, pl.ds(c0, width)] = (
                dst[to, pl.ds(c0, width)].astype(F32) + got.astype(F32)
            ).astype(BF16)
            return carry

        lax.fori_loop(0, count // 64, step, 0)

    def serve_one(job):
        n, s, r1, _, _, c0, width, rows, _ = job
        one, two, _, _ = axes(job)
        for k in range(2):
            second = lax.rem(two + 1 + k, 2)
            send_one(job, k).wait_recv()
            add_rows(
                s, (one * 2 + second) * 4 * rows, r1, second * 4 * rows, 4 * rows, c0, width
            )
            if k == 0:
                send_two(job).start()

    def serve_two(job):
        n, s, _, r2, _, c0, width, rows, _ = job
        one, two, _, _ = axes(job)
        send_two(job).wait_recv()
        add_rows(s, (one * 2 + two) * 4 * rows, r2, 0, 4 * rows, c0, width)
        for step in range(1, 4):
            send_three(job, step).start()

    def serve_three(job, dst):
        n, s, _, _, r3, c0, width, rows, _ = job
        one, two, _, _ = axes(job)
        for step in range(1, 4):
            send_three(job, step).wait_recv()

        def add(i, carry):
            cols = pl.ds(c0, width)
            total = s[
                pl.ds(al((one * 2 + two) * 4 * rows + z * rows + i * 64, 64), 64), cols
            ].astype(F32)
            for step in range(3):
                total += r3[pl.ds(al(step * rows + i * 64, 64), 64), cols].astype(F32)
            dst[pl.ds(al(i * 64, 64), 64), cols] = total
            return carry

        lax.fori_loop(0, rows // 64, add, 0)

    def settle(job):
        for k in range(2):
            send_one(job, k).wait_send()
        send_two(job).wait_send()
        for step in range(1, 4):
            send_three(job, step).wait_send()

    for first, last in ((0, 2), (2, 4)):
        weight_grad(jobs[0], first, last, gb_t, act, 0)
        weight_grad(jobs[1], first, last, gb_t, act, 1024)

    def act_back(i, carry):
        rows = pl.ds(al(i * 256, 256), 256)
        g_t[rows, :] = (mm(wd[rows, :], gb_t[...]) * g_t[rows, :].astype(F32)).astype(BF16)
        return carry

    lax.fori_loop(0, 8, act_back, 0)
    for first, last in ((0, 2), (2, 4)):
        weight_grad(jobs[2], first, last, g_t, xm, 0)
        weight_grad(jobs[3], first, last, g_t, xm, 512)
    ones = jnp.ones((16, PACK), BF16)
    for i in range(2):
        aux_s[0, pl.ds(5 + 2 * b + i, 1), :] = mm_nt(ones, g_t[i * 1024 : i * 1024 + 1024, :])[0:1]

    def mlp_back(tok_at, dst, i):
        at = pl.ds(al(i * 256, 256), 256)
        dst[:, at] = mm(wu[at, :], g_t[:, pl.ds(tok_at, TOK)]).T

    lax.fori_loop(0, 4, lambda i, c: (mlp_back(oth_tok, part_send, i), c)[1], 0)
    mlp_back_copy = to_core(8, part_send, part_recv)
    mlp_back_copy.start()
    lax.fori_loop(0, 4, lambda i, c: (mlp_back(own_tok, part_own, i), c)[1], 0)
    mlp_back_copy.wait()

    def hidden_back(i, carry):
        sum_c, sum_b = carry
        rows = pl.ds(al(i * CHUNK, CHUNK), CHUNK)
        h = hid[rows, :]
        back, part_c = norm_back(
            h, inv_rms(h), gain_c[...], part_own[rows, :] + part_recv[rows, :]
        )
        g_hidden = cot[rows, :].astype(F32) + back
        hid[rows, :] = g_hidden
        v = branch[rows, :]
        back, part_b = norm_back(v, inv_rms(v), gain_b[...], g_hidden)
        nat[rows, :] = back.astype(BF16)
        return sum_c + part_c, sum_b + part_b

    sum_gain_c, sum_gain_b = lax.fori_loop(0, TOK // CHUNK, hidden_back, (zero_row, zero_row))
    aux_s[0, 3:4, :] = sum_gain_c
    aux_s[0, 2:3, :] = sum_gain_b
    turn_to(gba_t)
    own_gba = gba_t.at[:, pl.ds(own_tok, TOK)]
    gba_copy = to_core(9, own_gba, own_gba)
    gba_copy.start()
    gba_copy.wait()

    weight_grad(jobs[4], 0, 4, gba_t, attn_nat, 0)
    ga_t[...] = mm(wo[pl.ds(own_cols, HALF_D), :], gba_t[...]).astype(BF16)
    serve_one(jobs[0])
    serve_one(jobs[1])

    gq, gk, gv = g_t.at[pl.ds(0, D)], g_t.at[pl.ds(D, D)], gb_t

    def attend_back(p, carry):
        slab_cols = pl.ds(al(p * 128, 128), 128)
        for which in range(2):
            rows = pl.ds(al(p * 128 + which * 64, 64), 64)
            to = pl.ds(al(own_cols + p * 128 + which * 64, 64), 64)
            grads_k, grads_v, grads_q = [], [], []
            for block in range(2):
                cols = slice(block * TOK, block * TOK + TOK)
                keys = (block + 1) * TOK
                q_rows = q_t[rows, cols]
                g_rows = ga_t[rows, cols]
                delta = jnp.sum(g_rows.astype(F32) * attn_t[rows, cols], axis=0, keepdims=True)
                scores = mm(k_n[:keys, slab_cols], slab(q_rows, which)) + mask[:keys, cols]
                probs = jnp.exp(scores - lse[pl.ds(p * 2 + which, 1), cols])
                g_probs = mm(v_n[:keys, slab_cols], slab(g_rows, which))
                g_scores = (probs * (g_probs - delta)).astype(BF16)
                grads_q.append(mm(k_t[rows, :keys], g_scores) * 0.125)
                grads_k.append(mm_nt(q_rows, g_scores))
                grads_v.append(mm_nt(g_rows, probs.astype(BF16)))
            for parts, dst in ((grads_q, gq), (grads_k, gk)):
                if dst is gq:
                    full = jnp.concatenate(parts, axis=1)
                else:
                    full = jnp.concatenate(
                        [parts[0] + parts[1][:, :TOK], parts[1][:, TOK:]], axis=1
                    )
                low, high = full[:32], full[32:]
                cos, sin = rope[0], rope[1]
                dst[to, :] = jnp.concatenate(
                    [low * cos + high * sin, high * cos - low * sin], axis=0
                ).astype(BF16)
            gv[to, :] = jnp.concatenate(
                [grads_v[0] + grads_v[1][:, :TOK], grads_v[1][:, TOK:]], axis=1
            ).astype(BF16)
        return carry

    lax.fori_loop(0, 4, attend_back, 0)
    own_heads = pl.ds(own_cols, HALF_D)
    head_copies = [
        to_core(10 + i, ref.at[own_heads], ref.at[own_heads]) for i, ref in enumerate((gq, gk, gv))
    ]
    for copy in head_copies:
        copy.start()
    serve_one(jobs[2])
    serve_one(jobs[3])

    def in_back(tok_at, dst, i):
        at = pl.ds(al(i * 256, 256), 256)
        cols = pl.ds(tok_at, TOK)
        total = mm(wq[at, :], gq[own_heads, cols])
        total += mm(wk[at, :], gk[own_heads, cols])
        total += mm(wv[at, :], gv[own_heads, cols])
        dst[:, at] = total.T

    lax.fori_loop(0, 4, lambda i, c: (in_back(oth_tok, part_send, i), c)[1], 0)
    in_back_copy = to_core(13, part_send, part_recv)
    in_back_copy.start()
    for copy in head_copies:
        copy.wait()
    for first, last in ((0, 2), (2, 4)):
        for job, lhs in zip(jobs[5:], (gq, gk, gv)):
            weight_grad(job, first, last, lhs, xin, own_cols)
    lax.fori_loop(0, 4, lambda i, c: (in_back(own_tok, part_own, i), c)[1], 0)
    in_back_copy.wait()

    def token_back(i, carry):
        rows = pl.ds(al(i * CHUNK, CHUNK), CHUNK)
        v = tok[rows, :].astype(F32)
        back, part_a = norm_back(
            v, inv_rms(v), gain_a[...], part_own[rows, :] + part_recv[rows, :]
        )
        grad_tok[rows, :] = (hid[rows, :] + back).astype(BF16)
        return carry + part_a

    aux_s[0, 1:2, :] = lax.fori_loop(0, TOK // CHUNK, token_back, zero_row)

    z_low = (dp + 4 - 8 * lax.rem(z, 2), b)
    z_high = z_peer(2)
    aux_copies = []

    def aux_start(k, peer):
        copy = pltpu.make_async_remote_copy(
            src_ref=aux_s.at[k], dst_ref=aux_r.at[k], send_sem=a_send.at[k],
            recv_sem=a_recv.at[k], device_id=peer, device_id_type=MESH_ID,
        )
        copy.start()
        aux_copies.append(copy)

    def aux_end(k):
        aux_copies[k].wait_recv()
        aux_s[k + 1] = aux_s[k] + aux_r[k]

    aux_start(0, core_peer)
    serve_two(jobs[0])
    serve_two(jobs[1])
    aux_end(0)
    aux_start(1, x_peer)
    serve_one(jobs[4])
    aux_end(1)
    aux_start(2, y_peer)
    serve_one(jobs[5])
    aux_end(2)
    aux_start(3, z_low)
    serve_two(jobs[2])
    aux_end(3)
    aux_start(4, z_high)
    serve_two(jobs[3])
    aux_end(4)
    o_aux[...] = aux_s[5]
    serve_three(jobs[0], fin_down)
    serve_three(jobs[1], fin_down)
    oth_cut = pl.ds(al(other * 32, 32), 32)
    own_cut = pl.ds(al(b * 32, 32), 32)
    down_final = to_core(14, fin_down.at[oth_cut], rec_down)
    down_final.start()
    serve_one(jobs[6])
    serve_one(jobs[7])
    serve_two(jobs[4])
    serve_two(jobs[5])
    serve_three(jobs[2], o_up)
    serve_three(jobs[3], o_up)
    down_final.wait()

    def place_down(j, carry):
        from_cols = pl.ds(al(j * 128, 128), 128)
        o_down[:, pl.ds(al((2 * j + b) * 128, 128), 128)] = fin_down[own_cut, from_cols]
        o_down[:, pl.ds(al((2 * j + other) * 128, 128), 128)] = rec_down[:, from_cols]
        return carry

    lax.fori_loop(0, 16, place_down, 0)
    serve_two(jobs[6])
    serve_two(jobs[7])
    for job in jobs[4:]:
        serve_three(job, fin_late)
    late_final = to_core(15, fin_late.at[oth_cut], rec_late)
    late_final.start()
    for job in jobs:
        settle(job)
    for copy in aux_copies:
        copy.wait_send()
    late_final.wait()
    for i in range(4):
        cols = slice(i * 512, i * 512 + 512)
        o_late[i, :, pl.ds(own_cols, HALF_D)] = fin_late[own_cut, cols]
        o_late[i, :, pl.ds(oth_cols, HALF_D)] = rec_late[:, cols]


def layer_on_device(
    tokens, doc_lengths, w_query, w_key, w_value, w_out, w_up, w_down, bias_up, bias_down,
    gain_pre_attn, gain_post_attn, gain_pre_mlp, gain_post_mlp, cotangent,
):
    def v16(*shape):
        return pltpu.VMEM(shape, BF16)

    def v32(*shape):
        return pltpu.VMEM(shape, F32)

    dma = pltpu.SemaphoreType.DMA
    vmem = pl.BlockSpec(memory_space=pltpu.VMEM)
    scratch = [
        v16(1024, 512), v16(1024, 512), v16(1024, 512), v16(1024, 1024),
        v16(1024, 2048), v16(2048, 1024),
        v16(512, 1024),
        v16(512, 512), v16(512, 512), v16(512, 512), v16(512, 512), v16(512, 512),
        v32(512, 512), v32(512, 512), v16(512, 512), v16(256, 512),
        v32(256, 1024), v32(256, 1024), v16(512, 1024),
        v16(512, 2048), v16(2048, 512),
        v32(256, 1024), v32(256, 1024), v32(256, 1024), v16(256, 1024),
        v16(1024, 512), v16(1024, 512), v16(512, 512),
        v32(2, 32, 512), v32(8, 512), v32(2, 256, 128),
        v16(1024, 2048), v16(512, 2048), v16(256, 2048), v16(192, 2048),
        v16(1024, 1024), v16(512, 1024), v16(384, 1024),
        v16(512, 2048), v16(256, 2048), v16(192, 2048),
        v32(64, 2048), v32(64, 2048), v32(32, 2048), v32(32, 2048),
        v32(6, 16, 1024), v32(5, 16, 1024),
        dma((36,)), dma((16,)), dma((16,)), dma((8, 6)), dma((8, 6)), dma((5,)), dma((5,)),
    ]
    out, grad_tok, rms, down, up, late, aux = pl.pallas_call(
        layer_kernel,
        out_shape=(
            jax.ShapeDtypeStruct((TOK, D), BF16),
            jax.ShapeDtypeStruct((TOK, D), BF16),
            jax.ShapeDtypeStruct((2, TOK), F32),
            jax.ShapeDtypeStruct((32, FF), F32),
            jax.ShapeDtypeStruct((128, D), F32),
            jax.ShapeDtypeStruct((4, 32, D), F32),
            jax.ShapeDtypeStruct((16, D), F32),
        ),
        in_specs=[pl.BlockSpec(memory_space=pltpu.SMEM)]
        + [vmem] * 8
        + [pl.BlockSpec(memory_space=pl.ANY)] * 6,
        out_specs=[vmem] * 7,
        scratch_shapes=scratch,
        compiler_params=pltpu.CompilerParams(
            collective_id=0, has_side_effects=True, vmem_limit_bytes=VMEM_BYTES
        ),
    )(
        doc_lengths, tokens, cotangent,
        gain_pre_attn[None], gain_post_attn[None], gain_pre_mlp[None], gain_post_mlp[None],
        bias_up.reshape(32, 128), bias_down[None],
        w_query, w_key, w_value, w_out, w_up, w_down,
    )
    dp = lax.axis_index("dp")
    b = lax.axis_index("blk")
    at = (dp * 2 + b) * 32
    small = lax.dynamic_slice(aux, (0, at), (5, 32))
    bias_rows = lax.dynamic_slice(
        aux, (5 + 2 * b + dp // 8, lax.rem(dp, 8) * 128), (1, 128)
    )[0]
    return (
        out, grad_tok, late[1].T, late[2].T, late[3].T, late[0].T, up.T, down.T,
        bias_rows, small[0], small[1], small[2], small[3], small[4], rms,
    )


def solution(mesh):
    placed = (
        P(("dp", "blk"), None),
        P("dp", None),
        P(),
        P(),
        P(),
        P(),
        P(),
        P(),
        P(),
        P(),
        P(),
        P(),
        P(),
        P(),
        P(("dp", "blk"), None),
    )
    paired = mesh.shape["blk"] == 2 and mesh.shape["dp"] == 16
    return jax.shard_map(
        layer_on_device if paired else on_device,
        mesh=mesh,
        in_specs=placed,
        out_specs=(
            P(("dp", "blk"), None),
            P(("dp", "blk"), None),
            P(None, ("dp", "blk")),
            P(None, ("dp", "blk")),
            P(None, ("dp", "blk")),
            P(None, ("dp", "blk")),
            P(None, ("dp", "blk")),
            P(None, ("dp", "blk")),
            P(("dp", "blk")),
            P(("dp", "blk")),
            P(("dp", "blk")),
            P(("dp", "blk")),
            P(("dp", "blk")),
            P(("dp", "blk")),
            P(None, ("dp", "blk")),
        ),
        check_vma=False,
    )
```

```python
import math

import jax
import jax.numpy as jnp
from jax import lax
from jax.experimental import pallas as pl
from jax.experimental.pallas import tpu as pltpu
from jax.sharding import PartitionSpec as P

D = 1024
H = 16
HD = 64


eps = 1e-06
neg_big = -1e30


def rms_norm(values, gain_row):
    return values * lax.rsqrt(jnp.mean(values * values, axis=-1, keepdims=True) + eps) * gain_row


def rotate(head_rows, position):
    half_size = head_rows.shape[-1] // 2
    frequency = 10000.0 ** (-2.0 * jnp.arange(half_size, dtype=jnp.float32) / head_rows.shape[-1])
    angles = position.astype(jnp.float32)[:, None] * frequency[None, :]
    cosine = jnp.cos(angles)[:, None, :]
    sine_part = jnp.sin(angles)[:, None, :]
    low_half = head_rows[..., :half_size]
    high_half = head_rows[..., half_size:]
    return jnp.concatenate(
        [low_half * cosine - high_half * sine_part, low_half * sine_part + high_half * cosine],
        axis=-1,
    )


def doc_layout(lengths, total_rows):
    index_row = jnp.arange(total_rows, dtype=jnp.int32)
    doc_ends = jnp.stack(
        [
            lengths[0],
            lengths[0] + lengths[1],
            lengths[0] + lengths[1] + lengths[2],
            lengths[0] + lengths[1] + lengths[2] + lengths[3],
        ]
    )
    segment = jnp.sum((index_row[:, None] >= doc_ends[None, :3]).astype(jnp.int32), axis=1)
    starts = doc_ends - lengths
    matches = segment[:, None] == jnp.arange(4, dtype=jnp.int32)[None, :]
    return (index_row, jnp.sum(jnp.where(matches, starts[None, :], 0), axis=1))


def block_mask(query_index, query_start, key_first, width):
    key_index = key_first + jnp.arange(width, dtype=jnp.int32)
    return (key_index[None, :] <= query_index[:, None]) & (
        key_index[None, :] >= query_start[:, None]
    )


def on_device(
    tokens,
    doc_lengths,
    w_query,
    w_key,
    w_value,
    w_out,
    w_up,
    w_down,
    bias_up,
    bias_down,
    gain_pre_attn,
    gain_post_attn,
    gain_pre_mlp,
    gain_post_mlp,
    cotangent,
):
    row_count = tokens.shape[0]
    cycle_size = lax.axis_size("blk")
    group_rows = row_count * cycle_size
    first_row = lax.axis_index("blk") * row_count
    index_all, start_all = doc_layout(doc_lengths[0], group_rows)
    query_index = lax.dynamic_slice_in_dim(index_all, first_row, row_count)
    query_start = lax.dynamic_slice_in_dim(start_all, first_row, row_count)
    position = query_index - query_start
    query_last = first_row + row_count - 1
    start_least = jnp.min(query_start)
    scale = HD ** (-0.5)
    tokens_f = tokens.astype(jnp.float32)
    normed_in, back_pre_attn = jax.vjp(rms_norm, tokens_f, gain_pre_attn)
    attn_in = normed_in.astype(jnp.bfloat16)
    query_pre = jnp.dot(attn_in, w_query, preferred_element_type=jnp.float32)
    key_pre = jnp.dot(attn_in, w_key, preferred_element_type=jnp.float32)
    value_pre = jnp.dot(attn_in, w_value, preferred_element_type=jnp.float32)
    queries, back_rot_query = jax.vjp(
        lambda arr: rotate(arr, position), query_pre.reshape(row_count, H, HD)
    )
    keys_rot, back_rot_key = jax.vjp(
        lambda arr: rotate(arr, position), key_pre.reshape(row_count, H, HD)
    )
    queries_low = queries.astype(jnp.bfloat16)
    keys_low = keys_rot.reshape(row_count, D).astype(jnp.bfloat16)
    values_low = value_pre.astype(jnp.bfloat16)
    initial = (
        jnp.full((H, row_count), neg_big, jnp.float32),
        jnp.zeros((H, row_count), jnp.float32),
        jnp.zeros((row_count, H, HD), jnp.float32),
    )
    key_piece = lax.all_gather(keys_low, "blk", axis=0, tiled=True)
    value_piece = lax.all_gather(values_low, "blk", axis=0, tiled=True)
    piece_rows = key_piece.shape[0]
    fold_width = math.gcd(piece_rows, 512)

    def one_block(state, number):
        key_first = number * fold_width

        def one_compute(state):
            running_top, totals, accum = state
            keys_blk = lax.dynamic_slice_in_dim(
                key_piece, number * fold_width, fold_width, 0
            ).reshape(fold_width, H, HD)
            values_blk = lax.dynamic_slice_in_dim(
                value_piece, number * fold_width, fold_width, 0
            ).reshape(fold_width, H, HD)
            scores = (
                jnp.einsum(
                    "qhd,khd->hqk", queries_low, keys_blk, preferred_element_type=jnp.float32
                )
                * scale
            )
            allowed = block_mask(query_index, query_start, key_first, fold_width)[None]
            scores = jnp.where(allowed, scores, neg_big)
            new_top = jnp.maximum(running_top, jnp.max(scores, axis=-1))
            weights = jnp.where(allowed, jnp.exp(scores - new_top[..., None]), 0.0)
            factor = jnp.exp(running_top - new_top)
            totals = totals * factor + jnp.sum(weights, axis=-1)
            accum = accum * jnp.transpose(factor)[:, :, None] + jnp.einsum(
                "hqk,khd->qhd",
                weights.astype(jnp.bfloat16),
                values_blk,
                preferred_element_type=jnp.float32,
            )
            return (new_top, totals, accum)

        active = (key_first <= query_last) & (key_first + fold_width - 1 >= start_least)
        return (lax.cond(active, one_compute, lambda state: state, state), None)

    result, unused = lax.scan(
        one_block, initial, jnp.arange(piece_rows // fold_width, dtype=jnp.int32)
    )
    running_top, totals, accum = result
    attn_full = accum / jnp.transpose(totals)[:, :, None]
    log_total = running_top + jnp.log(totals)
    attn_low = attn_full.reshape(row_count, D).astype(jnp.bfloat16)
    branch_attn = jnp.dot(attn_low, w_out, preferred_element_type=jnp.float32)
    post_attn, back_post_attn = jax.vjp(rms_norm, branch_attn, gain_post_attn)
    hidden_res = tokens_f + post_attn
    normed_mlp, back_pre_mlp = jax.vjp(rms_norm, hidden_res, gain_pre_mlp)
    mlp_in = normed_mlp.astype(jnp.bfloat16)
    pre_act = jnp.dot(mlp_in, w_up, preferred_element_type=jnp.float32) + bias_up
    activated, back_gelu = jax.vjp(lambda arr: jax.nn.gelu(arr, approximate=True), pre_act)
    act_low = activated.astype(jnp.bfloat16)
    branch_mlp = jnp.dot(act_low, w_down, preferred_element_type=jnp.float32) + bias_down
    post_mlp, back_post_mlp = jax.vjp(rms_norm, branch_mlp, gain_post_mlp)
    output = (hidden_res + post_mlp).astype(jnp.bfloat16)
    branch_rms = jnp.stack(
        [
            jnp.sqrt(jnp.mean(branch_attn * branch_attn, axis=-1) + eps),
            jnp.sqrt(jnp.mean(branch_mlp * branch_mlp, axis=-1) + eps),
        ]
    )
    grad_out_f = cotangent.astype(jnp.float32)
    grad_branch_mlp, grad_gain_post_mlp = back_post_mlp(grad_out_f)
    grad_mlp_low = grad_branch_mlp.astype(jnp.bfloat16)
    grad_bias_down = jnp.sum(grad_mlp_low.astype(jnp.float32), axis=0)
    grad_down = jnp.einsum("tf,td->df", act_low, grad_mlp_low, preferred_element_type=jnp.float32)
    grad_act = jnp.einsum("td,fd->tf", grad_mlp_low, w_down, preferred_element_type=jnp.float32)
    (grad_pre_act,) = back_gelu(grad_act)
    grad_pre_low = grad_pre_act.astype(jnp.bfloat16)
    grad_bias_up = jnp.sum(grad_pre_low.astype(jnp.float32), axis=0)
    grad_up = jnp.einsum("td,tf->fd", mlp_in, grad_pre_low, preferred_element_type=jnp.float32)
    grad_normed_mlp = jnp.einsum(
        "tf,df->td", grad_pre_low, w_up, preferred_element_type=jnp.float32
    )
    grad_res_part, grad_gain_pre_mlp = back_pre_mlp(grad_normed_mlp)
    grad_hidden = grad_out_f + grad_res_part
    grad_branch_attn, grad_gain_post_attn = back_post_attn(grad_hidden)
    grad_branch_low = grad_branch_attn.astype(jnp.bfloat16)
    grad_w_out = jnp.einsum(
        "td,te->ed", attn_low, grad_branch_low, preferred_element_type=jnp.float32
    )
    grad_attn = jnp.einsum("te,de->td", grad_branch_low, w_out, preferred_element_type=jnp.float32)
    grad_attn_low = grad_attn.astype(jnp.bfloat16).reshape(row_count, H, HD)
    delta = jnp.einsum("qhd,qhd->hq", grad_attn_low.astype(jnp.float32), attn_full)
    key_source, value_source = key_piece, value_piece
    width = math.gcd(group_rows, 512)

    def back_block(grad_query_acc, number):
        key_first = number * width

        def back_compute(grad_query_acc):
            keys_blk = lax.dynamic_slice_in_dim(key_source, key_first, width, 0).reshape(
                width, H, HD
            )
            values_blk = lax.dynamic_slice_in_dim(value_source, key_first, width, 0).reshape(
                width, H, HD
            )
            scores = (
                jnp.einsum(
                    "qhd,khd->hqk", queries_low, keys_blk, preferred_element_type=jnp.float32
                )
                * scale
            )
            allowed = block_mask(query_index, query_start, key_first, width)[None]
            probs = jnp.where(allowed, jnp.exp(scores - log_total[..., None]), 0.0)
            grad_probs = jnp.einsum(
                "qhd,khd->hqk", grad_attn_low, values_blk, preferred_element_type=jnp.float32
            )
            grad_scores = (probs * (grad_probs - delta[..., None])).astype(jnp.bfloat16)
            grad_query_acc = (
                grad_query_acc
                + jnp.einsum(
                    "hqk,khd->qhd", grad_scores, keys_blk, preferred_element_type=jnp.float32
                )
                * scale
            )
            grad_keys_blk = (
                jnp.einsum(
                    "hqk,qhd->khd", grad_scores, queries_low, preferred_element_type=jnp.float32
                )
                * scale
            )
            grad_values_blk = jnp.einsum(
                "hqk,qhd->khd",
                probs.astype(jnp.bfloat16),
                grad_attn_low,
                preferred_element_type=jnp.float32,
            )
            return (
                grad_query_acc,
                (grad_keys_blk.reshape(width, D), grad_values_blk.reshape(width, D)),
            )

        def skipped(grad_query_acc):
            return (
                grad_query_acc,
                (jnp.zeros((width, D), jnp.float32), jnp.zeros((width, D), jnp.float32)),
            )

        active = (key_first <= query_last) & (key_first + width - 1 >= start_least)
        return lax.cond(active, back_compute, skipped, grad_query_acc)

    grad_query_acc, stacked = lax.scan(
        back_block,
        jnp.zeros((row_count, H, HD), jnp.float32),
        jnp.arange(group_rows // width, dtype=jnp.int32),
    )
    grad_keys_all = stacked[0].reshape(group_rows, D)
    grad_values_all = stacked[1].reshape(group_rows, D)
    grad_keys_mine, grad_values_mine = (
        lax.psum_scatter(
            grad_keys_all.astype(jnp.bfloat16), "blk", scatter_dimension=0, tiled=True
        ).astype(jnp.float32),
        lax.psum_scatter(
            grad_values_all.astype(jnp.bfloat16), "blk", scatter_dimension=0, tiled=True
        ).astype(jnp.float32),
    )
    (grad_key_pre,) = back_rot_key(grad_keys_mine.reshape(row_count, H, HD))
    (grad_query_pre,) = back_rot_query(grad_query_acc)
    grad_key_low = grad_key_pre.reshape(row_count, D).astype(jnp.bfloat16)
    grad_query_low = grad_query_pre.reshape(row_count, D).astype(jnp.bfloat16)
    grad_value_low = grad_values_mine.astype(jnp.bfloat16)
    grad_query = jnp.einsum(
        "td,te->ed", attn_in, grad_query_low, preferred_element_type=jnp.float32
    )
    grad_key = jnp.einsum("td,te->ed", attn_in, grad_key_low, preferred_element_type=jnp.float32)
    grad_value = jnp.einsum(
        "td,te->ed", attn_in, grad_value_low, preferred_element_type=jnp.float32
    )
    grad_normed_in = (
        jnp.einsum("te,de->td", grad_query_low, w_query, preferred_element_type=jnp.float32)
        + jnp.einsum("te,de->td", grad_key_low, w_key, preferred_element_type=jnp.float32)
        + jnp.einsum("te,de->td", grad_value_low, w_value, preferred_element_type=jnp.float32)
    )
    grad_tokens_part, grad_gain_pre_attn = back_pre_attn(grad_normed_in)
    grad_tokens = (grad_hidden + grad_tokens_part).astype(jnp.bfloat16)
    count = lax.axis_size(("dp", "blk"))
    low = jnp.bfloat16
    pieces = [
        part.astype(low).reshape(count, -1, D)
        for part in (grad_query, grad_key, grad_value, grad_w_out, grad_up, grad_down)
    ]
    small = [
        part.reshape(count, -1)
        for part in (
            grad_bias_up,
            grad_bias_down,
            grad_gain_pre_attn,
            grad_gain_post_attn,
            grad_gain_pre_mlp,
            grad_gain_post_mlp,
        )
    ]
    sizes = [part.shape[1] for part in pieces]
    summed = lax.psum_scatter(
        jnp.concatenate(pieces, axis=1), ("dp", "blk"), scatter_dimension=0
    ).astype(jnp.float32)
    small_sizes = [part.shape[1] for part in small]
    small_flat = jnp.concatenate(small, axis=1)
    padding = -small_flat.shape[1] % 128
    small_flat = jnp.pad(small_flat, ((0, 0), (0, padding)))
    small_summed = lax.psum_scatter(small_flat, ("dp", "blk"), scatter_dimension=0)
    cuts = [sum(sizes[: i + 1]) for i in range(len(sizes) - 1)]
    parts = jnp.split(summed, cuts, axis=0)
    parts[5] = parts[5].reshape(D // count, -1)
    small_cuts = [sum(small_sizes[: i + 1]) for i in range(len(small_sizes))]
    small_parts = jnp.split(small_summed, small_cuts, axis=0)[:6]
    return (output, grad_tokens, *[part.T for part in parts], *small_parts, branch_rms)


MESH_ID = pl.DeviceIdType.MESH
F32 = jnp.float32
BF16 = jnp.bfloat16
TOK = 256
PACK = 512
FF = 4096
HALF_FF = 2048
HALF_D = 512
CHUNK = 32
VMEM_BYTES = 62 * 1024 * 1024
UNIT_ORDER = (
    "wvxy",
    "xywv",
    "yxwv",
    "wvxy",
    "yxwv",
    "wvyx",
    "xywv",
    "yxwv",
    "yxwv",
    "xywv",
    "xywv",
    "yxwv",
)
SLOTS = (
    (0, 1, 10, 11, 20, 21,),
    (),
    (),
    (),
    (),
    (),
    (30, 31, 40, 41, 60, 61,),
    (2, 3, 12, 13, 22, 23,),
    (),
    (),
    (),
    (),
    (70,),
    (50, 90, 62, 91, 63, 42, 43, 51, 32, 33, 24, 4, 14,),
    (),
    (),
    (71, 72, 80, 64,),
    (5, 25, 15, 92,),
    (6, 100, 93, 44,),
    (73, 52, 81, 82,),
    (26, 74, 16, 65,),
    (53, 34, 110, 94, 102, 83, 66, 101, 45, 84, 35, 75, 103, 111, 36,),
    (112, 46, 95, 104, 76, 85, 54, 113, 114, 96, 55, 86, 105, 56, 115, 106, 116,),
)


def mm(a, b):
    return jnp.dot(a, b, preferred_element_type=F32)


def mm_nt(a, b):
    return lax.dot_general(a, b, (((1,), (1,)), ((), ())), preferred_element_type=F32)


def al(offset, step):
    return pl.multiple_of(offset, step)


def norm_back(v, r, gain, grad):
    scaled = grad * gain
    inner = jnp.mean(v * scaled, axis=-1, keepdims=True)
    return r * scaled - v * (r * r * r * inner), jnp.sum(grad * v * r, axis=0, keepdims=True)


def inv_rms(v):
    return lax.rsqrt(jnp.mean(v * v, axis=-1, keepdims=True) + eps)


def layer_kernel(
    doc, tok, cot, gain_a, gain_b, gain_c, gain_d, bias_up, bias_down,
    wq_hbm, wk_hbm, wv_hbm, wo_hbm, wu_hbm, wd_hbm,
    out, grad_tok, rms, o_down, o_up, o_late, o_aux,
    wq, wk, wv, wo, wu, wd, xin, q_t, k_t, v_t, k_n, v_n, mask, attn_t, attn_nat, attn_oth,
    branch, hid, xm, act, g_t, part_send, part_recv, part_own, nat, gb_t, gba_t, ga_t,
    rope, lse, stat, s_down, r1_down, r2_down, r3_down, r4_down, r1_up, r2_up, r3_up, r4_up,
    r1_late, r2_late, r3_late, r4_late, fin_down, fin_late, rec_down, rec_late, aux_s, aux_r,
    w_sem, c_send, c_recv, rs_send, rs_recv, a_send, a_recv,
):
    dp = lax.axis_index("dp")
    b = lax.axis_index("blk")
    x = lax.rem(dp, 2)
    y = lax.rem(dp // 2, 2)
    z = dp // 4
    other = 1 - b
    core_peer = (dp, other)
    x_peer = (dp + 1 - 2 * x, b)
    y_peer = (dp + 2 - 4 * y, b)

    z_low = (dp + 4 - 8 * lax.rem(z, 2), b)
    z_high = (dp + 8 - 16 * (z // 2), b)
    barrier = pltpu.get_barrier_semaphore()
    for peer in (core_peer, x_peer, y_peer, z_low, z_high):
        pl.semaphore_signal(barrier, inc=1, device_id=peer, device_id_type=MESH_ID)

    own_cols = al(b * HALF_D, HALF_D)
    oth_cols = al(other * HALF_D, HALF_D)
    own_tok = al(b * TOK, TOK)
    oth_tok = al(other * TOK, TOK)

    w_copies = [
        pltpu.make_async_copy(src.at[:, pl.ds(own_cols, HALF_D)], dst, w_sem.at[i])
        for i, (src, dst) in enumerate(((wq_hbm, wq), (wk_hbm, wk), (wv_hbm, wv)))
    ]
    w_copies.append(pltpu.make_async_copy(wo_hbm, wo, w_sem.at[3]))
    for copy in w_copies:
        copy.start()

    def up_copy(j):
        return pltpu.make_async_copy(
            wu_hbm.at[:, pl.ds(al((2 * j + b) * 128, 128), 128)],
            wu.at[:, pl.ds(al(j * 128, 128), 128)],
            w_sem.at[4 + j],
        )

    def down_copy(j):
        return pltpu.make_async_copy(
            wd_hbm.at[pl.ds(al((2 * j + b) * 128, 128), 128)],
            wd.at[pl.ds(al(j * 128, 128), 128)],
            w_sem.at[20 + j],
        )

    lax.fori_loop(0, 16, lambda j, c: (up_copy(j).start(), c)[1], 0)
    lax.fori_loop(0, 16, lambda j, c: (down_copy(j).start(), c)[1], 0)

    def to_core(k, src, dst):
        return pltpu.make_async_remote_copy(
            src_ref=src, dst_ref=dst, send_sem=c_send.at[k], recv_sem=c_recv.at[k],
            device_id=core_peer, device_id_type=MESH_ID,
        )

    def pre_attn(i, carry):
        rows = pl.ds(al(i * CHUNK, CHUNK), CHUNK)
        v = tok[rows, :].astype(F32)
        xin[pl.ds(al(own_tok + i * CHUNK, CHUNK), CHUNK), :] = (
            v * inv_rms(v) * gain_a[...]
        ).astype(BF16)
        return carry

    lax.fori_loop(0, TOK // CHUNK, pre_attn, 0)
    pl.semaphore_wait(barrier, 5)
    own_rows = xin.at[pl.ds(own_tok, TOK)]
    xin_copy = to_core(0, own_rows, own_rows)
    xin_copy.start()

    end_a = doc[0, 0]
    end_b = end_a + doc[0, 1]
    end_c = end_b + doc[0, 2]
    index_row = lax.broadcasted_iota(jnp.int32, (1, PACK), 1)
    start_row = jnp.where(
        index_row >= end_c,
        end_c,
        jnp.where(index_row >= end_b, end_b, jnp.where(index_row >= end_a, end_a, 0)),
    )
    position = (index_row - start_row).astype(F32)
    freq = jnp.exp(
        lax.broadcasted_iota(jnp.int32, (32, PACK), 0).astype(F32) * (-math.log(10000.0) / 32.0)
    )
    angle = position * freq
    rope[0] = jnp.cos(angle)
    rope[1] = jnp.sin(angle)

    def fill_mask(i, carry):
        rows = pl.ds(al(i * 64, 64), 64)
        key_index = lax.broadcasted_iota(jnp.int32, (64, PACK), 0) + i * 64
        query_index = lax.broadcasted_iota(jnp.int32, (64, PACK), 1)
        allowed = (key_index <= query_index) & (key_index >= start_row)
        mask[rows, :] = jnp.where(allowed, 0.0, neg_big)
        return carry

    lax.fori_loop(0, 8, fill_mask, 0)

    def project(tok_at):
        rows = pl.ds(tok_at, TOK)
        cos = rope[0, :, rows]
        sin = rope[1, :, rows]
        x_rows = xin[rows, :]

        def turned(w, scale):
            flat = mm(x_rows, w[...]).T.reshape(8, 2, 32, TOK)
            low, high = flat[:, 0], flat[:, 1]
            both = jnp.stack([low * cos - high * sin, low * sin + high * cos], axis=1)
            return (both * scale).reshape(HALF_D, TOK).astype(BF16)

        q_t[:, rows] = turned(wq, 0.125)
        keys = turned(wk, 1.0)
        k_t[:, rows] = keys
        k_n[rows, :] = keys.T
        values = mm(x_rows, wv[...]).astype(BF16)
        v_n[rows, :] = values
        v_t[:, rows] = values.T

    for copy in w_copies[:3]:
        copy.wait()
    project(own_tok)
    xin_copy.wait()
    project(oth_tok)

    zeros = jnp.zeros((64, TOK), BF16)

    def slab(head_rows, which):
        return jnp.concatenate([head_rows, zeros] if which == 0 else [zeros, head_rows], axis=0)

    def attend(p, carry):
        slab_cols = pl.ds(al(p * 128, 128), 128)
        for which in range(2):
            rows = pl.ds(al(p * 128 + which * 64, 64), 64)
            for block in range(2):
                cols = slice(block * TOK, block * TOK + TOK)
                keys = (block + 1) * TOK
                scores = mm(k_n[:keys, slab_cols], slab(q_t[rows, cols], which)) + mask[:keys, cols]
                top = jnp.max(scores, axis=0, keepdims=True)
                weights = jnp.exp(scores - top)
                total = jnp.sum(weights, axis=0, keepdims=True)
                attn_t[rows, cols] = mm(v_t[rows, :keys], weights.astype(BF16)) * (1.0 / total)
                lse[pl.ds(p * 2 + which, 1), cols] = top + jnp.log(total)
        attn_nat[:, slab_cols] = attn_t[pl.ds(al(p * 128, 128), 128), :].T.astype(BF16)
        to_core(
            1 + p, attn_nat.at[pl.ds(oth_tok, TOK), slab_cols], attn_oth.at[:, slab_cols]
        ).start()
        return carry

    lax.fori_loop(0, 4, attend, 0)

    w_copies[3].wait()
    branch[...] = mm(attn_nat[pl.ds(own_tok, TOK), :], wo[pl.ds(own_cols, HALF_D), :])

    def attn_copy(p):
        cols = pl.ds(al(p * 128, 128), 128)
        return to_core(1 + p, attn_nat.at[pl.ds(oth_tok, TOK), cols], attn_oth.at[:, cols])

    lax.fori_loop(0, 4, lambda p, c: (attn_copy(p).wait(), c)[1], 0)
    branch[...] += mm(attn_oth[...], wo[pl.ds(oth_cols, HALF_D), :])

    def post_attn(i, carry):
        rows = pl.ds(al(i * CHUNK, CHUNK), CHUNK)
        v = branch[rows, :]
        square = jnp.mean(v * v, axis=-1, keepdims=True) + eps
        stat[0, rows, :] = jnp.broadcast_to(jnp.sqrt(square), (CHUNK, 128))
        h = tok[rows, :].astype(F32) + v * lax.rsqrt(square) * gain_b[...]
        hid[rows, :] = h
        xm[pl.ds(al(own_tok + i * CHUNK, CHUNK), CHUNK), :] = (
            h * inv_rms(h) * gain_c[...]
        ).astype(BF16)
        return carry

    lax.fori_loop(0, TOK // CHUNK, post_attn, 0)
    own_rows_m = xm.at[pl.ds(own_tok, TOK)]
    xm_copy = to_core(5, own_rows_m, own_rows_m)
    xm_copy.start()

    def up_step(tok_at, i):
        cols = pl.ds(al(i * 256, 256), 256)
        rows = pl.ds(tok_at, TOK)
        bias = jnp.concatenate(
            [bias_up[pl.ds(4 * i + b, 1), :], bias_up[pl.ds(4 * i + 2 + b, 1), :]], axis=1
        )
        pre = mm(xm[rows, :], wu[:, cols]) + bias
        square = pre * pre
        th = jnp.tanh(pre * (0.7978845608 + (0.7978845608 * 0.044715) * square))
        half = 0.5 + 0.5 * th
        act[rows, cols] = (pre * half).astype(BF16)
        slope = half + pre * (0.5 - 0.5 * th * th) * (
            0.7978845608 + (0.7978845608 * 0.134145) * square
        )
        g_t[cols, rows] = slope.astype(BF16).T

    lax.fori_loop(0, 16, lambda j, c: (up_copy(j).wait(), c)[1], 0)
    lax.fori_loop(0, 8, lambda i, c: (up_step(own_tok, i), c)[1], 0)
    xm_copy.wait()
    lax.fori_loop(0, 8, lambda i, c: (up_step(oth_tok, i), c)[1], 0)
    lax.fori_loop(0, 16, lambda j, c: (down_copy(j).wait(), c)[1], 0)

    def down_step(tok_at, dst, i):
        cols = pl.ds(al(i * 256, 256), 256)
        dst[:, cols] = mm(act[pl.ds(tok_at, TOK), :], wd[:, cols])

    lax.fori_loop(0, 4, lambda i, c: (down_step(oth_tok, part_send, i), c)[1], 0)
    mlp_copy = to_core(6, part_send, part_recv)
    mlp_copy.start()
    lax.fori_loop(0, 4, lambda i, c: (down_step(own_tok, part_own, i), c)[1], 0)
    mlp_copy.wait()

    def post_mlp(i, carry):
        sum_bias, sum_gain = carry
        rows = pl.ds(al(i * CHUNK, CHUNK), CHUNK)
        v = part_own[rows, :] + part_recv[rows, :] + bias_down[...]
        square = jnp.mean(v * v, axis=-1, keepdims=True) + eps
        stat[1, rows, :] = jnp.broadcast_to(jnp.sqrt(square), (CHUNK, 128))
        r = lax.rsqrt(square)
        out[rows, :] = (hid[rows, :] + v * r * gain_d[...]).astype(BF16)
        back, gain_part = norm_back(v, r, gain_d[...], cot[rows, :].astype(F32))
        back = back.astype(BF16)
        nat[rows, :] = back
        return (
            sum_bias + jnp.sum(back.astype(F32), axis=0, keepdims=True),
            sum_gain + gain_part,
        )

    zero_row = jnp.zeros((1, D), F32)
    sum_bias_down, sum_gain_d = lax.fori_loop(0, TOK // CHUNK, post_mlp, (zero_row, zero_row))
    aux_s[0] = jnp.zeros((16, D), F32)
    aux_s[0, 0:1, :] = sum_bias_down
    aux_s[0, 4:5, :] = sum_gain_d
    for i in range(2):
        rms[i : i + 1, :] = stat[i].T[0:1, :]

    def turn_to(dst):
        def step(i, carry):
            cols = pl.ds(al(i * 256, 256), 256)
            dst[cols, pl.ds(own_tok, TOK)] = nat[:, cols].T
            return carry

        lax.fori_loop(0, 4, step, 0)

    turn_to(gb_t)
    own_gb = gb_t.at[:, pl.ds(own_tok, TOK)]
    gb_copy = to_core(7, own_gb, own_gb)
    gb_copy.start()
    gb_copy.wait()

    down_refs = (s_down, r1_down, r2_down, r3_down, r4_down)
    up_refs = (wd, r1_up, r2_up, r3_up, r4_up)
    late_refs = (wu, r1_late, r2_late, r3_late, r4_late)
    units = (
        [(down_refs, 512 * i, 512, 64) for i in range(4)]
        + [(up_refs, 256 * i, 256, 128) for i in range(4)]
        + [(late_refs, 512 * i, 512, 64) for i in range(4)]
    )
    place = {
        "x": (x, 1, x_peer),
        "y": (y, 2, y_peer),
        "w": (lax.rem(z, 2), 4, z_low),
        "v": (z // 2, 8, z_high),
    }

    def unit_axes(n):
        return [place[letter] for letter in UNIT_ORDER[n]]

    def kept(n, steps):
        rows = units[n][3]
        return sum(
            (axis[0] * (8 >> i) * rows for i, axis in enumerate(unit_axes(n)[:steps])), 0
        )

    def unit_copy(n, k):
        refs, c0, width, rows = units[n]
        axes = unit_axes(n)
        cols = pl.ds(c0, width)
        if k < 2:
            bit, _, peer = axes[0]
            second = lax.rem(axes[1][0] + 1 + k, 2)
            count = 4 * rows
            src = refs[0].at[pl.ds(al(((1 - bit) * 2 + second) * count, count), count), cols]
            dst = refs[1].at[pl.ds(al(second * count, count), count), cols]
        else:
            bit, _, peer = axes[k - 1]
            count = (16 >> k) * rows
            at = kept(n, k - 1) + (1 - bit) * count
            src = refs[0].at[pl.ds(al(at, count), count), cols]
            dst = refs[k].at[:, cols]
        return pltpu.make_async_remote_copy(
            src_ref=src, dst_ref=dst, send_sem=rs_send.at[n, k], recv_sem=rs_recv.at[n, k],
            device_id=peer, device_id_type=MESH_ID,
        )

    def add_rows(n, at, arrived, arrived_at, count):
        refs, c0, width, _ = units[n]
        cols = pl.ds(c0, width)

        def step(i, carry):
            to = pl.ds(al(at + i * 64, 64), 64)
            got = refs[arrived][pl.ds(al(arrived_at + i * 64, 64), 64), cols]
            refs[0][to, cols] = (refs[0][to, cols].astype(F32) + got.astype(F32)).astype(BF16)
            return carry

        lax.fori_loop(0, count // 64, step, 0)

    def serve(n, k):
        refs, c0, width, rows = units[n]
        axes = unit_axes(n)
        unit_copy(n, k).wait_recv()
        if k < 2:
            second = lax.rem(axes[1][0] + 1 + k, 2)
            add_rows(n, kept(n, 1) + second * 4 * rows, 1, second * 4 * rows, 4 * rows)
            if k == 0:
                unit_copy(n, 2).start()
        elif k < 4:
            count = (8 >> k) * rows
            bit = axes[k][0]
            add_rows(n, kept(n, k) + (1 - bit) * count, k, (1 - bit) * count, count)
            unit_copy(n, k + 1).start()
            add_rows(n, kept(n, k) + bit * count, k, bit * count, count)
        else:
            cols = pl.ds(c0, width)
            dst = fin_down if n < 4 else o_up if n < 8 else fin_late
            dst[:, cols] = refs[0][pl.ds(al(kept(n, 4), rows), rows), cols].astype(F32) + refs[4][
                :, cols
            ].astype(F32)
            if dst is not o_up:
                final_copy(n).start()

    oth_cut = pl.ds(al(other * 32, 32), 32)
    own_cut = pl.ds(al(b * 32, 32), 32)

    def final_copy(n):
        _, c0, width, _ = units[n]
        cols = pl.ds(c0, width)
        src, dst = (fin_down, rec_down) if n < 4 else (fin_late, rec_late)
        return to_core(14 + n, src.at[oth_cut, cols], dst.at[:, cols])

    def slot(i):
        for code in SLOTS[i]:
            n, k = code // 10, code % 10
            if k < 2:
                unit_copy(n, k).start()
            else:
                serve(n, k - 2)

    def weight_grad(n, first, last, lhs, rhs, rhs_at):
        refs, c0, width, rows = units[n]
        axes = unit_axes(n)
        for g in range(first, last):
            i = lax.rem(axes[0][0] + 1 + g // 2, 2)
            j = lax.rem(axes[1][0] + 1 + g % 2, 2)
            base = i * axes[0][1] + j * axes[1][1]
            tails = [p * axes[2][1] + q * axes[3][1] for p in range(2) for q in range(2)]
            left = jnp.concatenate(
                [lhs[pl.ds(al((base + tail) * rows, rows), rows), :] for tail in tails], axis=0
            )
            right = rhs[:, pl.ds(al(rhs_at, 256), width)]
            at = pl.ds(al((i * 2 + j) * 4 * rows, 4 * rows), 4 * rows)
            refs[0][at, pl.ds(c0, width)] = mm(left, right).astype(BF16)

    for first in (0, 2):
        for n in range(4):
            weight_grad(n, first, first + 2, gb_t, act, 512 * n)
        slot(first // 2)

    def act_back(i, carry):
        rows = pl.ds(al(i * 256, 256), 256)
        g_t[rows, :] = (mm(wd[rows, :], gb_t[...]) * g_t[rows, :].astype(F32)).astype(BF16)
        return carry

    lax.fori_loop(0, 8, act_back, 0)
    slot(2)
    for first in (0, 2):
        for n in range(4, 8):
            weight_grad(n, first, first + 2, g_t, xm, 256 * (n - 4))
        slot(3 + first // 2)

    def mlp_back(tok_at, dst, i):
        at = pl.ds(al(i * 256, 256), 256)
        dst[:, at] = mm(wu[at, :], g_t[:, pl.ds(tok_at, TOK)]).T

    lax.fori_loop(0, 4, lambda i, c: (mlp_back(oth_tok, part_send, i), c)[1], 0)
    mlp_back_copy = to_core(8, part_send, part_recv)
    mlp_back_copy.start()
    slot(5)
    lax.fori_loop(0, 4, lambda i, c: (mlp_back(own_tok, part_own, i), c)[1], 0)
    ones = jnp.ones((16, PACK), BF16)
    for i in range(2):
        aux_s[0, pl.ds(5 + 2 * b + i, 1), :] = mm_nt(ones, g_t[i * 1024 : i * 1024 + 1024, :])[0:1]
    slot(6)
    mlp_back_copy.wait()

    def hidden_back(i, carry):
        sum_c, sum_b = carry
        rows = pl.ds(al(i * CHUNK, CHUNK), CHUNK)
        h = hid[rows, :]
        back, part_c = norm_back(
            h, inv_rms(h), gain_c[...], part_own[rows, :] + part_recv[rows, :]
        )
        g_hidden = cot[rows, :].astype(F32) + back
        hid[rows, :] = g_hidden
        v = branch[rows, :]
        back, part_b = norm_back(v, inv_rms(v), gain_b[...], g_hidden)
        nat[rows, :] = back.astype(BF16)
        return sum_c + part_c, sum_b + part_b

    sum_gain_c, sum_gain_b = lax.fori_loop(0, TOK // CHUNK, hidden_back, (zero_row, zero_row))
    aux_s[0, 3:4, :] = sum_gain_c
    aux_s[0, 2:3, :] = sum_gain_b
    turn_to(gba_t)
    own_gba = gba_t.at[:, pl.ds(own_tok, TOK)]
    gba_copy = to_core(9, own_gba, own_gba)
    gba_copy.start()
    slot(7)
    gba_copy.wait()

    weight_grad(8, 0, 4, gba_t, attn_nat, 0)
    slot(8)
    ga_t[...] = mm(wo[pl.ds(own_cols, HALF_D), :], gba_t[...]).astype(BF16)
    slot(9)

    gq, gk, gv = g_t.at[pl.ds(0, D)], g_t.at[pl.ds(D, D)], gb_t

    def attend_back(p, carry):
        slab_cols = pl.ds(al(p * 128, 128), 128)
        for which in range(2):
            rows = pl.ds(al(p * 128 + which * 64, 64), 64)
            to = pl.ds(al(own_cols + p * 128 + which * 64, 64), 64)
            grads_k, grads_v, grads_q = [], [], []
            for block in range(2):
                cols = slice(block * TOK, block * TOK + TOK)
                keys = (block + 1) * TOK
                q_rows = q_t[rows, cols]
                g_rows = ga_t[rows, cols]
                delta = jnp.sum(g_rows.astype(F32) * attn_t[rows, cols], axis=0, keepdims=True)
                scores = mm(k_n[:keys, slab_cols], slab(q_rows, which)) + mask[:keys, cols]
                probs = jnp.exp(scores - lse[pl.ds(p * 2 + which, 1), cols])
                g_probs = mm(v_n[:keys, slab_cols], slab(g_rows, which))
                g_scores = (probs * (g_probs - delta)).astype(BF16)
                grads_q.append(mm(k_t[rows, :keys], g_scores) * 0.125)
                grads_k.append(mm_nt(q_rows, g_scores))
                grads_v.append(mm_nt(g_rows, probs.astype(BF16)))
            for parts, dst in ((grads_q, gq), (grads_k, gk)):
                if dst is gq:
                    full = jnp.concatenate(parts, axis=1)
                else:
                    full = jnp.concatenate(
                        [parts[0] + parts[1][:, :TOK], parts[1][:, TOK:]], axis=1
                    )
                low, high = full[:32], full[32:]
                cos, sin = rope[0], rope[1]
                dst[to, :] = jnp.concatenate(
                    [low * cos + high * sin, high * cos - low * sin], axis=0
                ).astype(BF16)
            gv[to, :] = jnp.concatenate(
                [grads_v[0] + grads_v[1][:, :TOK], grads_v[1][:, TOK:]], axis=1
            ).astype(BF16)
        return carry

    lax.fori_loop(0, 2, attend_back, 0)
    slot(10)
    lax.fori_loop(2, 4, attend_back, 0)
    own_heads = pl.ds(own_cols, HALF_D)
    head_copies = [
        to_core(10 + i, ref.at[own_heads], ref.at[own_heads]) for i, ref in enumerate((gq, gk, gv))
    ]
    for copy in head_copies:
        copy.start()
    slot(11)

    def in_back(tok_at, dst, i):
        at = pl.ds(al(i * 256, 256), 256)
        cols = pl.ds(tok_at, TOK)
        total = mm(wq[at, :], gq[own_heads, cols])
        total += mm(wk[at, :], gk[own_heads, cols])
        total += mm(wv[at, :], gv[own_heads, cols])
        dst[:, at] = total.T

    lax.fori_loop(0, 4, lambda i, c: (in_back(oth_tok, part_send, i), c)[1], 0)
    in_back_copy = to_core(13, part_send, part_recv)
    in_back_copy.start()
    slot(12)
    for copy in head_copies:
        copy.wait()
    for first in (0, 2):
        for n, lhs in zip((9, 10, 11), (gq, gk, gv)):
            weight_grad(n, first, first + 2, lhs, xin, own_cols)
        slot(13 + first // 2)
    lax.fori_loop(0, 4, lambda i, c: (in_back(own_tok, part_own, i), c)[1], 0)
    slot(15)
    in_back_copy.wait()

    def token_back(i, carry):
        rows = pl.ds(al(i * CHUNK, CHUNK), CHUNK)
        v = tok[rows, :].astype(F32)
        back, part_a = norm_back(
            v, inv_rms(v), gain_a[...], part_own[rows, :] + part_recv[rows, :]
        )
        grad_tok[rows, :] = (hid[rows, :] + back).astype(BF16)
        return carry + part_a

    aux_s[0, 1:2, :] = lax.fori_loop(0, TOK // CHUNK, token_back, zero_row)

    aux_peers = (core_peer, x_peer, y_peer, z_low, z_high)

    def aux_copy(k):
        return pltpu.make_async_remote_copy(
            src_ref=aux_s.at[k], dst_ref=aux_r.at[k], send_sem=a_send.at[k],
            recv_sem=a_recv.at[k], device_id=aux_peers[k], device_id_type=MESH_ID,
        )

    aux_copy(0).start()
    for k in range(5):
        slot(16 + k)
        aux_copy(k).wait_recv()
        aux_s[k + 1] = aux_s[k] + aux_r[k]
        if k < 4:
            aux_copy(k + 1).start()
    o_aux[...] = aux_s[5]
    slot(21)
    for n in range(4):
        final_copy(n).wait()

    def place_down(j, carry):
        from_cols = pl.ds(al(j * 128, 128), 128)
        o_down[:, pl.ds(al((2 * j + b) * 128, 128), 128)] = fin_down[own_cut, from_cols]
        o_down[:, pl.ds(al((2 * j + other) * 128, 128), 128)] = rec_down[:, from_cols]
        return carry

    lax.fori_loop(0, 16, place_down, 0)
    slot(22)
    for n in range(12):
        for k in range(5):
            unit_copy(n, k).wait_send()
    for k in range(5):
        aux_copy(k).wait_send()
    for i in range(4):
        final_copy(8 + i).wait()
        cols = slice(i * 512, i * 512 + 512)
        o_late[i, :, pl.ds(own_cols, HALF_D)] = fin_late[own_cut, cols]
        o_late[i, :, pl.ds(oth_cols, HALF_D)] = rec_late[:, cols]


def layer_on_device(
    tokens, doc_lengths, w_query, w_key, w_value, w_out, w_up, w_down, bias_up, bias_down,
    gain_pre_attn, gain_post_attn, gain_pre_mlp, gain_post_mlp, cotangent,
):
    def v16(*shape):
        return pltpu.VMEM(shape, BF16)

    def v32(*shape):
        return pltpu.VMEM(shape, F32)

    dma = pltpu.SemaphoreType.DMA
    vmem = pl.BlockSpec(memory_space=pltpu.VMEM)
    scratch = [
        v16(1024, 512), v16(1024, 512), v16(1024, 512), v16(1024, 1024),
        v16(1024, 2048), v16(2048, 1024),
        v16(512, 1024),
        v16(512, 512), v16(512, 512), v16(512, 512), v16(512, 512), v16(512, 512),
        v32(512, 512), v32(512, 512), v16(512, 512), v16(256, 512),
        v32(256, 1024), v32(256, 1024), v16(512, 1024),
        v16(512, 2048), v16(2048, 512),
        v32(256, 1024), v32(256, 1024), v32(256, 1024), v16(256, 1024),
        v16(1024, 512), v16(1024, 512), v16(512, 512),
        v32(2, 32, 512), v32(8, 512), v32(2, 256, 128),
        v16(1024, 2048), v16(512, 2048), v16(256, 2048), v16(128, 2048), v16(64, 2048),
        v16(1024, 1024), v16(512, 1024), v16(256, 1024), v16(128, 1024),
        v16(512, 2048), v16(256, 2048), v16(128, 2048), v16(64, 2048),
        v32(64, 2048), v32(64, 2048), v32(32, 2048), v32(32, 2048),
        v32(6, 16, 1024), v32(5, 16, 1024),
        dma((36,)), dma((26,)), dma((26,)), dma((12, 5)), dma((12, 5)), dma((5,)), dma((5,)),
    ]
    out, grad_tok, rms, down, up, late, aux = pl.pallas_call(
        layer_kernel,
        out_shape=(
            jax.ShapeDtypeStruct((TOK, D), BF16),
            jax.ShapeDtypeStruct((TOK, D), BF16),
            jax.ShapeDtypeStruct((2, TOK), F32),
            jax.ShapeDtypeStruct((32, FF), F32),
            jax.ShapeDtypeStruct((128, D), F32),
            jax.ShapeDtypeStruct((4, 32, D), F32),
            jax.ShapeDtypeStruct((16, D), F32),
        ),
        in_specs=[pl.BlockSpec(memory_space=pltpu.SMEM)]
        + [vmem] * 8
        + [pl.BlockSpec(memory_space=pl.ANY)] * 6,
        out_specs=[vmem] * 7,
        scratch_shapes=scratch,
        compiler_params=pltpu.CompilerParams(
            collective_id=0, has_side_effects=True, vmem_limit_bytes=VMEM_BYTES
        ),
    )(
        doc_lengths, tokens, cotangent,
        gain_pre_attn[None], gain_post_attn[None], gain_pre_mlp[None], gain_post_mlp[None],
        bias_up.reshape(32, 128), bias_down[None],
        w_query, w_key, w_value, w_out, w_up, w_down,
    )
    dp = lax.axis_index("dp")
    b = lax.axis_index("blk")
    at = (dp * 2 + b) * 32
    small = lax.dynamic_slice(aux, (0, at), (5, 32))
    bias_rows = lax.dynamic_slice(
        aux, (5 + 2 * b + dp // 8, lax.rem(dp, 8) * 128), (1, 128)
    )[0]
    return (
        out, grad_tok, late[1].T, late[2].T, late[3].T, late[0].T, up.T, down.T,
        bias_rows, small[0], small[1], small[2], small[3], small[4], rms,
    )


def solution(mesh):
    placed = (
        P(("dp", "blk"), None),
        P("dp", None),
        P(),
        P(),
        P(),
        P(),
        P(),
        P(),
        P(),
        P(),
        P(),
        P(),
        P(),
        P(),
        P(("dp", "blk"), None),
    )
    paired = mesh.shape["blk"] == 2 and mesh.shape["dp"] == 16
    return jax.shard_map(
        layer_on_device if paired else on_device,
        mesh=mesh,
        in_specs=placed,
        out_specs=(
            P(("dp", "blk"), None),
            P(("dp", "blk"), None),
            P(None, ("dp", "blk")),
            P(None, ("dp", "blk")),
            P(None, ("dp", "blk")),
            P(None, ("dp", "blk")),
            P(None, ("dp", "blk")),
            P(None, ("dp", "blk")),
            P(("dp", "blk")),
            P(("dp", "blk")),
            P(("dp", "blk")),
            P(("dp", "blk")),
            P(("dp", "blk")),
            P(("dp", "blk")),
            P(None, ("dp", "blk")),
        ),
        check_vma=False,
    )
```

```python
import math

import jax
import jax.numpy as jnp
from jax import lax
from jax.experimental import pallas as pl
from jax.experimental.pallas import tpu as pltpu
from jax.sharding import PartitionSpec as P

D = 1024
H = 16
HD = 64


eps = 1e-06
neg_big = -1e30


def rms_norm(values, gain_row):
    return values * lax.rsqrt(jnp.mean(values * values, axis=-1, keepdims=True) + eps) * gain_row


def rotate(head_rows, position):
    half_size = head_rows.shape[-1] // 2
    frequency = 10000.0 ** (-2.0 * jnp.arange(half_size, dtype=jnp.float32) / head_rows.shape[-1])
    angles = position.astype(jnp.float32)[:, None] * frequency[None, :]
    cosine = jnp.cos(angles)[:, None, :]
    sine_part = jnp.sin(angles)[:, None, :]
    low_half = head_rows[..., :half_size]
    high_half = head_rows[..., half_size:]
    return jnp.concatenate(
        [low_half * cosine - high_half * sine_part, low_half * sine_part + high_half * cosine],
        axis=-1,
    )


def doc_layout(lengths, total_rows):
    index_row = jnp.arange(total_rows, dtype=jnp.int32)
    doc_ends = jnp.stack(
        [
            lengths[0],
            lengths[0] + lengths[1],
            lengths[0] + lengths[1] + lengths[2],
            lengths[0] + lengths[1] + lengths[2] + lengths[3],
        ]
    )
    segment = jnp.sum((index_row[:, None] >= doc_ends[None, :3]).astype(jnp.int32), axis=1)
    starts = doc_ends - lengths
    matches = segment[:, None] == jnp.arange(4, dtype=jnp.int32)[None, :]
    return (index_row, jnp.sum(jnp.where(matches, starts[None, :], 0), axis=1))


def block_mask(query_index, query_start, key_first, width):
    key_index = key_first + jnp.arange(width, dtype=jnp.int32)
    return (key_index[None, :] <= query_index[:, None]) & (
        key_index[None, :] >= query_start[:, None]
    )


def on_device(
    tokens,
    doc_lengths,
    w_query,
    w_key,
    w_value,
    w_out,
    w_up,
    w_down,
    bias_up,
    bias_down,
    gain_pre_attn,
    gain_post_attn,
    gain_pre_mlp,
    gain_post_mlp,
    cotangent,
):
    row_count = tokens.shape[0]
    cycle_size = lax.axis_size("blk")
    group_rows = row_count * cycle_size
    first_row = lax.axis_index("blk") * row_count
    index_all, start_all = doc_layout(doc_lengths[0], group_rows)
    query_index = lax.dynamic_slice_in_dim(index_all, first_row, row_count)
    query_start = lax.dynamic_slice_in_dim(start_all, first_row, row_count)
    position = query_index - query_start
    query_last = first_row + row_count - 1
    start_least = jnp.min(query_start)
    scale = HD ** (-0.5)
    tokens_f = tokens.astype(jnp.float32)
    normed_in, back_pre_attn = jax.vjp(rms_norm, tokens_f, gain_pre_attn)
    attn_in = normed_in.astype(jnp.bfloat16)
    query_pre = jnp.dot(attn_in, w_query, preferred_element_type=jnp.float32)
    key_pre = jnp.dot(attn_in, w_key, preferred_element_type=jnp.float32)
    value_pre = jnp.dot(attn_in, w_value, preferred_element_type=jnp.float32)
    queries, back_rot_query = jax.vjp(
        lambda arr: rotate(arr, position), query_pre.reshape(row_count, H, HD)
    )
    keys_rot, back_rot_key = jax.vjp(
        lambda arr: rotate(arr, position), key_pre.reshape(row_count, H, HD)
    )
    queries_low = queries.astype(jnp.bfloat16)
    keys_low = keys_rot.reshape(row_count, D).astype(jnp.bfloat16)
    values_low = value_pre.astype(jnp.bfloat16)
    initial = (
        jnp.full((H, row_count), neg_big, jnp.float32),
        jnp.zeros((H, row_count), jnp.float32),
        jnp.zeros((row_count, H, HD), jnp.float32),
    )
    key_piece = lax.all_gather(keys_low, "blk", axis=0, tiled=True)
    value_piece = lax.all_gather(values_low, "blk", axis=0, tiled=True)
    piece_rows = key_piece.shape[0]
    fold_width = math.gcd(piece_rows, 512)

    def one_block(state, number):
        key_first = number * fold_width

        def one_compute(state):
            running_top, totals, accum = state
            keys_blk = lax.dynamic_slice_in_dim(
                key_piece, number * fold_width, fold_width, 0
            ).reshape(fold_width, H, HD)
            values_blk = lax.dynamic_slice_in_dim(
                value_piece, number * fold_width, fold_width, 0
            ).reshape(fold_width, H, HD)
            scores = (
                jnp.einsum(
                    "qhd,khd->hqk", queries_low, keys_blk, preferred_element_type=jnp.float32
                )
                * scale
            )
            allowed = block_mask(query_index, query_start, key_first, fold_width)[None]
            scores = jnp.where(allowed, scores, neg_big)
            new_top = jnp.maximum(running_top, jnp.max(scores, axis=-1))
            weights = jnp.where(allowed, jnp.exp(scores - new_top[..., None]), 0.0)
            factor = jnp.exp(running_top - new_top)
            totals = totals * factor + jnp.sum(weights, axis=-1)
            accum = accum * jnp.transpose(factor)[:, :, None] + jnp.einsum(
                "hqk,khd->qhd",
                weights.astype(jnp.bfloat16),
                values_blk,
                preferred_element_type=jnp.float32,
            )
            return (new_top, totals, accum)

        active = (key_first <= query_last) & (key_first + fold_width - 1 >= start_least)
        return (lax.cond(active, one_compute, lambda state: state, state), None)

    result, unused = lax.scan(
        one_block, initial, jnp.arange(piece_rows // fold_width, dtype=jnp.int32)
    )
    running_top, totals, accum = result
    attn_full = accum / jnp.transpose(totals)[:, :, None]
    log_total = running_top + jnp.log(totals)
    attn_low = attn_full.reshape(row_count, D).astype(jnp.bfloat16)
    branch_attn = jnp.dot(attn_low, w_out, preferred_element_type=jnp.float32)
    post_attn, back_post_attn = jax.vjp(rms_norm, branch_attn, gain_post_attn)
    hidden_res = tokens_f + post_attn
    normed_mlp, back_pre_mlp = jax.vjp(rms_norm, hidden_res, gain_pre_mlp)
    mlp_in = normed_mlp.astype(jnp.bfloat16)
    pre_act = jnp.dot(mlp_in, w_up, preferred_element_type=jnp.float32) + bias_up
    activated, back_gelu = jax.vjp(lambda arr: jax.nn.gelu(arr, approximate=True), pre_act)
    act_low = activated.astype(jnp.bfloat16)
    branch_mlp = jnp.dot(act_low, w_down, preferred_element_type=jnp.float32) + bias_down
    post_mlp, back_post_mlp = jax.vjp(rms_norm, branch_mlp, gain_post_mlp)
    output = (hidden_res + post_mlp).astype(jnp.bfloat16)
    branch_rms = jnp.stack(
        [
            jnp.sqrt(jnp.mean(branch_attn * branch_attn, axis=-1) + eps),
            jnp.sqrt(jnp.mean(branch_mlp * branch_mlp, axis=-1) + eps),
        ]
    )
    grad_out_f = cotangent.astype(jnp.float32)
    grad_branch_mlp, grad_gain_post_mlp = back_post_mlp(grad_out_f)
    grad_mlp_low = grad_branch_mlp.astype(jnp.bfloat16)
    grad_bias_down = jnp.sum(grad_mlp_low.astype(jnp.float32), axis=0)
    grad_down = jnp.einsum("tf,td->df", act_low, grad_mlp_low, preferred_element_type=jnp.float32)
    grad_act = jnp.einsum("td,fd->tf", grad_mlp_low, w_down, preferred_element_type=jnp.float32)
    (grad_pre_act,) = back_gelu(grad_act)
    grad_pre_low = grad_pre_act.astype(jnp.bfloat16)
    grad_bias_up = jnp.sum(grad_pre_low.astype(jnp.float32), axis=0)
    grad_up = jnp.einsum("td,tf->fd", mlp_in, grad_pre_low, preferred_element_type=jnp.float32)
    grad_normed_mlp = jnp.einsum(
        "tf,df->td", grad_pre_low, w_up, preferred_element_type=jnp.float32
    )
    grad_res_part, grad_gain_pre_mlp = back_pre_mlp(grad_normed_mlp)
    grad_hidden = grad_out_f + grad_res_part
    grad_branch_attn, grad_gain_post_attn = back_post_attn(grad_hidden)
    grad_branch_low = grad_branch_attn.astype(jnp.bfloat16)
    grad_w_out = jnp.einsum(
        "td,te->ed", attn_low, grad_branch_low, preferred_element_type=jnp.float32
    )
    grad_attn = jnp.einsum("te,de->td", grad_branch_low, w_out, preferred_element_type=jnp.float32)
    grad_attn_low = grad_attn.astype(jnp.bfloat16).reshape(row_count, H, HD)
    delta = jnp.einsum("qhd,qhd->hq", grad_attn_low.astype(jnp.float32), attn_full)
    key_source, value_source = key_piece, value_piece
    width = math.gcd(group_rows, 512)

    def back_block(grad_query_acc, number):
        key_first = number * width

        def back_compute(grad_query_acc):
            keys_blk = lax.dynamic_slice_in_dim(key_source, key_first, width, 0).reshape(
                width, H, HD
            )
            values_blk = lax.dynamic_slice_in_dim(value_source, key_first, width, 0).reshape(
                width, H, HD
            )
            scores = (
                jnp.einsum(
                    "qhd,khd->hqk", queries_low, keys_blk, preferred_element_type=jnp.float32
                )
                * scale
            )
            allowed = block_mask(query_index, query_start, key_first, width)[None]
            probs = jnp.where(allowed, jnp.exp(scores - log_total[..., None]), 0.0)
            grad_probs = jnp.einsum(
                "qhd,khd->hqk", grad_attn_low, values_blk, preferred_element_type=jnp.float32
            )
            grad_scores = (probs * (grad_probs - delta[..., None])).astype(jnp.bfloat16)
            grad_query_acc = (
                grad_query_acc
                + jnp.einsum(
                    "hqk,khd->qhd", grad_scores, keys_blk, preferred_element_type=jnp.float32
                )
                * scale
            )
            grad_keys_blk = (
                jnp.einsum(
                    "hqk,qhd->khd", grad_scores, queries_low, preferred_element_type=jnp.float32
                )
                * scale
            )
            grad_values_blk = jnp.einsum(
                "hqk,qhd->khd",
                probs.astype(jnp.bfloat16),
                grad_attn_low,
                preferred_element_type=jnp.float32,
            )
            return (
                grad_query_acc,
                (grad_keys_blk.reshape(width, D), grad_values_blk.reshape(width, D)),
            )

        def skipped(grad_query_acc):
            return (
                grad_query_acc,
                (jnp.zeros((width, D), jnp.float32), jnp.zeros((width, D), jnp.float32)),
            )

        active = (key_first <= query_last) & (key_first + width - 1 >= start_least)
        return lax.cond(active, back_compute, skipped, grad_query_acc)

    grad_query_acc, stacked = lax.scan(
        back_block,
        jnp.zeros((row_count, H, HD), jnp.float32),
        jnp.arange(group_rows // width, dtype=jnp.int32),
    )
    grad_keys_all = stacked[0].reshape(group_rows, D)
    grad_values_all = stacked[1].reshape(group_rows, D)
    grad_keys_mine, grad_values_mine = (
        lax.psum_scatter(
            grad_keys_all.astype(jnp.bfloat16), "blk", scatter_dimension=0, tiled=True
        ).astype(jnp.float32),
        lax.psum_scatter(
            grad_values_all.astype(jnp.bfloat16), "blk", scatter_dimension=0, tiled=True
        ).astype(jnp.float32),
    )
    (grad_key_pre,) = back_rot_key(grad_keys_mine.reshape(row_count, H, HD))
    (grad_query_pre,) = back_rot_query(grad_query_acc)
    grad_key_low = grad_key_pre.reshape(row_count, D).astype(jnp.bfloat16)
    grad_query_low = grad_query_pre.reshape(row_count, D).astype(jnp.bfloat16)
    grad_value_low = grad_values_mine.astype(jnp.bfloat16)
    grad_query = jnp.einsum(
        "td,te->ed", attn_in, grad_query_low, preferred_element_type=jnp.float32
    )
    grad_key = jnp.einsum("td,te->ed", attn_in, grad_key_low, preferred_element_type=jnp.float32)
    grad_value = jnp.einsum(
        "td,te->ed", attn_in, grad_value_low, preferred_element_type=jnp.float32
    )
    grad_normed_in = (
        jnp.einsum("te,de->td", grad_query_low, w_query, preferred_element_type=jnp.float32)
        + jnp.einsum("te,de->td", grad_key_low, w_key, preferred_element_type=jnp.float32)
        + jnp.einsum("te,de->td", grad_value_low, w_value, preferred_element_type=jnp.float32)
    )
    grad_tokens_part, grad_gain_pre_attn = back_pre_attn(grad_normed_in)
    grad_tokens = (grad_hidden + grad_tokens_part).astype(jnp.bfloat16)
    count = lax.axis_size(("dp", "blk"))
    low = jnp.bfloat16
    pieces = [
        part.astype(low).reshape(count, -1, D)
        for part in (grad_query, grad_key, grad_value, grad_w_out, grad_up, grad_down)
    ]
    small = [
        part.reshape(count, -1)
        for part in (
            grad_bias_up,
            grad_bias_down,
            grad_gain_pre_attn,
            grad_gain_post_attn,
            grad_gain_pre_mlp,
            grad_gain_post_mlp,
        )
    ]
    sizes = [part.shape[1] for part in pieces]
    summed = lax.psum_scatter(
        jnp.concatenate(pieces, axis=1), ("dp", "blk"), scatter_dimension=0
    ).astype(jnp.float32)
    small_sizes = [part.shape[1] for part in small]
    small_flat = jnp.concatenate(small, axis=1)
    padding = -small_flat.shape[1] % 128
    small_flat = jnp.pad(small_flat, ((0, 0), (0, padding)))
    small_summed = lax.psum_scatter(small_flat, ("dp", "blk"), scatter_dimension=0)
    cuts = [sum(sizes[: i + 1]) for i in range(len(sizes) - 1)]
    parts = jnp.split(summed, cuts, axis=0)
    parts[5] = parts[5].reshape(D // count, -1)
    small_cuts = [sum(small_sizes[: i + 1]) for i in range(len(small_sizes))]
    small_parts = jnp.split(small_summed, small_cuts, axis=0)[:6]
    return (output, grad_tokens, *[part.T for part in parts], *small_parts, branch_rms)


MESH_ID = pl.DeviceIdType.MESH
F32 = jnp.float32
BF16 = jnp.bfloat16
TOK = 256
PACK = 512
FF = 4096
HALF_FF = 2048
HALF_D = 512
CHUNK = 32
VMEM_BYTES = 62 * 1024 * 1024
UNIT_ORDER = (
    "xywv",
    "xwyv",
    "ywxv",
    "wvxy",
    "yxwv",
    "wvyx",
    "xwvy",
    "yxwv",
    "xywv",
    "ywxv",
    "yxwv",
    "xywv",
)
SLOTS = (
    (0, 1, 20, 21, 30, 31,),
    (),
    (),
    (10, 40, 50,),
    (2, 22, 32,),
    (),
    (3, 11, 23,),
    (33, 41, 60,),
    (12, 42,),
    (34,),
    (4, 70, 13, 52,),
    (71,),
    (43, 62, 24,),
    (),
    (90,),
    (44, 72,),
    (61, 91, 35, 25, 120, 14, 73, 5, 26, 74, 92, 6, 80, 63, 81, 100, 64, 93, 36, 121, 45, 15, 110, 82, 65, 51, 75, 102, 46, 122, 83, 16,),
    (76, 101, 84, 111, 66, 94, 112, 53, 54, 103, 104, 123, 85, 113, 114, 124, 55, 95, 86, 105, 56, 96, 115, 106, 116,),
)


def mm(a, b):
    return jnp.dot(a, b, preferred_element_type=F32)


def mm_nt(a, b):
    return lax.dot_general(a, b, (((1,), (1,)), ((), ())), preferred_element_type=F32)


def al(offset, step):
    return pl.multiple_of(offset, step)


def norm_back(v, r, gain, grad):
    scaled = grad * gain
    inner = jnp.mean(v * scaled, axis=-1, keepdims=True)
    return r * scaled - v * (r * r * r * inner), jnp.sum(grad * v * r, axis=0, keepdims=True)


def inv_rms(v):
    return lax.rsqrt(jnp.mean(v * v, axis=-1, keepdims=True) + eps)


def layer_kernel(
    doc, tok, cot, gain_a, gain_b, gain_c, gain_d, bias_up, bias_down,
    wq_hbm, wk_hbm, wv_hbm, wo_hbm, wu_hbm, wd_hbm,
    out, grad_tok, rms, o_down, o_up, o_out, o_query, o_key, o_value,
    small_up, small_down, small_a, small_b, small_c, small_d,
    fin_up, wq, wk, wv, wo, wu, wd, xin, q_t, k_t, v_t, k_n, v_n, mask, attn_t, attn_nat, attn_oth,
    branch, hid, xm, act, g_t, part_send, part_recv, part_own, nat, gb_t, gba_t, ga_t,
    rope, lse, stat, s_down, r1_down, r2_down, r3_down, r4_down, r1_up, r2_up, r3_up, r4_up,
    r1_late, r2_late, r3_late, r4_late, fin_down, fin_late, rec_down, rec_late, aux_s, aux_r,
    w_sem, c_send, c_recv, rs_send, rs_recv, a_send, a_recv,
):
    dp = lax.axis_index("dp")
    b = lax.axis_index("blk")
    x = lax.rem(dp, 2)
    y = lax.rem(dp // 2, 2)
    z = dp // 4
    other = 1 - b
    core_peer = (dp, other)
    x_peer = (dp + 1 - 2 * x, b)
    y_peer = (dp + 2 - 4 * y, b)

    z_low = (dp + 4 - 8 * lax.rem(z, 2), b)
    z_high = (dp + 8 - 16 * (z // 2), b)
    barrier = pltpu.get_barrier_semaphore()
    for peer in (core_peer, x_peer, y_peer, z_low, z_high):
        pl.semaphore_signal(barrier, inc=1, device_id=peer, device_id_type=MESH_ID)

    own_cols = al(b * HALF_D, HALF_D)
    oth_cols = al(other * HALF_D, HALF_D)
    own_tok = al(b * TOK, TOK)
    oth_tok = al(other * TOK, TOK)

    w_copies = [
        pltpu.make_async_copy(src.at[:, pl.ds(own_cols, HALF_D)], dst, w_sem.at[i])
        for i, (src, dst) in enumerate(((wq_hbm, wq), (wk_hbm, wk), (wv_hbm, wv)))
    ]
    w_copies.append(pltpu.make_async_copy(wo_hbm, wo, w_sem.at[3]))
    for copy in w_copies:
        copy.start()

    def up_copy(j):
        return pltpu.make_async_copy(
            wu_hbm.at[:, pl.ds(al((2 * j + b) * 128, 128), 128)],
            wu.at[:, pl.ds(al(j * 128, 128), 128)],
            w_sem.at[4 + j],
        )

    def down_copy(j):
        return pltpu.make_async_copy(
            wd_hbm.at[pl.ds(al((2 * j + b) * 128, 128), 128)],
            wd.at[pl.ds(al(j * 128, 128), 128)],
            w_sem.at[20 + j],
        )

    lax.fori_loop(0, 16, lambda j, c: (up_copy(j).start(), c)[1], 0)
    lax.fori_loop(0, 16, lambda j, c: (down_copy(j).start(), c)[1], 0)

    def to_core(k, src, dst):
        return pltpu.make_async_remote_copy(
            src_ref=src, dst_ref=dst, send_sem=c_send.at[k], recv_sem=c_recv.at[k],
            device_id=core_peer, device_id_type=MESH_ID,
        )

    def pre_attn(i, carry):
        rows = pl.ds(al(i * CHUNK, CHUNK), CHUNK)
        v = tok[rows, :].astype(F32)
        xin[pl.ds(al(own_tok + i * CHUNK, CHUNK), CHUNK), :] = (
            v * inv_rms(v) * gain_a[...]
        ).astype(BF16)
        return carry

    lax.fori_loop(0, TOK // CHUNK, pre_attn, 0)
    pl.semaphore_wait(barrier, 5)
    own_rows = xin.at[pl.ds(own_tok, TOK)]
    xin_copy = to_core(0, own_rows, own_rows)
    xin_copy.start()

    end_a = doc[0, 0]
    end_b = end_a + doc[0, 1]
    end_c = end_b + doc[0, 2]
    index_row = lax.broadcasted_iota(jnp.int32, (1, PACK), 1)
    start_row = jnp.where(
        index_row >= end_c,
        end_c,
        jnp.where(index_row >= end_b, end_b, jnp.where(index_row >= end_a, end_a, 0)),
    )
    position = (index_row - start_row).astype(F32)
    freq = jnp.exp(
        lax.broadcasted_iota(jnp.int32, (32, PACK), 0).astype(F32) * (-math.log(10000.0) / 32.0)
    )
    angle = position * freq
    rope[0] = jnp.cos(angle)
    rope[1] = jnp.sin(angle)

    def fill_mask(i, carry):
        rows = pl.ds(al(i * 64, 64), 64)
        key_index = lax.broadcasted_iota(jnp.int32, (64, PACK), 0) + i * 64
        query_index = lax.broadcasted_iota(jnp.int32, (64, PACK), 1)
        allowed = (key_index <= query_index) & (key_index >= start_row)
        mask[rows, :] = jnp.where(allowed, 0.0, neg_big)
        return carry

    lax.fori_loop(0, 8, fill_mask, 0)

    def project(tok_at):
        rows = pl.ds(tok_at, TOK)
        cos = rope[0, :, rows]
        sin = rope[1, :, rows]
        x_rows = xin[rows, :]

        def turned(w, scale):
            flat = mm(x_rows, w[...]).T.reshape(8, 2, 32, TOK)
            low, high = flat[:, 0], flat[:, 1]
            both = jnp.stack([low * cos - high * sin, low * sin + high * cos], axis=1)
            return (both * scale).reshape(HALF_D, TOK).astype(BF16)

        q_t[:, rows] = turned(wq, 0.125)
        keys = turned(wk, 1.0)
        k_t[:, rows] = keys
        k_n[rows, :] = keys.T
        values = mm(x_rows, wv[...]).astype(BF16)
        v_n[rows, :] = values
        v_t[:, rows] = values.T

    for copy in w_copies[:3]:
        copy.wait()
    project(own_tok)
    xin_copy.wait()
    project(oth_tok)

    zeros = jnp.zeros((64, TOK), BF16)

    def slab(head_rows, which):
        return jnp.concatenate([head_rows, zeros] if which == 0 else [zeros, head_rows], axis=0)

    def attend(p, carry):
        slab_cols = pl.ds(al(p * 128, 128), 128)
        for which in range(2):
            rows = pl.ds(al(p * 128 + which * 64, 64), 64)
            for block in range(2):
                cols = slice(block * TOK, block * TOK + TOK)
                keys = (block + 1) * TOK
                scores = mm(k_n[:keys, slab_cols], slab(q_t[rows, cols], which)) + mask[:keys, cols]
                top = jnp.max(scores, axis=0, keepdims=True)
                weights = jnp.exp(scores - top)
                total = jnp.sum(weights, axis=0, keepdims=True)
                attn_t[rows, cols] = mm(v_t[rows, :keys], weights.astype(BF16)) * (1.0 / total)
                lse[pl.ds(p * 2 + which, 1), cols] = top + jnp.log(total)
        attn_nat[:, slab_cols] = attn_t[pl.ds(al(p * 128, 128), 128), :].T.astype(BF16)
        to_core(
            1 + p, attn_nat.at[pl.ds(oth_tok, TOK), slab_cols], attn_oth.at[:, slab_cols]
        ).start()
        return carry

    lax.fori_loop(0, 4, attend, 0)

    w_copies[3].wait()
    branch[...] = mm(attn_nat[pl.ds(own_tok, TOK), :], wo[pl.ds(own_cols, HALF_D), :])

    def attn_copy(p):
        cols = pl.ds(al(p * 128, 128), 128)
        return to_core(1 + p, attn_nat.at[pl.ds(oth_tok, TOK), cols], attn_oth.at[:, cols])

    lax.fori_loop(0, 4, lambda p, c: (attn_copy(p).wait(), c)[1], 0)
    branch[...] += mm(attn_oth[...], wo[pl.ds(oth_cols, HALF_D), :])

    def post_attn(i, carry):
        rows = pl.ds(al(i * CHUNK, CHUNK), CHUNK)
        v = branch[rows, :]
        square = jnp.mean(v * v, axis=-1, keepdims=True) + eps
        stat[0, rows, :] = jnp.broadcast_to(jnp.sqrt(square), (CHUNK, 128))
        h = tok[rows, :].astype(F32) + v * lax.rsqrt(square) * gain_b[...]
        hid[rows, :] = h
        xm[pl.ds(al(own_tok + i * CHUNK, CHUNK), CHUNK), :] = (
            h * inv_rms(h) * gain_c[...]
        ).astype(BF16)
        return carry

    lax.fori_loop(0, TOK // CHUNK, post_attn, 0)
    own_rows_m = xm.at[pl.ds(own_tok, TOK)]
    xm_copy = to_core(5, own_rows_m, own_rows_m)
    xm_copy.start()

    def up_step(tok_at, i):
        cols = pl.ds(al(i * 256, 256), 256)
        rows = pl.ds(tok_at, TOK)
        bias = jnp.concatenate(
            [bias_up[pl.ds(4 * i + b, 1), :], bias_up[pl.ds(4 * i + 2 + b, 1), :]], axis=1
        )
        pre = mm(xm[rows, :], wu[:, cols]) + bias
        square = pre * pre
        th = jnp.tanh(pre * (0.7978845608 + (0.7978845608 * 0.044715) * square))
        half = 0.5 + 0.5 * th
        act[rows, cols] = (pre * half).astype(BF16)
        slope = half + pre * (0.5 - 0.5 * th * th) * (
            0.7978845608 + (0.7978845608 * 0.134145) * square
        )
        g_t[cols, rows] = slope.astype(BF16).T

    lax.fori_loop(0, 16, lambda j, c: (up_copy(j).wait(), c)[1], 0)
    lax.fori_loop(0, 8, lambda i, c: (up_step(own_tok, i), c)[1], 0)
    xm_copy.wait()
    lax.fori_loop(0, 8, lambda i, c: (up_step(oth_tok, i), c)[1], 0)
    lax.fori_loop(0, 16, lambda j, c: (down_copy(j).wait(), c)[1], 0)

    def down_step(tok_at, dst, i):
        cols = pl.ds(al(i * 256, 256), 256)
        dst[:, cols] = mm(act[pl.ds(tok_at, TOK), :], wd[:, cols])

    lax.fori_loop(0, 4, lambda i, c: (down_step(oth_tok, part_send, i), c)[1], 0)
    mlp_copy = to_core(6, part_send, part_recv)
    mlp_copy.start()
    lax.fori_loop(0, 4, lambda i, c: (down_step(own_tok, part_own, i), c)[1], 0)
    mlp_copy.wait()

    def post_mlp(i, carry):
        sum_bias, sum_gain = carry
        rows = pl.ds(al(i * CHUNK, CHUNK), CHUNK)
        v = part_own[rows, :] + part_recv[rows, :] + bias_down[...]
        square = jnp.mean(v * v, axis=-1, keepdims=True) + eps
        stat[1, rows, :] = jnp.broadcast_to(jnp.sqrt(square), (CHUNK, 128))
        r = lax.rsqrt(square)
        out[rows, :] = (hid[rows, :] + v * r * gain_d[...]).astype(BF16)
        back, gain_part = norm_back(v, r, gain_d[...], cot[rows, :].astype(F32))
        back = back.astype(BF16)
        nat[rows, :] = back
        return (
            sum_bias + jnp.sum(back.astype(F32), axis=0, keepdims=True),
            sum_gain + gain_part,
        )

    zero_row = jnp.zeros((1, D), F32)
    sum_bias_down, sum_gain_d = lax.fori_loop(0, TOK // CHUNK, post_mlp, (zero_row, zero_row))
    aux_s[0] = jnp.zeros((16, D), F32)
    aux_s[0, 0:1, :] = sum_bias_down
    aux_s[0, 4:5, :] = sum_gain_d
    for i in range(2):
        rms[i : i + 1, :] = stat[i].T[0:1, :]

    def turn_to(dst):
        def step(i, carry):
            cols = pl.ds(al(i * 256, 256), 256)
            dst[cols, pl.ds(own_tok, TOK)] = nat[:, cols].T
            return carry

        lax.fori_loop(0, 4, step, 0)

    turn_to(gb_t)
    own_gb = gb_t.at[:, pl.ds(own_tok, TOK)]
    gb_copy = to_core(7, own_gb, own_gb)
    gb_copy.start()
    gb_copy.wait()

    down_refs = (s_down, r1_down, r2_down, r3_down, r4_down)
    up_refs = (wd, r1_up, r2_up, r3_up, r4_up)
    late_refs = (wu, r1_late, r2_late, r3_late, r4_late)
    units = (
        [(down_refs, 512 * i, 512, 64) for i in range(4)]
        + [(up_refs, 256 * i, 256, 128) for i in range(4)]
        + [(late_refs, 512 * i, 512, 64) for i in range(4)]
    )
    place = {
        "x": (x, 1, x_peer),
        "y": (y, 2, y_peer),
        "w": (lax.rem(z, 2), 4, z_low),
        "v": (z // 2, 8, z_high),
    }

    def unit_axes(n):
        return [place[letter] for letter in UNIT_ORDER[n]]

    def kept(n, steps):
        rows = units[n][3]
        return sum(
            (axis[0] * (8 >> i) * rows for i, axis in enumerate(unit_axes(n)[:steps])), 0
        )

    def unit_copy(n, k):
        refs, c0, width, rows = units[n]
        axes = unit_axes(n)
        cols = pl.ds(c0, width)
        if k < 2:
            bit, _, peer = axes[0]
            second = lax.rem(axes[1][0] + 1 + k, 2)
            count = 4 * rows
            src = refs[0].at[pl.ds(al(((1 - bit) * 2 + second) * count, count), count), cols]
            dst = refs[1].at[pl.ds(al(second * count, count), count), cols]
        else:
            bit, _, peer = axes[k - 1]
            count = (16 >> k) * rows
            at = kept(n, k - 1) + (1 - bit) * count
            src = refs[0].at[pl.ds(al(at, count), count), cols]
            dst = refs[k].at[:, cols]
        return pltpu.make_async_remote_copy(
            src_ref=src, dst_ref=dst, send_sem=rs_send.at[n, k], recv_sem=rs_recv.at[n, k],
            device_id=peer, device_id_type=MESH_ID,
        )

    def add_rows(n, at, arrived, arrived_at, count):
        refs, c0, width, _ = units[n]
        cols = pl.ds(c0, width)

        def step(i, carry):
            to = pl.ds(al(at + i * 64, 64), 64)
            got = refs[arrived][pl.ds(al(arrived_at + i * 64, 64), 64), cols]
            refs[0][to, cols] = (refs[0][to, cols].astype(F32) + got.astype(F32)).astype(BF16)
            return carry

        lax.fori_loop(0, count // 64, step, 0)

    def serve(n, k):
        refs, c0, width, rows = units[n]
        axes = unit_axes(n)
        unit_copy(n, k).wait_recv()
        if k < 2:
            second = lax.rem(axes[1][0] + 1 + k, 2)
            add_rows(n, kept(n, 1) + second * 4 * rows, 1, second * 4 * rows, 4 * rows)
            if k == 0:
                unit_copy(n, 2).start()
        elif k < 4:
            count = (8 >> k) * rows
            bit = axes[k][0]
            add_rows(n, kept(n, k) + (1 - bit) * count, k, (1 - bit) * count, count)
            unit_copy(n, k + 1).start()
            add_rows(n, kept(n, k) + bit * count, k, bit * count, count)
        else:
            cols = pl.ds(c0, width)
            dst = fin_down if n < 4 else fin_up if n < 8 else fin_late
            dst[:, cols] = refs[0][pl.ds(al(kept(n, 4), rows), rows), cols].astype(F32) + refs[4][
                :, cols
            ].astype(F32)
            if dst is fin_up:
                o_up[c0 : c0 + width, :] = fin_up[:, cols].T
            else:
                final_copy(n).start()

    oth_cut = pl.ds(al(other * 32, 32), 32)
    own_cut = pl.ds(al(b * 32, 32), 32)

    def final_copy(n):
        _, c0, width, _ = units[n]
        cols = pl.ds(c0, width)
        src, dst = (fin_down, rec_down) if n < 4 else (fin_late, rec_late)
        return to_core(14 + n, src.at[oth_cut, cols], dst.at[:, cols])

    aux_peers = (core_peer, x_peer, y_peer, z_low, z_high)

    def aux_copy(k):
        return pltpu.make_async_remote_copy(
            src_ref=aux_s.at[k], dst_ref=aux_r.at[k], send_sem=a_send.at[k],
            recv_sem=a_recv.at[k], device_id=aux_peers[k], device_id_type=MESH_ID,
        )

    def aux_end(k):
        aux_copy(k).wait_recv()
        aux_s[k + 1] = aux_s[k] + aux_r[k]
        if k < 4:
            aux_copy(k + 1).start()

    def slot(i):
        for code in SLOTS[i]:
            n, k = code // 10, code % 10
            if n == 12:
                aux_end(k)
            elif k < 2:
                unit_copy(n, k).start()
            else:
                serve(n, k - 2)

    def weight_grad(n, first, last, lhs, rhs, rhs_at):
        refs, c0, width, rows = units[n]
        axes = unit_axes(n)
        for g in range(first, last):
            i = lax.rem(axes[0][0] + 1 + g // 2, 2)
            j = lax.rem(axes[1][0] + 1 + g % 2, 2)
            base = i * axes[0][1] + j * axes[1][1]
            tails = [p * axes[2][1] + q * axes[3][1] for p in range(2) for q in range(2)]
            left = jnp.concatenate(
                [lhs[pl.ds(al((base + tail) * rows, rows), rows), :] for tail in tails], axis=0
            )
            right = rhs[:, pl.ds(al(rhs_at, 256), width)]
            at = pl.ds(al((i * 2 + j) * 4 * rows, 4 * rows), 4 * rows)
            refs[0][at, pl.ds(c0, width)] = mm(left, right).astype(BF16)

    for first in (0, 2):
        for n in range(4):
            weight_grad(n, first, first + 2, gb_t, act, 512 * n)
        slot(first // 2)

    def act_back(i, carry):
        rows = pl.ds(al(i * 256, 256), 256)
        g_t[rows, :] = (mm(wd[rows, :], gb_t[...]) * g_t[rows, :].astype(F32)).astype(BF16)
        return carry

    lax.fori_loop(0, 8, act_back, 0)
    slot(2)
    for first in (0, 2):
        for n in range(4, 8):
            weight_grad(n, first, first + 2, g_t, xm, 256 * (n - 4))
        slot(3 + first // 2)

    def mlp_back(tok_at, dst, i):
        at = pl.ds(al(i * 256, 256), 256)
        dst[:, at] = mm(wu[at, :], g_t[:, pl.ds(tok_at, TOK)]).T

    lax.fori_loop(0, 4, lambda i, c: (mlp_back(oth_tok, part_send, i), c)[1], 0)
    mlp_back_copy = to_core(8, part_send, part_recv)
    mlp_back_copy.start()
    slot(5)
    lax.fori_loop(0, 4, lambda i, c: (mlp_back(own_tok, part_own, i), c)[1], 0)
    ones = jnp.ones((16, PACK), BF16)
    for i in range(2):
        aux_s[0, pl.ds(8 + 2 * b + i, 1), :] = mm_nt(ones, g_t[i * 1024 : i * 1024 + 1024, :])[0:1]
    slot(6)
    mlp_back_copy.wait()

    def hidden_back(i, carry):
        sum_c, sum_b = carry
        rows = pl.ds(al(i * CHUNK, CHUNK), CHUNK)
        h = hid[rows, :]
        back, part_c = norm_back(
            h, inv_rms(h), gain_c[...], part_own[rows, :] + part_recv[rows, :]
        )
        g_hidden = cot[rows, :].astype(F32) + back
        hid[rows, :] = g_hidden
        v = branch[rows, :]
        back, part_b = norm_back(v, inv_rms(v), gain_b[...], g_hidden)
        nat[rows, :] = back.astype(BF16)
        return sum_c + part_c, sum_b + part_b

    sum_gain_c, sum_gain_b = lax.fori_loop(0, TOK // CHUNK, hidden_back, (zero_row, zero_row))
    aux_s[0, 3:4, :] = sum_gain_c
    aux_s[0, 2:3, :] = sum_gain_b
    turn_to(gba_t)
    own_gba = gba_t.at[:, pl.ds(own_tok, TOK)]
    gba_copy = to_core(9, own_gba, own_gba)
    gba_copy.start()
    slot(7)
    gba_copy.wait()

    weight_grad(8, 0, 4, gba_t, attn_nat, 0)
    slot(8)
    ga_t[...] = mm(wo[pl.ds(own_cols, HALF_D), :], gba_t[...]).astype(BF16)
    slot(9)

    gq, gk, gv = g_t.at[pl.ds(0, D)], g_t.at[pl.ds(D, D)], gb_t

    def attend_back(p, carry):
        slab_cols = pl.ds(al(p * 128, 128), 128)
        for which in range(2):
            rows = pl.ds(al(p * 128 + which * 64, 64), 64)
            to = pl.ds(al(own_cols + p * 128 + which * 64, 64), 64)
            grads_k, grads_v, grads_q = [], [], []
            for block in range(2):
                cols = slice(block * TOK, block * TOK + TOK)
                keys = (block + 1) * TOK
                q_rows = q_t[rows, cols]
                g_rows = ga_t[rows, cols]
                delta = jnp.sum(g_rows.astype(F32) * attn_t[rows, cols], axis=0, keepdims=True)
                scores = mm(k_n[:keys, slab_cols], slab(q_rows, which)) + mask[:keys, cols]
                probs = jnp.exp(scores - lse[pl.ds(p * 2 + which, 1), cols])
                g_probs = mm(v_n[:keys, slab_cols], slab(g_rows, which))
                g_scores = (probs * (g_probs - delta)).astype(BF16)
                grads_q.append(mm(k_t[rows, :keys], g_scores) * 0.125)
                grads_k.append(mm_nt(q_rows, g_scores))
                grads_v.append(mm_nt(g_rows, probs.astype(BF16)))
            for parts, dst in ((grads_q, gq), (grads_k, gk)):
                if dst is gq:
                    full = jnp.concatenate(parts, axis=1)
                else:
                    full = jnp.concatenate(
                        [parts[0] + parts[1][:, :TOK], parts[1][:, TOK:]], axis=1
                    )
                low, high = full[:32], full[32:]
                cos, sin = rope[0], rope[1]
                dst[to, :] = jnp.concatenate(
                    [low * cos + high * sin, high * cos - low * sin], axis=0
                ).astype(BF16)
            gv[to, :] = jnp.concatenate(
                [grads_v[0] + grads_v[1][:, :TOK], grads_v[1][:, TOK:]], axis=1
            ).astype(BF16)
        return carry

    lax.fori_loop(0, 2, attend_back, 0)
    slot(10)
    lax.fori_loop(2, 4, attend_back, 0)
    own_heads = pl.ds(own_cols, HALF_D)
    head_copies = [
        to_core(10 + i, ref.at[own_heads], ref.at[own_heads]) for i, ref in enumerate((gq, gk, gv))
    ]
    for copy in head_copies:
        copy.start()
    slot(11)

    def in_back(tok_at, dst, i):
        at = pl.ds(al(i * 256, 256), 256)
        cols = pl.ds(tok_at, TOK)
        total = mm(wq[at, :], gq[own_heads, cols])
        total += mm(wk[at, :], gk[own_heads, cols])
        total += mm(wv[at, :], gv[own_heads, cols])
        dst[:, at] = total.T

    lax.fori_loop(0, 4, lambda i, c: (in_back(oth_tok, part_send, i), c)[1], 0)
    in_back_copy = to_core(13, part_send, part_recv)
    in_back_copy.start()
    slot(12)
    for copy in head_copies:
        copy.wait()
    for first in (0, 2):
        for n, lhs in zip((9, 10, 11), (gq, gk, gv)):
            weight_grad(n, first, first + 2, lhs, xin, own_cols)
        slot(13 + first // 2)
    lax.fori_loop(0, 4, lambda i, c: (in_back(own_tok, part_own, i), c)[1], 0)
    slot(15)
    in_back_copy.wait()

    def token_back(i, carry):
        rows = pl.ds(al(i * CHUNK, CHUNK), CHUNK)
        v = tok[rows, :].astype(F32)
        back, part_a = norm_back(
            v, inv_rms(v), gain_a[...], part_own[rows, :] + part_recv[rows, :]
        )
        grad_tok[rows, :] = (hid[rows, :] + back).astype(BF16)
        return carry + part_a

    aux_s[0, 1:2, :] = lax.fori_loop(0, TOK // CHUNK, token_back, zero_row)

    aux_copy(0).start()
    slot(16)
    for n in range(4):
        final_copy(n).wait()

    def place_down(j, carry):
        from_cols = pl.ds(al(j * 128, 128), 128)
        o_down[:, pl.ds(al((2 * j + b) * 128, 128), 128)] = fin_down[own_cut, from_cols]
        o_down[:, pl.ds(al((2 * j + other) * 128, 128), 128)] = rec_down[:, from_cols]
        return carry

    lax.fori_loop(0, 16, place_down, 0)
    slot(17)
    device = dp * 2 + b
    at = pl.ds(al(device // 4 * 128, 128), 128)
    lines = pltpu.roll(aux_s[5, 0:8, at], lax.rem(128 - lax.rem(device, 4) * 32, 128), 1)
    for i, ref in enumerate((small_down, small_a, small_b, small_c, small_d)):
        ref[...] = lines[i, :32]
    lines = aux_s[5, 8:16, pl.ds(al(lax.rem(dp, 8) * 128, 128), 128)]
    chosen = lax.broadcasted_iota(jnp.int32, (8, 128), 0) == 2 * b + dp // 8
    small_up[...] = jnp.sum(jnp.where(chosen, lines, 0.0), axis=0)
    for n in range(12):
        for k in range(5):
            unit_copy(n, k).wait_send()
    for k in range(5):
        aux_copy(k).wait_send()
    for i in range(4):
        final_copy(8 + i).wait()
        cols = slice(i * 512, i * 512 + 512)
        dst = (o_out, o_query, o_key, o_value)[i]
        dst[:, pl.ds(own_cols, HALF_D)] = fin_late[own_cut, cols]
        dst[:, pl.ds(oth_cols, HALF_D)] = rec_late[:, cols]


def finish_kernel(*refs):
    count = len(refs) // 3
    sems = refs[-1]
    gets = [
        pltpu.make_async_copy(refs[i], refs[2 * count + i], sems.at[0, i]) for i in range(count)
    ]
    puts = [
        pltpu.make_async_copy(refs[2 * count + i], refs[count + i], sems.at[1, i])
        for i in range(count)
    ]
    for copy in gets:
        copy.start()
    for get, put in zip(gets, puts):
        get.wait()
        put.start()
    for copy in puts:
        copy.wait()


def layer_on_device(
    tokens, doc_lengths, w_query, w_key, w_value, w_out, w_up, w_down, bias_up, bias_down,
    gain_pre_attn, gain_post_attn, gain_pre_mlp, gain_post_mlp, cotangent,
):
    def v16(*shape):
        return pltpu.VMEM(shape, BF16)

    def v32(*shape):
        return pltpu.VMEM(shape, F32)

    dma = pltpu.SemaphoreType.DMA
    vmem = pl.BlockSpec(memory_space=pltpu.VMEM)
    scratch = [
        v32(128, 1024),
        v16(1024, 512), v16(1024, 512), v16(1024, 512), v16(1024, 1024),
        v16(1024, 2048), v16(2048, 1024),
        v16(512, 1024),
        v16(512, 512), v16(512, 512), v16(512, 512), v16(512, 512), v16(512, 512),
        v32(512, 512), v32(512, 512), v16(512, 512), v16(256, 512),
        v32(256, 1024), v32(256, 1024), v16(512, 1024),
        v16(512, 2048), v16(2048, 512),
        v32(256, 1024), v32(256, 1024), v32(256, 1024), v16(256, 1024),
        v16(1024, 512), v16(1024, 512), v16(512, 512),
        v32(2, 32, 512), v32(8, 512), v32(2, 256, 128),
        v16(1024, 2048), v16(512, 2048), v16(256, 2048), v16(128, 2048), v16(64, 2048),
        v16(1024, 1024), v16(512, 1024), v16(256, 1024), v16(128, 1024),
        v16(512, 2048), v16(256, 2048), v16(128, 2048), v16(64, 2048),
        v32(64, 2048), v32(64, 2048), v32(32, 2048), v32(32, 2048),
        v32(6, 16, 1024), v32(5, 16, 1024),
        dma((36,)), dma((26,)), dma((26,)), dma((12, 5)), dma((12, 5)), dma((5,)), dma((5,)),
    ]
    shapes = [((TOK, D), BF16)] * 2 + [((2, TOK), F32), ((32, FF), F32), ((D, 128), F32)]
    shapes += [((32, D), F32)] * 4 + [((128,), F32)] + [((32,), F32)] * 5
    shapes = [jax.ShapeDtypeStruct(*shape) for shape in shapes]
    results = pl.pallas_call(
        layer_kernel,
        out_shape=shapes,
        in_specs=[pl.BlockSpec(memory_space=pltpu.SMEM)]
        + [vmem] * 8
        + [pl.BlockSpec(memory_space=pl.ANY)] * 6,
        out_specs=[vmem] * 15,
        scratch_shapes=scratch,
        compiler_params=pltpu.CompilerParams(
            collective_id=0, has_side_effects=True, vmem_limit_bytes=VMEM_BYTES
        ),
    )(
        doc_lengths, tokens, cotangent,
        gain_pre_attn[None], gain_post_attn[None], gain_pre_mlp[None], gain_post_mlp[None],
        bias_up.reshape(32, 128), bias_down[None],
        w_query, w_key, w_value, w_out, w_up, w_down,
    )
    hbm = pl.BlockSpec(memory_space=pltpu.HBM)
    out, grad_tok, rms, gd, gu, go, gq, gk, gv, small_up, small_down, sa, sb, sc, sd = pl.pallas_call(
        finish_kernel,
        out_shape=shapes,
        in_specs=[hbm] * 15,
        out_specs=[hbm] * 15,
        scratch_shapes=[pltpu.VMEM(s.shape, s.dtype) for s in shapes] + [dma((2, 15))],
    )(*results)
    return (
        out, grad_tok, gq.T, gk.T, gv.T, go.T, gu, gd.T, small_up, small_down, sa, sb, sc, sd, rms
    )


def solution(mesh):
    placed = (
        P(("dp", "blk"), None),
        P("dp", None),
        P(),
        P(),
        P(),
        P(),
        P(),
        P(),
        P(),
        P(),
        P(),
        P(),
        P(),
        P(),
        P(("dp", "blk"), None),
    )
    paired = mesh.shape["blk"] == 2 and mesh.shape["dp"] == 16
    return jax.shard_map(
        layer_on_device if paired else on_device,
        mesh=mesh,
        in_specs=placed,
        out_specs=(
            P(("dp", "blk"), None),
            P(("dp", "blk"), None),
            P(None, ("dp", "blk")),
            P(None, ("dp", "blk")),
            P(None, ("dp", "blk")),
            P(None, ("dp", "blk")),
            P(None, ("dp", "blk")),
            P(None, ("dp", "blk")),
            P(("dp", "blk")),
            P(("dp", "blk")),
            P(("dp", "blk")),
            P(("dp", "blk")),
            P(("dp", "blk")),
            P(("dp", "blk")),
            P(None, ("dp", "blk")),
        ),
        check_vma=False,
    )
```

```python
import math

import jax
import jax.numpy as jnp
from jax import lax
from jax.experimental import pallas as pl
from jax.experimental.pallas import tpu as pltpu
from jax.sharding import PartitionSpec as P

D = 1024
H = 16
HD = 64


eps = 1e-06
neg_big = -1e30


def rms_norm(values, gain_row):
    return values * lax.rsqrt(jnp.mean(values * values, axis=-1, keepdims=True) + eps) * gain_row


def rotate(head_rows, position):
    half_size = head_rows.shape[-1] // 2
    frequency = 10000.0 ** (-2.0 * jnp.arange(half_size, dtype=jnp.float32) / head_rows.shape[-1])
    angles = position.astype(jnp.float32)[:, None] * frequency[None, :]
    cosine = jnp.cos(angles)[:, None, :]
    sine_part = jnp.sin(angles)[:, None, :]
    low_half = head_rows[..., :half_size]
    high_half = head_rows[..., half_size:]
    return jnp.concatenate(
        [low_half * cosine - high_half * sine_part, low_half * sine_part + high_half * cosine],
        axis=-1,
    )


def doc_layout(lengths, total_rows):
    index_row = jnp.arange(total_rows, dtype=jnp.int32)
    doc_ends = jnp.stack(
        [
            lengths[0],
            lengths[0] + lengths[1],
            lengths[0] + lengths[1] + lengths[2],
            lengths[0] + lengths[1] + lengths[2] + lengths[3],
        ]
    )
    segment = jnp.sum((index_row[:, None] >= doc_ends[None, :3]).astype(jnp.int32), axis=1)
    starts = doc_ends - lengths
    matches = segment[:, None] == jnp.arange(4, dtype=jnp.int32)[None, :]
    return (index_row, jnp.sum(jnp.where(matches, starts[None, :], 0), axis=1))


def block_mask(query_index, query_start, key_first, width):
    key_index = key_first + jnp.arange(width, dtype=jnp.int32)
    return (key_index[None, :] <= query_index[:, None]) & (
        key_index[None, :] >= query_start[:, None]
    )


def on_device(
    tokens,
    doc_lengths,
    w_query,
    w_key,
    w_value,
    w_out,
    w_up,
    w_down,
    bias_up,
    bias_down,
    gain_pre_attn,
    gain_post_attn,
    gain_pre_mlp,
    gain_post_mlp,
    cotangent,
):
    row_count = tokens.shape[0]
    cycle_size = lax.axis_size("blk")
    group_rows = row_count * cycle_size
    first_row = lax.axis_index("blk") * row_count
    index_all, start_all = doc_layout(doc_lengths[0], group_rows)
    query_index = lax.dynamic_slice_in_dim(index_all, first_row, row_count)
    query_start = lax.dynamic_slice_in_dim(start_all, first_row, row_count)
    position = query_index - query_start
    query_last = first_row + row_count - 1
    start_least = jnp.min(query_start)
    scale = HD ** (-0.5)
    tokens_f = tokens.astype(jnp.float32)
    normed_in, back_pre_attn = jax.vjp(rms_norm, tokens_f, gain_pre_attn)
    attn_in = normed_in.astype(jnp.bfloat16)
    query_pre = jnp.dot(attn_in, w_query, preferred_element_type=jnp.float32)
    key_pre = jnp.dot(attn_in, w_key, preferred_element_type=jnp.float32)
    value_pre = jnp.dot(attn_in, w_value, preferred_element_type=jnp.float32)
    queries, back_rot_query = jax.vjp(
        lambda arr: rotate(arr, position), query_pre.reshape(row_count, H, HD)
    )
    keys_rot, back_rot_key = jax.vjp(
        lambda arr: rotate(arr, position), key_pre.reshape(row_count, H, HD)
    )
    queries_low = queries.astype(jnp.bfloat16)
    keys_low = keys_rot.reshape(row_count, D).astype(jnp.bfloat16)
    values_low = value_pre.astype(jnp.bfloat16)
    initial = (
        jnp.full((H, row_count), neg_big, jnp.float32),
        jnp.zeros((H, row_count), jnp.float32),
        jnp.zeros((row_count, H, HD), jnp.float32),
    )
    key_piece = lax.all_gather(keys_low, "blk", axis=0, tiled=True)
    value_piece = lax.all_gather(values_low, "blk", axis=0, tiled=True)
    piece_rows = key_piece.shape[0]
    fold_width = math.gcd(piece_rows, 512)

    def one_block(state, number):
        key_first = number * fold_width

        def one_compute(state):
            running_top, totals, accum = state
            keys_blk = lax.dynamic_slice_in_dim(
                key_piece, number * fold_width, fold_width, 0
            ).reshape(fold_width, H, HD)
            values_blk = lax.dynamic_slice_in_dim(
                value_piece, number * fold_width, fold_width, 0
            ).reshape(fold_width, H, HD)
            scores = (
                jnp.einsum(
                    "qhd,khd->hqk", queries_low, keys_blk, preferred_element_type=jnp.float32
                )
                * scale
            )
            allowed = block_mask(query_index, query_start, key_first, fold_width)[None]
            scores = jnp.where(allowed, scores, neg_big)
            new_top = jnp.maximum(running_top, jnp.max(scores, axis=-1))
            weights = jnp.where(allowed, jnp.exp(scores - new_top[..., None]), 0.0)
            factor = jnp.exp(running_top - new_top)
            totals = totals * factor + jnp.sum(weights, axis=-1)
            accum = accum * jnp.transpose(factor)[:, :, None] + jnp.einsum(
                "hqk,khd->qhd",
                weights.astype(jnp.bfloat16),
                values_blk,
                preferred_element_type=jnp.float32,
            )
            return (new_top, totals, accum)

        active = (key_first <= query_last) & (key_first + fold_width - 1 >= start_least)
        return (lax.cond(active, one_compute, lambda state: state, state), None)

    result, unused = lax.scan(
        one_block, initial, jnp.arange(piece_rows // fold_width, dtype=jnp.int32)
    )
    running_top, totals, accum = result
    attn_full = accum / jnp.transpose(totals)[:, :, None]
    log_total = running_top + jnp.log(totals)
    attn_low = attn_full.reshape(row_count, D).astype(jnp.bfloat16)
    branch_attn = jnp.dot(attn_low, w_out, preferred_element_type=jnp.float32)
    post_attn, back_post_attn = jax.vjp(rms_norm, branch_attn, gain_post_attn)
    hidden_res = tokens_f + post_attn
    normed_mlp, back_pre_mlp = jax.vjp(rms_norm, hidden_res, gain_pre_mlp)
    mlp_in = normed_mlp.astype(jnp.bfloat16)
    pre_act = jnp.dot(mlp_in, w_up, preferred_element_type=jnp.float32) + bias_up
    activated, back_gelu = jax.vjp(lambda arr: jax.nn.gelu(arr, approximate=True), pre_act)
    act_low = activated.astype(jnp.bfloat16)
    branch_mlp = jnp.dot(act_low, w_down, preferred_element_type=jnp.float32) + bias_down
    post_mlp, back_post_mlp = jax.vjp(rms_norm, branch_mlp, gain_post_mlp)
    output = (hidden_res + post_mlp).astype(jnp.bfloat16)
    branch_rms = jnp.stack(
        [
            jnp.sqrt(jnp.mean(branch_attn * branch_attn, axis=-1) + eps),
            jnp.sqrt(jnp.mean(branch_mlp * branch_mlp, axis=-1) + eps),
        ]
    )
    grad_out_f = cotangent.astype(jnp.float32)
    grad_branch_mlp, grad_gain_post_mlp = back_post_mlp(grad_out_f)
    grad_mlp_low = grad_branch_mlp.astype(jnp.bfloat16)
    grad_bias_down = jnp.sum(grad_mlp_low.astype(jnp.float32), axis=0)
    grad_down = jnp.einsum("tf,td->df", act_low, grad_mlp_low, preferred_element_type=jnp.float32)
    grad_act = jnp.einsum("td,fd->tf", grad_mlp_low, w_down, preferred_element_type=jnp.float32)
    (grad_pre_act,) = back_gelu(grad_act)
    grad_pre_low = grad_pre_act.astype(jnp.bfloat16)
    grad_bias_up = jnp.sum(grad_pre_low.astype(jnp.float32), axis=0)
    grad_up = jnp.einsum("td,tf->fd", mlp_in, grad_pre_low, preferred_element_type=jnp.float32)
    grad_normed_mlp = jnp.einsum(
        "tf,df->td", grad_pre_low, w_up, preferred_element_type=jnp.float32
    )
    grad_res_part, grad_gain_pre_mlp = back_pre_mlp(grad_normed_mlp)
    grad_hidden = grad_out_f + grad_res_part
    grad_branch_attn, grad_gain_post_attn = back_post_attn(grad_hidden)
    grad_branch_low = grad_branch_attn.astype(jnp.bfloat16)
    grad_w_out = jnp.einsum(
        "td,te->ed", attn_low, grad_branch_low, preferred_element_type=jnp.float32
    )
    grad_attn = jnp.einsum("te,de->td", grad_branch_low, w_out, preferred_element_type=jnp.float32)
    grad_attn_low = grad_attn.astype(jnp.bfloat16).reshape(row_count, H, HD)
    delta = jnp.einsum("qhd,qhd->hq", grad_attn_low.astype(jnp.float32), attn_full)
    key_source, value_source = key_piece, value_piece
    width = math.gcd(group_rows, 512)

    def back_block(grad_query_acc, number):
        key_first = number * width

        def back_compute(grad_query_acc):
            keys_blk = lax.dynamic_slice_in_dim(key_source, key_first, width, 0).reshape(
                width, H, HD
            )
            values_blk = lax.dynamic_slice_in_dim(value_source, key_first, width, 0).reshape(
                width, H, HD
            )
            scores = (
                jnp.einsum(
                    "qhd,khd->hqk", queries_low, keys_blk, preferred_element_type=jnp.float32
                )
                * scale
            )
            allowed = block_mask(query_index, query_start, key_first, width)[None]
            probs = jnp.where(allowed, jnp.exp(scores - log_total[..., None]), 0.0)
            grad_probs = jnp.einsum(
                "qhd,khd->hqk", grad_attn_low, values_blk, preferred_element_type=jnp.float32
            )
            grad_scores = (probs * (grad_probs - delta[..., None])).astype(jnp.bfloat16)
            grad_query_acc = (
                grad_query_acc
                + jnp.einsum(
                    "hqk,khd->qhd", grad_scores, keys_blk, preferred_element_type=jnp.float32
                )
                * scale
            )
            grad_keys_blk = (
                jnp.einsum(
                    "hqk,qhd->khd", grad_scores, queries_low, preferred_element_type=jnp.float32
                )
                * scale
            )
            grad_values_blk = jnp.einsum(
                "hqk,qhd->khd",
                probs.astype(jnp.bfloat16),
                grad_attn_low,
                preferred_element_type=jnp.float32,
            )
            return (
                grad_query_acc,
                (grad_keys_blk.reshape(width, D), grad_values_blk.reshape(width, D)),
            )

        def skipped(grad_query_acc):
            return (
                grad_query_acc,
                (jnp.zeros((width, D), jnp.float32), jnp.zeros((width, D), jnp.float32)),
            )

        active = (key_first <= query_last) & (key_first + width - 1 >= start_least)
        return lax.cond(active, back_compute, skipped, grad_query_acc)

    grad_query_acc, stacked = lax.scan(
        back_block,
        jnp.zeros((row_count, H, HD), jnp.float32),
        jnp.arange(group_rows // width, dtype=jnp.int32),
    )
    grad_keys_all = stacked[0].reshape(group_rows, D)
    grad_values_all = stacked[1].reshape(group_rows, D)
    grad_keys_mine, grad_values_mine = (
        lax.psum_scatter(
            grad_keys_all.astype(jnp.bfloat16), "blk", scatter_dimension=0, tiled=True
        ).astype(jnp.float32),
        lax.psum_scatter(
            grad_values_all.astype(jnp.bfloat16), "blk", scatter_dimension=0, tiled=True
        ).astype(jnp.float32),
    )
    (grad_key_pre,) = back_rot_key(grad_keys_mine.reshape(row_count, H, HD))
    (grad_query_pre,) = back_rot_query(grad_query_acc)
    grad_key_low = grad_key_pre.reshape(row_count, D).astype(jnp.bfloat16)
    grad_query_low = grad_query_pre.reshape(row_count, D).astype(jnp.bfloat16)
    grad_value_low = grad_values_mine.astype(jnp.bfloat16)
    grad_query = jnp.einsum(
        "td,te->ed", attn_in, grad_query_low, preferred_element_type=jnp.float32
    )
    grad_key = jnp.einsum("td,te->ed", attn_in, grad_key_low, preferred_element_type=jnp.float32)
    grad_value = jnp.einsum(
        "td,te->ed", attn_in, grad_value_low, preferred_element_type=jnp.float32
    )
    grad_normed_in = (
        jnp.einsum("te,de->td", grad_query_low, w_query, preferred_element_type=jnp.float32)
        + jnp.einsum("te,de->td", grad_key_low, w_key, preferred_element_type=jnp.float32)
        + jnp.einsum("te,de->td", grad_value_low, w_value, preferred_element_type=jnp.float32)
    )
    grad_tokens_part, grad_gain_pre_attn = back_pre_attn(grad_normed_in)
    grad_tokens = (grad_hidden + grad_tokens_part).astype(jnp.bfloat16)
    count = lax.axis_size(("dp", "blk"))
    low = jnp.bfloat16
    pieces = [
        part.astype(low).reshape(count, -1, D)
        for part in (grad_query, grad_key, grad_value, grad_w_out, grad_up, grad_down)
    ]
    small = [
        part.reshape(count, -1)
        for part in (
            grad_bias_up,
            grad_bias_down,
            grad_gain_pre_attn,
            grad_gain_post_attn,
            grad_gain_pre_mlp,
            grad_gain_post_mlp,
        )
    ]
    sizes = [part.shape[1] for part in pieces]
    summed = lax.psum_scatter(
        jnp.concatenate(pieces, axis=1), ("dp", "blk"), scatter_dimension=0
    ).astype(jnp.float32)
    small_sizes = [part.shape[1] for part in small]
    small_flat = jnp.concatenate(small, axis=1)
    padding = -small_flat.shape[1] % 128
    small_flat = jnp.pad(small_flat, ((0, 0), (0, padding)))
    small_summed = lax.psum_scatter(small_flat, ("dp", "blk"), scatter_dimension=0)
    cuts = [sum(sizes[: i + 1]) for i in range(len(sizes) - 1)]
    parts = jnp.split(summed, cuts, axis=0)
    parts[5] = parts[5].reshape(D // count, -1)
    small_cuts = [sum(small_sizes[: i + 1]) for i in range(len(small_sizes))]
    small_parts = jnp.split(small_summed, small_cuts, axis=0)[:6]
    return (output, grad_tokens, *[part.T for part in parts], *small_parts, branch_rms)


MESH_ID = pl.DeviceIdType.MESH
F32 = jnp.float32
BF16 = jnp.bfloat16
TOK = 256
PACK = 512
FF = 4096
HALF_FF = 2048
HALF_D = 512
CHUNK = 128
VMEM_BYTES = 62 * 1024 * 1024
UNIT_ORDER = (
    "xywv",
    "xwyv",
    "ywxv",
    "wvxy",
    "yxwv",
    "wvyx",
    "xwvy",
    "yxwv",
    "xywv",
    "ywxv",
    "yxwv",
    "xywv",
)
SLOTS = (
    (0, 1, 20, 21, 30, 31,),
    (),
    (),
    (10, 40, 50,),
    (2, 22, 32,),
    (),
    (3, 11, 23,),
    (33, 41, 60,),
    (12, 42,),
    (34,),
    (4, 70, 13, 52,),
    (71,),
    (43, 62, 24,),
    (),
    (90,),
    (44, 72,),
    (61, 91, 35, 25, 120, 14, 73, 5, 26, 74, 92, 6, 80, 63, 81, 100, 64, 93, 36, 121, 45, 15, 110, 82, 65, 51, 75, 102, 46, 122, 83, 16,),
    (76, 101, 84, 111, 66, 94, 112, 53, 54, 103, 104, 123, 85, 113, 114, 124, 55, 95, 86, 105, 56, 96, 115, 106, 116,),
)


def mm(a, b):
    return jnp.dot(a, b, preferred_element_type=F32)


def mm_nt(a, b):
    return lax.dot_general(a, b, (((1,), (1,)), ((), ())), preferred_element_type=F32)


def al(offset, step):
    return pl.multiple_of(offset, step)


def norm_back(v, r, gain, grad):
    scaled = grad * gain
    inner = jnp.mean(v * scaled, axis=-1, keepdims=True)
    return r * scaled - v * (r * r * r * inner), jnp.sum(grad * v * r, axis=0, keepdims=True)


def inv_rms(v):
    return lax.rsqrt(jnp.mean(v * v, axis=-1, keepdims=True) + eps)


def layer_kernel(
    doc, tok, cot, gain_a, gain_b, gain_c, gain_d, bias_up, bias_down,
    wq_hbm, wk_hbm, wv_hbm, wo_hbm, wu_hbm, wd_hbm,
    out, grad_tok, rms, o_down, o_up, o_out, o_query, o_key, o_value,
    small_up, small_down, small_a, small_b, small_c, small_d,
    fin_up, wq, wk, wv, wo, wu, wd, xin, q_t, k_t, v_t, k_n, v_n, mask, attn_t, attn_nat, attn_oth,
    branch, hid, xm, act, g_t, part_send, part_recv, part_own, nat, gb_t, gba_t, ga_t,
    rope, lse, stat, s_down, r1_down, r2_down, r3_down, r4_down, r1_up, r2_up, r3_up, r4_up,
    r1_late, r2_late, r3_late, r4_late, fin_down, fin_late, rec_down, rec_late, aux_s, aux_r,
    w_sem, c_send, c_recv, rs_send, rs_recv, a_send, a_recv,
):
    dp = lax.axis_index("dp")
    b = lax.axis_index("blk")
    x = lax.rem(dp, 2)
    y = lax.rem(dp // 2, 2)
    z = dp // 4
    other = 1 - b
    core_peer = (dp, other)
    x_peer = (dp + 1 - 2 * x, b)
    y_peer = (dp + 2 - 4 * y, b)

    z_low = (dp + 4 - 8 * lax.rem(z, 2), b)
    z_high = (dp + 8 - 16 * (z // 2), b)
    barrier = pltpu.get_barrier_semaphore()
    for peer in (core_peer, x_peer, y_peer, z_low, z_high):
        pl.semaphore_signal(barrier, inc=1, device_id=peer, device_id_type=MESH_ID)

    own_cols = al(b * HALF_D, HALF_D)
    oth_cols = al(other * HALF_D, HALF_D)
    own_tok = al(b * TOK, TOK)
    oth_tok = al(other * TOK, TOK)

    w_copies = [
        pltpu.make_async_copy(src.at[:, pl.ds(own_cols, HALF_D)], dst, w_sem.at[i])
        for i, (src, dst) in enumerate(((wq_hbm, wq), (wk_hbm, wk), (wv_hbm, wv)))
    ]
    w_copies.append(pltpu.make_async_copy(wo_hbm, wo, w_sem.at[3]))
    for copy in w_copies:
        copy.start()

    def up_copy(j):
        return pltpu.make_async_copy(
            wu_hbm.at[:, pl.ds(al((2 * j + b) * 128, 128), 128)],
            wu.at[:, pl.ds(al(j * 128, 128), 128)],
            w_sem.at[4 + j],
        )

    def down_copy(j):
        return pltpu.make_async_copy(
            wd_hbm.at[pl.ds(al((2 * j + b) * 128, 128), 128)],
            wd.at[pl.ds(al(j * 128, 128), 128)],
            w_sem.at[20 + j],
        )

    lax.fori_loop(0, 16, lambda j, c: (up_copy(j).start(), c)[1], 0)
    lax.fori_loop(0, 16, lambda j, c: (down_copy(j).start(), c)[1], 0)

    def to_core(k, src, dst):
        return pltpu.make_async_remote_copy(
            src_ref=src, dst_ref=dst, send_sem=c_send.at[k], recv_sem=c_recv.at[k],
            device_id=core_peer, device_id_type=MESH_ID,
        )

    def pre_attn(i, carry):
        rows = pl.ds(al(i * CHUNK, CHUNK), CHUNK)
        v = tok[rows, :].astype(F32)
        xin[pl.ds(al(own_tok + i * CHUNK, CHUNK), CHUNK), :] = (
            v * inv_rms(v) * gain_a[...]
        ).astype(BF16)
        return carry

    lax.fori_loop(0, TOK // CHUNK, pre_attn, 0)
    pl.semaphore_wait(barrier, 5)
    own_rows = xin.at[pl.ds(own_tok, TOK)]
    xin_copy = to_core(0, own_rows, own_rows)
    xin_copy.start()

    end_a = doc[0, 0]
    end_b = end_a + doc[0, 1]
    end_c = end_b + doc[0, 2]
    index_row = lax.broadcasted_iota(jnp.int32, (1, PACK), 1)
    start_row = jnp.where(
        index_row >= end_c,
        end_c,
        jnp.where(index_row >= end_b, end_b, jnp.where(index_row >= end_a, end_a, 0)),
    )
    position = (index_row - start_row).astype(F32)
    freq = jnp.exp(
        lax.broadcasted_iota(jnp.int32, (32, PACK), 0).astype(F32) * (-math.log(10000.0) / 32.0)
    )
    angle = position * freq
    rope[0] = jnp.cos(angle)
    rope[1] = jnp.sin(angle)

    def fill_mask(i, carry):
        rows = pl.ds(al(i * 64, 64), 64)
        key_index = lax.broadcasted_iota(jnp.int32, (64, PACK), 0) + i * 64
        query_index = lax.broadcasted_iota(jnp.int32, (64, PACK), 1)
        allowed = (key_index <= query_index) & (key_index >= start_row)
        mask[rows, :] = jnp.where(allowed, 0.0, neg_big)
        return carry

    lax.fori_loop(0, 8, fill_mask, 0)

    def project(tok_at):
        rows = pl.ds(tok_at, TOK)
        cos = rope[0, :, rows]
        sin = rope[1, :, rows]
        x_rows = xin[rows, :]

        def turned(w, scale):
            flat = mm(x_rows, w[...]).T.reshape(8, 2, 32, TOK)
            low, high = flat[:, 0], flat[:, 1]
            both = jnp.stack([low * cos - high * sin, low * sin + high * cos], axis=1)
            return (both * scale).reshape(HALF_D, TOK).astype(BF16)

        q_t[:, rows] = turned(wq, 0.125)
        keys = turned(wk, 1.0)
        k_t[:, rows] = keys
        k_n[rows, :] = keys.T
        values = mm(x_rows, wv[...]).astype(BF16)
        v_n[rows, :] = values
        v_t[:, rows] = values.T

    for copy in w_copies[:3]:
        copy.wait()
    project(own_tok)
    xin_copy.wait()
    project(oth_tok)

    zeros = jnp.zeros((64, TOK), BF16)

    def slab(head_rows, which):
        return jnp.concatenate([head_rows, zeros] if which == 0 else [zeros, head_rows], axis=0)

    def attend(p, carry):
        slab_cols = pl.ds(al(p * 128, 128), 128)
        parts = [
            (w, pl.ds(al(p * 128 + w * 64, 64), 64), slice(i * TOK, i * TOK + TOK), (i + 1) * TOK)
            for i in (1, 0)
            for w in (0, 1)
        ]
        scores = [
            mm(k_n[:keys, slab_cols], slab(q_t[rows, cols], w)) + mask[:keys, cols]
            for w, rows, cols, keys in parts
        ]
        tops = [jnp.max(score, axis=0, keepdims=True) for score in scores]
        weights = [jnp.exp(score - top) for score, top in zip(scores, tops)]
        totals = [jnp.sum(weight, axis=0, keepdims=True) for weight in weights]
        for (w, rows, cols, keys), weight, top, total in zip(parts, weights, tops, totals):
            attn_t[rows, cols] = mm(v_t[rows, :keys], weight.astype(BF16)) * (1.0 / total)
            lse[pl.ds(p * 2 + w, 1), cols] = top + jnp.log(total)
        attn_nat[:, slab_cols] = attn_t[pl.ds(al(p * 128, 128), 128), :].T.astype(BF16)
        to_core(
            1 + p, attn_nat.at[pl.ds(oth_tok, TOK), slab_cols], attn_oth.at[:, slab_cols]
        ).start()
        return carry

    lax.fori_loop(0, 4, attend, 0)

    w_copies[3].wait()
    branch[...] = mm(attn_nat[pl.ds(own_tok, TOK), :], wo[pl.ds(own_cols, HALF_D), :])

    def attn_copy(p):
        cols = pl.ds(al(p * 128, 128), 128)
        return to_core(1 + p, attn_nat.at[pl.ds(oth_tok, TOK), cols], attn_oth.at[:, cols])

    lax.fori_loop(0, 4, lambda p, c: (attn_copy(p).wait(), c)[1], 0)
    branch[...] += mm(attn_oth[...], wo[pl.ds(oth_cols, HALF_D), :])

    def post_attn(i, carry):
        rows = pl.ds(al(i * CHUNK, CHUNK), CHUNK)
        v = branch[rows, :]
        square = jnp.mean(v * v, axis=-1, keepdims=True) + eps
        stat[0, rows, :] = jnp.broadcast_to(jnp.sqrt(square), (CHUNK, 128))
        h = tok[rows, :].astype(F32) + v * lax.rsqrt(square) * gain_b[...]
        hid[rows, :] = h
        xm[pl.ds(al(own_tok + i * CHUNK, CHUNK), CHUNK), :] = (
            h * inv_rms(h) * gain_c[...]
        ).astype(BF16)
        return carry

    lax.fori_loop(0, TOK // CHUNK, post_attn, 0)
    own_rows_m = xm.at[pl.ds(own_tok, TOK)]
    xm_copy = to_core(5, own_rows_m, own_rows_m)
    xm_copy.start()

    def up_step(tok_at, i):
        cols = pl.ds(al(i * 1024, 1024), 1024)
        rows = pl.ds(tok_at, TOK)
        bias = jnp.concatenate(
            [bias_up[pl.ds(16 * i + 2 * j + b, 1), :] for j in range(8)], axis=1
        )
        pre = mm(xm[rows, :], wu[:, cols]) + bias
        square = pre * pre
        th = jnp.tanh(pre * (0.7978845608 + (0.7978845608 * 0.044715) * square))
        half = 0.5 + 0.5 * th
        act[rows, cols] = (pre * half).astype(BF16)
        slope = half + pre * (0.5 - 0.5 * th * th) * (
            0.7978845608 + (0.7978845608 * 0.134145) * square
        )
        g_t[cols, rows] = slope.astype(BF16).T

    lax.fori_loop(0, 16, lambda j, c: (up_copy(j).wait(), c)[1], 0)
    lax.fori_loop(0, 2, lambda i, c: (up_step(own_tok, i), c)[1], 0)
    xm_copy.wait()
    lax.fori_loop(0, 2, lambda i, c: (up_step(oth_tok, i), c)[1], 0)
    lax.fori_loop(0, 16, lambda j, c: (down_copy(j).wait(), c)[1], 0)

    def down_step(tok_at, dst, i):
        cols = pl.ds(al(i * 1024, 1024), 1024)
        dst[:, cols] = mm(act[pl.ds(tok_at, TOK), :], wd[:, cols])

    down_step(oth_tok, part_send, 0)
    mlp_copy = to_core(6, part_send, part_recv)
    mlp_copy.start()
    down_step(own_tok, part_own, 0)
    mlp_copy.wait()

    def post_mlp(i, carry):
        sum_bias, sum_gain = carry
        rows = pl.ds(al(i * CHUNK, CHUNK), CHUNK)
        v = part_own[rows, :] + part_recv[rows, :] + bias_down[...]
        square = jnp.mean(v * v, axis=-1, keepdims=True) + eps
        stat[1, rows, :] = jnp.broadcast_to(jnp.sqrt(square), (CHUNK, 128))
        r = lax.rsqrt(square)
        out[rows, :] = (hid[rows, :] + v * r * gain_d[...]).astype(BF16)
        back, gain_part = norm_back(v, r, gain_d[...], cot[rows, :].astype(F32))
        back = back.astype(BF16)
        nat[rows, :] = back
        return (
            sum_bias + jnp.sum(back.astype(F32), axis=0, keepdims=True),
            sum_gain + gain_part,
        )

    zero_row = jnp.zeros((1, D), F32)
    sum_bias_down, sum_gain_d = lax.fori_loop(0, TOK // CHUNK, post_mlp, (zero_row, zero_row))
    aux_s[0] = jnp.zeros((16, D), F32)
    aux_s[0, 0:1, :] = sum_bias_down
    aux_s[0, 4:5, :] = sum_gain_d
    for i in range(2):
        rms[i : i + 1, :] = stat[i].T[0:1, :]

    def turn_to(dst):
        def step(i, carry):
            cols = pl.ds(al(i * 256, 256), 256)
            dst[cols, pl.ds(own_tok, TOK)] = nat[:, cols].T
            return carry

        lax.fori_loop(0, 4, step, 0)

    turn_to(gb_t)
    own_gb = gb_t.at[:, pl.ds(own_tok, TOK)]
    gb_copy = to_core(7, own_gb, own_gb)
    gb_copy.start()
    gb_copy.wait()

    down_refs = (s_down, r1_down, r2_down, r3_down, r4_down)
    up_refs = (wd, r1_up, r2_up, r3_up, r4_up)
    late_refs = (wu, r1_late, r2_late, r3_late, r4_late)
    units = (
        [(down_refs, 512 * i, 512, 64) for i in range(4)]
        + [(up_refs, 256 * i, 256, 128) for i in range(4)]
        + [(late_refs, 512 * i, 512, 64) for i in range(4)]
    )
    place = {
        "x": (x, 1, x_peer),
        "y": (y, 2, y_peer),
        "w": (lax.rem(z, 2), 4, z_low),
        "v": (z // 2, 8, z_high),
    }

    def unit_axes(n):
        return [place[letter] for letter in UNIT_ORDER[n]]

    def kept(n, steps):
        rows = units[n][3]
        return sum(
            (axis[0] * (8 >> i) * rows for i, axis in enumerate(unit_axes(n)[:steps])), 0
        )

    def unit_copy(n, k):
        refs, c0, width, rows = units[n]
        axes = unit_axes(n)
        cols = pl.ds(c0, width)
        if k < 2:
            bit, _, peer = axes[0]
            second = lax.rem(axes[1][0] + 1 + k, 2)
            count = 4 * rows
            src = refs[0].at[pl.ds(al(((1 - bit) * 2 + second) * count, count), count), cols]
            dst = refs[1].at[pl.ds(al(second * count, count), count), cols]
        else:
            bit, _, peer = axes[k - 1]
            count = (16 >> k) * rows
            at = kept(n, k - 1) + (1 - bit) * count
            src = refs[0].at[pl.ds(al(at, count), count), cols]
            dst = refs[k].at[:, cols]
        return pltpu.make_async_remote_copy(
            src_ref=src, dst_ref=dst, send_sem=rs_send.at[n, k], recv_sem=rs_recv.at[n, k],
            device_id=peer, device_id_type=MESH_ID,
        )

    def add_rows(n, at, arrived, arrived_at, count):
        refs, c0, width, _ = units[n]
        cols = pl.ds(c0, width)

        def step(i, carry):
            to = pl.ds(al(at + i * 64, 64), 64)
            got = refs[arrived][pl.ds(al(arrived_at + i * 64, 64), 64), cols]
            refs[0][to, cols] = (refs[0][to, cols].astype(F32) + got.astype(F32)).astype(BF16)
            return carry

        lax.fori_loop(0, count // 64, step, 0)

    def serve(n, k):
        refs, c0, width, rows = units[n]
        axes = unit_axes(n)
        unit_copy(n, k).wait_recv()
        if k < 2:
            second = lax.rem(axes[1][0] + 1 + k, 2)
            add_rows(n, kept(n, 1) + second * 4 * rows, 1, second * 4 * rows, 4 * rows)
            if k == 0:
                unit_copy(n, 2).start()
        elif k < 4:
            count = (8 >> k) * rows
            bit = axes[k][0]
            add_rows(n, kept(n, k) + (1 - bit) * count, k, (1 - bit) * count, count)
            unit_copy(n, k + 1).start()
            add_rows(n, kept(n, k) + bit * count, k, bit * count, count)
        else:
            cols = pl.ds(c0, width)
            dst = fin_down if n < 4 else fin_up if n < 8 else fin_late
            dst[:, cols] = refs[0][pl.ds(al(kept(n, 4), rows), rows), cols].astype(F32) + refs[4][
                :, cols
            ].astype(F32)
            if dst is fin_up:
                o_up[c0 : c0 + width, :] = fin_up[:, cols].T
            else:
                final_copy(n).start()

    oth_cut = pl.ds(al(other * 32, 32), 32)
    own_cut = pl.ds(al(b * 32, 32), 32)

    def final_copy(n):
        _, c0, width, _ = units[n]
        cols = pl.ds(c0, width)
        src, dst = (fin_down, rec_down) if n < 4 else (fin_late, rec_late)
        return to_core(14 + n, src.at[oth_cut, cols], dst.at[:, cols])

    aux_peers = (core_peer, x_peer, y_peer, z_low, z_high)

    def aux_copy(k):
        return pltpu.make_async_remote_copy(
            src_ref=aux_s.at[k], dst_ref=aux_r.at[k], send_sem=a_send.at[k],
            recv_sem=a_recv.at[k], device_id=aux_peers[k], device_id_type=MESH_ID,
        )

    def aux_end(k):
        aux_copy(k).wait_recv()
        aux_s[k + 1] = aux_s[k] + aux_r[k]
        if k < 4:
            aux_copy(k + 1).start()

    def slot(i):
        for code in SLOTS[i]:
            n, k = code // 10, code % 10
            if n == 12:
                aux_end(k)
            elif k < 2:
                unit_copy(n, k).start()
            else:
                serve(n, k - 2)

    def weight_grad(n, first, last, lhs, rhs, rhs_at):
        refs, c0, width, rows = units[n]
        axes = unit_axes(n)
        for g in range(first, last):
            i = lax.rem(axes[0][0] + 1 + g // 2, 2)
            j = lax.rem(axes[1][0] + 1 + g % 2, 2)
            base = i * axes[0][1] + j * axes[1][1]
            tails = [p * axes[2][1] + q * axes[3][1] for p in range(2) for q in range(2)]
            left = jnp.concatenate(
                [lhs[pl.ds(al((base + tail) * rows, rows), rows), :] for tail in tails], axis=0
            )
            right = rhs[:, pl.ds(al(rhs_at, 256), width)]
            at = pl.ds(al((i * 2 + j) * 4 * rows, 4 * rows), 4 * rows)
            refs[0][at, pl.ds(c0, width)] = mm(left, right).astype(BF16)

    for first in (0, 2):
        for n in range(4):
            weight_grad(n, first, first + 2, gb_t, act, 512 * n)
        slot(first // 2)

    def act_back(i, carry):
        rows = pl.ds(al(i * 512, 512), 512)
        g_t[rows, :] = (mm(wd[rows, :], gb_t[...]) * g_t[rows, :].astype(F32)).astype(BF16)
        return carry

    lax.fori_loop(0, 4, act_back, 0)
    slot(2)
    for first in (0, 2):
        for n in range(4, 8):
            weight_grad(n, first, first + 2, g_t, xm, 256 * (n - 4))
        slot(3 + first // 2)

    def mlp_back(tok_at, dst, i):
        at = pl.ds(al(i * 512, 512), 512)
        dst[:, at] = mm(wu[at, :], g_t[:, pl.ds(tok_at, TOK)]).T

    lax.fori_loop(0, 2, lambda i, c: (mlp_back(oth_tok, part_send, i), c)[1], 0)
    mlp_back_copy = to_core(8, part_send, part_recv)
    mlp_back_copy.start()
    slot(5)
    lax.fori_loop(0, 2, lambda i, c: (mlp_back(own_tok, part_own, i), c)[1], 0)
    ones = jnp.ones((16, PACK), BF16)
    for i in range(2):
        aux_s[0, pl.ds(8 + 2 * b + i, 1), :] = mm_nt(ones, g_t[i * 1024 : i * 1024 + 1024, :])[0:1]
    slot(6)
    mlp_back_copy.wait()

    def hidden_back(i, carry):
        sum_c, sum_b = carry
        rows = pl.ds(al(i * CHUNK, CHUNK), CHUNK)
        h = hid[rows, :]
        back, part_c = norm_back(
            h, inv_rms(h), gain_c[...], part_own[rows, :] + part_recv[rows, :]
        )
        g_hidden = cot[rows, :].astype(F32) + back
        hid[rows, :] = g_hidden
        v = branch[rows, :]
        back, part_b = norm_back(v, inv_rms(v), gain_b[...], g_hidden)
        nat[rows, :] = back.astype(BF16)
        return sum_c + part_c, sum_b + part_b

    sum_gain_c, sum_gain_b = lax.fori_loop(0, TOK // CHUNK, hidden_back, (zero_row, zero_row))
    aux_s[0, 3:4, :] = sum_gain_c
    aux_s[0, 2:3, :] = sum_gain_b
    turn_to(gba_t)
    own_gba = gba_t.at[:, pl.ds(own_tok, TOK)]
    gba_copy = to_core(9, own_gba, own_gba)
    gba_copy.start()
    slot(7)
    gba_copy.wait()

    weight_grad(8, 0, 4, gba_t, attn_nat, 0)
    slot(8)
    ga_t[...] = mm(wo[pl.ds(own_cols, HALF_D), :], gba_t[...]).astype(BF16)
    slot(9)

    gq, gk, gv = g_t.at[pl.ds(0, D)], g_t.at[pl.ds(D, D)], gb_t

    def attend_back(p, carry):
        slab_cols = pl.ds(al(p * 128, 128), 128)
        parts = [
            (w, pl.ds(al(p * 128 + w * 64, 64), 64), slice(i * TOK, i * TOK + TOK), (i + 1) * TOK)
            for w in (0, 1)
            for i in (0, 1)
        ]
        deltas = [
            jnp.sum(ga_t[rows, cols].astype(F32) * attn_t[rows, cols], axis=0, keepdims=True)
            for w, rows, cols, keys in parts
        ]
        scores = [
            mm(k_n[:keys, slab_cols], slab(q_t[rows, cols], w)) + mask[:keys, cols]
            for w, rows, cols, keys in parts
        ]
        g_probs = [
            mm(v_n[:keys, slab_cols], slab(ga_t[rows, cols], w)) for w, rows, cols, keys in parts
        ]
        probs = [
            jnp.exp(score - lse[pl.ds(p * 2 + part[0], 1), part[2]])
            for score, part in zip(scores, parts)
        ]
        g_scores = [
            (prob * (g_prob - delta)).astype(BF16)
            for prob, g_prob, delta in zip(probs, g_probs, deltas)
        ]
        grads_q = [
            mm(k_t[rows, :keys], g_score) * 0.125
            for (w, rows, cols, keys), g_score in zip(parts, g_scores)
        ]
        grads_k = [
            mm_nt(q_t[rows, cols], g_score)
            for (w, rows, cols, keys), g_score in zip(parts, g_scores)
        ]
        grads_v = [
            mm_nt(ga_t[rows, cols], prob.astype(BF16))
            for (w, rows, cols, keys), prob in zip(parts, probs)
        ]

        def both(first, second):
            return jnp.concatenate([first + second[:, :TOK], second[:, TOK:]], axis=1)

        cos, sin = rope[0], rope[1]
        for w in range(2):
            to = pl.ds(al(own_cols + p * 128 + w * 64, 64), 64)
            full_q = jnp.concatenate(grads_q[2 * w : 2 * w + 2], axis=1)
            for full, dst in ((full_q, gq), (both(*grads_k[2 * w : 2 * w + 2]), gk)):
                low, high = full[:32], full[32:]
                dst[to, :] = jnp.concatenate(
                    [low * cos + high * sin, high * cos - low * sin], axis=0
                ).astype(BF16)
            gv[to, :] = both(*grads_v[2 * w : 2 * w + 2]).astype(BF16)
        return carry

    lax.fori_loop(0, 2, attend_back, 0)
    slot(10)
    lax.fori_loop(2, 4, attend_back, 0)
    own_heads = pl.ds(own_cols, HALF_D)
    head_copies = [
        to_core(10 + i, ref.at[own_heads], ref.at[own_heads]) for i, ref in enumerate((gq, gk, gv))
    ]
    for copy in head_copies:
        copy.start()
    slot(11)

    def in_back(tok_at, dst, i):
        at = pl.ds(al(i * 512, 512), 512)
        cols = pl.ds(tok_at, TOK)
        total = mm(wq[at, :], gq[own_heads, cols])
        total += mm(wk[at, :], gk[own_heads, cols])
        total += mm(wv[at, :], gv[own_heads, cols])
        dst[:, at] = total.T

    lax.fori_loop(0, 2, lambda i, c: (in_back(oth_tok, part_send, i), c)[1], 0)
    in_back_copy = to_core(13, part_send, part_recv)
    in_back_copy.start()
    slot(12)
    for copy in head_copies:
        copy.wait()
    for first in (0, 2):
        for n, lhs in zip((9, 10, 11), (gq, gk, gv)):
            weight_grad(n, first, first + 2, lhs, xin, own_cols)
        slot(13 + first // 2)
    lax.fori_loop(0, 2, lambda i, c: (in_back(own_tok, part_own, i), c)[1], 0)
    slot(15)
    in_back_copy.wait()

    def token_back(i, carry):
        rows = pl.ds(al(i * CHUNK, CHUNK), CHUNK)
        v = tok[rows, :].astype(F32)
        back, part_a = norm_back(
            v, inv_rms(v), gain_a[...], part_own[rows, :] + part_recv[rows, :]
        )
        grad_tok[rows, :] = (hid[rows, :] + back).astype(BF16)
        return carry + part_a

    aux_s[0, 1:2, :] = lax.fori_loop(0, TOK // CHUNK, token_back, zero_row)

    aux_copy(0).start()
    slot(16)
    for n in range(4):
        final_copy(n).wait()

    def place_down(j, carry):
        from_cols = pl.ds(al(j * 128, 128), 128)
        o_down[:, pl.ds(al((2 * j + b) * 128, 128), 128)] = fin_down[own_cut, from_cols]
        o_down[:, pl.ds(al((2 * j + other) * 128, 128), 128)] = rec_down[:, from_cols]
        return carry

    lax.fori_loop(0, 16, place_down, 0)
    slot(17)
    device = dp * 2 + b
    at = pl.ds(al(device // 4 * 128, 128), 128)
    lines = pltpu.roll(aux_s[5, 0:8, at], lax.rem(128 - lax.rem(device, 4) * 32, 128), 1)
    for i, ref in enumerate((small_down, small_a, small_b, small_c, small_d)):
        ref[...] = lines[i, :32]
    lines = aux_s[5, 8:16, pl.ds(al(lax.rem(dp, 8) * 128, 128), 128)]
    chosen = lax.broadcasted_iota(jnp.int32, (8, 128), 0) == 2 * b + dp // 8
    small_up[...] = jnp.sum(jnp.where(chosen, lines, 0.0), axis=0)
    for n in range(12):
        for k in range(5):
            unit_copy(n, k).wait_send()
    for k in range(5):
        aux_copy(k).wait_send()
    for i in range(4):
        final_copy(8 + i).wait()
        cols = slice(i * 512, i * 512 + 512)
        dst = (o_out, o_query, o_key, o_value)[i]
        dst[:, pl.ds(own_cols, HALF_D)] = fin_late[own_cut, cols]
        dst[:, pl.ds(oth_cols, HALF_D)] = rec_late[:, cols]


def finish_kernel(*refs):
    count = len(refs) // 3
    sems = refs[-1]
    gets = [
        pltpu.make_async_copy(refs[i], refs[2 * count + i], sems.at[0, i]) for i in range(count)
    ]
    puts = [
        pltpu.make_async_copy(refs[2 * count + i], refs[count + i], sems.at[1, i])
        for i in range(count)
    ]
    for copy in gets:
        copy.start()
    for get, put in zip(gets, puts):
        get.wait()
        put.start()
    for copy in puts:
        copy.wait()


def layer_on_device(
    tokens, doc_lengths, w_query, w_key, w_value, w_out, w_up, w_down, bias_up, bias_down,
    gain_pre_attn, gain_post_attn, gain_pre_mlp, gain_post_mlp, cotangent,
):
    def v16(*shape):
        return pltpu.VMEM(shape, BF16)

    def v32(*shape):
        return pltpu.VMEM(shape, F32)

    dma = pltpu.SemaphoreType.DMA
    vmem = pl.BlockSpec(memory_space=pltpu.VMEM)
    scratch = [
        v32(128, 1024),
        v16(1024, 512), v16(1024, 512), v16(1024, 512), v16(1024, 1024),
        v16(1024, 2048), v16(2048, 1024),
        v16(512, 1024),
        v16(512, 512), v16(512, 512), v16(512, 512), v16(512, 512), v16(512, 512),
        v32(512, 512), v32(512, 512), v16(512, 512), v16(256, 512),
        v32(256, 1024), v32(256, 1024), v16(512, 1024),
        v16(512, 2048), v16(2048, 512),
        v32(256, 1024), v32(256, 1024), v32(256, 1024), v16(256, 1024),
        v16(1024, 512), v16(1024, 512), v16(512, 512),
        v32(2, 32, 512), v32(8, 512), v32(2, 256, 128),
        v16(1024, 2048), v16(512, 2048), v16(256, 2048), v16(128, 2048), v16(64, 2048),
        v16(1024, 1024), v16(512, 1024), v16(256, 1024), v16(128, 1024),
        v16(512, 2048), v16(256, 2048), v16(128, 2048), v16(64, 2048),
        v32(64, 2048), v32(64, 2048), v32(32, 2048), v32(32, 2048),
        v32(6, 16, 1024), v32(5, 16, 1024),
        dma((36,)), dma((26,)), dma((26,)), dma((12, 5)), dma((12, 5)), dma((5,)), dma((5,)),
    ]
    shapes = [((TOK, D), BF16)] * 2 + [((2, TOK), F32), ((32, FF), F32), ((D, 128), F32)]
    shapes += [((32, D), F32)] * 4 + [((128,), F32)] + [((32,), F32)] * 5
    shapes = [jax.ShapeDtypeStruct(*shape) for shape in shapes]
    results = pl.pallas_call(
        layer_kernel,
        out_shape=shapes,
        in_specs=[pl.BlockSpec(memory_space=pltpu.SMEM)]
        + [vmem] * 8
        + [pl.BlockSpec(memory_space=pl.ANY)] * 6,
        out_specs=[vmem] * 15,
        scratch_shapes=scratch,
        compiler_params=pltpu.CompilerParams(
            collective_id=0, has_side_effects=True, vmem_limit_bytes=VMEM_BYTES
        ),
    )(
        doc_lengths, tokens, cotangent,
        gain_pre_attn[None], gain_post_attn[None], gain_pre_mlp[None], gain_post_mlp[None],
        bias_up.reshape(32, 128), bias_down[None],
        w_query, w_key, w_value, w_out, w_up, w_down,
    )
    hbm = pl.BlockSpec(memory_space=pltpu.HBM)
    out, grad_tok, rms, gd, gu, go, gq, gk, gv, small_up, small_down, sa, sb, sc, sd = pl.pallas_call(
        finish_kernel,
        out_shape=shapes,
        in_specs=[hbm] * 15,
        out_specs=[hbm] * 15,
        scratch_shapes=[pltpu.VMEM(s.shape, s.dtype) for s in shapes] + [dma((2, 15))],
    )(*results)
    return (
        out, grad_tok, gq.T, gk.T, gv.T, go.T, gu, gd.T, small_up, small_down, sa, sb, sc, sd, rms
    )


def solution(mesh):
    placed = (
        P(("dp", "blk"), None),
        P("dp", None),
        P(),
        P(),
        P(),
        P(),
        P(),
        P(),
        P(),
        P(),
        P(),
        P(),
        P(),
        P(),
        P(("dp", "blk"), None),
    )
    paired = mesh.shape["blk"] == 2 and mesh.shape["dp"] == 16
    return jax.shard_map(
        layer_on_device if paired else on_device,
        mesh=mesh,
        in_specs=placed,
        out_specs=(
            P(("dp", "blk"), None),
            P(("dp", "blk"), None),
            P(None, ("dp", "blk")),
            P(None, ("dp", "blk")),
            P(None, ("dp", "blk")),
            P(None, ("dp", "blk")),
            P(None, ("dp", "blk")),
            P(None, ("dp", "blk")),
            P(("dp", "blk")),
            P(("dp", "blk")),
            P(("dp", "blk")),
            P(("dp", "blk")),
            P(("dp", "blk")),
            P(("dp", "blk")),
            P(None, ("dp", "blk")),
        ),
        check_vma=False,
    )
```

```python
import math

import jax
import jax.numpy as jnp
from jax import lax
from jax.experimental import pallas as pl
from jax.experimental.pallas import tpu as pltpu
from jax.sharding import PartitionSpec as P

D = 1024
H = 16
HD = 64


eps = 1e-06
neg_big = -1e30


def rms_norm(values, gain_row):
    return values * lax.rsqrt(jnp.mean(values * values, axis=-1, keepdims=True) + eps) * gain_row


def rotate(head_rows, position):
    half_size = head_rows.shape[-1] // 2
    frequency = 10000.0 ** (-2.0 * jnp.arange(half_size, dtype=jnp.float32) / head_rows.shape[-1])
    angles = position.astype(jnp.float32)[:, None] * frequency[None, :]
    cosine = jnp.cos(angles)[:, None, :]
    sine_part = jnp.sin(angles)[:, None, :]
    low_half = head_rows[..., :half_size]
    high_half = head_rows[..., half_size:]
    return jnp.concatenate(
        [low_half * cosine - high_half * sine_part, low_half * sine_part + high_half * cosine],
        axis=-1,
    )


def doc_layout(lengths, total_rows):
    index_row = jnp.arange(total_rows, dtype=jnp.int32)
    doc_ends = jnp.stack(
        [
            lengths[0],
            lengths[0] + lengths[1],
            lengths[0] + lengths[1] + lengths[2],
            lengths[0] + lengths[1] + lengths[2] + lengths[3],
        ]
    )
    segment = jnp.sum((index_row[:, None] >= doc_ends[None, :3]).astype(jnp.int32), axis=1)
    starts = doc_ends - lengths
    matches = segment[:, None] == jnp.arange(4, dtype=jnp.int32)[None, :]
    return (index_row, jnp.sum(jnp.where(matches, starts[None, :], 0), axis=1))


def block_mask(query_index, query_start, key_first, width):
    key_index = key_first + jnp.arange(width, dtype=jnp.int32)
    return (key_index[None, :] <= query_index[:, None]) & (
        key_index[None, :] >= query_start[:, None]
    )


def on_device(
    tokens,
    doc_lengths,
    w_query,
    w_key,
    w_value,
    w_out,
    w_up,
    w_down,
    bias_up,
    bias_down,
    gain_pre_attn,
    gain_post_attn,
    gain_pre_mlp,
    gain_post_mlp,
    cotangent,
):
    row_count = tokens.shape[0]
    cycle_size = lax.axis_size("blk")
    group_rows = row_count * cycle_size
    first_row = lax.axis_index("blk") * row_count
    index_all, start_all = doc_layout(doc_lengths[0], group_rows)
    query_index = lax.dynamic_slice_in_dim(index_all, first_row, row_count)
    query_start = lax.dynamic_slice_in_dim(start_all, first_row, row_count)
    position = query_index - query_start
    query_last = first_row + row_count - 1
    start_least = jnp.min(query_start)
    scale = HD ** (-0.5)
    tokens_f = tokens.astype(jnp.float32)
    normed_in, back_pre_attn = jax.vjp(rms_norm, tokens_f, gain_pre_attn)
    attn_in = normed_in.astype(jnp.bfloat16)
    query_pre = jnp.dot(attn_in, w_query, preferred_element_type=jnp.float32)
    key_pre = jnp.dot(attn_in, w_key, preferred_element_type=jnp.float32)
    value_pre = jnp.dot(attn_in, w_value, preferred_element_type=jnp.float32)
    queries, back_rot_query = jax.vjp(
        lambda arr: rotate(arr, position), query_pre.reshape(row_count, H, HD)
    )
    keys_rot, back_rot_key = jax.vjp(
        lambda arr: rotate(arr, position), key_pre.reshape(row_count, H, HD)
    )
    queries_low = queries.astype(jnp.bfloat16)
    keys_low = keys_rot.reshape(row_count, D).astype(jnp.bfloat16)
    values_low = value_pre.astype(jnp.bfloat16)
    initial = (
        jnp.full((H, row_count), neg_big, jnp.float32),
        jnp.zeros((H, row_count), jnp.float32),
        jnp.zeros((row_count, H, HD), jnp.float32),
    )
    key_piece = lax.all_gather(keys_low, "blk", axis=0, tiled=True)
    value_piece = lax.all_gather(values_low, "blk", axis=0, tiled=True)
    piece_rows = key_piece.shape[0]
    fold_width = math.gcd(piece_rows, 512)

    def one_block(state, number):
        key_first = number * fold_width

        def one_compute(state):
            running_top, totals, accum = state
            keys_blk = lax.dynamic_slice_in_dim(
                key_piece, number * fold_width, fold_width, 0
            ).reshape(fold_width, H, HD)
            values_blk = lax.dynamic_slice_in_dim(
                value_piece, number * fold_width, fold_width, 0
            ).reshape(fold_width, H, HD)
            scores = (
                jnp.einsum(
                    "qhd,khd->hqk", queries_low, keys_blk, preferred_element_type=jnp.float32
                )
                * scale
            )
            allowed = block_mask(query_index, query_start, key_first, fold_width)[None]
            scores = jnp.where(allowed, scores, neg_big)
            new_top = jnp.maximum(running_top, jnp.max(scores, axis=-1))
            weights = jnp.where(allowed, jnp.exp(scores - new_top[..., None]), 0.0)
            factor = jnp.exp(running_top - new_top)
            totals = totals * factor + jnp.sum(weights, axis=-1)
            accum = accum * jnp.transpose(factor)[:, :, None] + jnp.einsum(
                "hqk,khd->qhd",
                weights.astype(jnp.bfloat16),
                values_blk,
                preferred_element_type=jnp.float32,
            )
            return (new_top, totals, accum)

        active = (key_first <= query_last) & (key_first + fold_width - 1 >= start_least)
        return (lax.cond(active, one_compute, lambda state: state, state), None)

    result, unused = lax.scan(
        one_block, initial, jnp.arange(piece_rows // fold_width, dtype=jnp.int32)
    )
    running_top, totals, accum = result
    attn_full = accum / jnp.transpose(totals)[:, :, None]
    log_total = running_top + jnp.log(totals)
    attn_low = attn_full.reshape(row_count, D).astype(jnp.bfloat16)
    branch_attn = jnp.dot(attn_low, w_out, preferred_element_type=jnp.float32)
    post_attn, back_post_attn = jax.vjp(rms_norm, branch_attn, gain_post_attn)
    hidden_res = tokens_f + post_attn
    normed_mlp, back_pre_mlp = jax.vjp(rms_norm, hidden_res, gain_pre_mlp)
    mlp_in = normed_mlp.astype(jnp.bfloat16)
    pre_act = jnp.dot(mlp_in, w_up, preferred_element_type=jnp.float32) + bias_up
    activated, back_gelu = jax.vjp(lambda arr: jax.nn.gelu(arr, approximate=True), pre_act)
    act_low = activated.astype(jnp.bfloat16)
    branch_mlp = jnp.dot(act_low, w_down, preferred_element_type=jnp.float32) + bias_down
    post_mlp, back_post_mlp = jax.vjp(rms_norm, branch_mlp, gain_post_mlp)
    output = (hidden_res + post_mlp).astype(jnp.bfloat16)
    branch_rms = jnp.stack(
        [
            jnp.sqrt(jnp.mean(branch_attn * branch_attn, axis=-1) + eps),
            jnp.sqrt(jnp.mean(branch_mlp * branch_mlp, axis=-1) + eps),
        ]
    )
    grad_out_f = cotangent.astype(jnp.float32)
    grad_branch_mlp, grad_gain_post_mlp = back_post_mlp(grad_out_f)
    grad_mlp_low = grad_branch_mlp.astype(jnp.bfloat16)
    grad_bias_down = jnp.sum(grad_mlp_low.astype(jnp.float32), axis=0)
    grad_down = jnp.einsum("tf,td->df", act_low, grad_mlp_low, preferred_element_type=jnp.float32)
    grad_act = jnp.einsum("td,fd->tf", grad_mlp_low, w_down, preferred_element_type=jnp.float32)
    (grad_pre_act,) = back_gelu(grad_act)
    grad_pre_low = grad_pre_act.astype(jnp.bfloat16)
    grad_bias_up = jnp.sum(grad_pre_low.astype(jnp.float32), axis=0)
    grad_up = jnp.einsum("td,tf->fd", mlp_in, grad_pre_low, preferred_element_type=jnp.float32)
    grad_normed_mlp = jnp.einsum(
        "tf,df->td", grad_pre_low, w_up, preferred_element_type=jnp.float32
    )
    grad_res_part, grad_gain_pre_mlp = back_pre_mlp(grad_normed_mlp)
    grad_hidden = grad_out_f + grad_res_part
    grad_branch_attn, grad_gain_post_attn = back_post_attn(grad_hidden)
    grad_branch_low = grad_branch_attn.astype(jnp.bfloat16)
    grad_w_out = jnp.einsum(
        "td,te->ed", attn_low, grad_branch_low, preferred_element_type=jnp.float32
    )
    grad_attn = jnp.einsum("te,de->td", grad_branch_low, w_out, preferred_element_type=jnp.float32)
    grad_attn_low = grad_attn.astype(jnp.bfloat16).reshape(row_count, H, HD)
    delta = jnp.einsum("qhd,qhd->hq", grad_attn_low.astype(jnp.float32), attn_full)
    key_source, value_source = key_piece, value_piece
    width = math.gcd(group_rows, 512)

    def back_block(grad_query_acc, number):
        key_first = number * width

        def back_compute(grad_query_acc):
            keys_blk = lax.dynamic_slice_in_dim(key_source, key_first, width, 0).reshape(
                width, H, HD
            )
            values_blk = lax.dynamic_slice_in_dim(value_source, key_first, width, 0).reshape(
                width, H, HD
            )
            scores = (
                jnp.einsum(
                    "qhd,khd->hqk", queries_low, keys_blk, preferred_element_type=jnp.float32
                )
                * scale
            )
            allowed = block_mask(query_index, query_start, key_first, width)[None]
            probs = jnp.where(allowed, jnp.exp(scores - log_total[..., None]), 0.0)
            grad_probs = jnp.einsum(
                "qhd,khd->hqk", grad_attn_low, values_blk, preferred_element_type=jnp.float32
            )
            grad_scores = (probs * (grad_probs - delta[..., None])).astype(jnp.bfloat16)
            grad_query_acc = (
                grad_query_acc
                + jnp.einsum(
                    "hqk,khd->qhd", grad_scores, keys_blk, preferred_element_type=jnp.float32
                )
                * scale
            )
            grad_keys_blk = (
                jnp.einsum(
                    "hqk,qhd->khd", grad_scores, queries_low, preferred_element_type=jnp.float32
                )
                * scale
            )
            grad_values_blk = jnp.einsum(
                "hqk,qhd->khd",
                probs.astype(jnp.bfloat16),
                grad_attn_low,
                preferred_element_type=jnp.float32,
            )
            return (
                grad_query_acc,
                (grad_keys_blk.reshape(width, D), grad_values_blk.reshape(width, D)),
            )

        def skipped(grad_query_acc):
            return (
                grad_query_acc,
                (jnp.zeros((width, D), jnp.float32), jnp.zeros((width, D), jnp.float32)),
            )

        active = (key_first <= query_last) & (key_first + width - 1 >= start_least)
        return lax.cond(active, back_compute, skipped, grad_query_acc)

    grad_query_acc, stacked = lax.scan(
        back_block,
        jnp.zeros((row_count, H, HD), jnp.float32),
        jnp.arange(group_rows // width, dtype=jnp.int32),
    )
    grad_keys_all = stacked[0].reshape(group_rows, D)
    grad_values_all = stacked[1].reshape(group_rows, D)
    grad_keys_mine, grad_values_mine = (
        lax.psum_scatter(
            grad_keys_all.astype(jnp.bfloat16), "blk", scatter_dimension=0, tiled=True
        ).astype(jnp.float32),
        lax.psum_scatter(
            grad_values_all.astype(jnp.bfloat16), "blk", scatter_dimension=0, tiled=True
        ).astype(jnp.float32),
    )
    (grad_key_pre,) = back_rot_key(grad_keys_mine.reshape(row_count, H, HD))
    (grad_query_pre,) = back_rot_query(grad_query_acc)
    grad_key_low = grad_key_pre.reshape(row_count, D).astype(jnp.bfloat16)
    grad_query_low = grad_query_pre.reshape(row_count, D).astype(jnp.bfloat16)
    grad_value_low = grad_values_mine.astype(jnp.bfloat16)
    grad_query = jnp.einsum(
        "td,te->ed", attn_in, grad_query_low, preferred_element_type=jnp.float32
    )
    grad_key = jnp.einsum("td,te->ed", attn_in, grad_key_low, preferred_element_type=jnp.float32)
    grad_value = jnp.einsum(
        "td,te->ed", attn_in, grad_value_low, preferred_element_type=jnp.float32
    )
    grad_normed_in = (
        jnp.einsum("te,de->td", grad_query_low, w_query, preferred_element_type=jnp.float32)
        + jnp.einsum("te,de->td", grad_key_low, w_key, preferred_element_type=jnp.float32)
        + jnp.einsum("te,de->td", grad_value_low, w_value, preferred_element_type=jnp.float32)
    )
    grad_tokens_part, grad_gain_pre_attn = back_pre_attn(grad_normed_in)
    grad_tokens = (grad_hidden + grad_tokens_part).astype(jnp.bfloat16)
    count = lax.axis_size(("dp", "blk"))
    low = jnp.bfloat16
    pieces = [
        part.astype(low).reshape(count, -1, D)
        for part in (grad_query, grad_key, grad_value, grad_w_out, grad_up, grad_down)
    ]
    small = [
        part.reshape(count, -1)
        for part in (
            grad_bias_up,
            grad_bias_down,
            grad_gain_pre_attn,
            grad_gain_post_attn,
            grad_gain_pre_mlp,
            grad_gain_post_mlp,
        )
    ]
    sizes = [part.shape[1] for part in pieces]
    summed = lax.psum_scatter(
        jnp.concatenate(pieces, axis=1), ("dp", "blk"), scatter_dimension=0
    ).astype(jnp.float32)
    small_sizes = [part.shape[1] for part in small]
    small_flat = jnp.concatenate(small, axis=1)
    padding = -small_flat.shape[1] % 128
    small_flat = jnp.pad(small_flat, ((0, 0), (0, padding)))
    small_summed = lax.psum_scatter(small_flat, ("dp", "blk"), scatter_dimension=0)
    cuts = [sum(sizes[: i + 1]) for i in range(len(sizes) - 1)]
    parts = jnp.split(summed, cuts, axis=0)
    parts[5] = parts[5].reshape(D // count, -1)
    small_cuts = [sum(small_sizes[: i + 1]) for i in range(len(small_sizes))]
    small_parts = jnp.split(small_summed, small_cuts, axis=0)[:6]
    return (output, grad_tokens, *[part.T for part in parts], *small_parts, branch_rms)


MESH_ID = pl.DeviceIdType.MESH
F32 = jnp.float32
BF16 = jnp.bfloat16
TOK = 256
PACK = 512
FF = 4096
HALF_FF = 2048
HALF_D = 512
CHUNK = 128
VMEM_BYTES = 62 * 1024 * 1024
UNIT_ORDER = (
    "wxyv",
    "ywxv",
    "yxwv",
    "wyxv",
    "wyv",
    "ywv",
    "ywv",
    "ywv",
    "ywxv",
    "yxwv",
    "wxyv",
    "xywv",
    "xwyv",
    "xywv",
    "yxwv",
    "xywv",
)
SLOTS = (
    (0, 1, 10, 11,),
    (),
    (),
    (20, 30,),
    (2, 12,),
    (),
    (21,),
    (),
    (3, 13,),
    (22, 31, 80, 32,),
    (),
    (),
    (100,),
    (),
    (14, 81, 23,),
    (40, 82, 50, 33,),
    (34, 102,),
    (41, 51, 83, 160, 42, 4, 101, 84, 52, 43, 53, 24, 60, 103, 44, 15, 61, 5, 35, 54, 45, 70, 62, 104, 16, 110, 161, 111, 63, 85, 25, 6, 72, 120, 112, 105, 36, 71, 121, 113, 162, 64, 55, 90, 114, 130, 86, 122, 91, 73, 131, 26,),
    (123, 74, 106, 140, 92, 132, 65, 163, 150, 93, 133, 115, 75, 141, 142, 94, 164, 151, 134, 116, 152, 124, 95, 143, 144, 135, 96, 153, 154, 136, 145, 125, 155, 146, 126, 156,),
)


def mm(a, b):
    return jnp.dot(a, b, preferred_element_type=F32)


def mm_nt(a, b):
    return lax.dot_general(a, b, (((1,), (1,)), ((), ())), preferred_element_type=F32)


def al(offset, step):
    return pl.multiple_of(offset, step)


def norm_back(v, r, gain, grad):
    scaled = grad * gain
    inner = jnp.mean(v * scaled, axis=-1, keepdims=True)
    return r * scaled - v * (r * r * r * inner), jnp.sum(grad * v * r, axis=0, keepdims=True)


def inv_rms(v):
    return lax.rsqrt(jnp.mean(v * v, axis=-1, keepdims=True) + eps)


def layer_kernel(
    doc, tok, cot, gain_a, gain_b, gain_c, gain_d, bias_up, bias_down,
    wq_hbm, wk_hbm, wv_hbm, wo_hbm, wu_hbm, wd_hbm,
    out, grad_tok, rms, o_down, o_up, o_out, o_query, o_key, o_value,
    small_up, small_down, small_a, small_b, small_c, small_d,
    wq, wk, wv, wo, wu, wd, xin, q_t, k_t, v_t, k_n, v_n, mask, attn_t, attn_nat, attn_oth,
    branch, hid, xm, act, g_t, part_send, part_recv, part_own, nat, gb_t, gba_t, ga_t,
    rope, lse, stat, s_down, r1_down, r2_down, r3_down, r4_down, r1_up, r2_up, r3_up, xm_m, pre_m,
    r1_late, r2_late, r3_late, r4_late, fin_down, fin_late, rec_down, rec_late, aux_s, aux_r,
    w_sem, m_send, m_recv, c_send, c_recv, rs_send, rs_recv, a_send, a_recv,
):
    dp = lax.axis_index("dp")
    b = lax.axis_index("blk")
    x = lax.rem(dp, 2)
    y = lax.rem(dp // 2, 2)
    z = dp // 4
    other = 1 - b
    core_peer = (dp, other)
    x_peer = (dp + 1 - 2 * x, b)
    y_peer = (dp + 2 - 4 * y, b)

    z_low = (dp + 4 - 8 * lax.rem(z, 2), b)
    z_high = (dp + 8 - 16 * (z // 2), b)
    barrier = pltpu.get_barrier_semaphore()
    for peer in (core_peer, x_peer, y_peer, z_low, z_high):
        pl.semaphore_signal(barrier, inc=1, device_id=peer, device_id_type=MESH_ID)

    own_cols = al(b * HALF_D, HALF_D)
    oth_cols = al(other * HALF_D, HALF_D)
    own_tok = al(b * TOK, TOK)
    oth_tok = al(other * TOK, TOK)

    w_copies = [
        pltpu.make_async_copy(src.at[:, pl.ds(own_cols, HALF_D)], dst, w_sem.at[i])
        for i, (src, dst) in enumerate(((wq_hbm, wq), (wk_hbm, wk), (wv_hbm, wv)))
    ]
    w_copies.append(pltpu.make_async_copy(wo_hbm, wo, w_sem.at[3]))
    for copy in w_copies:
        copy.start()

    def up_copy(j):
        return pltpu.make_async_copy(
            wu_hbm.at[:, pl.ds(al((2 * j + b) * 128, 128), 128)],
            wu.at[:, pl.ds(al(j * 128, 128), 128)],
            w_sem.at[4 + j],
        )

    def down_copy(j):
        return pltpu.make_async_copy(
            wd_hbm.at[pl.ds(al((2 * j + b) * 128, 128), 128)],
            wd.at[pl.ds(al(j * 128, 128), 128)],
            w_sem.at[20 + j],
        )

    def to_core(k, src, dst):
        return pltpu.make_async_remote_copy(
            src_ref=src, dst_ref=dst, send_sem=c_send.at[k], recv_sem=c_recv.at[k],
            device_id=core_peer, device_id_type=MESH_ID,
        )

    def pre_attn(i, carry):
        rows = pl.ds(al(i * CHUNK, CHUNK), CHUNK)
        v = tok[rows, :].astype(F32)
        xin[pl.ds(al(own_tok + i * CHUNK, CHUNK), CHUNK), :] = (
            v * inv_rms(v) * gain_a[...]
        ).astype(BF16)
        return carry

    lax.fori_loop(0, TOK // CHUNK, pre_attn, 0)
    pl.semaphore_wait(barrier, 5)
    own_rows = xin.at[pl.ds(own_tok, TOK)]
    xin_copy = to_core(0, own_rows, own_rows)
    xin_copy.start()

    end_a = doc[0, 0]
    end_b = end_a + doc[0, 1]
    end_c = end_b + doc[0, 2]
    index_row = lax.broadcasted_iota(jnp.int32, (1, PACK), 1)
    start_row = jnp.where(
        index_row >= end_c,
        end_c,
        jnp.where(index_row >= end_b, end_b, jnp.where(index_row >= end_a, end_a, 0)),
    )
    position = (index_row - start_row).astype(F32)
    freq = jnp.exp(
        lax.broadcasted_iota(jnp.int32, (32, PACK), 0).astype(F32) * (-math.log(10000.0) / 32.0)
    )
    angle = position * freq
    rope[0] = jnp.cos(angle)
    rope[1] = jnp.sin(angle)

    def fill_mask(i, carry):
        rows = pl.ds(al(i * 64, 64), 64)
        key_index = lax.broadcasted_iota(jnp.int32, (64, PACK), 0) + i * 64
        query_index = lax.broadcasted_iota(jnp.int32, (64, PACK), 1)
        allowed = (key_index <= query_index) & (key_index >= start_row)
        mask[rows, :] = jnp.where(allowed, 0.0, neg_big)
        return carry

    lax.fori_loop(0, 8, fill_mask, 0)

    def project(tok_at):
        rows = pl.ds(tok_at, TOK)
        cos = rope[0, :, rows]
        sin = rope[1, :, rows]
        x_rows = xin[rows, :]

        def turned(w, scale):
            flat = mm(x_rows, w[...]).T.reshape(8, 2, 32, TOK)
            low, high = flat[:, 0], flat[:, 1]
            both = jnp.stack([low * cos - high * sin, low * sin + high * cos], axis=1)
            return (both * scale).reshape(HALF_D, TOK).astype(BF16)

        q_t[:, rows] = turned(wq, 0.125)
        keys = turned(wk, 1.0)
        k_t[:, rows] = keys
        k_n[rows, :] = keys.T
        values = mm(x_rows, wv[...]).astype(BF16)
        v_n[rows, :] = values
        v_t[:, rows] = values.T

    for copy in w_copies[:3]:
        copy.wait()
    lax.fori_loop(0, 16, lambda j, c: (up_copy(j).start(), c)[1], 0)
    lax.fori_loop(0, 16, lambda j, c: (down_copy(j).start(), c)[1], 0)
    project(own_tok)
    xin_copy.wait()
    project(oth_tok)

    zeros = jnp.zeros((64, TOK), BF16)

    def slab(head_rows, which):
        return jnp.concatenate([head_rows, zeros] if which == 0 else [zeros, head_rows], axis=0)

    def attend(p, carry):
        slab_cols = pl.ds(al(p * 128, 128), 128)
        parts = [
            (w, pl.ds(al(p * 128 + w * 64, 64), 64), slice(i * TOK, i * TOK + TOK), (i + 1) * TOK)
            for i in (1, 0)
            for w in (0, 1)
        ]
        scores = [
            mm(k_n[:keys, slab_cols], slab(q_t[rows, cols], w)) + mask[:keys, cols]
            for w, rows, cols, keys in parts
        ]
        tops = [jnp.max(score, axis=0, keepdims=True) for score in scores]
        weights = [jnp.exp(score - top) for score, top in zip(scores, tops)]
        totals = [jnp.sum(weight, axis=0, keepdims=True) for weight in weights]
        for (w, rows, cols, keys), weight, top, total in zip(parts, weights, tops, totals):
            attn_t[rows, cols] = mm(v_t[rows, :keys], weight.astype(BF16)) * (1.0 / total)
            lse[pl.ds(p * 2 + w, 1), cols] = top + jnp.log(total)
        attn_nat[:, slab_cols] = attn_t[pl.ds(al(p * 128, 128), 128), :].T.astype(BF16)
        to_core(
            1 + p, attn_nat.at[pl.ds(oth_tok, TOK), slab_cols], attn_oth.at[:, slab_cols]
        ).start()
        return carry

    lax.fori_loop(0, 4, attend, 0)

    w_copies[3].wait()
    branch[...] = mm(attn_nat[pl.ds(own_tok, TOK), :], wo[pl.ds(own_cols, HALF_D), :])

    def attn_copy(p):
        cols = pl.ds(al(p * 128, 128), 128)
        return to_core(1 + p, attn_nat.at[pl.ds(oth_tok, TOK), cols], attn_oth.at[:, cols])

    lax.fori_loop(0, 4, lambda p, c: (attn_copy(p).wait(), c)[1], 0)
    branch[...] += mm(attn_oth[...], wo[pl.ds(oth_cols, HALF_D), :])

    def post_attn(i, carry):
        rows = pl.ds(al(i * CHUNK, CHUNK), CHUNK)
        v = branch[rows, :]
        square = jnp.mean(v * v, axis=-1, keepdims=True) + eps
        stat[0, rows, :] = jnp.broadcast_to(jnp.sqrt(square), (CHUNK, 128))
        h = tok[rows, :].astype(F32) + v * lax.rsqrt(square) * gain_b[...]
        hid[rows, :] = h
        xm[pl.ds(al(own_tok + i * CHUNK, CHUNK), CHUNK), :] = (
            h * inv_rms(h) * gain_c[...]
        ).astype(BF16)
        return carry

    lax.fori_loop(0, TOK // CHUNK, post_attn, 0)
    own_rows_m = xm.at[pl.ds(own_tok, TOK)]
    xm_copy = to_core(5, own_rows_m, own_rows_m)
    xm_copy.start()
    xm_mate = pltpu.make_async_remote_copy(
        src_ref=own_rows_m, dst_ref=xm_m.at[pl.ds(own_tok, TOK)], send_sem=m_send.at[8],
        recv_sem=m_recv.at[8], device_id=x_peer, device_id_type=MESH_ID,
    )
    xm_mate.start()

    def up_step(tok_at, i):
        cols = pl.ds(al(i * 1024, 1024), 1024)
        rows = pl.ds(tok_at, TOK)
        bias = jnp.concatenate(
            [bias_up[pl.ds(16 * i + 2 * j + b, 1), :] for j in range(8)], axis=1
        )
        pre = mm(xm[rows, :], wu[:, cols]) + bias
        square = pre * pre
        th = jnp.tanh(pre * (0.7978845608 + (0.7978845608 * 0.044715) * square))
        half = 0.5 + 0.5 * th
        act[rows, cols] = (pre * half).astype(BF16)
        slope = half + pre * (0.5 - 0.5 * th * th) * (
            0.7978845608 + (0.7978845608 * 0.134145) * square
        )
        g_t[cols, rows] = slope.astype(BF16).T

    lax.fori_loop(0, 16, lambda j, c: (up_copy(j).wait(), c)[1], 0)
    lax.fori_loop(0, 2, lambda i, c: (up_step(own_tok, i), c)[1], 0)
    xm_copy.wait()
    lax.fori_loop(0, 2, lambda i, c: (up_step(oth_tok, i), c)[1], 0)
    lax.fori_loop(0, 16, lambda j, c: (down_copy(j).wait(), c)[1], 0)

    def down_step(tok_at, dst, i):
        cols = slice(i * 512, i * 512 + 512)
        dst[:, cols] = mm(act[pl.ds(tok_at, TOK), :], wd[:, cols]).astype(dst.dtype)

    mlp_copies = [
        to_core(k, part_send.at[:, pl.ds(i * 512, 512)], part_recv.at[:, pl.ds(i * 512, 512)])
        for i, k in ((0, 6), (1, 31))
    ]
    for i in range(2):
        down_step(oth_tok, part_send, i)
        mlp_copies[i].start()
    for i in range(2):
        down_step(own_tok, part_own, i)
    for copy in mlp_copies:
        copy.wait()
    def post_mlp(i, carry):
        sum_bias, sum_gain = carry
        rows = pl.ds(al(i * CHUNK, CHUNK), CHUNK)
        v = part_own[rows, :] + part_recv[rows, :].astype(F32) + bias_down[...]
        square = jnp.mean(v * v, axis=-1, keepdims=True) + eps
        stat[1, rows, :] = jnp.broadcast_to(jnp.sqrt(square), (CHUNK, 128))
        r = lax.rsqrt(square)
        out[rows, :] = (hid[rows, :] + v * r * gain_d[...]).astype(BF16)
        back, gain_part = norm_back(v, r, gain_d[...], cot[rows, :].astype(F32))
        back = back.astype(BF16)
        nat[rows, :] = back
        return (
            sum_bias + jnp.sum(back.astype(F32), axis=0, keepdims=True),
            sum_gain + gain_part,
        )

    def turn_and_send(dst, i, k):
        tok_cols = pl.ds(al(own_tok + i * CHUNK, CHUNK), CHUNK)
        for j in range(4):
            cols = slice(j * 256, j * 256 + 256)
            dst[cols, tok_cols] = nat[i * CHUNK : i * CHUNK + CHUNK, cols].T
        part = dst.at[:, tok_cols]
        copy = to_core(k, part, part)
        copy.start()
        return copy

    zero_row = jnp.zeros((1, D), F32)
    sums = (zero_row, zero_row)
    gb_copies = []
    for i, k in ((0, 7), (1, 32)):
        sums = post_mlp(i, sums)
        gb_copies.append(turn_and_send(gb_t, i, k))
    sum_bias_down, sum_gain_d = sums
    aux_s[0] = jnp.zeros((16, D), F32)
    aux_s[0, 0:1, :] = sum_bias_down
    aux_s[0, 4:5, :] = sum_gain_d
    for i in range(2):
        rms[i : i + 1, :] = stat[i].T[0:1, :]

    for copy in gb_copies:
        copy.wait()
    down_refs = (s_down, r1_down, r2_down, r3_down, r4_down)
    up_refs = (wd, r1_up, r2_up, r3_up)
    late_refs = (wu, r1_late, r2_late, r3_late, r4_late)
    units = (
        [(down_refs, 512 * i, 512, 64) for i in range(4)]
        + [(up_refs, 256 * i, 256, 128) for i in range(4)]
        + [(late_refs, 256 * i, 256, 64) for i in range(8)]
    )
    place = {
        "x": (x, 1, x_peer),
        "y": (y, 2, y_peer),
        "w": (lax.rem(z, 2), 4, z_low),
        "v": (z // 2, 8, z_high),
    }

    def unit_axes(n):
        return [place[letter] for letter in UNIT_ORDER[n]]

    def kept(n, steps):
        axes = unit_axes(n)
        step = 2 ** len(axes) // 2 * units[n][3]
        return sum((axis[0] * (step >> i) for i, axis in enumerate(axes[:steps])), 0)

    def unit_copy(n, k):
        refs, c0, width, rows = units[n]
        axes = unit_axes(n)
        span = 2 ** len(axes)
        cols = pl.ds(c0, width)
        if k < 2:
            bit, _, peer = axes[0]
            second = lax.rem(axes[1][0] + 1 + k, 2)
            count = span // 4 * rows
            src = refs[0].at[pl.ds(al(((1 - bit) * 2 + second) * count, count), count), cols]
            dst = refs[1].at[pl.ds(al(second * count, count), count), cols]
        else:
            bit, _, peer = axes[k - 1]
            count = (span >> k) * rows
            at = kept(n, k - 1) + (1 - bit) * count
            src = refs[0].at[pl.ds(al(at, count), count), cols]
            dst = refs[k].at[:, cols]
        return pltpu.make_async_remote_copy(
            src_ref=src, dst_ref=dst, send_sem=rs_send.at[n, k], recv_sem=rs_recv.at[n, k],
            device_id=peer, device_id_type=MESH_ID,
        )

    def add_rows(n, at, arrived, arrived_at, count):
        refs, c0, width, _ = units[n]
        cols = pl.ds(c0, width)

        def step(i, carry):
            to = pl.ds(al(at + i * 64, 64), 64)
            got = refs[arrived][pl.ds(al(arrived_at + i * 64, 64), 64), cols]
            refs[0][to, cols] = (refs[0][to, cols].astype(F32) + got.astype(F32)).astype(BF16)
            return carry

        lax.fori_loop(0, count // 64, step, 0)

    def serve(n, k):
        refs, c0, width, rows = units[n]
        axes = unit_axes(n)
        last = len(axes)
        span = 2**last
        unit_copy(n, k).wait_recv()
        if k < 2:
            second = lax.rem(axes[1][0] + 1 + k, 2)
            count = span // 4 * rows
            add_rows(n, kept(n, 1) + second * count, 1, second * count, count)
            if k == 0:
                unit_copy(n, 2).start()
        elif k < last:
            count = (span // 2 >> k) * rows
            bit = axes[k][0]
            add_rows(n, kept(n, k) + (1 - bit) * count, k, (1 - bit) * count, count)
            unit_copy(n, k + 1).start()
            add_rows(n, kept(n, k) + bit * count, k, bit * count, count)
        else:
            cols = pl.ds(c0, width)
            mine = refs[0][pl.ds(al(kept(n, last), rows), rows), cols].astype(F32)
            total = mine + refs[last][:, cols].astype(F32)
            if 4 <= n < 8:
                o_up[c0 : c0 + width, :] = total.T
            else:
                (fin_down if n < 4 else fin_late)[:, cols] = total
                final_copy(n).start()

    oth_cut = pl.ds(al(other * 32, 32), 32)
    own_cut = pl.ds(al(b * 32, 32), 32)

    def final_copy(n):
        _, c0, width, _ = units[n]
        cols = pl.ds(c0, width)
        src, dst = (fin_down, rec_down) if n < 4 else (fin_late, rec_late)
        return to_core(14 + n, src.at[oth_cut, cols], dst.at[:, cols])

    aux_peers = (core_peer, x_peer, y_peer, z_low, z_high)

    def aux_copy(k):
        return pltpu.make_async_remote_copy(
            src_ref=aux_s.at[k], dst_ref=aux_r.at[k], send_sem=a_send.at[k],
            recv_sem=a_recv.at[k], device_id=aux_peers[k], device_id_type=MESH_ID,
        )

    def aux_end(k):
        aux_copy(k).wait_recv()
        aux_s[k + 1] = aux_s[k] + aux_r[k]
        if k < 4:
            aux_copy(k + 1).start()

    def slot(i):
        for code in SLOTS[i]:
            n, k = code // 10, code % 10
            if n == len(units):
                aux_end(k)
            elif k < 2:
                unit_copy(n, k).start()
            else:
                serve(n, k - 2)

    def weight_grad(n, first, last, *terms):
        refs, c0, width, rows = units[n]
        axes = unit_axes(n)
        fixed = x if len(axes) == 3 else 0
        tails = [0]
        for axis in axes[2:]:
            tails = [tail + p * axis[1] for tail in tails for p in range(2)]
        count = len(tails) * rows
        for g in range(first, last):
            i = lax.rem(axes[0][0] + 1 + g // 2, 2)
            j = lax.rem(axes[1][0] + 1 + g % 2, 2)
            base = i * axes[0][1] + j * axes[1][1] + fixed
            total = None
            for left, right in terms:
                stack = jnp.concatenate([left(base + tail) for tail in tails], axis=0)
                part = mm(stack, right)
                total = part if total is None else total + part
            at = pl.ds(al((i * 2 + j) * count, count), count)
            refs[0][at, pl.ds(c0, width)] = total.astype(BF16)

    def rows_of(ref, rows):
        return lambda chip: ref[pl.ds(al(chip * rows, rows), rows), :]

    for first in (0, 2):
        for n in range(4):
            weight_grad(
                n, first, first + 2, (rows_of(gb_t, 64), act[:, 512 * n : 512 * n + 512])
            )
        slot(first // 2)

    def mate_copy(k):
        return pltpu.make_async_remote_copy(
            src_ref=g_t.at[pl.ds(al((2 * k + 1 - x) * 128, 128), 128)],
            dst_ref=pre_m.at[pl.ds(al(k * 128, 128), 128)],
            send_sem=m_send.at[k], recv_sem=m_recv.at[k],
            device_id=x_peer, device_id_type=MESH_ID,
        )

    def act_back(i, carry):
        rows = pl.ds(al(i * 512, 512), 512)
        g_t[rows, :] = (mm(wd[rows, :], gb_t[...]) * g_t[rows, :].astype(F32)).astype(BF16)
        for j in range(2):
            mate_copy(2 * i + j).start()
        return carry

    lax.fori_loop(0, 4, act_back, 0)
    xm_mate.wait()
    mate_rows = xm_m.at[pl.ds(own_tok, TOK)]
    xm_pass = to_core(30, mate_rows, mate_rows)
    xm_pass.start()
    slot(2)

    def mlp_back(tok_at, dst, i):
        at = pl.ds(al(i * 512, 512), 512)
        dst[:, at] = mm(wu[at, :], g_t[:, pl.ds(tok_at, TOK)]).T.astype(dst.dtype)

    lax.fori_loop(0, 2, lambda i, c: (mlp_back(oth_tok, part_send, i), c)[1], 0)
    mlp_back_copy = to_core(8, part_send, part_recv)
    mlp_back_copy.start()
    slot(3)
    lax.fori_loop(0, 2, lambda i, c: (mlp_back(own_tok, part_own, i), c)[1], 0)
    ones = jnp.ones((16, PACK), BF16)
    for i in range(2):
        aux_s[0, pl.ds(8 + 2 * b + i, 1), :] = mm_nt(ones, g_t[i * 1024 : i * 1024 + 1024, :])[0:1]
    slot(4)
    mlp_back_copy.wait()

    def hidden_back(i, carry):
        sum_c, sum_b = carry
        rows = pl.ds(al(i * CHUNK, CHUNK), CHUNK)
        h = hid[rows, :]
        back, part_c = norm_back(
            h, inv_rms(h), gain_c[...], part_own[rows, :] + part_recv[rows, :].astype(F32)
        )
        g_hidden = cot[rows, :].astype(F32) + back
        hid[rows, :] = g_hidden
        v = branch[rows, :]
        back, part_b = norm_back(v, inv_rms(v), gain_b[...], g_hidden)
        nat[rows, :] = back.astype(BF16)
        return sum_c + part_c, sum_b + part_b

    sums = (zero_row, zero_row)
    gba_copies = []
    for i, k in ((0, 9), (1, 33)):
        sums = hidden_back(i, sums)
        gba_copies.append(turn_and_send(gba_t, i, k))
    sum_gain_c, sum_gain_b = sums
    aux_s[0, 3:4, :] = sum_gain_c
    aux_s[0, 2:3, :] = sum_gain_b
    slot(5)
    for copy in gba_copies:
        copy.wait()

    for n in (8, 9):
        weight_grad(
            n, 0, 4, (rows_of(gba_t, 64), attn_nat[:, 256 * (n - 8) : 256 * (n - 8) + 256])
        )
    slot(6)
    ga_t[...] = mm(wo[pl.ds(own_cols, HALF_D), :], gba_t[...]).astype(BF16)
    slot(7)

    def head_grad(off):
        def rows(chip):
            at = al(off + chip // 8 * HALF_D, HALF_D)
            return act[pl.ds(al(lax.rem(chip, 8) * 64, 64), 64), pl.ds(at, HALF_D)]

        return rows

    own_q = pl.ds(al(own_cols, HALF_D), HALF_D)
    own_k = pl.ds(al(D + own_cols, HALF_D), HALF_D)
    gv = gb_t

    def attend_back(p, carry):
        slab_cols = pl.ds(al(p * 128, 128), 128)
        parts = [
            (w, pl.ds(al(p * 128 + w * 64, 64), 64), slice(i * TOK, i * TOK + TOK), (i + 1) * TOK)
            for w in (0, 1)
            for i in (0, 1)
        ]
        deltas = [
            jnp.sum(ga_t[rows, cols].astype(F32) * attn_t[rows, cols], axis=0, keepdims=True)
            for w, rows, cols, keys in parts
        ]
        scores = [
            mm(k_n[:keys, slab_cols], slab(q_t[rows, cols], w)) + mask[:keys, cols]
            for w, rows, cols, keys in parts
        ]
        g_probs = [
            mm(v_n[:keys, slab_cols], slab(ga_t[rows, cols], w)) for w, rows, cols, keys in parts
        ]
        probs = [
            jnp.exp(score - lse[pl.ds(p * 2 + part[0], 1), part[2]])
            for score, part in zip(scores, parts)
        ]
        g_scores = [
            (prob * (g_prob - delta)).astype(BF16)
            for prob, g_prob, delta in zip(probs, g_probs, deltas)
        ]
        grads_q = [
            mm(k_t[rows, :keys], g_score) * 0.125
            for (w, rows, cols, keys), g_score in zip(parts, g_scores)
        ]
        grads_k = [
            mm_nt(q_t[rows, cols], g_score)
            for (w, rows, cols, keys), g_score in zip(parts, g_scores)
        ]
        grads_v = [
            mm_nt(ga_t[rows, cols], prob.astype(BF16))
            for (w, rows, cols, keys), prob in zip(parts, probs)
        ]

        def both(first, second):
            return jnp.concatenate([first + second[:, :TOK], second[:, TOK:]], axis=1)

        cos, sin = rope[0], rope[1]
        for w in range(2):
            to = pl.ds(al(own_cols + p * 128 + w * 64, 64), 64)
            at = parts[2 * w][1]
            full_q = jnp.concatenate(grads_q[2 * w : 2 * w + 2], axis=1)
            for full, dst in ((full_q, own_q), (both(*grads_k[2 * w : 2 * w + 2]), own_k)):
                low, high = full[:32], full[32:]
                act[at, dst] = jnp.concatenate(
                    [low * cos + high * sin, high * cos - low * sin], axis=0
                ).astype(BF16)
            gv[to, :] = both(*grads_v[2 * w : 2 * w + 2]).astype(BF16)
        return carry

    lax.fori_loop(0, 2, attend_back, 0)
    slot(8)
    lax.fori_loop(2, 4, attend_back, 0)
    own_heads = pl.ds(own_cols, HALF_D)
    head_copies = [
        to_core(10 + i, ref, ref)
        for i, ref in enumerate((act.at[:, own_q], act.at[:, own_k], gv.at[own_heads]))
    ]
    for copy in head_copies:
        copy.start()
    slot(9)

    def in_back(tok_at, dst, i):
        at = pl.ds(al(i * 512, 512), 512)
        cols = pl.ds(tok_at, TOK)
        total = mm(wq[at, :], act[:, pl.ds(al(own_cols + tok_at, TOK), TOK)])
        total += mm(wk[at, :], act[:, pl.ds(al(D + own_cols + tok_at, TOK), TOK)])
        total += mm(wv[at, :], gv[own_heads, cols])
        dst[:, at] = total.T.astype(dst.dtype)

    lax.fori_loop(0, 2, lambda i, c: (in_back(oth_tok, part_send, i), c)[1], 0)
    in_back_copy = to_core(13, part_send, part_recv)
    in_back_copy.start()
    slot(10)
    for copy in head_copies:
        copy.wait()
    for first in (0, 2):
        for i, rows in enumerate((head_grad(0), head_grad(D), rows_of(gv, 64))):
            for j in range(2):
                cols = pl.ds(al(own_cols + 256 * j, 256), 256)
                weight_grad(10 + 2 * i + j, first, first + 2, (rows, xin[:, cols]))
        slot(11 + first // 2)
    lax.fori_loop(0, 2, lambda i, c: (in_back(own_tok, part_own, i), c)[1], 0)
    slot(13)
    in_back_copy.wait()

    def token_back(i, carry):
        rows = pl.ds(al(i * CHUNK, CHUNK), CHUNK)
        v = tok[rows, :].astype(F32)
        back, part_a = norm_back(
            v, inv_rms(v), gain_a[...], part_own[rows, :] + part_recv[rows, :].astype(F32)
        )
        grad_tok[rows, :] = (hid[rows, :] + back).astype(BF16)
        return carry + part_a

    aux_s[0, 1:2, :] = lax.fori_loop(0, TOK // CHUNK, token_back, zero_row)
    slot(14)

    for k in range(8):
        mate_copy(k).wait()
    xm_pass.wait()

    def mate_pre(chip):
        return pre_m[pl.ds(al(chip // 2 * 128, 128), 128), :]

    for first in (0, 2):
        for n in range(4, 8):
            cols = slice(256 * (n - 4), 256 * (n - 4) + 256)
            weight_grad(
                n, first, first + 2, (rows_of(g_t, 128), xm[:, cols]), (mate_pre, xm_m[:, cols])
            )
        slot(15 + first // 2)

    aux_copy(0).start()
    slot(17)
    for n in range(4):
        final_copy(n).wait()

    def place_down(j, carry):
        from_cols = pl.ds(al(j * 128, 128), 128)
        o_down[:, pl.ds(al((2 * j + b) * 128, 128), 128)] = fin_down[own_cut, from_cols]
        o_down[:, pl.ds(al((2 * j + other) * 128, 128), 128)] = rec_down[:, from_cols]
        return carry

    lax.fori_loop(0, 16, place_down, 0)
    slot(18)
    device = dp * 2 + b
    at = pl.ds(al(device // 4 * 128, 128), 128)
    lines = pltpu.roll(aux_s[5, 0:8, at], lax.rem(128 - lax.rem(device, 4) * 32, 128), 1)
    for i, ref in enumerate((small_down, small_a, small_b, small_c, small_d)):
        ref[...] = lines[i, :32]
    lines = aux_s[5, 8:16, pl.ds(al(lax.rem(dp, 8) * 128, 128), 128)]
    chosen = lax.broadcasted_iota(jnp.int32, (8, 128), 0) == 2 * b + dp // 8
    small_up[...] = jnp.sum(jnp.where(chosen, lines, 0.0), axis=0)
    for n in range(len(units)):
        for k in range(len(UNIT_ORDER[n]) + 1):
            unit_copy(n, k).wait_send()
    for k in range(5):
        aux_copy(k).wait_send()
    for i in range(4):
        final_copy(8 + 2 * i).wait()
        final_copy(9 + 2 * i).wait()
        cols = slice(i * 512, i * 512 + 512)
        dst = (o_out, o_query, o_key, o_value)[i]
        dst[:, pl.ds(own_cols, HALF_D)] = fin_late[own_cut, cols]
        dst[:, pl.ds(oth_cols, HALF_D)] = rec_late[:, cols]


def finish_kernel(*refs):
    count = len(refs) // 3
    sems = refs[-1]
    gets = [
        pltpu.make_async_copy(refs[i], refs[2 * count + i], sems.at[0, i]) for i in range(count)
    ]
    puts = [
        pltpu.make_async_copy(refs[2 * count + i], refs[count + i], sems.at[1, i])
        for i in range(count)
    ]
    for copy in gets:
        copy.start()
    for get, put in zip(gets, puts):
        get.wait()
        put.start()
    for copy in puts:
        copy.wait()


def layer_on_device(
    tokens, doc_lengths, w_query, w_key, w_value, w_out, w_up, w_down, bias_up, bias_down,
    gain_pre_attn, gain_post_attn, gain_pre_mlp, gain_post_mlp, cotangent,
):
    def v16(*shape):
        return pltpu.VMEM(shape, BF16)

    def v32(*shape):
        return pltpu.VMEM(shape, F32)

    dma = pltpu.SemaphoreType.DMA
    vmem = pl.BlockSpec(memory_space=pltpu.VMEM)
    scratch = [
        v16(1024, 512), v16(1024, 512), v16(1024, 512), v16(1024, 1024),
        v16(1024, 2048), v16(2048, 1024),
        v16(512, 1024),
        v16(512, 512), v16(512, 512), v16(512, 512), v16(512, 512), v16(512, 512),
        v32(512, 512), v32(512, 512), v16(512, 512), v16(256, 512),
        v32(256, 1024), v32(256, 1024), v16(512, 1024),
        v16(512, 2048), v16(2048, 512),
        v16(256, 1024), v16(256, 1024), v32(256, 1024), v16(256, 1024),
        v16(1024, 512), v16(1024, 512), v16(512, 512),
        v32(2, 32, 512), v32(8, 512), v32(2, 256, 128),
        v16(1024, 2048), v16(512, 2048), v16(256, 2048), v16(128, 2048), v16(64, 2048),
        v16(512, 1024), v16(256, 1024), v16(128, 1024), v16(512, 1024), v16(1024, 512),
        v16(512, 2048), v16(256, 2048), v16(128, 2048), v16(64, 2048),
        v32(64, 2048), v32(64, 2048), v32(32, 2048), v32(32, 2048),
        v32(6, 16, 1024), v32(5, 16, 1024),
        dma((36,)), dma((9,)), dma((9,)), dma((34,)), dma((34,)), dma((16, 5)), dma((16, 5)), dma((5,)), dma((5,)),
    ]
    shapes = [((TOK, D), BF16)] * 2 + [((2, TOK), F32), ((32, FF), F32), ((D, 128), F32)]
    shapes += [((32, D), F32)] * 4 + [((128,), F32)] + [((32,), F32)] * 5
    shapes = [jax.ShapeDtypeStruct(*shape) for shape in shapes]
    results = pl.pallas_call(
        layer_kernel,
        out_shape=shapes,
        in_specs=[pl.BlockSpec(memory_space=pltpu.SMEM)]
        + [vmem] * 8
        + [pl.BlockSpec(memory_space=pl.ANY)] * 6,
        out_specs=[vmem] * 15,
        scratch_shapes=scratch,
        compiler_params=pltpu.CompilerParams(
            collective_id=0, has_side_effects=True, vmem_limit_bytes=VMEM_BYTES
        ),
    )(
        doc_lengths, tokens, cotangent,
        gain_pre_attn[None], gain_post_attn[None], gain_pre_mlp[None], gain_post_mlp[None],
        bias_up.reshape(32, 128), bias_down[None],
        w_query, w_key, w_value, w_out, w_up, w_down,
    )
    hbm = pl.BlockSpec(memory_space=pltpu.HBM)
    out, grad_tok, rms, gd, gu, go, gq, gk, gv, small_up, small_down, sa, sb, sc, sd = pl.pallas_call(
        finish_kernel,
        out_shape=shapes,
        in_specs=[hbm] * 15,
        out_specs=[hbm] * 15,
        scratch_shapes=[pltpu.VMEM(s.shape, s.dtype) for s in shapes] + [dma((2, 15))],
    )(*results)
    return (
        out, grad_tok, gq.T, gk.T, gv.T, go.T, gu, gd.T, small_up, small_down, sa, sb, sc, sd, rms
    )


def solution(mesh):
    placed = (
        P(("dp", "blk"), None),
        P("dp", None),
        P(),
        P(),
        P(),
        P(),
        P(),
        P(),
        P(),
        P(),
        P(),
        P(),
        P(),
        P(),
        P(("dp", "blk"), None),
    )
    paired = mesh.shape["blk"] == 2 and mesh.shape["dp"] == 16
    return jax.shard_map(
        layer_on_device if paired else on_device,
        mesh=mesh,
        in_specs=placed,
        out_specs=(
            P(("dp", "blk"), None),
            P(("dp", "blk"), None),
            P(None, ("dp", "blk")),
            P(None, ("dp", "blk")),
            P(None, ("dp", "blk")),
            P(None, ("dp", "blk")),
            P(None, ("dp", "blk")),
            P(None, ("dp", "blk")),
            P(("dp", "blk")),
            P(("dp", "blk")),
            P(("dp", "blk")),
            P(("dp", "blk")),
            P(("dp", "blk")),
            P(("dp", "blk")),
            P(None, ("dp", "blk")),
        ),
        check_vma=False,
    )
```

```python
import math

import jax
import jax.numpy as jnp
from jax import lax
from jax.experimental import pallas as pl
from jax.experimental.pallas import tpu as pltpu
from jax.sharding import PartitionSpec as P

D = 1024
H = 16
HD = 64


eps = 1e-06
neg_big = -1e30


def rms_norm(values, gain_row):
    return values * lax.rsqrt(jnp.mean(values * values, axis=-1, keepdims=True) + eps) * gain_row


def rotate(head_rows, position):
    half_size = head_rows.shape[-1] // 2
    frequency = 10000.0 ** (-2.0 * jnp.arange(half_size, dtype=jnp.float32) / head_rows.shape[-1])
    angles = position.astype(jnp.float32)[:, None] * frequency[None, :]
    cosine = jnp.cos(angles)[:, None, :]
    sine_part = jnp.sin(angles)[:, None, :]
    low_half = head_rows[..., :half_size]
    high_half = head_rows[..., half_size:]
    return jnp.concatenate(
        [low_half * cosine - high_half * sine_part, low_half * sine_part + high_half * cosine],
        axis=-1,
    )


def doc_layout(lengths, total_rows):
    index_row = jnp.arange(total_rows, dtype=jnp.int32)
    doc_ends = jnp.stack(
        [
            lengths[0],
            lengths[0] + lengths[1],
            lengths[0] + lengths[1] + lengths[2],
            lengths[0] + lengths[1] + lengths[2] + lengths[3],
        ]
    )
    segment = jnp.sum((index_row[:, None] >= doc_ends[None, :3]).astype(jnp.int32), axis=1)
    starts = doc_ends - lengths
    matches = segment[:, None] == jnp.arange(4, dtype=jnp.int32)[None, :]
    return (index_row, jnp.sum(jnp.where(matches, starts[None, :], 0), axis=1))


def block_mask(query_index, query_start, key_first, width):
    key_index = key_first + jnp.arange(width, dtype=jnp.int32)
    return (key_index[None, :] <= query_index[:, None]) & (
        key_index[None, :] >= query_start[:, None]
    )


def on_device(
    tokens,
    doc_lengths,
    w_query,
    w_key,
    w_value,
    w_out,
    w_up,
    w_down,
    bias_up,
    bias_down,
    gain_pre_attn,
    gain_post_attn,
    gain_pre_mlp,
    gain_post_mlp,
    cotangent,
):
    row_count = tokens.shape[0]
    cycle_size = lax.axis_size("blk")
    group_rows = row_count * cycle_size
    first_row = lax.axis_index("blk") * row_count
    index_all, start_all = doc_layout(doc_lengths[0], group_rows)
    query_index = lax.dynamic_slice_in_dim(index_all, first_row, row_count)
    query_start = lax.dynamic_slice_in_dim(start_all, first_row, row_count)
    position = query_index - query_start
    query_last = first_row + row_count - 1
    start_least = jnp.min(query_start)
    scale = HD ** (-0.5)
    tokens_f = tokens.astype(jnp.float32)
    normed_in, back_pre_attn = jax.vjp(rms_norm, tokens_f, gain_pre_attn)
    attn_in = normed_in.astype(jnp.bfloat16)
    query_pre = jnp.dot(attn_in, w_query, preferred_element_type=jnp.float32)
    key_pre = jnp.dot(attn_in, w_key, preferred_element_type=jnp.float32)
    value_pre = jnp.dot(attn_in, w_value, preferred_element_type=jnp.float32)
    queries, back_rot_query = jax.vjp(
        lambda arr: rotate(arr, position), query_pre.reshape(row_count, H, HD)
    )
    keys_rot, back_rot_key = jax.vjp(
        lambda arr: rotate(arr, position), key_pre.reshape(row_count, H, HD)
    )
    queries_low = queries.astype(jnp.bfloat16)
    keys_low = keys_rot.reshape(row_count, D).astype(jnp.bfloat16)
    values_low = value_pre.astype(jnp.bfloat16)
    initial = (
        jnp.full((H, row_count), neg_big, jnp.float32),
        jnp.zeros((H, row_count), jnp.float32),
        jnp.zeros((row_count, H, HD), jnp.float32),
    )
    key_piece = lax.all_gather(keys_low, "blk", axis=0, tiled=True)
    value_piece = lax.all_gather(values_low, "blk", axis=0, tiled=True)
    piece_rows = key_piece.shape[0]
    fold_width = math.gcd(piece_rows, 512)

    def one_block(state, number):
        key_first = number * fold_width

        def one_compute(state):
            running_top, totals, accum = state
            keys_blk = lax.dynamic_slice_in_dim(
                key_piece, number * fold_width, fold_width, 0
            ).reshape(fold_width, H, HD)
            values_blk = lax.dynamic_slice_in_dim(
                value_piece, number * fold_width, fold_width, 0
            ).reshape(fold_width, H, HD)
            scores = (
                jnp.einsum(
                    "qhd,khd->hqk", queries_low, keys_blk, preferred_element_type=jnp.float32
                )
                * scale
            )
            allowed = block_mask(query_index, query_start, key_first, fold_width)[None]
            scores = jnp.where(allowed, scores, neg_big)
            new_top = jnp.maximum(running_top, jnp.max(scores, axis=-1))
            weights = jnp.where(allowed, jnp.exp(scores - new_top[..., None]), 0.0)
            factor = jnp.exp(running_top - new_top)
            totals = totals * factor + jnp.sum(weights, axis=-1)
            accum = accum * jnp.transpose(factor)[:, :, None] + jnp.einsum(
                "hqk,khd->qhd",
                weights.astype(jnp.bfloat16),
                values_blk,
                preferred_element_type=jnp.float32,
            )
            return (new_top, totals, accum)

        active = (key_first <= query_last) & (key_first + fold_width - 1 >= start_least)
        return (lax.cond(active, one_compute, lambda state: state, state), None)

    result, unused = lax.scan(
        one_block, initial, jnp.arange(piece_rows // fold_width, dtype=jnp.int32)
    )
    running_top, totals, accum = result
    attn_full = accum / jnp.transpose(totals)[:, :, None]
    log_total = running_top + jnp.log(totals)
    attn_low = attn_full.reshape(row_count, D).astype(jnp.bfloat16)
    branch_attn = jnp.dot(attn_low, w_out, preferred_element_type=jnp.float32)
    post_attn, back_post_attn = jax.vjp(rms_norm, branch_attn, gain_post_attn)
    hidden_res = tokens_f + post_attn
    normed_mlp, back_pre_mlp = jax.vjp(rms_norm, hidden_res, gain_pre_mlp)
    mlp_in = normed_mlp.astype(jnp.bfloat16)
    pre_act = jnp.dot(mlp_in, w_up, preferred_element_type=jnp.float32) + bias_up
    activated, back_gelu = jax.vjp(lambda arr: jax.nn.gelu(arr, approximate=True), pre_act)
    act_low = activated.astype(jnp.bfloat16)
    branch_mlp = jnp.dot(act_low, w_down, preferred_element_type=jnp.float32) + bias_down
    post_mlp, back_post_mlp = jax.vjp(rms_norm, branch_mlp, gain_post_mlp)
    output = (hidden_res + post_mlp).astype(jnp.bfloat16)
    branch_rms = jnp.stack(
        [
            jnp.sqrt(jnp.mean(branch_attn * branch_attn, axis=-1) + eps),
            jnp.sqrt(jnp.mean(branch_mlp * branch_mlp, axis=-1) + eps),
        ]
    )
    grad_out_f = cotangent.astype(jnp.float32)
    grad_branch_mlp, grad_gain_post_mlp = back_post_mlp(grad_out_f)
    grad_mlp_low = grad_branch_mlp.astype(jnp.bfloat16)
    grad_bias_down = jnp.sum(grad_mlp_low.astype(jnp.float32), axis=0)
    grad_down = jnp.einsum("tf,td->df", act_low, grad_mlp_low, preferred_element_type=jnp.float32)
    grad_act = jnp.einsum("td,fd->tf", grad_mlp_low, w_down, preferred_element_type=jnp.float32)
    (grad_pre_act,) = back_gelu(grad_act)
    grad_pre_low = grad_pre_act.astype(jnp.bfloat16)
    grad_bias_up = jnp.sum(grad_pre_low.astype(jnp.float32), axis=0)
    grad_up = jnp.einsum("td,tf->fd", mlp_in, grad_pre_low, preferred_element_type=jnp.float32)
    grad_normed_mlp = jnp.einsum(
        "tf,df->td", grad_pre_low, w_up, preferred_element_type=jnp.float32
    )
    grad_res_part, grad_gain_pre_mlp = back_pre_mlp(grad_normed_mlp)
    grad_hidden = grad_out_f + grad_res_part
    grad_branch_attn, grad_gain_post_attn = back_post_attn(grad_hidden)
    grad_branch_low = grad_branch_attn.astype(jnp.bfloat16)
    grad_w_out = jnp.einsum(
        "td,te->ed", attn_low, grad_branch_low, preferred_element_type=jnp.float32
    )
    grad_attn = jnp.einsum("te,de->td", grad_branch_low, w_out, preferred_element_type=jnp.float32)
    grad_attn_low = grad_attn.astype(jnp.bfloat16).reshape(row_count, H, HD)
    delta = jnp.einsum("qhd,qhd->hq", grad_attn_low.astype(jnp.float32), attn_full)
    key_source, value_source = key_piece, value_piece
    width = math.gcd(group_rows, 512)

    def back_block(grad_query_acc, number):
        key_first = number * width

        def back_compute(grad_query_acc):
            keys_blk = lax.dynamic_slice_in_dim(key_source, key_first, width, 0).reshape(
                width, H, HD
            )
            values_blk = lax.dynamic_slice_in_dim(value_source, key_first, width, 0).reshape(
                width, H, HD
            )
            scores = (
                jnp.einsum(
                    "qhd,khd->hqk", queries_low, keys_blk, preferred_element_type=jnp.float32
                )
                * scale
            )
            allowed = block_mask(query_index, query_start, key_first, width)[None]
            probs = jnp.where(allowed, jnp.exp(scores - log_total[..., None]), 0.0)
            grad_probs = jnp.einsum(
                "qhd,khd->hqk", grad_attn_low, values_blk, preferred_element_type=jnp.float32
            )
            grad_scores = (probs * (grad_probs - delta[..., None])).astype(jnp.bfloat16)
            grad_query_acc = (
                grad_query_acc
                + jnp.einsum(
                    "hqk,khd->qhd", grad_scores, keys_blk, preferred_element_type=jnp.float32
                )
                * scale
            )
            grad_keys_blk = (
                jnp.einsum(
                    "hqk,qhd->khd", grad_scores, queries_low, preferred_element_type=jnp.float32
                )
                * scale
            )
            grad_values_blk = jnp.einsum(
                "hqk,qhd->khd",
                probs.astype(jnp.bfloat16),
                grad_attn_low,
                preferred_element_type=jnp.float32,
            )
            return (
                grad_query_acc,
                (grad_keys_blk.reshape(width, D), grad_values_blk.reshape(width, D)),
            )

        def skipped(grad_query_acc):
            return (
                grad_query_acc,
                (jnp.zeros((width, D), jnp.float32), jnp.zeros((width, D), jnp.float32)),
            )

        active = (key_first <= query_last) & (key_first + width - 1 >= start_least)
        return lax.cond(active, back_compute, skipped, grad_query_acc)

    grad_query_acc, stacked = lax.scan(
        back_block,
        jnp.zeros((row_count, H, HD), jnp.float32),
        jnp.arange(group_rows // width, dtype=jnp.int32),
    )
    grad_keys_all = stacked[0].reshape(group_rows, D)
    grad_values_all = stacked[1].reshape(group_rows, D)
    grad_keys_mine, grad_values_mine = (
        lax.psum_scatter(
            grad_keys_all.astype(jnp.bfloat16), "blk", scatter_dimension=0, tiled=True
        ).astype(jnp.float32),
        lax.psum_scatter(
            grad_values_all.astype(jnp.bfloat16), "blk", scatter_dimension=0, tiled=True
        ).astype(jnp.float32),
    )
    (grad_key_pre,) = back_rot_key(grad_keys_mine.reshape(row_count, H, HD))
    (grad_query_pre,) = back_rot_query(grad_query_acc)
    grad_key_low = grad_key_pre.reshape(row_count, D).astype(jnp.bfloat16)
    grad_query_low = grad_query_pre.reshape(row_count, D).astype(jnp.bfloat16)
    grad_value_low = grad_values_mine.astype(jnp.bfloat16)
    grad_query = jnp.einsum(
        "td,te->ed", attn_in, grad_query_low, preferred_element_type=jnp.float32
    )
    grad_key = jnp.einsum("td,te->ed", attn_in, grad_key_low, preferred_element_type=jnp.float32)
    grad_value = jnp.einsum(
        "td,te->ed", attn_in, grad_value_low, preferred_element_type=jnp.float32
    )
    grad_normed_in = (
        jnp.einsum("te,de->td", grad_query_low, w_query, preferred_element_type=jnp.float32)
        + jnp.einsum("te,de->td", grad_key_low, w_key, preferred_element_type=jnp.float32)
        + jnp.einsum("te,de->td", grad_value_low, w_value, preferred_element_type=jnp.float32)
    )
    grad_tokens_part, grad_gain_pre_attn = back_pre_attn(grad_normed_in)
    grad_tokens = (grad_hidden + grad_tokens_part).astype(jnp.bfloat16)
    count = lax.axis_size(("dp", "blk"))
    low = jnp.bfloat16
    pieces = [
        part.astype(low).reshape(count, -1, D)
        for part in (grad_query, grad_key, grad_value, grad_w_out, grad_up, grad_down)
    ]
    small = [
        part.reshape(count, -1)
        for part in (
            grad_bias_up,
            grad_bias_down,
            grad_gain_pre_attn,
            grad_gain_post_attn,
            grad_gain_pre_mlp,
            grad_gain_post_mlp,
        )
    ]
    sizes = [part.shape[1] for part in pieces]
    summed = lax.psum_scatter(
        jnp.concatenate(pieces, axis=1), ("dp", "blk"), scatter_dimension=0
    ).astype(jnp.float32)
    small_sizes = [part.shape[1] for part in small]
    small_flat = jnp.concatenate(small, axis=1)
    padding = -small_flat.shape[1] % 128
    small_flat = jnp.pad(small_flat, ((0, 0), (0, padding)))
    small_summed = lax.psum_scatter(small_flat, ("dp", "blk"), scatter_dimension=0)
    cuts = [sum(sizes[: i + 1]) for i in range(len(sizes) - 1)]
    parts = jnp.split(summed, cuts, axis=0)
    parts[5] = parts[5].reshape(D // count, -1)
    small_cuts = [sum(small_sizes[: i + 1]) for i in range(len(small_sizes))]
    small_parts = jnp.split(small_summed, small_cuts, axis=0)[:6]
    return (output, grad_tokens, *[part.T for part in parts], *small_parts, branch_rms)


MESH_ID = pl.DeviceIdType.MESH
F32 = jnp.float32
BF16 = jnp.bfloat16
TOK = 256
PACK = 512
FF = 4096
HALF_FF = 2048
HALF_D = 512
CHUNK = 128
VMEM_BYTES = 62 * 1024 * 1024
UNIT_ORDER = (
    "ywvx",
    "wvxy",
    "ywxv",
    "yxwv",
    "wyv",
    "ywv",
    "ywv",
    "ywv",
    "yxwv",
    "yxwv",
    "wxyv",
    "xywv",
    "xywv",
    "xwyv",
    "xywv",
    "xwyv",
)
SLOTS = (
    (0, 1, 10, 11,),
    (),
    (),
    (20,),
    (2, 12,),
    (),
    (21,),
    (),
    (3, 13,),
    (30,),
    (4, 22,),
    (),
    (31,),
    (110,),
    (14, 100, 23,),
    (40, 50, 111, 5, 32,),
    (24, 112,),
    (41, 33, 160, 102, 15, 101, 42, 52, 113, 6, 114, 51, 43, 16, 103, 60, 44, 34, 61, 115, 120, 53, 54, 25, 45, 70, 161, 62, 121, 35, 104, 116, 63, 130, 55, 122, 72, 131, 26, 123, 71, 162, 64, 105, 140, 36,),
    (132, 80, 124, 141, 133, 81, 73, 150, 163, 74, 65, 106, 90, 142, 82, 134, 143, 125, 151, 83, 152, 164, 75, 92, 126, 84, 91, 144, 135, 153, 154, 85, 145, 93, 94, 136, 155, 86, 146, 95, 156, 96,),
)


def mm(a, b):
    return jnp.dot(a, b, preferred_element_type=F32)


def mm_nt(a, b):
    return lax.dot_general(a, b, (((1,), (1,)), ((), ())), preferred_element_type=F32)


def al(offset, step):
    return pl.multiple_of(offset, step)


def norm_back(v, r, gain, grad):
    scaled = grad * gain
    inner = jnp.mean(v * scaled, axis=-1, keepdims=True)
    return r * scaled - v * (r * r * r * inner), jnp.sum(grad * v * r, axis=0, keepdims=True)


def inv_rms(v):
    return lax.rsqrt(jnp.mean(v * v, axis=-1, keepdims=True) + eps)


def layer_kernel(
    doc, tok, cot, gain_a, gain_b, gain_c, gain_d, bias_up, bias_down,
    wq_hbm, wk_hbm, wv_hbm, wo_hbm, wu_hbm, wd_hbm,
    *refs,
):
    results, refs = refs[:15], refs[15:]
    (
        out, grad_tok, rms, o_down, o_up, o_out, o_query, o_key, o_value,
        small_up, small_down, small_a, small_b, small_c, small_d, o_sem,
        wq, wk, wv, wo, wu, wd, xin, q_t, k_t, v_t, k_n, v_n, mask, attn_t, attn_nat,
        branch, hid, xm, act, g_t, part_send, part_recv, part_own, nat, gb_t,
        rope, lse, stat, s_down, r1_down, r2_down, r3_down, r4_down, r1_up, r2_up, r3_up, xm_m, pre_m,
        r1_late, r2_late, r3_late, r4_late, aux_s, aux_r,
        w_sem, m_send, m_recv, c_send, c_recv, rs_send, rs_recv, a_send, a_recv,
    ) = refs
    held = (
        out, grad_tok, rms, o_down, o_up, o_out, o_query, o_key, o_value,
        small_up, small_down, small_a, small_b, small_c, small_d,
    )

    def hand_over(i):
        return pltpu.make_async_copy(held[i], results[i], o_sem.at[i])

    dp = lax.axis_index("dp")
    b = lax.axis_index("blk")
    x = lax.rem(dp, 2)
    y = lax.rem(dp // 2, 2)
    z = dp // 4
    other = 1 - b
    core_peer = (dp, other)
    x_peer = (dp + 1 - 2 * x, b)
    y_peer = (dp + 2 - 4 * y, b)

    z_low = (dp + 4 - 8 * lax.rem(z, 2), b)
    z_high = (dp + 8 - 16 * (z // 2), b)
    barrier = pltpu.get_barrier_semaphore()
    for peer in (core_peer, x_peer, y_peer, z_low, z_high):
        pl.semaphore_signal(barrier, inc=1, device_id=peer, device_id_type=MESH_ID)

    own_cols = al(b * HALF_D, HALF_D)
    oth_cols = al(other * HALF_D, HALF_D)
    own_tok = al(b * TOK, TOK)
    oth_tok = al(other * TOK, TOK)

    w_copies = [
        pltpu.make_async_copy(src.at[:, pl.ds(own_cols, HALF_D)], dst, w_sem.at[i])
        for i, (src, dst) in enumerate(((wq_hbm, wq), (wk_hbm, wk), (wv_hbm, wv)))
    ]
    w_copies.append(pltpu.make_async_copy(wo_hbm, wo, w_sem.at[3]))
    for copy in w_copies:
        copy.start()

    def up_copy(j):
        return pltpu.make_async_copy(
            wu_hbm.at[:, pl.ds(al((2 * j + b) * 128, 128), 128)],
            wu.at[:, pl.ds(al(j * 128, 128), 128)],
            w_sem.at[4],
        )

    def down_copy(j):
        return pltpu.make_async_copy(
            wd_hbm.at[pl.ds(al((2 * j + b) * 128, 128), 128)],
            wd.at[pl.ds(al(j * 128, 128), 128)],
            w_sem.at[5],
        )

    def to_core(k, src, dst):
        return pltpu.make_async_remote_copy(
            src_ref=src, dst_ref=dst, send_sem=c_send.at[k], recv_sem=c_recv.at[k],
            device_id=core_peer, device_id_type=MESH_ID,
        )

    end_a = doc[0, 0]
    end_b = end_a + doc[0, 1]
    end_c = end_b + doc[0, 2]
    index_row = lax.broadcasted_iota(jnp.int32, (1, PACK), 1)
    start_row = jnp.where(
        index_row >= end_c,
        end_c,
        jnp.where(index_row >= end_b, end_b, jnp.where(index_row >= end_a, end_a, 0)),
    )
    position = (index_row - start_row).astype(F32)
    freq = jnp.exp(
        lax.broadcasted_iota(jnp.int32, (32, PACK), 0).astype(F32) * (-math.log(10000.0) / 32.0)
    )
    angle = position * freq
    rope[0] = jnp.cos(angle)
    rope[1] = jnp.sin(angle)

    def fill_mask(i, carry):
        rows = pl.ds(al(i * 64, 64), 64)
        key_index = lax.broadcasted_iota(jnp.int32, (64, PACK), 0) + i * 64
        query_index = lax.broadcasted_iota(jnp.int32, (64, PACK), 1)
        allowed = (key_index <= query_index) & (key_index >= start_row)
        mask[rows, :] = jnp.where(allowed, 0.0, neg_big).astype(BF16)
        return carry

    lax.fori_loop(0, 8, fill_mask, 0)

    def pre_attn(i, carry):
        rows = pl.ds(al(i * CHUNK, CHUNK), CHUNK)
        v = tok[rows, :].astype(F32)
        xin[pl.ds(al(own_tok + i * CHUNK, CHUNK), CHUNK), :] = (
            v * inv_rms(v) * gain_a[...]
        ).astype(BF16)
        return carry

    lax.fori_loop(0, TOK // CHUNK, pre_attn, 0)
    pl.semaphore_wait(barrier, 5)
    own_rows = xin.at[pl.ds(own_tok, TOK)]
    xin_copy = to_core(0, own_rows, own_rows)
    xin_copy.start()
    lax.fori_loop(0, 16, lambda j, c: (up_copy(j).start(), c)[1], 0)
    lax.fori_loop(0, 16, lambda j, c: (down_copy(j).start(), c)[1], 0)

    attn_oth = nat.at[:, pl.ds(0, PACK)]

    def project(tok_at):
        rows = pl.ds(tok_at, TOK)
        cos = rope[0, :, rows]
        sin = rope[1, :, rows]
        x_rows = xin[rows, :]

        def turned(w, scale):
            flat = mm(x_rows, w[...]).T.reshape(8, 2, 32, TOK)
            low, high = flat[:, 0], flat[:, 1]
            both = jnp.stack([low * cos - high * sin, low * sin + high * cos], axis=1)
            return (both * scale).reshape(HALF_D, TOK).astype(BF16)

        q_t[:, rows] = turned(wq, 0.125)
        keys = turned(wk, 1.0)
        k_t[:, rows] = keys
        k_n[rows, :] = keys.T
        values = mm(x_rows, wv[...]).astype(BF16)
        v_n[rows, :] = values
        v_t[:, rows] = values.T

    for copy in w_copies[:3]:
        copy.wait()
    project(own_tok)
    xin_copy.wait()
    project(oth_tok)

    zeros = jnp.zeros((64, TOK), BF16)

    def slab(head_rows, which):
        return jnp.concatenate([head_rows, zeros] if which == 0 else [zeros, head_rows], axis=0)

    def attend(p, carry):
        slab_cols = pl.ds(al(p * 128, 128), 128)
        parts = [
            (w, pl.ds(al(p * 128 + w * 64, 64), 64), slice(i * TOK, i * TOK + TOK), (i + 1) * TOK)
            for i in (1, 0)
            for w in (0, 1)
        ]
        scores = [
            mm(k_n[:keys, slab_cols], slab(q_t[rows, cols], w)) + mask[:keys, cols].astype(F32)
            for w, rows, cols, keys in parts
        ]
        tops = [jnp.max(score, axis=0, keepdims=True) for score in scores]
        weights = [jnp.exp(score - top) for score, top in zip(scores, tops)]
        totals = [jnp.sum(weight, axis=0, keepdims=True) for weight in weights]
        for (w, rows, cols, keys), weight, top, total in zip(parts, weights, tops, totals):
            attn_t[rows, cols] = mm(v_t[rows, :keys], weight.astype(BF16)) * (1.0 / total)
            lse[pl.ds(p * 2 + w, 1), cols] = top + jnp.log(total)
        attn_nat[:, slab_cols] = attn_t[pl.ds(al(p * 128, 128), 128), :].T.astype(BF16)
        to_core(
            1 + p, attn_nat.at[pl.ds(oth_tok, TOK), slab_cols], attn_oth.at[:, slab_cols]
        ).start()
        return carry

    lax.fori_loop(0, 4, attend, 0)

    w_copies[3].wait()
    branch[...] = mm(attn_nat[pl.ds(own_tok, TOK), :], wo[pl.ds(own_cols, HALF_D), :])

    def attn_copy(p):
        cols = pl.ds(al(p * 128, 128), 128)
        return to_core(1 + p, attn_nat.at[pl.ds(oth_tok, TOK), cols], attn_oth.at[:, cols])

    lax.fori_loop(0, 4, lambda p, c: (attn_copy(p).wait(), c)[1], 0)
    branch[...] += mm(attn_oth[...], wo[pl.ds(oth_cols, HALF_D), :])

    def post_attn(i, carry):
        rows = pl.ds(al(i * CHUNK, CHUNK), CHUNK)
        v = branch[rows, :]
        square = jnp.mean(v * v, axis=-1, keepdims=True) + eps
        stat[0, rows, :] = jnp.broadcast_to(jnp.sqrt(square), (CHUNK, 128))
        h = tok[rows, :].astype(F32) + v * lax.rsqrt(square) * gain_b[...]
        hid[rows, :] = h
        xm[pl.ds(al(own_tok + i * CHUNK, CHUNK), CHUNK), :] = (
            h * inv_rms(h) * gain_c[...]
        ).astype(BF16)
        return carry

    lax.fori_loop(0, TOK // CHUNK, post_attn, 0)
    own_rows_m = xm.at[pl.ds(own_tok, TOK)]
    xm_copy = to_core(5, own_rows_m, own_rows_m)
    xm_copy.start()
    xm_mate = pltpu.make_async_remote_copy(
        src_ref=own_rows_m, dst_ref=xm_m.at[pl.ds(own_tok, TOK)], send_sem=m_send.at[1],
        recv_sem=m_recv.at[1], device_id=x_peer, device_id_type=MESH_ID,
    )
    xm_mate.start()

    def up_step(tok_at, i):
        cols = pl.ds(al(i * 1024, 1024), 1024)
        rows = pl.ds(tok_at, TOK)
        bias = jnp.concatenate(
            [bias_up[pl.ds(16 * i + 2 * j + b, 1), :] for j in range(8)], axis=1
        )
        pre = mm(xm[rows, :], wu[:, cols]) + bias
        square = pre * pre
        th = jnp.tanh(pre * (0.7978845608 + (0.7978845608 * 0.044715) * square))
        half = 0.5 + 0.5 * th
        act[rows, cols] = (pre * half).astype(BF16)
        slope = half + pre * (0.5 - 0.5 * th * th) * (
            0.7978845608 + (0.7978845608 * 0.134145) * square
        )
        g_t[cols, rows] = slope.astype(BF16).T

    pltpu.make_async_copy(wu_hbm.at[:, pl.ds(0, HALF_FF)], wu, w_sem.at[4]).wait()
    lax.fori_loop(0, 2, lambda i, c: (up_step(own_tok, i), c)[1], 0)
    xm_copy.wait()
    lax.fori_loop(0, 2, lambda i, c: (up_step(oth_tok, i), c)[1], 0)
    pltpu.make_async_copy(wd_hbm.at[pl.ds(0, HALF_FF)], wd, w_sem.at[5]).wait()

    def down_step(tok_at, dst, i):
        cols = slice(i * 512, i * 512 + 512)
        dst[:, cols] = mm(act[pl.ds(tok_at, TOK), :], wd[:, cols]).astype(dst.dtype)

    mlp_copies = [
        to_core(k, part_send.at[:, pl.ds(i * 512, 512)], part_recv.at[:, pl.ds(i * 512, 512)])
        for i, k in ((0, 6), (1, 15))
    ]
    for i in range(2):
        down_step(oth_tok, part_send, i)
        mlp_copies[i].start()
    for i in range(2):
        down_step(own_tok, part_own, i)
    for copy in mlp_copies:
        copy.wait()
    def post_mlp(i, carry):
        sum_bias, sum_gain = carry
        rows = pl.ds(al(i * CHUNK, CHUNK), CHUNK)
        v = part_own[rows, :] + part_recv[rows, :].astype(F32) + bias_down[...]
        square = jnp.mean(v * v, axis=-1, keepdims=True) + eps
        stat[1, rows, :] = jnp.broadcast_to(jnp.sqrt(square), (CHUNK, 128))
        r = lax.rsqrt(square)
        out[rows, :] = (hid[rows, :] + v * r * gain_d[...]).astype(BF16)
        back, gain_part = norm_back(v, r, gain_d[...], cot[rows, :].astype(F32))
        back = back.astype(BF16)
        nat[rows, :] = back
        return (
            sum_bias + jnp.sum(back.astype(F32), axis=0, keepdims=True),
            sum_gain + gain_part,
        )

    def turn_and_send(dst, i, k):
        tok_cols = pl.ds(al(own_tok + i * CHUNK, CHUNK), CHUNK)
        for j in range(4):
            cols = slice(j * 256, j * 256 + 256)
            dst[cols, tok_cols] = nat[i * CHUNK : i * CHUNK + CHUNK, cols].T
        part = dst.at[:, tok_cols]
        copy = to_core(k, part, part)
        copy.start()
        return copy

    zero_row = jnp.zeros((1, D), F32)
    sums = (zero_row, zero_row)
    gb_copies = []
    for i, k in ((0, 7), (1, 16)):
        sums = post_mlp(i, sums)
        gb_copies.append(turn_and_send(gb_t, i, k))
    sum_bias_down, sum_gain_d = sums
    aux_s[0] = jnp.zeros((16, D), F32)
    aux_s[0, 0:1, :] = sum_bias_down
    aux_s[0, 4:5, :] = sum_gain_d
    for i in range(2):
        rms[i : i + 1, :] = stat[i].T[0:1, :]
    hand_over(0).start()
    hand_over(2).start()

    for copy in gb_copies:
        copy.wait()
    down_refs = (s_down, r1_down, r2_down, r3_down, r4_down)
    up_refs = (wd, r1_up, r2_up, r3_up)
    late_refs = (wu, r1_late, r2_late, r3_late, r4_late)
    units = (
        [(down_refs, 512 * i, 512, 64) for i in range(4)]
        + [(up_refs, 256 * i, 256, 128) for i in range(4)]
        + [(late_refs, 256 * i, 256, 64) for i in range(8)]
    )
    place = {
        "x": (x, 1, x_peer),
        "y": (y, 2, y_peer),
        "w": (lax.rem(z, 2), 4, z_low),
        "v": (z // 2, 8, z_high),
    }

    def unit_axes(n):
        return [place[letter] for letter in UNIT_ORDER[n]]

    def kept(n, steps):
        axes = unit_axes(n)
        step = 2 ** len(axes) // 2 * units[n][3]
        return sum((axis[0] * (step >> i) for i, axis in enumerate(axes[:steps])), 0)

    def unit_copy(n, k):
        refs, c0, width, rows = units[n]
        axes = unit_axes(n)
        span = 2 ** len(axes)
        cols = pl.ds(c0, width)
        if k < 2:
            bit, _, peer = axes[0]
            second = lax.rem(axes[1][0] + 1 + k, 2)
            count = span // 4 * rows
            src = refs[0].at[pl.ds(al(((1 - bit) * 2 + second) * count, count), count), cols]
            dst = refs[1].at[pl.ds(al(second * count, count), count), cols]
        else:
            bit, _, peer = axes[k - 1]
            count = (span >> k) * rows
            at = kept(n, k - 1) + (1 - bit) * count
            src = refs[0].at[pl.ds(al(at, count), count), cols]
            dst = refs[k].at[:, cols]
        return pltpu.make_async_remote_copy(
            src_ref=src, dst_ref=dst, send_sem=rs_send.at[n], recv_sem=rs_recv.at[n, k],
            device_id=peer, device_id_type=MESH_ID,
        )

    def add_rows(n, at, arrived, arrived_at, count):
        refs, c0, width, _ = units[n]
        cols = pl.ds(c0, width)

        def step(i, carry):
            to = pl.ds(al(at + i * 64, 64), 64)
            got = refs[arrived][pl.ds(al(arrived_at + i * 64, 64), 64), cols]
            refs[0][to, cols] = (refs[0][to, cols].astype(F32) + got.astype(F32)).astype(BF16)
            return carry

        lax.fori_loop(0, count // 64, step, 0)

    def serve(n, k):
        refs, c0, width, rows = units[n]
        axes = unit_axes(n)
        last = len(axes)
        span = 2**last
        unit_copy(n, k).wait_recv()
        if k < 2:
            second = lax.rem(axes[1][0] + 1 + k, 2)
            count = span // 4 * rows
            add_rows(n, kept(n, 1) + second * count, 1, second * count, count)
            if k == 0:
                unit_copy(n, 2).start()
        elif k < last:
            count = (span // 2 >> k) * rows
            bit = axes[k][0]
            add_rows(n, kept(n, k) + (1 - bit) * count, k, (1 - bit) * count, count)
            unit_copy(n, k + 1).start()
            add_rows(n, kept(n, k) + bit * count, k, bit * count, count)
        else:
            cols = pl.ds(c0, width)
            mine = refs[0][pl.ds(al(kept(n, last), rows), rows), cols].astype(F32)
            total = mine + refs[last][:, cols].astype(F32)
            if 4 <= n < 8:
                o_up[c0 : c0 + width, :] = total.T
            else:
                at, to = final_at(n)
                part_own[at : at + 64, to : to + width] = total
                final_copy(n).start()

    def final_at(n):
        return (64 * n, 0) if n < 4 else (64 * ((n - 8) // 2), 512 + 256 * (n % 2))

    def final_rows(n, half):
        at, to = final_at(n)
        return pl.ds(al(at + half * 32, 32), 32), pl.ds(to, units[n][2])

    def final_copy(n):
        at, to = (32 * n, 0) if n < 4 else (128 + 32 * ((n - 8) // 2), 256 * (n % 2))
        dst = attn_t.at[pl.ds(at, 32), pl.ds(to, units[n][2])]
        return final_with(part_own.at[final_rows(n, other)], dst, 18 if n < 4 else 19)

    def final_with(src, dst, k):
        return pltpu.make_async_remote_copy(
            src_ref=src, dst_ref=dst, send_sem=c_send.at[18], recv_sem=c_recv.at[k],
            device_id=core_peer, device_id_type=MESH_ID,
        )

    aux_peers = (core_peer, x_peer, y_peer, z_low, z_high)

    def aux_sum(k):
        return aux_s.at[0] if k == 0 else hid.at[pl.ds(16 * k, 16)]

    def aux_copy(k):
        return pltpu.make_async_remote_copy(
            src_ref=aux_sum(k), dst_ref=aux_r.at[k], send_sem=a_send.at[k],
            recv_sem=a_recv.at[k], device_id=aux_peers[k], device_id_type=MESH_ID,
        )

    def aux_end(k):
        aux_copy(k).wait_recv()
        aux_sum(k + 1)[...] = aux_sum(k)[...] + aux_r[k]
        if k < 4:
            aux_copy(k + 1).start()

    def slot(i):
        for code in SLOTS[i]:
            n, k = code // 10, code % 10
            if n == len(units):
                aux_end(k)
            elif k < 2:
                unit_copy(n, k).start()
            else:
                serve(n, k - 2)

    def weight_grad(n, first, last, *terms):
        refs, c0, width, rows = units[n]
        axes = unit_axes(n)
        fixed = x if len(axes) == 3 else 0
        tails = [0]
        for axis in axes[2:]:
            tails = [tail + p * axis[1] for tail in tails for p in range(2)]
        count = len(tails) * rows
        for g in range(first, last):
            i = lax.rem(axes[0][0] + 1 + g // 2, 2)
            j = lax.rem(axes[1][0] + 1 + g % 2, 2)
            base = i * axes[0][1] + j * axes[1][1] + fixed
            total = None
            for left, right in terms:
                stack = jnp.concatenate([left(base + tail) for tail in tails], axis=0)
                part = mm(stack, right)
                total = part if total is None else total + part
            at = pl.ds(al((i * 2 + j) * count, count), count)
            refs[0][at, pl.ds(c0, width)] = total.astype(BF16)

    def rows_of(ref, rows):
        return lambda chip: ref[pl.ds(al(chip * rows, rows), rows), :]

    for first in (0, 2):
        for n in range(4):
            weight_grad(
                n, first, first + 2, (rows_of(gb_t, 64), act[:, 512 * n : 512 * n + 512])
            )
        slot(first // 2)

    def mate_copy(k):
        return pltpu.make_async_remote_copy(
            src_ref=g_t.at[pl.ds(al((2 * k + 1 - x) * 128, 128), 128)],
            dst_ref=pre_m.at[pl.ds(al(k * 128, 128), 128)],
            send_sem=m_send.at[0], recv_sem=m_recv.at[0],
            device_id=x_peer, device_id_type=MESH_ID,
        )

    def act_back(i, carry):
        rows = pl.ds(al(i * 512, 512), 512)
        g_t[rows, :] = (mm(wd[rows, :], gb_t[...]) * g_t[rows, :].astype(F32)).astype(BF16)
        for j in range(2):
            mate_copy(2 * i + j).start()
        return carry

    lax.fori_loop(0, 4, act_back, 0)
    slot(2)

    def mlp_back(tok_at, dst, i):
        at = pl.ds(al(i * 512, 512), 512)
        dst[:, at] = mm(wu[at, :], g_t[:, pl.ds(tok_at, TOK)]).T.astype(dst.dtype)

    lax.fori_loop(0, 2, lambda i, c: (mlp_back(oth_tok, part_send, i), c)[1], 0)
    mlp_back_copy = to_core(8, part_send, part_recv)
    mlp_back_copy.start()
    slot(3)
    xm_mate.wait()
    mate_rows = xm_m.at[pl.ds(own_tok, TOK)]
    xm_pass = to_core(14, mate_rows, mate_rows)
    xm_pass.start()
    lax.fori_loop(0, 2, lambda i, c: (mlp_back(own_tok, part_own, i), c)[1], 0)
    ones = jnp.ones((16, PACK), BF16)
    for i in range(2):
        aux_s[0, pl.ds(8 + 2 * b + i, 1), :] = mm_nt(ones, g_t[i * 1024 : i * 1024 + 1024, :])[0:1]
    slot(4)
    mlp_back_copy.wait()

    gba_t = wd.at[pl.ds(D, D), pl.ds(0, PACK)]
    ga_t = wd.at[pl.ds(D, HALF_D), pl.ds(PACK, PACK)]

    def hidden_back(i, carry):
        sum_c, sum_b = carry
        rows = pl.ds(al(i * CHUNK, CHUNK), CHUNK)
        h = hid[rows, :]
        back, part_c = norm_back(
            h, inv_rms(h), gain_c[...], part_own[rows, :] + part_recv[rows, :].astype(F32)
        )
        g_hidden = cot[rows, :].astype(F32) + back
        hid[rows, :] = g_hidden
        v = branch[rows, :]
        back, part_b = norm_back(v, inv_rms(v), gain_b[...], g_hidden)
        nat[rows, :] = back.astype(BF16)
        return sum_c + part_c, sum_b + part_b

    sums = (zero_row, zero_row)
    gba_copies = []
    for i, k in ((0, 9), (1, 17)):
        sums = hidden_back(i, sums)
        gba_copies.append(turn_and_send(gba_t, i, k))
    sum_gain_c, sum_gain_b = sums
    aux_s[0, 3:4, :] = sum_gain_c
    aux_s[0, 2:3, :] = sum_gain_b
    slot(5)
    for copy in gba_copies:
        copy.wait()

    for n in (8, 9):
        weight_grad(
            n, 0, 4, (rows_of(gba_t, 64), attn_nat[:, 256 * (n - 8) : 256 * (n - 8) + 256])
        )
    slot(6)
    ga_t[...] = mm(wo[pl.ds(own_cols, HALF_D), :], gba_t[...]).astype(BF16)
    slot(7)

    def head_grad(off):
        def rows(chip):
            at = al(off + chip // 8 * HALF_D, HALF_D)
            return act[pl.ds(al(lax.rem(chip, 8) * 64, 64), 64), pl.ds(at, HALF_D)]

        return rows

    own_q = pl.ds(al(own_cols, HALF_D), HALF_D)
    own_k = pl.ds(al(D + own_cols, HALF_D), HALF_D)
    gv = gb_t

    def attend_back(p, carry):
        slab_cols = pl.ds(al(p * 128, 128), 128)
        parts = [
            (w, pl.ds(al(p * 128 + w * 64, 64), 64), slice(i * TOK, i * TOK + TOK), (i + 1) * TOK)
            for w in (0, 1)
            for i in (0, 1)
        ]
        deltas = [
            jnp.sum(ga_t[rows, cols].astype(F32) * attn_t[rows, cols], axis=0, keepdims=True)
            for w, rows, cols, keys in parts
        ]
        scores = [
            mm(k_n[:keys, slab_cols], slab(q_t[rows, cols], w)) + mask[:keys, cols].astype(F32)
            for w, rows, cols, keys in parts
        ]
        g_probs = [
            mm(v_n[:keys, slab_cols], slab(ga_t[rows, cols], w)) for w, rows, cols, keys in parts
        ]
        probs = [
            jnp.exp(score - lse[pl.ds(p * 2 + part[0], 1), part[2]])
            for score, part in zip(scores, parts)
        ]
        g_scores = [
            (prob * (g_prob - delta)).astype(BF16)
            for prob, g_prob, delta in zip(probs, g_probs, deltas)
        ]
        grads_q = [
            mm(k_t[rows, :keys], g_score) * 0.125
            for (w, rows, cols, keys), g_score in zip(parts, g_scores)
        ]
        grads_k = [
            mm_nt(q_t[rows, cols], g_score)
            for (w, rows, cols, keys), g_score in zip(parts, g_scores)
        ]
        grads_v = [
            mm_nt(ga_t[rows, cols], prob.astype(BF16))
            for (w, rows, cols, keys), prob in zip(parts, probs)
        ]

        def both(first, second):
            return jnp.concatenate([first + second[:, :TOK], second[:, TOK:]], axis=1)

        cos, sin = rope[0], rope[1]
        for w in range(2):
            to = pl.ds(al(own_cols + p * 128 + w * 64, 64), 64)
            at = parts[2 * w][1]
            full_q = jnp.concatenate(grads_q[2 * w : 2 * w + 2], axis=1)
            for full, dst in ((full_q, own_q), (both(*grads_k[2 * w : 2 * w + 2]), own_k)):
                low, high = full[:32], full[32:]
                act[at, dst] = jnp.concatenate(
                    [low * cos + high * sin, high * cos - low * sin], axis=0
                ).astype(BF16)
            gv[to, :] = both(*grads_v[2 * w : 2 * w + 2]).astype(BF16)
        return carry

    lax.fori_loop(0, 2, attend_back, 0)
    slot(8)
    lax.fori_loop(2, 4, attend_back, 0)
    own_heads = pl.ds(own_cols, HALF_D)
    head_copies = [
        to_core(10 + i, ref, ref)
        for i, ref in enumerate((act.at[:, own_q], act.at[:, own_k], gv.at[own_heads]))
    ]
    for copy in head_copies:
        copy.start()
    slot(9)

    def in_back(tok_at, dst, i):
        at = pl.ds(al(i * 512, 512), 512)
        cols = pl.ds(tok_at, TOK)
        total = mm(wq[at, :], act[:, pl.ds(al(own_cols + tok_at, TOK), TOK)])
        total += mm(wk[at, :], act[:, pl.ds(al(D + own_cols + tok_at, TOK), TOK)])
        total += mm(wv[at, :], gv[own_heads, cols])
        dst[:, at] = total.T.astype(dst.dtype)

    lax.fori_loop(0, 2, lambda i, c: (in_back(oth_tok, part_send, i), c)[1], 0)
    in_back_copy = to_core(13, part_send, part_recv)
    in_back_copy.start()
    slot(10)
    for copy in head_copies:
        copy.wait()
    for first in (0, 2):
        for i, rows in enumerate((head_grad(0), head_grad(D), rows_of(gv, 64))):
            for j in range(2):
                cols = pl.ds(al(own_cols + 256 * j, 256), 256)
                weight_grad(10 + 2 * i + j, first, first + 2, (rows, xin[:, cols]))
        slot(11 + first // 2)
    lax.fori_loop(0, 2, lambda i, c: (in_back(own_tok, part_own, i), c)[1], 0)
    slot(13)
    in_back_copy.wait()

    def token_back(i, carry):
        rows = pl.ds(al(i * CHUNK, CHUNK), CHUNK)
        v = tok[rows, :].astype(F32)
        back, part_a = norm_back(
            v, inv_rms(v), gain_a[...], part_own[rows, :] + part_recv[rows, :].astype(F32)
        )
        grad_tok[rows, :] = (hid[rows, :] + back).astype(BF16)
        return carry + part_a

    aux_s[0, 1:2, :] = lax.fori_loop(0, TOK // CHUNK, token_back, zero_row)
    hand_over(1).start()
    slot(14)

    pltpu.make_async_remote_copy(
        src_ref=pre_m, dst_ref=pre_m, send_sem=m_send.at[0], recv_sem=m_recv.at[0],
        device_id=x_peer, device_id_type=MESH_ID,
    ).wait()
    xm_pass.wait()

    def mate_pre(chip):
        return pre_m[pl.ds(al(chip // 2 * 128, 128), 128), :]

    for first in (0, 2):
        for n in range(4, 8):
            cols = slice(256 * (n - 4), 256 * (n - 4) + 256)
            weight_grad(
                n, first, first + 2, (rows_of(g_t, 128), xm[:, cols]), (mate_pre, xm_m[:, cols])
            )
        slot(15 + first // 2)

    aux_copy(0).start()
    slot(17)
    finals = attn_t.at[pl.ds(0, 128)]
    final_with(finals, finals, 18).wait_recv()

    for j in range(16):
        rows, _ = final_rows(j // 4, b)
        at = j % 4 * 128
        o_down[:, pl.ds(al((2 * j + b) * 128, 128), 128)] = part_own[rows, at : at + 128]
        o_down[:, pl.ds(al((2 * j + other) * 128, 128), 128)] = attn_t[
            j // 4 * 32 : j // 4 * 32 + 32, at : at + 128
        ]
    hand_over(3).start()
    slot(18)
    hand_over(4).start()
    device = dp * 2 + b
    at = pl.ds(al(device // 4 * 128, 128), 128)
    lines = pltpu.roll(aux_sum(5)[0:8, at], lax.rem(128 - lax.rem(device, 4) * 32, 128), 1)
    for i, ref in enumerate((small_down, small_a, small_b, small_c, small_d)):
        ref[...] = lines[i, :32]
    lines = aux_sum(5)[8:16, pl.ds(al(lax.rem(dp, 8) * 128, 128), 128)]
    chosen = lax.broadcasted_iota(jnp.int32, (8, 128), 0) == 2 * b + dp // 8
    small_up[...] = jnp.sum(jnp.where(chosen, lines, 0.0), axis=0)
    for i in range(9, 15):
        hand_over(i).start()
    for n, (refs, c0, width, rows) in enumerate(units):
        sent = refs[0].at[pl.ds(0, (2 ** len(UNIT_ORDER[n]) - 1) * rows), pl.ds(c0, width)]
        pltpu.make_async_remote_copy(
            src_ref=sent, dst_ref=sent, send_sem=rs_send.at[n], recv_sem=rs_recv.at[n, 0],
            device_id=x_peer, device_id_type=MESH_ID,
        ).wait_send()
    for k in range(5):
        aux_copy(k).wait_send()
    whole = part_own.at[pl.ds(0, 128)]
    final_with(whole, whole, 18).wait_send()
    finals = attn_t.at[pl.ds(128, 128)]
    final_with(finals, finals, 19).wait_recv()
    for i in range(4):
        dst = (o_out, o_query, o_key, o_value)[i]
        rows, _ = final_rows(8 + 2 * i, b)
        dst[:, pl.ds(own_cols, HALF_D)] = part_own[rows, 512:]
        dst[:, pl.ds(oth_cols, HALF_D)] = attn_t[128 + 32 * i : 160 + 32 * i, :]
        hand_over(5 + i).start()
    for i in range(15):
        hand_over(i).wait()


def finish_kernel(*refs):
    count = len(refs) // 3
    sems = refs[-1]
    gets = [
        pltpu.make_async_copy(refs[i], refs[2 * count + i], sems.at[i]) for i in range(count)
    ]
    puts = [
        pltpu.make_async_copy(refs[2 * count + i], refs[count + i], sems.at[i])
        for i in range(count)
    ]
    for copy in gets:
        copy.start()
    for get, put in zip(gets, puts):
        get.wait()
        put.start()
    for copy in puts:
        copy.wait()


def layer_on_device(
    tokens, doc_lengths, w_query, w_key, w_value, w_out, w_up, w_down, bias_up, bias_down,
    gain_pre_attn, gain_post_attn, gain_pre_mlp, gain_post_mlp, cotangent,
):
    def v16(*shape):
        return pltpu.VMEM(shape, BF16)

    def v32(*shape):
        return pltpu.VMEM(shape, F32)

    dma = pltpu.SemaphoreType.DMA
    vmem = pl.BlockSpec(memory_space=pltpu.VMEM)
    hbm = pl.BlockSpec(memory_space=pltpu.HBM)
    shapes = [((TOK, D), BF16)] * 2 + [((2, TOK), F32), ((32, FF), F32), ((D, 128), F32)]
    shapes += [((32, D), F32)] * 4 + [((128,), F32)] + [((32,), F32)] * 5
    shapes = [jax.ShapeDtypeStruct(*shape) for shape in shapes]
    scratch = [pltpu.VMEM(shape.shape, shape.dtype) for shape in shapes] + [dma((15,))]
    scratch += [
        v16(1024, 512), v16(1024, 512), v16(1024, 512), v16(1024, 1024),
        v16(1024, 2048), v16(2048, 1024),
        v16(512, 1024),
        v16(512, 512), v16(512, 512), v16(512, 512), v16(512, 512), v16(512, 512),
        v16(512, 512), v32(512, 512), v16(512, 512),
        v32(256, 1024), v32(256, 1024), v16(512, 1024),
        v16(512, 2048), v16(2048, 512),
        v16(256, 1024), v16(256, 1024), v32(256, 1024), v16(256, 1024),
        v16(1024, 512),
        v32(2, 32, 512), v32(8, 512), v32(2, 256, 128),
        v16(1024, 2048), v16(512, 2048), v16(256, 2048), v16(128, 2048), v16(64, 2048),
        v16(512, 1024), v16(256, 1024), v16(128, 1024), v16(512, 1024), v16(1024, 512),
        v16(512, 2048), v16(256, 2048), v16(128, 2048), v16(64, 2048),
        v32(1, 16, 1024), v32(5, 16, 1024),
        dma((6,)), dma((2,)), dma((2,)), dma((20,)), dma((20,)), dma((16,)), dma((16, 5)), dma((5,)), dma((5,)),
    ]
    results = pl.pallas_call(
        layer_kernel,
        out_shape=shapes,
        in_specs=[pl.BlockSpec(memory_space=pltpu.SMEM)]
        + [vmem] * 8
        + [pl.BlockSpec(memory_space=pl.ANY)] * 6,
        out_specs=[hbm] * 15,
        scratch_shapes=scratch,
        compiler_params=pltpu.CompilerParams(
            collective_id=0, has_side_effects=True, vmem_limit_bytes=VMEM_BYTES
        ),
    )(
        doc_lengths, tokens, cotangent,
        gain_pre_attn[None], gain_post_attn[None], gain_pre_mlp[None], gain_post_mlp[None],
        bias_up.reshape(32, 128), bias_down[None],
        w_query, w_key, w_value, w_out, w_up, w_down,
    )
    out, grad_tok, rms, gd, gu, go, gq, gk, gv, small_up, small_down, sa, sb, sc, sd = pl.pallas_call(
        finish_kernel,
        out_shape=shapes,
        in_specs=[hbm] * 15,
        out_specs=[hbm] * 15,
        scratch_shapes=[pltpu.VMEM(s.shape, s.dtype) for s in shapes] + [dma((15,))],
    )(*results)
    return (
        out, grad_tok, gq.T, gk.T, gv.T, go.T, gu, gd.T, small_up, small_down, sa, sb, sc, sd, rms
    )


def solution(mesh):
    placed = (
        P(("dp", "blk"), None),
        P("dp", None),
        P(),
        P(),
        P(),
        P(),
        P(),
        P(),
        P(),
        P(),
        P(),
        P(),
        P(),
        P(),
        P(("dp", "blk"), None),
    )
    paired = mesh.shape["blk"] == 2 and mesh.shape["dp"] == 16
    return jax.shard_map(
        layer_on_device if paired else on_device,
        mesh=mesh,
        in_specs=placed,
        out_specs=(
            P(("dp", "blk"), None),
            P(("dp", "blk"), None),
            P(None, ("dp", "blk")),
            P(None, ("dp", "blk")),
            P(None, ("dp", "blk")),
            P(None, ("dp", "blk")),
            P(None, ("dp", "blk")),
            P(None, ("dp", "blk")),
            P(("dp", "blk")),
            P(("dp", "blk")),
            P(("dp", "blk")),
            P(("dp", "blk")),
            P(("dp", "blk")),
            P(("dp", "blk")),
            P(None, ("dp", "blk")),
        ),
        check_vma=False,
    )
```

```python
import math

import jax
import jax.numpy as jnp
from jax import lax
from jax.experimental import pallas as pl
from jax.experimental.pallas import tpu as pltpu
from jax.sharding import PartitionSpec as P

D = 1024
H = 16
HD = 64


eps = 1e-06
neg_big = -1e30


def rms_norm(values, gain_row):
    return values * lax.rsqrt(jnp.mean(values * values, axis=-1, keepdims=True) + eps) * gain_row


def rotate(head_rows, position):
    half_size = head_rows.shape[-1] // 2
    frequency = 10000.0 ** (-2.0 * jnp.arange(half_size, dtype=jnp.float32) / head_rows.shape[-1])
    angles = position.astype(jnp.float32)[:, None] * frequency[None, :]
    cosine = jnp.cos(angles)[:, None, :]
    sine_part = jnp.sin(angles)[:, None, :]
    low_half = head_rows[..., :half_size]
    high_half = head_rows[..., half_size:]
    return jnp.concatenate(
        [low_half * cosine - high_half * sine_part, low_half * sine_part + high_half * cosine],
        axis=-1,
    )


def doc_layout(lengths, total_rows):
    index_row = jnp.arange(total_rows, dtype=jnp.int32)
    doc_ends = jnp.stack(
        [
            lengths[0],
            lengths[0] + lengths[1],
            lengths[0] + lengths[1] + lengths[2],
            lengths[0] + lengths[1] + lengths[2] + lengths[3],
        ]
    )
    segment = jnp.sum((index_row[:, None] >= doc_ends[None, :3]).astype(jnp.int32), axis=1)
    starts = doc_ends - lengths
    matches = segment[:, None] == jnp.arange(4, dtype=jnp.int32)[None, :]
    return (index_row, jnp.sum(jnp.where(matches, starts[None, :], 0), axis=1))


def block_mask(query_index, query_start, key_first, width):
    key_index = key_first + jnp.arange(width, dtype=jnp.int32)
    return (key_index[None, :] <= query_index[:, None]) & (
        key_index[None, :] >= query_start[:, None]
    )


def on_device(
    tokens,
    doc_lengths,
    w_query,
    w_key,
    w_value,
    w_out,
    w_up,
    w_down,
    bias_up,
    bias_down,
    gain_pre_attn,
    gain_post_attn,
    gain_pre_mlp,
    gain_post_mlp,
    cotangent,
):
    row_count = tokens.shape[0]
    cycle_size = lax.axis_size("blk")
    group_rows = row_count * cycle_size
    first_row = lax.axis_index("blk") * row_count
    index_all, start_all = doc_layout(doc_lengths[0], group_rows)
    query_index = lax.dynamic_slice_in_dim(index_all, first_row, row_count)
    query_start = lax.dynamic_slice_in_dim(start_all, first_row, row_count)
    position = query_index - query_start
    query_last = first_row + row_count - 1
    start_least = jnp.min(query_start)
    scale = HD ** (-0.5)
    tokens_f = tokens.astype(jnp.float32)
    normed_in, back_pre_attn = jax.vjp(rms_norm, tokens_f, gain_pre_attn)
    attn_in = normed_in.astype(jnp.bfloat16)
    query_pre = jnp.dot(attn_in, w_query, preferred_element_type=jnp.float32)
    key_pre = jnp.dot(attn_in, w_key, preferred_element_type=jnp.float32)
    value_pre = jnp.dot(attn_in, w_value, preferred_element_type=jnp.float32)
    queries, back_rot_query = jax.vjp(
        lambda arr: rotate(arr, position), query_pre.reshape(row_count, H, HD)
    )
    keys_rot, back_rot_key = jax.vjp(
        lambda arr: rotate(arr, position), key_pre.reshape(row_count, H, HD)
    )
    queries_low = queries.astype(jnp.bfloat16)
    keys_low = keys_rot.reshape(row_count, D).astype(jnp.bfloat16)
    values_low = value_pre.astype(jnp.bfloat16)
    initial = (
        jnp.full((H, row_count), neg_big, jnp.float32),
        jnp.zeros((H, row_count), jnp.float32),
        jnp.zeros((row_count, H, HD), jnp.float32),
    )
    key_piece = lax.all_gather(keys_low, "blk", axis=0, tiled=True)
    value_piece = lax.all_gather(values_low, "blk", axis=0, tiled=True)
    piece_rows = key_piece.shape[0]
    fold_width = math.gcd(piece_rows, 512)

    def one_block(state, number):
        key_first = number * fold_width

        def one_compute(state):
            running_top, totals, accum = state
            keys_blk = lax.dynamic_slice_in_dim(
                key_piece, number * fold_width, fold_width, 0
            ).reshape(fold_width, H, HD)
            values_blk = lax.dynamic_slice_in_dim(
                value_piece, number * fold_width, fold_width, 0
            ).reshape(fold_width, H, HD)
            scores = (
                jnp.einsum(
                    "qhd,khd->hqk", queries_low, keys_blk, preferred_element_type=jnp.float32
                )
                * scale
            )
            allowed = block_mask(query_index, query_start, key_first, fold_width)[None]
            scores = jnp.where(allowed, scores, neg_big)
            new_top = jnp.maximum(running_top, jnp.max(scores, axis=-1))
            weights = jnp.where(allowed, jnp.exp(scores - new_top[..., None]), 0.0)
            factor = jnp.exp(running_top - new_top)
            totals = totals * factor + jnp.sum(weights, axis=-1)
            accum = accum * jnp.transpose(factor)[:, :, None] + jnp.einsum(
                "hqk,khd->qhd",
                weights.astype(jnp.bfloat16),
                values_blk,
                preferred_element_type=jnp.float32,
            )
            return (new_top, totals, accum)

        active = (key_first <= query_last) & (key_first + fold_width - 1 >= start_least)
        return (lax.cond(active, one_compute, lambda state: state, state), None)

    result, unused = lax.scan(
        one_block, initial, jnp.arange(piece_rows // fold_width, dtype=jnp.int32)
    )
    running_top, totals, accum = result
    attn_full = accum / jnp.transpose(totals)[:, :, None]
    log_total = running_top + jnp.log(totals)
    attn_low = attn_full.reshape(row_count, D).astype(jnp.bfloat16)
    branch_attn = jnp.dot(attn_low, w_out, preferred_element_type=jnp.float32)
    post_attn, back_post_attn = jax.vjp(rms_norm, branch_attn, gain_post_attn)
    hidden_res = tokens_f + post_attn
    normed_mlp, back_pre_mlp = jax.vjp(rms_norm, hidden_res, gain_pre_mlp)
    mlp_in = normed_mlp.astype(jnp.bfloat16)
    pre_act = jnp.dot(mlp_in, w_up, preferred_element_type=jnp.float32) + bias_up
    activated, back_gelu = jax.vjp(lambda arr: jax.nn.gelu(arr, approximate=True), pre_act)
    act_low = activated.astype(jnp.bfloat16)
    branch_mlp = jnp.dot(act_low, w_down, preferred_element_type=jnp.float32) + bias_down
    post_mlp, back_post_mlp = jax.vjp(rms_norm, branch_mlp, gain_post_mlp)
    output = (hidden_res + post_mlp).astype(jnp.bfloat16)
    branch_rms = jnp.stack(
        [
            jnp.sqrt(jnp.mean(branch_attn * branch_attn, axis=-1) + eps),
            jnp.sqrt(jnp.mean(branch_mlp * branch_mlp, axis=-1) + eps),
        ]
    )
    grad_out_f = cotangent.astype(jnp.float32)
    grad_branch_mlp, grad_gain_post_mlp = back_post_mlp(grad_out_f)
    grad_mlp_low = grad_branch_mlp.astype(jnp.bfloat16)
    grad_bias_down = jnp.sum(grad_mlp_low.astype(jnp.float32), axis=0)
    grad_down = jnp.einsum("tf,td->df", act_low, grad_mlp_low, preferred_element_type=jnp.float32)
    grad_act = jnp.einsum("td,fd->tf", grad_mlp_low, w_down, preferred_element_type=jnp.float32)
    (grad_pre_act,) = back_gelu(grad_act)
    grad_pre_low = grad_pre_act.astype(jnp.bfloat16)
    grad_bias_up = jnp.sum(grad_pre_low.astype(jnp.float32), axis=0)
    grad_up = jnp.einsum("td,tf->fd", mlp_in, grad_pre_low, preferred_element_type=jnp.float32)
    grad_normed_mlp = jnp.einsum(
        "tf,df->td", grad_pre_low, w_up, preferred_element_type=jnp.float32
    )
    grad_res_part, grad_gain_pre_mlp = back_pre_mlp(grad_normed_mlp)
    grad_hidden = grad_out_f + grad_res_part
    grad_branch_attn, grad_gain_post_attn = back_post_attn(grad_hidden)
    grad_branch_low = grad_branch_attn.astype(jnp.bfloat16)
    grad_w_out = jnp.einsum(
        "td,te->ed", attn_low, grad_branch_low, preferred_element_type=jnp.float32
    )
    grad_attn = jnp.einsum("te,de->td", grad_branch_low, w_out, preferred_element_type=jnp.float32)
    grad_attn_low = grad_attn.astype(jnp.bfloat16).reshape(row_count, H, HD)
    delta = jnp.einsum("qhd,qhd->hq", grad_attn_low.astype(jnp.float32), attn_full)
    key_source, value_source = key_piece, value_piece
    width = math.gcd(group_rows, 512)

    def back_block(grad_query_acc, number):
        key_first = number * width

        def back_compute(grad_query_acc):
            keys_blk = lax.dynamic_slice_in_dim(key_source, key_first, width, 0).reshape(
                width, H, HD
            )
            values_blk = lax.dynamic_slice_in_dim(value_source, key_first, width, 0).reshape(
                width, H, HD
            )
            scores = (
                jnp.einsum(
                    "qhd,khd->hqk", queries_low, keys_blk, preferred_element_type=jnp.float32
                )
                * scale
            )
            allowed = block_mask(query_index, query_start, key_first, width)[None]
            probs = jnp.where(allowed, jnp.exp(scores - log_total[..., None]), 0.0)
            grad_probs = jnp.einsum(
                "qhd,khd->hqk", grad_attn_low, values_blk, preferred_element_type=jnp.float32
            )
            grad_scores = (probs * (grad_probs - delta[..., None])).astype(jnp.bfloat16)
            grad_query_acc = (
                grad_query_acc
                + jnp.einsum(
                    "hqk,khd->qhd", grad_scores, keys_blk, preferred_element_type=jnp.float32
                )
                * scale
            )
            grad_keys_blk = (
                jnp.einsum(
                    "hqk,qhd->khd", grad_scores, queries_low, preferred_element_type=jnp.float32
                )
                * scale
            )
            grad_values_blk = jnp.einsum(
                "hqk,qhd->khd",
                probs.astype(jnp.bfloat16),
                grad_attn_low,
                preferred_element_type=jnp.float32,
            )
            return (
                grad_query_acc,
                (grad_keys_blk.reshape(width, D), grad_values_blk.reshape(width, D)),
            )

        def skipped(grad_query_acc):
            return (
                grad_query_acc,
                (jnp.zeros((width, D), jnp.float32), jnp.zeros((width, D), jnp.float32)),
            )

        active = (key_first <= query_last) & (key_first + width - 1 >= start_least)
        return lax.cond(active, back_compute, skipped, grad_query_acc)

    grad_query_acc, stacked = lax.scan(
        back_block,
        jnp.zeros((row_count, H, HD), jnp.float32),
        jnp.arange(group_rows // width, dtype=jnp.int32),
    )
    grad_keys_all = stacked[0].reshape(group_rows, D)
    grad_values_all = stacked[1].reshape(group_rows, D)
    grad_keys_mine, grad_values_mine = (
        lax.psum_scatter(
            grad_keys_all.astype(jnp.bfloat16), "blk", scatter_dimension=0, tiled=True
        ).astype(jnp.float32),
        lax.psum_scatter(
            grad_values_all.astype(jnp.bfloat16), "blk", scatter_dimension=0, tiled=True
        ).astype(jnp.float32),
    )
    (grad_key_pre,) = back_rot_key(grad_keys_mine.reshape(row_count, H, HD))
    (grad_query_pre,) = back_rot_query(grad_query_acc)
    grad_key_low = grad_key_pre.reshape(row_count, D).astype(jnp.bfloat16)
    grad_query_low = grad_query_pre.reshape(row_count, D).astype(jnp.bfloat16)
    grad_value_low = grad_values_mine.astype(jnp.bfloat16)
    grad_query = jnp.einsum(
        "td,te->ed", attn_in, grad_query_low, preferred_element_type=jnp.float32
    )
    grad_key = jnp.einsum("td,te->ed", attn_in, grad_key_low, preferred_element_type=jnp.float32)
    grad_value = jnp.einsum(
        "td,te->ed", attn_in, grad_value_low, preferred_element_type=jnp.float32
    )
    grad_normed_in = (
        jnp.einsum("te,de->td", grad_query_low, w_query, preferred_element_type=jnp.float32)
        + jnp.einsum("te,de->td", grad_key_low, w_key, preferred_element_type=jnp.float32)
        + jnp.einsum("te,de->td", grad_value_low, w_value, preferred_element_type=jnp.float32)
    )
    grad_tokens_part, grad_gain_pre_attn = back_pre_attn(grad_normed_in)
    grad_tokens = (grad_hidden + grad_tokens_part).astype(jnp.bfloat16)
    count = lax.axis_size(("dp", "blk"))
    low = jnp.bfloat16
    pieces = [
        part.astype(low).reshape(count, -1, D)
        for part in (grad_query, grad_key, grad_value, grad_w_out, grad_up, grad_down)
    ]
    small = [
        part.reshape(count, -1)
        for part in (
            grad_bias_up,
            grad_bias_down,
            grad_gain_pre_attn,
            grad_gain_post_attn,
            grad_gain_pre_mlp,
            grad_gain_post_mlp,
        )
    ]
    sizes = [part.shape[1] for part in pieces]
    summed = lax.psum_scatter(
        jnp.concatenate(pieces, axis=1), ("dp", "blk"), scatter_dimension=0
    ).astype(jnp.float32)
    small_sizes = [part.shape[1] for part in small]
    small_flat = jnp.concatenate(small, axis=1)
    padding = -small_flat.shape[1] % 128
    small_flat = jnp.pad(small_flat, ((0, 0), (0, padding)))
    small_summed = lax.psum_scatter(small_flat, ("dp", "blk"), scatter_dimension=0)
    cuts = [sum(sizes[: i + 1]) for i in range(len(sizes) - 1)]
    parts = jnp.split(summed, cuts, axis=0)
    parts[5] = parts[5].reshape(D // count, -1)
    small_cuts = [sum(small_sizes[: i + 1]) for i in range(len(small_sizes))]
    small_parts = jnp.split(small_summed, small_cuts, axis=0)[:6]
    return (output, grad_tokens, *[part.T for part in parts], *small_parts, branch_rms)


MESH_ID = pl.DeviceIdType.MESH
F32 = jnp.float32
BF16 = jnp.bfloat16
TOK = 256
PACK = 512
FF = 4096
HALF_FF = 2048
HALF_D = 512
CHUNK = 128
VMEM_BYTES = 62 * 1024 * 1024
UNIT_ORDER = (
    "ywvx",
    "wvxy",
    "ywxv",
    "yxwv",
    "wyv",
    "ywv",
    "ywv",
    "ywv",
    "yxwv",
    "yxwv",
    "wxyv",
    "xywv",
    "xywv",
    "xwyv",
    "xywv",
    "xwyv",
)
SLOTS = (
    (0, 1, 10, 11,),
    (),
    (),
    (20,),
    (2, 12,),
    (),
    (21,),
    (),
    (3, 13,),
    (30,),
    (4, 22,),
    (),
    (31,),
    (110,),
    (14, 100, 23,),
    (40, 50, 111, 5, 32,),
    (24, 112,),
    (41, 33, 160, 102, 15, 101, 42, 52, 113, 6, 114, 51, 43, 16, 103, 60, 44, 34, 61, 115, 120, 53, 54, 25, 45, 70, 161, 62, 121, 35, 104, 116, 63, 130, 55, 122, 72, 131, 26, 123, 71, 162, 64, 105, 140, 36,),
    (132, 80, 124, 141, 133, 81, 73, 150, 163, 74, 65, 106, 90, 142, 82, 134, 143, 125, 151, 83, 152, 164, 75, 92, 126, 84, 91, 144, 135, 153, 154, 85, 145, 93, 94, 136, 155, 86, 146, 95, 156, 96,),
)


def mm(a, b):
    return jnp.dot(a, b, preferred_element_type=F32)


def mm_nt(a, b):
    return lax.dot_general(a, b, (((1,), (1,)), ((), ())), preferred_element_type=F32)


def al(offset, step):
    return pl.multiple_of(offset, step)


def norm_back(v, r, gain, grad):
    scaled = grad * gain
    inner = jnp.mean(v * scaled, axis=-1, keepdims=True)
    return r * scaled - v * (r * r * r * inner), jnp.sum(grad * v * r, axis=0, keepdims=True)


def inv_rms(v):
    return lax.rsqrt(jnp.mean(v * v, axis=-1, keepdims=True) + eps)


def layer_kernel(
    doc, tok, cot, gain_a, gain_b, gain_c, gain_d, bias_up, bias_down,
    wq_hbm, wk_hbm, wv_hbm, wo_hbm, wu_hbm, wd_hbm,
    *refs,
):
    results, refs = refs[:15], refs[15:]
    (
        out, grad_tok, rms, o_down, o_up, o_out, o_query, o_key, o_value,
        small_up, small_down, small_a, small_b, small_c, small_d, o_sem,
        wq, wk, wv, wo, wu, wd, xin, q_t, k_t, v_t, k_n, v_n, mask, attn_t, attn_nat,
        branch, hid, xm, act, g_t, part_send, part_recv, part_own, nat, gb_t,
        rope, lse, stat, s_down, r1_down, r2_down, r3_down, r4_down, r1_up, r2_up, r3_up, xm_m, pre_m,
        r1_late, r2_late, r3_late, r4_late, aux_s, aux_r,
        w_sem, m_send, m_recv, c_send, c_recv, rs_send, rs_recv, a_send, a_recv,
    ) = refs
    held = (
        out, grad_tok, rms, o_down, o_up, o_out, o_query, o_key, o_value,
        small_up, small_down, small_a, small_b, small_c, small_d,
    )

    def hand_over(i):
        return pltpu.make_async_copy(held[i], results[i], o_sem.at[i])

    dp = lax.axis_index("dp")
    b = lax.axis_index("blk")
    x = lax.rem(dp, 2)
    y = lax.rem(dp // 2, 2)
    z = dp // 4
    other = 1 - b
    core_peer = (dp, other)
    x_peer = (dp + 1 - 2 * x, b)
    y_peer = (dp + 2 - 4 * y, b)

    z_low = (dp + 4 - 8 * lax.rem(z, 2), b)
    z_high = (dp + 8 - 16 * (z // 2), b)
    barrier = pltpu.get_barrier_semaphore()
    for peer in (core_peer, x_peer, y_peer, z_low, z_high):
        pl.semaphore_signal(barrier, inc=1, device_id=peer, device_id_type=MESH_ID)

    own_cols = al(b * HALF_D, HALF_D)
    oth_cols = al(other * HALF_D, HALF_D)
    own_tok = al(b * TOK, TOK)
    oth_tok = al(other * TOK, TOK)

    w_copies = [
        pltpu.make_async_copy(src.at[:, pl.ds(own_cols, HALF_D)], dst, w_sem.at[i])
        for i, (src, dst) in enumerate(((wq_hbm, wq), (wk_hbm, wk), (wv_hbm, wv)))
    ]
    w_copies.append(pltpu.make_async_copy(wo_hbm, wo, w_sem.at[3]))
    for copy in w_copies:
        copy.start()

    def up_copy(j):
        return pltpu.make_async_copy(
            wu_hbm.at[:, pl.ds(al((2 * j + b) * 128, 128), 128)],
            wu.at[:, pl.ds(al(j * 128, 128), 128)],
            w_sem.at[4],
        )

    def down_copy(j):
        return pltpu.make_async_copy(
            wd_hbm.at[pl.ds(al((2 * j + b) * 128, 128), 128)],
            wd.at[pl.ds(al(j * 128, 128), 128)],
            w_sem.at[5],
        )

    def to_core(k, src, dst):
        return pltpu.make_async_remote_copy(
            src_ref=src, dst_ref=dst, send_sem=c_send.at[k], recv_sem=c_recv.at[k],
            device_id=core_peer, device_id_type=MESH_ID,
        )

    end_a = doc[0, 0]
    end_b = end_a + doc[0, 1]
    end_c = end_b + doc[0, 2]
    index_row = lax.broadcasted_iota(jnp.int32, (1, PACK), 1)
    start_row = jnp.where(
        index_row >= end_c,
        end_c,
        jnp.where(index_row >= end_b, end_b, jnp.where(index_row >= end_a, end_a, 0)),
    )
    position = (index_row - start_row).astype(F32)
    freq = jnp.exp(
        lax.broadcasted_iota(jnp.int32, (32, PACK), 0).astype(F32) * (-math.log(10000.0) / 32.0)
    )
    angle = position * freq
    rope[0] = jnp.cos(angle)
    rope[1] = jnp.sin(angle)

    def fill_mask(i, carry):
        rows = pl.ds(al(i * 64, 64), 64)
        key_index = lax.broadcasted_iota(jnp.int32, (64, PACK), 0) + i * 64
        query_index = lax.broadcasted_iota(jnp.int32, (64, PACK), 1)
        allowed = (key_index <= query_index) & (key_index >= start_row)
        mask[rows, :] = jnp.where(allowed, 0.0, neg_big)
        return carry

    lax.fori_loop(0, 8, fill_mask, 0)

    def pre_attn(i, carry):
        rows = pl.ds(al(i * CHUNK, CHUNK), CHUNK)
        v = tok[rows, :].astype(F32)
        xin[pl.ds(al(own_tok + i * CHUNK, CHUNK), CHUNK), :] = (
            v * inv_rms(v) * gain_a[...]
        ).astype(BF16)
        return carry

    lax.fori_loop(0, TOK // CHUNK, pre_attn, 0)
    pl.semaphore_wait(barrier, 5)
    own_rows = xin.at[pl.ds(own_tok, TOK)]
    xin_copy = to_core(0, own_rows, own_rows)
    xin_copy.start()
    lax.fori_loop(0, 16, lambda j, c: (up_copy(j).start(), c)[1], 0)
    lax.fori_loop(0, 16, lambda j, c: (down_copy(j).start(), c)[1], 0)

    attn_oth = nat.at[:, pl.ds(0, PACK)]

    def project(tok_at):
        rows = pl.ds(tok_at, TOK)
        cos = rope[0, :, rows]
        sin = rope[1, :, rows]
        x_rows = xin[rows, :]

        def turned(w, scale):
            flat = mm(x_rows, w[...]).T.reshape(8, 2, 32, TOK)
            low, high = flat[:, 0], flat[:, 1]
            both = jnp.stack([low * cos - high * sin, low * sin + high * cos], axis=1)
            return (both * scale).reshape(HALF_D, TOK).astype(BF16)

        q_t[:, rows] = turned(wq, 0.125)
        keys = turned(wk, 1.0)
        k_t[:, rows] = keys
        k_n[rows, :] = keys.T
        values = mm(x_rows, wv[...]).astype(BF16)
        v_n[rows, :] = values
        v_t[:, rows] = values.T

    for copy in w_copies[:3]:
        copy.wait()
    project(own_tok)
    xin_copy.wait()
    project(oth_tok)

    zeros = jnp.zeros((64, TOK), BF16)

    def slab(head_rows, which):
        return jnp.concatenate([head_rows, zeros] if which == 0 else [zeros, head_rows], axis=0)

    def attend(i, carry):
        pairs = [2 * i, 2 * i + 1]
        slabs = [pl.ds(al(p * 128, 128), 128) for p in pairs]
        parts = [
            (
                w, pl.ds(al(pairs[e] * 128 + w * 64, 64), 64),
                slice(block * TOK, block * TOK + TOK), (block + 1) * TOK, e,
            )
            for e in (0, 1)
            for block in (1, 0)
            for w in (0, 1)
        ]
        scores = [
            mm(k_n[:keys, slabs[e]], slab(q_t[rows, cols], w)) + mask[:keys, cols]
            for w, rows, cols, keys, e in parts
        ]
        tops = [jnp.max(score, axis=0, keepdims=True) for score in scores]
        weights = [jnp.exp(score - top) for score, top in zip(scores, tops)]
        totals = [jnp.sum(weight, axis=0, keepdims=True) for weight in weights]
        for (w, rows, cols, keys, e), weight, top, total in zip(parts, weights, tops, totals):
            attn_t[rows, cols] = mm(v_t[rows, :keys], weight.astype(BF16)) * (1.0 / total)
            lse[pl.ds(pairs[e] * 2 + w, 1), cols] = top + jnp.log(total)
        for p, slab_cols in zip(pairs, slabs):
            attn_nat[:, slab_cols] = attn_t[pl.ds(al(p * 128, 128), 128), :].T.astype(BF16)
            to_core(
                1 + p, attn_nat.at[pl.ds(oth_tok, TOK), slab_cols], attn_oth.at[:, slab_cols]
            ).start()
        return carry

    lax.fori_loop(0, 2, attend, 0)

    w_copies[3].wait()
    branch[...] = mm(attn_nat[pl.ds(own_tok, TOK), :], wo[pl.ds(own_cols, HALF_D), :])

    def attn_copy(p):
        cols = pl.ds(al(p * 128, 128), 128)
        return to_core(1 + p, attn_nat.at[pl.ds(oth_tok, TOK), cols], attn_oth.at[:, cols])

    lax.fori_loop(0, 4, lambda p, c: (attn_copy(p).wait(), c)[1], 0)
    branch[...] += mm(attn_oth[...], wo[pl.ds(oth_cols, HALF_D), :])

    def post_attn(i, carry):
        rows = pl.ds(al(i * CHUNK, CHUNK), CHUNK)
        v = branch[rows, :]
        square = jnp.mean(v * v, axis=-1, keepdims=True) + eps
        stat[0, rows, :] = jnp.broadcast_to(jnp.sqrt(square), (CHUNK, 128))
        h = tok[rows, :].astype(F32) + v * lax.rsqrt(square) * gain_b[...]
        hid[rows, :] = h
        xm[pl.ds(al(own_tok + i * CHUNK, CHUNK), CHUNK), :] = (
            h * inv_rms(h) * gain_c[...]
        ).astype(BF16)
        return carry

    lax.fori_loop(0, TOK // CHUNK, post_attn, 0)
    own_rows_m = xm.at[pl.ds(own_tok, TOK)]
    xm_copy = to_core(5, own_rows_m, own_rows_m)
    xm_copy.start()
    xm_mate = pltpu.make_async_remote_copy(
        src_ref=own_rows_m, dst_ref=xm_m.at[pl.ds(own_tok, TOK)], send_sem=m_send.at[1],
        recv_sem=m_recv.at[1], device_id=x_peer, device_id_type=MESH_ID,
    )
    xm_mate.start()

    def up_step(tok_at, i):
        cols = pl.ds(al(i * 1024, 1024), 1024)
        rows = pl.ds(tok_at, TOK)
        bias = jnp.concatenate(
            [bias_up[pl.ds(16 * i + 2 * j + b, 1), :] for j in range(8)], axis=1
        )
        pre = mm(xm[rows, :], wu[:, cols]) + bias
        square = pre * pre
        th = jnp.tanh(pre * (0.7978845608 + (0.7978845608 * 0.044715) * square))
        half = 0.5 + 0.5 * th
        act[rows, cols] = (pre * half).astype(BF16)
        slope = half + pre * (0.5 - 0.5 * th * th) * (
            0.7978845608 + (0.7978845608 * 0.134145) * square
        )
        g_t[cols, rows] = slope.astype(BF16).T

    pltpu.make_async_copy(wu_hbm.at[:, pl.ds(0, HALF_FF)], wu, w_sem.at[4]).wait()
    lax.fori_loop(0, 2, lambda i, c: (up_step(own_tok, i), c)[1], 0)
    xm_copy.wait()
    lax.fori_loop(0, 2, lambda i, c: (up_step(oth_tok, i), c)[1], 0)
    pltpu.make_async_copy(wd_hbm.at[pl.ds(0, HALF_FF)], wd, w_sem.at[5]).wait()

    def down_step(tok_at, dst, i):
        cols = slice(i * 512, i * 512 + 512)
        dst[:, cols] = mm(act[pl.ds(tok_at, TOK), :], wd[:, cols]).astype(dst.dtype)

    mlp_copies = [
        to_core(k, part_send.at[:, pl.ds(i * 512, 512)], part_recv.at[:, pl.ds(i * 512, 512)])
        for i, k in ((0, 6), (1, 15))
    ]
    for i in range(2):
        down_step(oth_tok, part_send, i)
        mlp_copies[i].start()
    for i in range(2):
        down_step(own_tok, part_own, i)
    for copy in mlp_copies:
        copy.wait()
    def post_mlp(i, carry):
        sum_bias, sum_gain = carry
        rows = pl.ds(al(i * CHUNK, CHUNK), CHUNK)
        v = part_own[rows, :] + part_recv[rows, :].astype(F32) + bias_down[...]
        square = jnp.mean(v * v, axis=-1, keepdims=True) + eps
        stat[1, rows, :] = jnp.broadcast_to(jnp.sqrt(square), (CHUNK, 128))
        r = lax.rsqrt(square)
        out[rows, :] = (hid[rows, :] + v * r * gain_d[...]).astype(BF16)
        back, gain_part = norm_back(v, r, gain_d[...], cot[rows, :].astype(F32))
        back = back.astype(BF16)
        nat[rows, :] = back
        return (
            sum_bias + jnp.sum(back.astype(F32), axis=0, keepdims=True),
            sum_gain + gain_part,
        )

    def turn_and_send(dst, i, k):
        tok_cols = pl.ds(al(own_tok + i * CHUNK, CHUNK), CHUNK)
        for j in range(4):
            cols = slice(j * 256, j * 256 + 256)
            dst[cols, tok_cols] = nat[i * CHUNK : i * CHUNK + CHUNK, cols].T
        part = dst.at[:, tok_cols]
        copy = to_core(k, part, part)
        copy.start()
        return copy

    zero_row = jnp.zeros((1, D), F32)
    sums = (zero_row, zero_row)
    gb_copies = []
    for i, k in ((0, 7), (1, 16)):
        sums = post_mlp(i, sums)
        gb_copies.append(turn_and_send(gb_t, i, k))
    sum_bias_down, sum_gain_d = sums
    aux_s[0] = jnp.zeros((16, D), F32)
    aux_s[0, 0:1, :] = sum_bias_down
    aux_s[0, 4:5, :] = sum_gain_d
    for i in range(2):
        rms[i : i + 1, :] = stat[i].T[0:1, :]
    hand_over(0).start()
    hand_over(2).start()

    for copy in gb_copies:
        copy.wait()
    down_refs = (s_down, r1_down, r2_down, r3_down, r4_down)
    up_refs = (wd, r1_up, r2_up, r3_up)
    late_refs = (wu, r1_late, r2_late, r3_late, r4_late)
    units = (
        [(down_refs, 512 * i, 512, 64) for i in range(4)]
        + [(up_refs, 256 * i, 256, 128) for i in range(4)]
        + [(late_refs, 256 * i, 256, 64) for i in range(8)]
    )
    place = {
        "x": (x, 1, x_peer),
        "y": (y, 2, y_peer),
        "w": (lax.rem(z, 2), 4, z_low),
        "v": (z // 2, 8, z_high),
    }

    def unit_axes(n):
        return [place[letter] for letter in UNIT_ORDER[n]]

    def kept(n, steps):
        axes = unit_axes(n)
        step = 2 ** len(axes) // 2 * units[n][3]
        return sum((axis[0] * (step >> i) for i, axis in enumerate(axes[:steps])), 0)

    def unit_copy(n, k):
        refs, c0, width, rows = units[n]
        axes = unit_axes(n)
        span = 2 ** len(axes)
        cols = pl.ds(c0, width)
        if k < 2:
            bit, _, peer = axes[0]
            second = lax.rem(axes[1][0] + 1 + k, 2)
            count = span // 4 * rows
            src = refs[0].at[pl.ds(al(((1 - bit) * 2 + second) * count, count), count), cols]
            dst = refs[1].at[pl.ds(al(second * count, count), count), cols]
        else:
            bit, _, peer = axes[k - 1]
            count = (span >> k) * rows
            at = kept(n, k - 1) + (1 - bit) * count
            src = refs[0].at[pl.ds(al(at, count), count), cols]
            dst = refs[k].at[:, cols]
        return pltpu.make_async_remote_copy(
            src_ref=src, dst_ref=dst, send_sem=rs_send.at[n], recv_sem=rs_recv.at[n, k],
            device_id=peer, device_id_type=MESH_ID,
        )

    def add_rows(n, at, arrived, arrived_at, count):
        refs, c0, width, _ = units[n]
        cols = pl.ds(c0, width)

        def step(i, carry):
            to = pl.ds(al(at + i * 64, 64), 64)
            got = refs[arrived][pl.ds(al(arrived_at + i * 64, 64), 64), cols]
            refs[0][to, cols] = (refs[0][to, cols].astype(F32) + got.astype(F32)).astype(BF16)
            return carry

        lax.fori_loop(0, count // 64, step, 0)

    def serve(n, k):
        refs, c0, width, rows = units[n]
        axes = unit_axes(n)
        last = len(axes)
        span = 2**last
        unit_copy(n, k).wait_recv()
        if k < 2:
            second = lax.rem(axes[1][0] + 1 + k, 2)
            count = span // 4 * rows
            add_rows(n, kept(n, 1) + second * count, 1, second * count, count)
            if k == 0:
                unit_copy(n, 2).start()
        elif k < last:
            count = (span // 2 >> k) * rows
            bit = axes[k][0]
            add_rows(n, kept(n, k) + (1 - bit) * count, k, (1 - bit) * count, count)
            unit_copy(n, k + 1).start()
            add_rows(n, kept(n, k) + bit * count, k, bit * count, count)
        else:
            cols = pl.ds(c0, width)
            mine = refs[0][pl.ds(al(kept(n, last), rows), rows), cols].astype(F32)
            total = mine + refs[last][:, cols].astype(F32)
            if 4 <= n < 8:
                o_up[c0 : c0 + width, :] = total.T
            else:
                at, to = final_at(n)
                part_own[at : at + 64, to : to + width] = total
                final_copy(n).start()

    def final_at(n):
        return (64 * n, 0) if n < 4 else (64 * ((n - 8) // 2), 512 + 256 * (n % 2))

    def final_rows(n, half):
        at, to = final_at(n)
        return pl.ds(al(at + half * 32, 32), 32), pl.ds(to, units[n][2])

    def final_copy(n):
        at, to = (32 * n, 0) if n < 4 else (128 + 32 * ((n - 8) // 2), 256 * (n % 2))
        dst = attn_t.at[pl.ds(at, 32), pl.ds(to, units[n][2])]
        return final_with(part_own.at[final_rows(n, other)], dst, 18 if n < 4 else 19)

    def final_with(src, dst, k):
        return pltpu.make_async_remote_copy(
            src_ref=src, dst_ref=dst, send_sem=c_send.at[18], recv_sem=c_recv.at[k],
            device_id=core_peer, device_id_type=MESH_ID,
        )

    aux_peers = (core_peer, x_peer, y_peer, z_low, z_high)

    def aux_sum(k):
        return aux_s.at[0] if k == 0 else hid.at[pl.ds(16 * k, 16)]

    def aux_copy(k):
        return pltpu.make_async_remote_copy(
            src_ref=aux_sum(k), dst_ref=aux_r.at[k], send_sem=a_send.at[k],
            recv_sem=a_recv.at[k], device_id=aux_peers[k], device_id_type=MESH_ID,
        )

    def aux_end(k):
        aux_copy(k).wait_recv()
        aux_sum(k + 1)[...] = aux_sum(k)[...] + aux_r[k]
        if k < 4:
            aux_copy(k + 1).start()

    def slot(i):
        for code in SLOTS[i]:
            n, k = code // 10, code % 10
            if n == len(units):
                aux_end(k)
            elif k < 2:
                unit_copy(n, k).start()
            else:
                serve(n, k - 2)

    def weight_grad(n, first, last, *terms):
        refs, c0, width, rows = units[n]
        axes = unit_axes(n)
        fixed = x if len(axes) == 3 else 0
        tails = [0]
        for axis in axes[2:]:
            tails = [tail + p * axis[1] for tail in tails for p in range(2)]
        count = len(tails) * rows
        for g in range(first, last):
            i = lax.rem(axes[0][0] + 1 + g // 2, 2)
            j = lax.rem(axes[1][0] + 1 + g % 2, 2)
            base = i * axes[0][1] + j * axes[1][1] + fixed
            total = None
            for left, right in terms:
                stack = jnp.concatenate([left(base + tail) for tail in tails], axis=0)
                part = mm(stack, right)
                total = part if total is None else total + part
            at = pl.ds(al((i * 2 + j) * count, count), count)
            refs[0][at, pl.ds(c0, width)] = total.astype(BF16)

    def rows_of(ref, rows):
        return lambda chip: ref[pl.ds(al(chip * rows, rows), rows), :]

    for first in (0, 2):
        for n in range(4):
            weight_grad(
                n, first, first + 2, (rows_of(gb_t, 64), act[:, 512 * n : 512 * n + 512])
            )
        slot(first // 2)

    def mate_copy(k):
        return pltpu.make_async_remote_copy(
            src_ref=g_t.at[pl.ds(al((2 * k + 1 - x) * 128, 128), 128)],
            dst_ref=pre_m.at[pl.ds(al(k * 128, 128), 128)],
            send_sem=m_send.at[0], recv_sem=m_recv.at[0],
            device_id=x_peer, device_id_type=MESH_ID,
        )

    def act_back(i, carry):
        rows = pl.ds(al(i * 512, 512), 512)
        g_t[rows, :] = (mm(wd[rows, :], gb_t[...]) * g_t[rows, :].astype(F32)).astype(BF16)
        for j in range(2):
            mate_copy(2 * i + j).start()
        return carry

    lax.fori_loop(0, 4, act_back, 0)
    slot(2)

    def mlp_back(tok_at, dst, i):
        at = pl.ds(al(i * 512, 512), 512)
        dst[:, at] = mm(wu[at, :], g_t[:, pl.ds(tok_at, TOK)]).T.astype(dst.dtype)

    lax.fori_loop(0, 2, lambda i, c: (mlp_back(oth_tok, part_send, i), c)[1], 0)
    mlp_back_copy = to_core(8, part_send, part_recv)
    mlp_back_copy.start()
    slot(3)
    xm_mate.wait()
    mate_rows = xm_m.at[pl.ds(own_tok, TOK)]
    xm_pass = to_core(14, mate_rows, mate_rows)
    xm_pass.start()
    lax.fori_loop(0, 2, lambda i, c: (mlp_back(own_tok, part_own, i), c)[1], 0)
    ones = jnp.ones((16, PACK), BF16)
    for i in range(2):
        aux_s[0, pl.ds(8 + 2 * b + i, 1), :] = mm_nt(ones, g_t[i * 1024 : i * 1024 + 1024, :])[0:1]
    slot(4)
    mlp_back_copy.wait()

    gba_t = wd.at[pl.ds(D, D), pl.ds(0, PACK)]
    ga_t = wd.at[pl.ds(D, HALF_D), pl.ds(PACK, PACK)]

    def hidden_back(i, carry):
        sum_c, sum_b = carry
        rows = pl.ds(al(i * CHUNK, CHUNK), CHUNK)
        h = hid[rows, :]
        back, part_c = norm_back(
            h, inv_rms(h), gain_c[...], part_own[rows, :] + part_recv[rows, :].astype(F32)
        )
        g_hidden = cot[rows, :].astype(F32) + back
        hid[rows, :] = g_hidden
        v = branch[rows, :]
        back, part_b = norm_back(v, inv_rms(v), gain_b[...], g_hidden)
        nat[rows, :] = back.astype(BF16)
        return sum_c + part_c, sum_b + part_b

    sums = (zero_row, zero_row)
    gba_copies = []
    for i, k in ((0, 9), (1, 17)):
        sums = hidden_back(i, sums)
        gba_copies.append(turn_and_send(gba_t, i, k))
    sum_gain_c, sum_gain_b = sums
    aux_s[0, 3:4, :] = sum_gain_c
    aux_s[0, 2:3, :] = sum_gain_b
    slot(5)
    for copy in gba_copies:
        copy.wait()

    for n in (8, 9):
        weight_grad(
            n, 0, 4, (rows_of(gba_t, 64), attn_nat[:, 256 * (n - 8) : 256 * (n - 8) + 256])
        )
    slot(6)
    ga_t[...] = mm(wo[pl.ds(own_cols, HALF_D), :], gba_t[...]).astype(BF16)
    slot(7)

    def head_grad(off):
        def rows(chip):
            at = al(off + chip // 8 * HALF_D, HALF_D)
            return act[pl.ds(al(lax.rem(chip, 8) * 64, 64), 64), pl.ds(at, HALF_D)]

        return rows

    own_q = pl.ds(al(own_cols, HALF_D), HALF_D)
    own_k = pl.ds(al(D + own_cols, HALF_D), HALF_D)
    gv = gb_t

    def attend_back(p, carry):
        slab_cols = pl.ds(al(p * 128, 128), 128)
        parts = [
            (w, pl.ds(al(p * 128 + w * 64, 64), 64), slice(i * TOK, i * TOK + TOK), (i + 1) * TOK)
            for w in (0, 1)
            for i in (0, 1)
        ]
        deltas = [
            jnp.sum(ga_t[rows, cols].astype(F32) * attn_t[rows, cols], axis=0, keepdims=True)
            for w, rows, cols, keys in parts
        ]
        scores = [
            mm(k_n[:keys, slab_cols], slab(q_t[rows, cols], w)) + mask[:keys, cols]
            for w, rows, cols, keys in parts
        ]
        g_probs = [
            mm(v_n[:keys, slab_cols], slab(ga_t[rows, cols], w)) for w, rows, cols, keys in parts
        ]
        probs = [
            jnp.exp(score - lse[pl.ds(p * 2 + part[0], 1), part[2]])
            for score, part in zip(scores, parts)
        ]
        g_scores = [
            (prob * (g_prob - delta)).astype(BF16)
            for prob, g_prob, delta in zip(probs, g_probs, deltas)
        ]
        grads_q = [
            mm(k_t[rows, :keys], g_score) * 0.125
            for (w, rows, cols, keys), g_score in zip(parts, g_scores)
        ]
        grads_k = [
            mm_nt(q_t[rows, cols], g_score)
            for (w, rows, cols, keys), g_score in zip(parts, g_scores)
        ]
        grads_v = [
            mm_nt(ga_t[rows, cols], prob.astype(BF16))
            for (w, rows, cols, keys), prob in zip(parts, probs)
        ]

        def both(first, second):
            return jnp.concatenate([first + second[:, :TOK], second[:, TOK:]], axis=1)

        cos, sin = rope[0], rope[1]
        for w in range(2):
            to = pl.ds(al(own_cols + p * 128 + w * 64, 64), 64)
            at = parts[2 * w][1]
            full_q = jnp.concatenate(grads_q[2 * w : 2 * w + 2], axis=1)
            for full, dst in ((full_q, own_q), (both(*grads_k[2 * w : 2 * w + 2]), own_k)):
                low, high = full[:32], full[32:]
                act[at, dst] = jnp.concatenate(
                    [low * cos + high * sin, high * cos - low * sin], axis=0
                ).astype(BF16)
            gv[to, :] = both(*grads_v[2 * w : 2 * w + 2]).astype(BF16)
        return carry

    lax.fori_loop(0, 2, attend_back, 0)
    slot(8)
    lax.fori_loop(2, 4, attend_back, 0)
    own_heads = pl.ds(own_cols, HALF_D)
    head_copies = [
        to_core(10 + i, ref, ref)
        for i, ref in enumerate((act.at[:, own_q], act.at[:, own_k], gv.at[own_heads]))
    ]
    for copy in head_copies:
        copy.start()
    slot(9)

    def in_back(tok_at, dst, i):
        at = pl.ds(al(i * 512, 512), 512)
        cols = pl.ds(tok_at, TOK)
        total = mm(wq[at, :], act[:, pl.ds(al(own_cols + tok_at, TOK), TOK)])
        total += mm(wk[at, :], act[:, pl.ds(al(D + own_cols + tok_at, TOK), TOK)])
        total += mm(wv[at, :], gv[own_heads, cols])
        dst[:, at] = total.T.astype(dst.dtype)

    lax.fori_loop(0, 2, lambda i, c: (in_back(oth_tok, part_send, i), c)[1], 0)
    in_back_copy = to_core(13, part_send, part_recv)
    in_back_copy.start()
    slot(10)
    for copy in head_copies:
        copy.wait()
    for first in (0, 2):
        for i, rows in enumerate((head_grad(0), head_grad(D), rows_of(gv, 64))):
            for j in range(2):
                cols = pl.ds(al(own_cols + 256 * j, 256), 256)
                weight_grad(10 + 2 * i + j, first, first + 2, (rows, xin[:, cols]))
        slot(11 + first // 2)
    lax.fori_loop(0, 2, lambda i, c: (in_back(own_tok, part_own, i), c)[1], 0)
    slot(13)
    in_back_copy.wait()

    def token_back(i, carry):
        rows = pl.ds(al(i * CHUNK, CHUNK), CHUNK)
        v = tok[rows, :].astype(F32)
        back, part_a = norm_back(
            v, inv_rms(v), gain_a[...], part_own[rows, :] + part_recv[rows, :].astype(F32)
        )
        grad_tok[rows, :] = (hid[rows, :] + back).astype(BF16)
        return carry + part_a

    aux_s[0, 1:2, :] = lax.fori_loop(0, TOK // CHUNK, token_back, zero_row)
    hand_over(1).start()
    slot(14)

    pltpu.make_async_remote_copy(
        src_ref=pre_m, dst_ref=pre_m, send_sem=m_send.at[0], recv_sem=m_recv.at[0],
        device_id=x_peer, device_id_type=MESH_ID,
    ).wait()
    xm_pass.wait()

    def mate_pre(chip):
        return pre_m[pl.ds(al(chip // 2 * 128, 128), 128), :]

    for first in (0, 2):
        for n in range(4, 8):
            cols = slice(256 * (n - 4), 256 * (n - 4) + 256)
            weight_grad(
                n, first, first + 2, (rows_of(g_t, 128), xm[:, cols]), (mate_pre, xm_m[:, cols])
            )
        slot(15 + first // 2)

    aux_copy(0).start()
    slot(17)
    finals = attn_t.at[pl.ds(0, 128)]
    final_with(finals, finals, 18).wait_recv()

    for j in range(16):
        rows, _ = final_rows(j // 4, b)
        at = j % 4 * 128
        o_down[:, pl.ds(al((2 * j + b) * 128, 128), 128)] = part_own[rows, at : at + 128]
        o_down[:, pl.ds(al((2 * j + other) * 128, 128), 128)] = attn_t[
            j // 4 * 32 : j // 4 * 32 + 32, at : at + 128
        ]
    hand_over(3).start()
    slot(18)
    hand_over(4).start()
    device = dp * 2 + b
    at = pl.ds(al(device // 4 * 128, 128), 128)
    lines = pltpu.roll(aux_sum(5)[0:8, at], lax.rem(128 - lax.rem(device, 4) * 32, 128), 1)
    for i, ref in enumerate((small_down, small_a, small_b, small_c, small_d)):
        ref[...] = lines[i, :32]
    lines = aux_sum(5)[8:16, pl.ds(al(lax.rem(dp, 8) * 128, 128), 128)]
    chosen = lax.broadcasted_iota(jnp.int32, (8, 128), 0) == 2 * b + dp // 8
    small_up[...] = jnp.sum(jnp.where(chosen, lines, 0.0), axis=0)
    for i in range(9, 15):
        hand_over(i).start()
    for n, (refs, c0, width, rows) in enumerate(units):
        sent = refs[0].at[pl.ds(0, (2 ** len(UNIT_ORDER[n]) - 1) * rows), pl.ds(c0, width)]
        pltpu.make_async_remote_copy(
            src_ref=sent, dst_ref=sent, send_sem=rs_send.at[n], recv_sem=rs_recv.at[n, 0],
            device_id=x_peer, device_id_type=MESH_ID,
        ).wait_send()
    for k in range(5):
        aux_copy(k).wait_send()
    whole = part_own.at[pl.ds(0, 128)]
    final_with(whole, whole, 18).wait_send()
    finals = attn_t.at[pl.ds(128, 128)]
    final_with(finals, finals, 19).wait_recv()
    for i in range(4):
        dst = (o_out, o_query, o_key, o_value)[i]
        rows, _ = final_rows(8 + 2 * i, b)
        dst[:, pl.ds(own_cols, HALF_D)] = part_own[rows, 512:]
        dst[:, pl.ds(oth_cols, HALF_D)] = attn_t[128 + 32 * i : 160 + 32 * i, :]
        hand_over(5 + i).start()
    for i in range(15):
        hand_over(i).wait()


def finish_kernel(*refs):
    count = len(refs) // 3
    sems = refs[-1]
    gets = [
        pltpu.make_async_copy(refs[i], refs[2 * count + i], sems.at[i]) for i in range(count)
    ]
    puts = [
        pltpu.make_async_copy(refs[2 * count + i], refs[count + i], sems.at[i])
        for i in range(count)
    ]
    for copy in gets:
        copy.start()
    for get, put in zip(gets, puts):
        get.wait()
        put.start()
    for copy in puts:
        copy.wait()


def layer_on_device(
    tokens, doc_lengths, w_query, w_key, w_value, w_out, w_up, w_down, bias_up, bias_down,
    gain_pre_attn, gain_post_attn, gain_pre_mlp, gain_post_mlp, cotangent,
):
    def v16(*shape):
        return pltpu.VMEM(shape, BF16)

    def v32(*shape):
        return pltpu.VMEM(shape, F32)

    dma = pltpu.SemaphoreType.DMA
    vmem = pl.BlockSpec(memory_space=pltpu.VMEM)
    hbm = pl.BlockSpec(memory_space=pltpu.HBM)
    shapes = [((TOK, D), BF16)] * 2 + [((2, TOK), F32), ((32, FF), F32), ((D, 128), F32)]
    shapes += [((32, D), F32)] * 4 + [((128,), F32)] + [((32,), F32)] * 5
    shapes = [jax.ShapeDtypeStruct(*shape) for shape in shapes]
    scratch = [pltpu.VMEM(shape.shape, shape.dtype) for shape in shapes] + [dma((15,))]
    scratch += [
        v16(1024, 512), v16(1024, 512), v16(1024, 512), v16(1024, 1024),
        v16(1024, 2048), v16(2048, 1024),
        v16(512, 1024),
        v16(512, 512), v16(512, 512), v16(512, 512), v16(512, 512), v16(512, 512),
        v32(512, 512), v32(512, 512), v16(512, 512),
        v32(256, 1024), v32(256, 1024), v16(512, 1024),
        v16(512, 2048), v16(2048, 512),
        v16(256, 1024), v16(256, 1024), v32(256, 1024), v16(256, 1024),
        v16(1024, 512),
        v32(2, 32, 512), v32(8, 512), v32(2, 256, 128),
        v16(1024, 2048), v16(512, 2048), v16(256, 2048), v16(128, 2048), v16(64, 2048),
        v16(512, 1024), v16(256, 1024), v16(128, 1024), v16(512, 1024), v16(1024, 512),
        v16(512, 2048), v16(256, 2048), v16(128, 2048), v16(64, 2048),
        v32(1, 16, 1024), v32(5, 16, 1024),
        dma((6,)), dma((2,)), dma((2,)), dma((20,)), dma((20,)), dma((16,)), dma((16, 5)), dma((5,)), dma((5,)),
    ]
    results = pl.pallas_call(
        layer_kernel,
        out_shape=shapes,
        in_specs=[pl.BlockSpec(memory_space=pltpu.SMEM)]
        + [vmem] * 8
        + [pl.BlockSpec(memory_space=pl.ANY)] * 6,
        out_specs=[hbm] * 15,
        scratch_shapes=scratch,
        compiler_params=pltpu.CompilerParams(
            collective_id=0, has_side_effects=True, vmem_limit_bytes=VMEM_BYTES
        ),
    )(
        doc_lengths, tokens, cotangent,
        gain_pre_attn[None], gain_post_attn[None], gain_pre_mlp[None], gain_post_mlp[None],
        bias_up.reshape(32, 128), bias_down[None],
        w_query, w_key, w_value, w_out, w_up, w_down,
    )
    out, grad_tok, rms, gd, gu, go, gq, gk, gv, small_up, small_down, sa, sb, sc, sd = pl.pallas_call(
        finish_kernel,
        out_shape=shapes,
        in_specs=[hbm] * 15,
        out_specs=[hbm] * 15,
        scratch_shapes=[pltpu.VMEM(s.shape, s.dtype) for s in shapes] + [dma((15,))],
    )(*results)
    return (
        out, grad_tok, gq.T, gk.T, gv.T, go.T, gu, gd.T, small_up, small_down, sa, sb, sc, sd, rms
    )


def solution(mesh):
    placed = (
        P(("dp", "blk"), None),
        P("dp", None),
        P(),
        P(),
        P(),
        P(),
        P(),
        P(),
        P(),
        P(),
        P(),
        P(),
        P(),
        P(),
        P(("dp", "blk"), None),
    )
    paired = mesh.shape["blk"] == 2 and mesh.shape["dp"] == 16
    return jax.shard_map(
        layer_on_device if paired else on_device,
        mesh=mesh,
        in_specs=placed,
        out_specs=(
            P(("dp", "blk"), None),
            P(("dp", "blk"), None),
            P(None, ("dp", "blk")),
            P(None, ("dp", "blk")),
            P(None, ("dp", "blk")),
            P(None, ("dp", "blk")),
            P(None, ("dp", "blk")),
            P(None, ("dp", "blk")),
            P(("dp", "blk")),
            P(("dp", "blk")),
            P(("dp", "blk")),
            P(("dp", "blk")),
            P(("dp", "blk")),
            P(("dp", "blk")),
            P(None, ("dp", "blk")),
        ),
        check_vma=False,
    )
```

```python
import math

import jax
import jax.numpy as jnp
from jax import lax
from jax.experimental import pallas as pl
from jax.experimental.pallas import tpu as pltpu
from jax.sharding import PartitionSpec as P

D = 1024
H = 16
HD = 64


eps = 1e-06
neg_big = -1e30


def rms_norm(values, gain_row):
    return values * lax.rsqrt(jnp.mean(values * values, axis=-1, keepdims=True) + eps) * gain_row


def rotate(head_rows, position):
    half_size = head_rows.shape[-1] // 2
    frequency = 10000.0 ** (-2.0 * jnp.arange(half_size, dtype=jnp.float32) / head_rows.shape[-1])
    angles = position.astype(jnp.float32)[:, None] * frequency[None, :]
    cosine = jnp.cos(angles)[:, None, :]
    sine_part = jnp.sin(angles)[:, None, :]
    low_half = head_rows[..., :half_size]
    high_half = head_rows[..., half_size:]
    return jnp.concatenate(
        [low_half * cosine - high_half * sine_part, low_half * sine_part + high_half * cosine],
        axis=-1,
    )


def doc_layout(lengths, total_rows):
    index_row = jnp.arange(total_rows, dtype=jnp.int32)
    doc_ends = jnp.stack(
        [
            lengths[0],
            lengths[0] + lengths[1],
            lengths[0] + lengths[1] + lengths[2],
            lengths[0] + lengths[1] + lengths[2] + lengths[3],
        ]
    )
    segment = jnp.sum((index_row[:, None] >= doc_ends[None, :3]).astype(jnp.int32), axis=1)
    starts = doc_ends - lengths
    matches = segment[:, None] == jnp.arange(4, dtype=jnp.int32)[None, :]
    return (index_row, jnp.sum(jnp.where(matches, starts[None, :], 0), axis=1))


def block_mask(query_index, query_start, key_first, width):
    key_index = key_first + jnp.arange(width, dtype=jnp.int32)
    return (key_index[None, :] <= query_index[:, None]) & (
        key_index[None, :] >= query_start[:, None]
    )


def on_device(
    tokens,
    doc_lengths,
    w_query,
    w_key,
    w_value,
    w_out,
    w_up,
    w_down,
    bias_up,
    bias_down,
    gain_pre_attn,
    gain_post_attn,
    gain_pre_mlp,
    gain_post_mlp,
    cotangent,
):
    row_count = tokens.shape[0]
    cycle_size = lax.axis_size("blk")
    group_rows = row_count * cycle_size
    first_row = lax.axis_index("blk") * row_count
    index_all, start_all = doc_layout(doc_lengths[0], group_rows)
    query_index = lax.dynamic_slice_in_dim(index_all, first_row, row_count)
    query_start = lax.dynamic_slice_in_dim(start_all, first_row, row_count)
    position = query_index - query_start
    query_last = first_row + row_count - 1
    start_least = jnp.min(query_start)
    scale = HD ** (-0.5)
    tokens_f = tokens.astype(jnp.float32)
    normed_in, back_pre_attn = jax.vjp(rms_norm, tokens_f, gain_pre_attn)
    attn_in = normed_in.astype(jnp.bfloat16)
    query_pre = jnp.dot(attn_in, w_query, preferred_element_type=jnp.float32)
    key_pre = jnp.dot(attn_in, w_key, preferred_element_type=jnp.float32)
    value_pre = jnp.dot(attn_in, w_value, preferred_element_type=jnp.float32)
    queries, back_rot_query = jax.vjp(
        lambda arr: rotate(arr, position), query_pre.reshape(row_count, H, HD)
    )
    keys_rot, back_rot_key = jax.vjp(
        lambda arr: rotate(arr, position), key_pre.reshape(row_count, H, HD)
    )
    queries_low = queries.astype(jnp.bfloat16)
    keys_low = keys_rot.reshape(row_count, D).astype(jnp.bfloat16)
    values_low = value_pre.astype(jnp.bfloat16)
    initial = (
        jnp.full((H, row_count), neg_big, jnp.float32),
        jnp.zeros((H, row_count), jnp.float32),
        jnp.zeros((row_count, H, HD), jnp.float32),
    )
    key_piece = lax.all_gather(keys_low, "blk", axis=0, tiled=True)
    value_piece = lax.all_gather(values_low, "blk", axis=0, tiled=True)
    piece_rows = key_piece.shape[0]
    fold_width = math.gcd(piece_rows, 512)

    def one_block(state, number):
        key_first = number * fold_width

        def one_compute(state):
            running_top, totals, accum = state
            keys_blk = lax.dynamic_slice_in_dim(
                key_piece, number * fold_width, fold_width, 0
            ).reshape(fold_width, H, HD)
            values_blk = lax.dynamic_slice_in_dim(
                value_piece, number * fold_width, fold_width, 0
            ).reshape(fold_width, H, HD)
            scores = (
                jnp.einsum(
                    "qhd,khd->hqk", queries_low, keys_blk, preferred_element_type=jnp.float32
                )
                * scale
            )
            allowed = block_mask(query_index, query_start, key_first, fold_width)[None]
            scores = jnp.where(allowed, scores, neg_big)
            new_top = jnp.maximum(running_top, jnp.max(scores, axis=-1))
            weights = jnp.where(allowed, jnp.exp(scores - new_top[..., None]), 0.0)
            factor = jnp.exp(running_top - new_top)
            totals = totals * factor + jnp.sum(weights, axis=-1)
            accum = accum * jnp.transpose(factor)[:, :, None] + jnp.einsum(
                "hqk,khd->qhd",
                weights.astype(jnp.bfloat16),
                values_blk,
                preferred_element_type=jnp.float32,
            )
            return (new_top, totals, accum)

        active = (key_first <= query_last) & (key_first + fold_width - 1 >= start_least)
        return (lax.cond(active, one_compute, lambda state: state, state), None)

    result, unused = lax.scan(
        one_block, initial, jnp.arange(piece_rows // fold_width, dtype=jnp.int32)
    )
    running_top, totals, accum = result
    attn_full = accum / jnp.transpose(totals)[:, :, None]
    log_total = running_top + jnp.log(totals)
    attn_low = attn_full.reshape(row_count, D).astype(jnp.bfloat16)
    branch_attn = jnp.dot(attn_low, w_out, preferred_element_type=jnp.float32)
    post_attn, back_post_attn = jax.vjp(rms_norm, branch_attn, gain_post_attn)
    hidden_res = tokens_f + post_attn
    normed_mlp, back_pre_mlp = jax.vjp(rms_norm, hidden_res, gain_pre_mlp)
    mlp_in = normed_mlp.astype(jnp.bfloat16)
    pre_act = jnp.dot(mlp_in, w_up, preferred_element_type=jnp.float32) + bias_up
    activated, back_gelu = jax.vjp(lambda arr: jax.nn.gelu(arr, approximate=True), pre_act)
    act_low = activated.astype(jnp.bfloat16)
    branch_mlp = jnp.dot(act_low, w_down, preferred_element_type=jnp.float32) + bias_down
    post_mlp, back_post_mlp = jax.vjp(rms_norm, branch_mlp, gain_post_mlp)
    output = (hidden_res + post_mlp).astype(jnp.bfloat16)
    branch_rms = jnp.stack(
        [
            jnp.sqrt(jnp.mean(branch_attn * branch_attn, axis=-1) + eps),
            jnp.sqrt(jnp.mean(branch_mlp * branch_mlp, axis=-1) + eps),
        ]
    )
    grad_out_f = cotangent.astype(jnp.float32)
    grad_branch_mlp, grad_gain_post_mlp = back_post_mlp(grad_out_f)
    grad_mlp_low = grad_branch_mlp.astype(jnp.bfloat16)
    grad_bias_down = jnp.sum(grad_mlp_low.astype(jnp.float32), axis=0)
    grad_down = jnp.einsum("tf,td->df", act_low, grad_mlp_low, preferred_element_type=jnp.float32)
    grad_act = jnp.einsum("td,fd->tf", grad_mlp_low, w_down, preferred_element_type=jnp.float32)
    (grad_pre_act,) = back_gelu(grad_act)
    grad_pre_low = grad_pre_act.astype(jnp.bfloat16)
    grad_bias_up = jnp.sum(grad_pre_low.astype(jnp.float32), axis=0)
    grad_up = jnp.einsum("td,tf->fd", mlp_in, grad_pre_low, preferred_element_type=jnp.float32)
    grad_normed_mlp = jnp.einsum(
        "tf,df->td", grad_pre_low, w_up, preferred_element_type=jnp.float32
    )
    grad_res_part, grad_gain_pre_mlp = back_pre_mlp(grad_normed_mlp)
    grad_hidden = grad_out_f + grad_res_part
    grad_branch_attn, grad_gain_post_attn = back_post_attn(grad_hidden)
    grad_branch_low = grad_branch_attn.astype(jnp.bfloat16)
    grad_w_out = jnp.einsum(
        "td,te->ed", attn_low, grad_branch_low, preferred_element_type=jnp.float32
    )
    grad_attn = jnp.einsum("te,de->td", grad_branch_low, w_out, preferred_element_type=jnp.float32)
    grad_attn_low = grad_attn.astype(jnp.bfloat16).reshape(row_count, H, HD)
    delta = jnp.einsum("qhd,qhd->hq", grad_attn_low.astype(jnp.float32), attn_full)
    key_source, value_source = key_piece, value_piece
    width = math.gcd(group_rows, 512)

    def back_block(grad_query_acc, number):
        key_first = number * width

        def back_compute(grad_query_acc):
            keys_blk = lax.dynamic_slice_in_dim(key_source, key_first, width, 0).reshape(
                width, H, HD
            )
            values_blk = lax.dynamic_slice_in_dim(value_source, key_first, width, 0).reshape(
                width, H, HD
            )
            scores = (
                jnp.einsum(
                    "qhd,khd->hqk", queries_low, keys_blk, preferred_element_type=jnp.float32
                )
                * scale
            )
            allowed = block_mask(query_index, query_start, key_first, width)[None]
            probs = jnp.where(allowed, jnp.exp(scores - log_total[..., None]), 0.0)
            grad_probs = jnp.einsum(
                "qhd,khd->hqk", grad_attn_low, values_blk, preferred_element_type=jnp.float32
            )
            grad_scores = (probs * (grad_probs - delta[..., None])).astype(jnp.bfloat16)
            grad_query_acc = (
                grad_query_acc
                + jnp.einsum(
                    "hqk,khd->qhd", grad_scores, keys_blk, preferred_element_type=jnp.float32
                )
                * scale
            )
            grad_keys_blk = (
                jnp.einsum(
                    "hqk,qhd->khd", grad_scores, queries_low, preferred_element_type=jnp.float32
                )
                * scale
            )
            grad_values_blk = jnp.einsum(
                "hqk,qhd->khd",
                probs.astype(jnp.bfloat16),
                grad_attn_low,
                preferred_element_type=jnp.float32,
            )
            return (
                grad_query_acc,
                (grad_keys_blk.reshape(width, D), grad_values_blk.reshape(width, D)),
            )

        def skipped(grad_query_acc):
            return (
                grad_query_acc,
                (jnp.zeros((width, D), jnp.float32), jnp.zeros((width, D), jnp.float32)),
            )

        active = (key_first <= query_last) & (key_first + width - 1 >= start_least)
        return lax.cond(active, back_compute, skipped, grad_query_acc)

    grad_query_acc, stacked = lax.scan(
        back_block,
        jnp.zeros((row_count, H, HD), jnp.float32),
        jnp.arange(group_rows // width, dtype=jnp.int32),
    )
    grad_keys_all = stacked[0].reshape(group_rows, D)
    grad_values_all = stacked[1].reshape(group_rows, D)
    grad_keys_mine, grad_values_mine = (
        lax.psum_scatter(
            grad_keys_all.astype(jnp.bfloat16), "blk", scatter_dimension=0, tiled=True
        ).astype(jnp.float32),
        lax.psum_scatter(
            grad_values_all.astype(jnp.bfloat16), "blk", scatter_dimension=0, tiled=True
        ).astype(jnp.float32),
    )
    (grad_key_pre,) = back_rot_key(grad_keys_mine.reshape(row_count, H, HD))
    (grad_query_pre,) = back_rot_query(grad_query_acc)
    grad_key_low = grad_key_pre.reshape(row_count, D).astype(jnp.bfloat16)
    grad_query_low = grad_query_pre.reshape(row_count, D).astype(jnp.bfloat16)
    grad_value_low = grad_values_mine.astype(jnp.bfloat16)
    grad_query = jnp.einsum(
        "td,te->ed", attn_in, grad_query_low, preferred_element_type=jnp.float32
    )
    grad_key = jnp.einsum("td,te->ed", attn_in, grad_key_low, preferred_element_type=jnp.float32)
    grad_value = jnp.einsum(
        "td,te->ed", attn_in, grad_value_low, preferred_element_type=jnp.float32
    )
    grad_normed_in = (
        jnp.einsum("te,de->td", grad_query_low, w_query, preferred_element_type=jnp.float32)
        + jnp.einsum("te,de->td", grad_key_low, w_key, preferred_element_type=jnp.float32)
        + jnp.einsum("te,de->td", grad_value_low, w_value, preferred_element_type=jnp.float32)
    )
    grad_tokens_part, grad_gain_pre_attn = back_pre_attn(grad_normed_in)
    grad_tokens = (grad_hidden + grad_tokens_part).astype(jnp.bfloat16)
    count = lax.axis_size(("dp", "blk"))
    low = jnp.bfloat16
    pieces = [
        part.astype(low).reshape(count, -1, D)
        for part in (grad_query, grad_key, grad_value, grad_w_out, grad_up, grad_down)
    ]
    small = [
        part.reshape(count, -1)
        for part in (
            grad_bias_up,
            grad_bias_down,
            grad_gain_pre_attn,
            grad_gain_post_attn,
            grad_gain_pre_mlp,
            grad_gain_post_mlp,
        )
    ]
    sizes = [part.shape[1] for part in pieces]
    summed = lax.psum_scatter(
        jnp.concatenate(pieces, axis=1), ("dp", "blk"), scatter_dimension=0
    ).astype(jnp.float32)
    small_sizes = [part.shape[1] for part in small]
    small_flat = jnp.concatenate(small, axis=1)
    padding = -small_flat.shape[1] % 128
    small_flat = jnp.pad(small_flat, ((0, 0), (0, padding)))
    small_summed = lax.psum_scatter(small_flat, ("dp", "blk"), scatter_dimension=0)
    cuts = [sum(sizes[: i + 1]) for i in range(len(sizes) - 1)]
    parts = jnp.split(summed, cuts, axis=0)
    parts[5] = parts[5].reshape(D // count, -1)
    small_cuts = [sum(small_sizes[: i + 1]) for i in range(len(small_sizes))]
    small_parts = jnp.split(small_summed, small_cuts, axis=0)[:6]
    return (output, grad_tokens, *[part.T for part in parts], *small_parts, branch_rms)


MESH_ID = pl.DeviceIdType.MESH
F32 = jnp.float32
BF16 = jnp.bfloat16
TOK = 256
PACK = 512
FF = 4096
HALF_FF = 2048
HALF_D = 512
CHUNK = 128
VMEM_BYTES = 62 * 1024 * 1024
UNIT_ORDER = (
    "ywvx",
    "wvxy",
    "ywxv",
    "yxwv",
    "wyv",
    "ywv",
    "ywv",
    "ywv",
    "yxwv",
    "yxwv",
    "wxyv",
    "xywv",
    "xywv",
    "xwyv",
    "xywv",
    "xwyv",
)
SLOTS = (
    (0, 1, 10, 11,),
    (),
    (),
    (20,),
    (2, 12,),
    (),
    (21,),
    (),
    (3, 13,),
    (30,),
    (4, 22,),
    (),
    (31,),
    (110,),
    (14, 100, 23,),
    (40, 50, 111, 5, 32,),
    (24, 112,),
    (41, 33, 160, 102, 15, 101, 42, 52, 113, 6, 114, 51, 43, 16, 103, 60, 44, 34, 61, 115, 120, 53, 54, 25, 45, 70, 161, 62, 121, 35, 104, 116, 63, 130, 55, 122, 72, 131, 26, 123, 71, 162, 64, 105, 140, 36,),
    (132, 80, 124, 141, 133, 81, 73, 150, 163, 74, 65, 106, 90, 142, 82, 134, 143, 125, 151, 83, 152, 164, 75, 92, 126, 84, 91, 144, 135, 153, 154, 85, 145, 93, 94, 136, 155, 86, 146, 95, 156, 96,),
)


def mm(a, b):
    return jnp.dot(a, b, preferred_element_type=F32)


def mm_nt(a, b):
    return lax.dot_general(a, b, (((1,), (1,)), ((), ())), preferred_element_type=F32)


def al(offset, step):
    return pl.multiple_of(offset, step)


def norm_back(v, r, gain, grad):
    scaled = grad * gain
    inner = jnp.mean(v * scaled, axis=-1, keepdims=True)
    return r * scaled - v * (r * r * r * inner), jnp.sum(grad * v * r, axis=0, keepdims=True)


def inv_rms(v):
    return lax.rsqrt(jnp.mean(v * v, axis=-1, keepdims=True) + eps)


def layer_kernel(
    doc, tok, cot, gain_a, gain_b, gain_c, gain_d, bias_up, bias_down,
    wq_hbm, wk_hbm, wv_hbm, wo_hbm, wu_hbm, wd_hbm,
    *refs,
):
    results, refs = refs[:15], refs[15:]
    (
        out, grad_tok, rms, o_down, o_up, o_out, o_query, o_key, o_value,
        small_up, small_down, small_a, small_b, small_c, small_d, o_sem,
        wq, wk, wv, wo, wu, wd, xin, q_t, k_t, v_t, k_n, v_n, mask, attn_t, attn_nat,
        branch, hid, xm, act, g_t, part_send, part_recv, part_own, nat, gb_t,
        rope, lse, stat, s_down, r1_down, r2_down, r3_down, r4_down, r1_up, r2_up, r3_up, xm_m, pre_m,
        r1_late, r2_late, r3_late, r4_late, aux_s, aux_r,
        w_sem, m_send, m_recv, c_send, c_recv, rs_send, rs_recv, a_send, a_recv,
    ) = refs
    held = (
        out, grad_tok, rms, o_down, o_up, o_out, o_query, o_key, o_value,
        small_up, small_down, small_a, small_b, small_c, small_d,
    )

    def hand_over(i):
        return pltpu.make_async_copy(held[i], results[i], o_sem.at[i])

    dp = lax.axis_index("dp")
    b = lax.axis_index("blk")
    x = lax.rem(dp, 2)
    y = lax.rem(dp // 2, 2)
    z = dp // 4
    other = 1 - b
    core_peer = (dp, other)
    x_peer = (dp + 1 - 2 * x, b)
    y_peer = (dp + 2 - 4 * y, b)

    z_low = (dp + 4 - 8 * lax.rem(z, 2), b)
    z_high = (dp + 8 - 16 * (z // 2), b)
    barrier = pltpu.get_barrier_semaphore()
    for peer in (core_peer, x_peer, y_peer, z_low, z_high):
        pl.semaphore_signal(barrier, inc=1, device_id=peer, device_id_type=MESH_ID)

    own_cols = al(b * HALF_D, HALF_D)
    oth_cols = al(other * HALF_D, HALF_D)
    own_tok = al(b * TOK, TOK)
    oth_tok = al(other * TOK, TOK)

    w_copies = [
        pltpu.make_async_copy(src.at[:, pl.ds(own_cols, HALF_D)], dst, w_sem.at[i])
        for i, (src, dst) in enumerate(((wq_hbm, wq), (wk_hbm, wk), (wv_hbm, wv)))
    ]
    w_copies.append(pltpu.make_async_copy(wo_hbm, wo, w_sem.at[3]))
    for copy in w_copies:
        copy.start()

    def up_copy(j):
        return pltpu.make_async_copy(
            wu_hbm.at[:, pl.ds(al((2 * j + b) * 128, 128), 128)],
            wu.at[:, pl.ds(al(j * 128, 128), 128)],
            w_sem.at[4],
        )

    def down_copy(j):
        return pltpu.make_async_copy(
            wd_hbm.at[pl.ds(al((2 * j + b) * 128, 128), 128)],
            wd.at[pl.ds(al(j * 128, 128), 128)],
            w_sem.at[5],
        )

    def to_core(k, src, dst):
        return pltpu.make_async_remote_copy(
            src_ref=src, dst_ref=dst, send_sem=c_send.at[k], recv_sem=c_recv.at[k],
            device_id=core_peer, device_id_type=MESH_ID,
        )

    end_a = doc[0, 0]
    end_b = end_a + doc[0, 1]
    end_c = end_b + doc[0, 2]
    index_row = lax.broadcasted_iota(jnp.int32, (1, PACK), 1)
    start_row = jnp.where(
        index_row >= end_c,
        end_c,
        jnp.where(index_row >= end_b, end_b, jnp.where(index_row >= end_a, end_a, 0)),
    )
    position = (index_row - start_row).astype(F32)
    freq = jnp.exp(
        lax.broadcasted_iota(jnp.int32, (32, PACK), 0).astype(F32) * (-math.log(10000.0) / 32.0)
    )
    angle = position * freq
    rope[0] = jnp.cos(angle)
    rope[1] = jnp.sin(angle)

    def fill_mask(i, carry):
        rows = pl.ds(al(i * 64, 64), 64)
        key_index = lax.broadcasted_iota(jnp.int32, (64, PACK), 0) + i * 64
        query_index = lax.broadcasted_iota(jnp.int32, (64, PACK), 1)
        allowed = (key_index <= query_index) & (key_index >= start_row)
        mask[rows, :] = jnp.where(allowed, 0.0, neg_big)
        return carry

    lax.fori_loop(0, 8, fill_mask, 0)

    def pre_attn(i, carry):
        rows = pl.ds(al(i * CHUNK, CHUNK), CHUNK)
        v = tok[rows, :].astype(F32)
        xin[pl.ds(al(own_tok + i * CHUNK, CHUNK), CHUNK), :] = (
            v * inv_rms(v) * gain_a[...]
        ).astype(BF16)
        return carry

    lax.fori_loop(0, TOK // CHUNK, pre_attn, 0)
    pl.semaphore_wait(barrier, 5)
    own_rows = xin.at[pl.ds(own_tok, TOK)]
    xin_copy = to_core(0, own_rows, own_rows)
    xin_copy.start()
    lax.fori_loop(0, 16, lambda j, c: (up_copy(j).start(), c)[1], 0)
    lax.fori_loop(0, 16, lambda j, c: (down_copy(j).start(), c)[1], 0)

    attn_oth = nat.at[:, pl.ds(0, PACK)]

    def project(tok_at):
        rows = pl.ds(tok_at, TOK)
        cos = rope[0, :, rows]
        sin = rope[1, :, rows]
        x_rows = xin[rows, :]

        def turned(w, scale):
            flat = mm(x_rows, w[...]).T.reshape(8, 2, 32, TOK)
            low, high = flat[:, 0], flat[:, 1]
            both = jnp.stack([low * cos - high * sin, low * sin + high * cos], axis=1)
            return (both * scale).reshape(HALF_D, TOK).astype(BF16)

        q_t[:, rows] = turned(wq, 0.125)
        keys = turned(wk, 1.0)
        k_t[:, rows] = keys
        k_n[rows, :] = keys.T
        values = mm(x_rows, wv[...]).astype(BF16)
        v_n[rows, :] = values
        v_t[:, rows] = values.T

    for copy in w_copies[:3]:
        copy.wait()
    project(own_tok)
    xin_copy.wait()
    project(oth_tok)

    zeros = jnp.zeros((64, TOK), BF16)

    def slab(head_rows, which):
        return jnp.concatenate([head_rows, zeros] if which == 0 else [zeros, head_rows], axis=0)

    def attend(i, carry):
        pairs = [2 * i, 2 * i + 1]
        slabs = [pl.ds(al(p * 128, 128), 128) for p in pairs]
        parts = [
            (
                w, pl.ds(al(pairs[e] * 128 + w * 64, 64), 64),
                slice(block * TOK, block * TOK + TOK), (block + 1) * TOK, e,
            )
            for e in (0, 1)
            for block in (1, 0)
            for w in (0, 1)
        ]
        scores = [
            mm(k_n[:keys, slabs[e]], slab(q_t[rows, cols], w)) + mask[:keys, cols]
            for w, rows, cols, keys, e in parts
        ]
        tops = [jnp.max(score, axis=0, keepdims=True) for score in scores]
        weights = [jnp.exp(score - top) for score, top in zip(scores, tops)]
        totals = [jnp.sum(weight, axis=0, keepdims=True) for weight in weights]
        for (w, rows, cols, keys, e), weight, top, total in zip(parts, weights, tops, totals):
            attn_t[rows, cols] = mm(v_t[rows, :keys], weight.astype(BF16)) * (1.0 / total)
            lse[pl.ds(pairs[e] * 2 + w, 1), cols] = top + jnp.log(total)
        for p, slab_cols in zip(pairs, slabs):
            attn_nat[:, slab_cols] = attn_t[pl.ds(al(p * 128, 128), 128), :].T.astype(BF16)
            to_core(
                1 + p, attn_nat.at[pl.ds(oth_tok, TOK), slab_cols], attn_oth.at[:, slab_cols]
            ).start()
        return carry

    lax.fori_loop(0, 2, attend, 0)

    w_copies[3].wait()
    branch[...] = mm(attn_nat[pl.ds(own_tok, TOK), :], wo[pl.ds(own_cols, HALF_D), :])

    def attn_copy(p):
        cols = pl.ds(al(p * 128, 128), 128)
        return to_core(1 + p, attn_nat.at[pl.ds(oth_tok, TOK), cols], attn_oth.at[:, cols])

    lax.fori_loop(0, 4, lambda p, c: (attn_copy(p).wait(), c)[1], 0)
    branch[...] += mm(attn_oth[...], wo[pl.ds(oth_cols, HALF_D), :])

    def post_attn(i, carry):
        rows = pl.ds(al(i * CHUNK, CHUNK), CHUNK)
        v = branch[rows, :]
        square = jnp.mean(v * v, axis=-1, keepdims=True) + eps
        stat[0, rows, :] = jnp.broadcast_to(jnp.sqrt(square), (CHUNK, 128))
        h = tok[rows, :].astype(F32) + v * lax.rsqrt(square) * gain_b[...]
        hid[rows, :] = h
        xm[pl.ds(al(own_tok + i * CHUNK, CHUNK), CHUNK), :] = (
            h * inv_rms(h) * gain_c[...]
        ).astype(BF16)
        return carry

    lax.fori_loop(0, TOK // CHUNK, post_attn, 0)
    own_rows_m = xm.at[pl.ds(own_tok, TOK)]
    xm_copy = to_core(5, own_rows_m, own_rows_m)
    xm_copy.start()
    xm_mate = pltpu.make_async_remote_copy(
        src_ref=own_rows_m, dst_ref=xm_m.at[pl.ds(own_tok, TOK)], send_sem=m_send.at[1],
        recv_sem=m_recv.at[1], device_id=x_peer, device_id_type=MESH_ID,
    )
    xm_mate.start()

    def up_step(tok_at, i):
        cols = pl.ds(al(i * 1024, 1024), 1024)
        rows = pl.ds(tok_at, TOK)
        bias = jnp.concatenate(
            [bias_up[pl.ds(16 * i + 2 * j + b, 1), :] for j in range(8)], axis=1
        )
        pre = mm(xm[rows, :], wu[:, cols]) + bias
        square = pre * pre
        th = jnp.tanh(pre * (0.7978845608 + (0.7978845608 * 0.044715) * square))
        half = 0.5 + 0.5 * th
        act[rows, cols] = (pre * half).astype(BF16)
        slope = half + pre * (0.5 - 0.5 * th * th) * (
            0.7978845608 + (0.7978845608 * 0.134145) * square
        )
        g_t[cols, rows] = slope.astype(BF16).T

    pltpu.make_async_copy(wu_hbm.at[:, pl.ds(0, HALF_FF)], wu, w_sem.at[4]).wait()
    lax.fori_loop(0, 2, lambda i, c: (up_step(own_tok, i), c)[1], 0)
    xm_copy.wait()
    lax.fori_loop(0, 2, lambda i, c: (up_step(oth_tok, i), c)[1], 0)
    pltpu.make_async_copy(wd_hbm.at[pl.ds(0, HALF_FF)], wd, w_sem.at[5]).wait()

    def down_step(tok_at, dst, i):
        cols = slice(i * 512, i * 512 + 512)
        dst[:, cols] = mm(act[pl.ds(tok_at, TOK), :], wd[:, cols]).astype(dst.dtype)

    mlp_copies = [
        to_core(k, part_send.at[:, pl.ds(i * 512, 512)], part_recv.at[:, pl.ds(i * 512, 512)])
        for i, k in ((0, 6), (1, 15))
    ]
    for i in range(2):
        down_step(oth_tok, part_send, i)
        mlp_copies[i].start()
    for i in range(2):
        down_step(own_tok, part_own, i)
    for copy in mlp_copies:
        copy.wait()
    def post_mlp(i, carry):
        sum_bias, sum_gain = carry
        rows = pl.ds(al(i * CHUNK, CHUNK), CHUNK)
        v = part_own[rows, :] + part_recv[rows, :].astype(F32) + bias_down[...]
        square = jnp.mean(v * v, axis=-1, keepdims=True) + eps
        stat[1, rows, :] = jnp.broadcast_to(jnp.sqrt(square), (CHUNK, 128))
        r = lax.rsqrt(square)
        out[rows, :] = (hid[rows, :] + v * r * gain_d[...]).astype(BF16)
        back, gain_part = norm_back(v, r, gain_d[...], cot[rows, :].astype(F32))
        back = back.astype(BF16)
        nat[rows, :] = back
        return (
            sum_bias + jnp.sum(back.astype(F32), axis=0, keepdims=True),
            sum_gain + gain_part,
        )

    def turn_and_send(dst, i, k):
        tok_cols = pl.ds(al(own_tok + i * CHUNK, CHUNK), CHUNK)
        for j in range(4):
            cols = slice(j * 256, j * 256 + 256)
            dst[cols, tok_cols] = nat[i * CHUNK : i * CHUNK + CHUNK, cols].T
        part = dst.at[:, tok_cols]
        copy = to_core(k, part, part)
        copy.start()
        return copy

    zero_row = jnp.zeros((1, D), F32)
    sums = (zero_row, zero_row)
    gb_copies = []
    for i, k in ((0, 7), (1, 16)):
        sums = post_mlp(i, sums)
        gb_copies.append(turn_and_send(gb_t, i, k))
    sum_bias_down, sum_gain_d = sums
    aux_s[0] = jnp.zeros((16, D), F32)
    aux_s[0, 0:1, :] = sum_bias_down
    aux_s[0, 4:5, :] = sum_gain_d
    for i in range(2):
        rms[i : i + 1, :] = stat[i].T[0:1, :]
    hand_over(0).start()
    hand_over(2).start()

    for copy in gb_copies:
        copy.wait()
    down_refs = (s_down, r1_down, r2_down, r3_down, r4_down)
    up_refs = (wd, r1_up, r2_up, r3_up)
    late_refs = (wu, r1_late, r2_late, r3_late, r4_late)
    units = (
        [(down_refs, 512 * i, 512, 64) for i in range(4)]
        + [(up_refs, 256 * i, 256, 128) for i in range(4)]
        + [(late_refs, 256 * i, 256, 64) for i in range(8)]
    )
    place = {
        "x": (x, 1, x_peer),
        "y": (y, 2, y_peer),
        "w": (lax.rem(z, 2), 4, z_low),
        "v": (z // 2, 8, z_high),
    }

    def unit_axes(n):
        return [place[letter] for letter in UNIT_ORDER[n]]

    def kept(n, steps):
        axes = unit_axes(n)
        step = 2 ** len(axes) // 2 * units[n][3]
        return sum((axis[0] * (step >> i) for i, axis in enumerate(axes[:steps])), 0)

    def unit_copy(n, k):
        refs, c0, width, rows = units[n]
        axes = unit_axes(n)
        span = 2 ** len(axes)
        cols = pl.ds(c0, width)
        if k < 2:
            bit, _, peer = axes[0]
            second = lax.rem(axes[1][0] + 1 + k, 2)
            count = span // 4 * rows
            src = refs[0].at[pl.ds(al(((1 - bit) * 2 + second) * count, count), count), cols]
            dst = refs[1].at[pl.ds(al(second * count, count), count), cols]
        else:
            bit, _, peer = axes[k - 1]
            count = (span >> k) * rows
            at = kept(n, k - 1) + (1 - bit) * count
            src = refs[0].at[pl.ds(al(at, count), count), cols]
            dst = refs[k].at[:, cols]
        return pltpu.make_async_remote_copy(
            src_ref=src, dst_ref=dst, send_sem=rs_send.at[n], recv_sem=rs_recv.at[n, k],
            device_id=peer, device_id_type=MESH_ID,
        )

    def add_rows(n, at, arrived, arrived_at, count):
        refs, c0, width, _ = units[n]
        cols = pl.ds(c0, width)

        def step(i, carry):
            to = pl.ds(al(at + i * 64, 64), 64)
            got = refs[arrived][pl.ds(al(arrived_at + i * 64, 64), 64), cols]
            refs[0][to, cols] = (refs[0][to, cols].astype(F32) + got.astype(F32)).astype(BF16)
            return carry

        lax.fori_loop(0, count // 64, step, 0)

    def serve(n, k):
        refs, c0, width, rows = units[n]
        axes = unit_axes(n)
        last = len(axes)
        span = 2**last
        unit_copy(n, k).wait_recv()
        if k < 2:
            second = lax.rem(axes[1][0] + 1 + k, 2)
            count = span // 4 * rows
            add_rows(n, kept(n, 1) + second * count, 1, second * count, count)
            if k == 0:
                unit_copy(n, 2).start()
        elif k < last:
            count = (span // 2 >> k) * rows
            bit = axes[k][0]
            add_rows(n, kept(n, k) + (1 - bit) * count, k, (1 - bit) * count, count)
            unit_copy(n, k + 1).start()
            add_rows(n, kept(n, k) + bit * count, k, bit * count, count)
        else:
            cols = pl.ds(c0, width)
            mine = refs[0][pl.ds(al(kept(n, last), rows), rows), cols].astype(F32)
            total = mine + refs[last][:, cols].astype(F32)
            if 4 <= n < 8:
                o_up[c0 : c0 + width, :] = total.T
            else:
                at, to = final_at(n)
                part_own[at : at + 64, to : to + width] = total
                final_copy(n).start()

    def final_at(n):
        return (64 * n, 0) if n < 4 else (64 * ((n - 8) // 2), 512 + 256 * (n % 2))

    def final_rows(n, half):
        at, to = final_at(n)
        return pl.ds(al(at + half * 32, 32), 32), pl.ds(to, units[n][2])

    def final_copy(n):
        at, to = (32 * n, 0) if n < 4 else (128 + 32 * ((n - 8) // 2), 256 * (n % 2))
        dst = attn_t.at[pl.ds(at, 32), pl.ds(to, units[n][2])]
        return final_with(part_own.at[final_rows(n, other)], dst, 18 if n < 4 else 19)

    def final_with(src, dst, k):
        return pltpu.make_async_remote_copy(
            src_ref=src, dst_ref=dst, send_sem=c_send.at[18], recv_sem=c_recv.at[k],
            device_id=core_peer, device_id_type=MESH_ID,
        )

    aux_peers = (core_peer, x_peer, y_peer, z_low, z_high)

    def aux_sum(k):
        return aux_s.at[0] if k == 0 else hid.at[pl.ds(16 * k, 16)]

    def aux_copy(k):
        return pltpu.make_async_remote_copy(
            src_ref=aux_sum(k), dst_ref=aux_r.at[k], send_sem=a_send.at[k],
            recv_sem=a_recv.at[k], device_id=aux_peers[k], device_id_type=MESH_ID,
        )

    def aux_end(k):
        aux_copy(k).wait_recv()
        aux_sum(k + 1)[...] = aux_sum(k)[...] + aux_r[k]
        if k < 4:
            aux_copy(k + 1).start()

    def slot(i, only=None):
        for code in SLOTS[i]:
            n, k = code // 10, code % 10
            if only is not None and n != only:
                continue
            if n == len(units):
                aux_end(k)
            elif k < 2:
                unit_copy(n, k).start()
            else:
                serve(n, k - 2)

    def weight_grad(n, first, last, *terms):
        refs, c0, width, rows = units[n]
        axes = unit_axes(n)
        fixed = x if len(axes) == 3 else 0
        tails = [0]
        for axis in axes[2:]:
            tails = [tail + p * axis[1] for tail in tails for p in range(2)]
        count = len(tails) * rows
        for g in range(first, last):
            i = lax.rem(axes[0][0] + 1 + g // 2, 2)
            j = lax.rem(axes[1][0] + 1 + g % 2, 2)
            base = i * axes[0][1] + j * axes[1][1] + fixed
            total = None
            for left, right in terms:
                stack = jnp.concatenate([left(base + tail) for tail in tails], axis=0)
                part = mm(stack, right)
                total = part if total is None else total + part
            at = pl.ds(al((i * 2 + j) * count, count), count)
            refs[0][at, pl.ds(c0, width)] = total.astype(BF16)

    def rows_of(ref, rows):
        return lambda chip: ref[pl.ds(al(chip * rows, rows), rows), :]

    for first in (0, 2):
        for n in range(4):
            weight_grad(
                n, first, first + 2, (rows_of(gb_t, 64), act[:, 512 * n : 512 * n + 512])
            )
            if first == 0:
                slot(0, n)
    slot(1)

    def mate_copy(k):
        return pltpu.make_async_remote_copy(
            src_ref=g_t.at[pl.ds(al((2 * k + 1 - x) * 128, 128), 128)],
            dst_ref=pre_m.at[pl.ds(al(k * 128, 128), 128)],
            send_sem=m_send.at[0], recv_sem=m_recv.at[0],
            device_id=x_peer, device_id_type=MESH_ID,
        )

    def act_back(i, carry):
        rows = pl.ds(al(i * 512, 512), 512)
        g_t[rows, :] = (mm(wd[rows, :], gb_t[...]) * g_t[rows, :].astype(F32)).astype(BF16)
        for j in range(2):
            mate_copy(2 * i + j).start()
        return carry

    lax.fori_loop(0, 4, act_back, 0)
    slot(2)

    def mlp_back(tok_at, dst, i):
        at = pl.ds(al(i * 512, 512), 512)
        dst[:, at] = mm(wu[at, :], g_t[:, pl.ds(tok_at, TOK)]).T.astype(dst.dtype)

    lax.fori_loop(0, 2, lambda i, c: (mlp_back(oth_tok, part_send, i), c)[1], 0)
    mlp_back_copy = to_core(8, part_send, part_recv)
    mlp_back_copy.start()
    slot(3)
    xm_mate.wait()
    mate_rows = xm_m.at[pl.ds(own_tok, TOK)]
    xm_pass = to_core(14, mate_rows, mate_rows)
    xm_pass.start()
    lax.fori_loop(0, 2, lambda i, c: (mlp_back(own_tok, part_own, i), c)[1], 0)
    ones = jnp.ones((16, PACK), BF16)
    for i in range(2):
        aux_s[0, pl.ds(8 + 2 * b + i, 1), :] = mm_nt(ones, g_t[i * 1024 : i * 1024 + 1024, :])[0:1]
    slot(4)
    mlp_back_copy.wait()

    gba_t = wd.at[pl.ds(D, D), pl.ds(0, PACK)]
    ga_t = wd.at[pl.ds(D, HALF_D), pl.ds(PACK, PACK)]

    def hidden_back(i, carry):
        sum_c, sum_b = carry
        rows = pl.ds(al(i * CHUNK, CHUNK), CHUNK)
        h = hid[rows, :]
        back, part_c = norm_back(
            h, inv_rms(h), gain_c[...], part_own[rows, :] + part_recv[rows, :].astype(F32)
        )
        g_hidden = cot[rows, :].astype(F32) + back
        hid[rows, :] = g_hidden
        v = branch[rows, :]
        back, part_b = norm_back(v, inv_rms(v), gain_b[...], g_hidden)
        nat[rows, :] = back.astype(BF16)
        return sum_c + part_c, sum_b + part_b

    sums = (zero_row, zero_row)
    gba_copies = []
    for i, k in ((0, 9), (1, 17)):
        sums = hidden_back(i, sums)
        gba_copies.append(turn_and_send(gba_t, i, k))
    sum_gain_c, sum_gain_b = sums
    aux_s[0, 3:4, :] = sum_gain_c
    aux_s[0, 2:3, :] = sum_gain_b
    slot(5)
    for copy in gba_copies:
        copy.wait()

    for n in (8, 9):
        weight_grad(
            n, 0, 4, (rows_of(gba_t, 64), attn_nat[:, 256 * (n - 8) : 256 * (n - 8) + 256])
        )
    slot(6)
    ga_t[...] = mm(wo[pl.ds(own_cols, HALF_D), :], gba_t[...]).astype(BF16)
    slot(7)

    def head_grad(off):
        def rows(chip):
            at = al(off + chip // 8 * HALF_D, HALF_D)
            return act[pl.ds(al(lax.rem(chip, 8) * 64, 64), 64), pl.ds(at, HALF_D)]

        return rows

    own_q = pl.ds(al(own_cols, HALF_D), HALF_D)
    own_k = pl.ds(al(D + own_cols, HALF_D), HALF_D)
    gv = gb_t

    def attend_back(p, carry):
        slab_cols = pl.ds(al(p * 128, 128), 128)
        parts = [
            (w, pl.ds(al(p * 128 + w * 64, 64), 64), slice(i * TOK, i * TOK + TOK), (i + 1) * TOK)
            for w in (0, 1)
            for i in (0, 1)
        ]
        deltas = [
            jnp.sum(ga_t[rows, cols].astype(F32) * attn_t[rows, cols], axis=0, keepdims=True)
            for w, rows, cols, keys in parts
        ]
        scores = [
            mm(k_n[:keys, slab_cols], slab(q_t[rows, cols], w)) + mask[:keys, cols]
            for w, rows, cols, keys in parts
        ]
        g_probs = [
            mm(v_n[:keys, slab_cols], slab(ga_t[rows, cols], w)) for w, rows, cols, keys in parts
        ]
        probs = [
            jnp.exp(score - lse[pl.ds(p * 2 + part[0], 1), part[2]])
            for score, part in zip(scores, parts)
        ]
        g_scores = [
            (prob * (g_prob - delta)).astype(BF16)
            for prob, g_prob, delta in zip(probs, g_probs, deltas)
        ]
        grads_q = [
            mm(k_t[rows, :keys], g_score) * 0.125
            for (w, rows, cols, keys), g_score in zip(parts, g_scores)
        ]
        grads_k = [
            mm_nt(q_t[rows, cols], g_score)
            for (w, rows, cols, keys), g_score in zip(parts, g_scores)
        ]
        grads_v = [
            mm_nt(ga_t[rows, cols], prob.astype(BF16))
            for (w, rows, cols, keys), prob in zip(parts, probs)
        ]

        def both(first, second):
            return jnp.concatenate([first + second[:, :TOK], second[:, TOK:]], axis=1)

        cos, sin = rope[0], rope[1]
        for w in range(2):
            to = pl.ds(al(own_cols + p * 128 + w * 64, 64), 64)
            at = parts[2 * w][1]
            full_q = jnp.concatenate(grads_q[2 * w : 2 * w + 2], axis=1)
            for full, dst in ((full_q, own_q), (both(*grads_k[2 * w : 2 * w + 2]), own_k)):
                low, high = full[:32], full[32:]
                act[at, dst] = jnp.concatenate(
                    [low * cos + high * sin, high * cos - low * sin], axis=0
                ).astype(BF16)
            gv[to, :] = both(*grads_v[2 * w : 2 * w + 2]).astype(BF16)
        return carry

    lax.fori_loop(0, 2, attend_back, 0)
    slot(8)
    lax.fori_loop(2, 4, attend_back, 0)
    own_heads = pl.ds(own_cols, HALF_D)
    head_copies = [
        to_core(10 + i, ref, ref)
        for i, ref in enumerate((act.at[:, own_q], act.at[:, own_k], gv.at[own_heads]))
    ]
    for copy in head_copies:
        copy.start()
    slot(9)

    def in_back(tok_at, dst, i):
        at = pl.ds(al(i * 512, 512), 512)
        cols = pl.ds(tok_at, TOK)
        total = mm(wq[at, :], act[:, pl.ds(al(own_cols + tok_at, TOK), TOK)])
        total += mm(wk[at, :], act[:, pl.ds(al(D + own_cols + tok_at, TOK), TOK)])
        total += mm(wv[at, :], gv[own_heads, cols])
        dst[:, at] = total.T.astype(dst.dtype)

    lax.fori_loop(0, 2, lambda i, c: (in_back(oth_tok, part_send, i), c)[1], 0)
    in_back_copy = to_core(13, part_send, part_recv)
    in_back_copy.start()
    slot(10)
    for copy in head_copies:
        copy.wait()
    for first in (0, 2):
        for i, rows in enumerate((head_grad(0), head_grad(D), rows_of(gv, 64))):
            for j in range(2):
                cols = pl.ds(al(own_cols + 256 * j, 256), 256)
                weight_grad(10 + 2 * i + j, first, first + 2, (rows, xin[:, cols]))
        slot(11 + first // 2)
    lax.fori_loop(0, 2, lambda i, c: (in_back(own_tok, part_own, i), c)[1], 0)
    slot(13)
    in_back_copy.wait()

    def token_back(i, carry):
        rows = pl.ds(al(i * CHUNK, CHUNK), CHUNK)
        v = tok[rows, :].astype(F32)
        back, part_a = norm_back(
            v, inv_rms(v), gain_a[...], part_own[rows, :] + part_recv[rows, :].astype(F32)
        )
        grad_tok[rows, :] = (hid[rows, :] + back).astype(BF16)
        return carry + part_a

    aux_s[0, 1:2, :] = lax.fori_loop(0, TOK // CHUNK, token_back, zero_row)
    hand_over(1).start()
    slot(14)

    pltpu.make_async_remote_copy(
        src_ref=pre_m, dst_ref=pre_m, send_sem=m_send.at[0], recv_sem=m_recv.at[0],
        device_id=x_peer, device_id_type=MESH_ID,
    ).wait()
    xm_pass.wait()

    def mate_pre(chip):
        return pre_m[pl.ds(al(chip // 2 * 128, 128), 128), :]

    for first in (0, 2):
        for n in range(4, 8):
            cols = slice(256 * (n - 4), 256 * (n - 4) + 256)
            weight_grad(
                n, first, first + 2, (rows_of(g_t, 128), xm[:, cols]), (mate_pre, xm_m[:, cols])
            )
        slot(15 + first // 2)

    aux_copy(0).start()
    slot(17)
    finals = attn_t.at[pl.ds(0, 128)]
    final_with(finals, finals, 18).wait_recv()

    for j in range(16):
        rows, _ = final_rows(j // 4, b)
        at = j % 4 * 128
        o_down[:, pl.ds(al((2 * j + b) * 128, 128), 128)] = part_own[rows, at : at + 128]
        o_down[:, pl.ds(al((2 * j + other) * 128, 128), 128)] = attn_t[
            j // 4 * 32 : j // 4 * 32 + 32, at : at + 128
        ]
    hand_over(3).start()
    slot(18)
    hand_over(4).start()
    device = dp * 2 + b
    at = pl.ds(al(device // 4 * 128, 128), 128)
    lines = pltpu.roll(aux_sum(5)[0:8, at], lax.rem(128 - lax.rem(device, 4) * 32, 128), 1)
    for i, ref in enumerate((small_down, small_a, small_b, small_c, small_d)):
        ref[...] = lines[i, :32]
    lines = aux_sum(5)[8:16, pl.ds(al(lax.rem(dp, 8) * 128, 128), 128)]
    chosen = lax.broadcasted_iota(jnp.int32, (8, 128), 0) == 2 * b + dp // 8
    small_up[...] = jnp.sum(jnp.where(chosen, lines, 0.0), axis=0)
    for i in range(9, 15):
        hand_over(i).start()
    for n, (refs, c0, width, rows) in enumerate(units):
        sent = refs[0].at[pl.ds(0, (2 ** len(UNIT_ORDER[n]) - 1) * rows), pl.ds(c0, width)]
        pltpu.make_async_remote_copy(
            src_ref=sent, dst_ref=sent, send_sem=rs_send.at[n], recv_sem=rs_recv.at[n, 0],
            device_id=x_peer, device_id_type=MESH_ID,
        ).wait_send()
    for k in range(5):
        aux_copy(k).wait_send()
    whole = part_own.at[pl.ds(0, 128)]
    final_with(whole, whole, 18).wait_send()
    finals = attn_t.at[pl.ds(128, 128)]
    final_with(finals, finals, 19).wait_recv()
    for i in range(4):
        dst = (o_out, o_query, o_key, o_value)[i]
        rows, _ = final_rows(8 + 2 * i, b)
        dst[:, pl.ds(own_cols, HALF_D)] = part_own[rows, 512:]
        dst[:, pl.ds(oth_cols, HALF_D)] = attn_t[128 + 32 * i : 160 + 32 * i, :]
        hand_over(5 + i).start()
    for i in range(15):
        hand_over(i).wait()


def finish_kernel(*refs):
    count = len(refs) // 3
    sems = refs[-1]
    gets = [
        pltpu.make_async_copy(refs[i], refs[2 * count + i], sems.at[i]) for i in range(count)
    ]
    puts = [
        pltpu.make_async_copy(refs[2 * count + i], refs[count + i], sems.at[i])
        for i in range(count)
    ]
    for copy in gets:
        copy.start()
    for get, put in zip(gets, puts):
        get.wait()
        put.start()
    for copy in puts:
        copy.wait()


def layer_on_device(
    tokens, doc_lengths, w_query, w_key, w_value, w_out, w_up, w_down, bias_up, bias_down,
    gain_pre_attn, gain_post_attn, gain_pre_mlp, gain_post_mlp, cotangent,
):
    def v16(*shape):
        return pltpu.VMEM(shape, BF16)

    def v32(*shape):
        return pltpu.VMEM(shape, F32)

    dma = pltpu.SemaphoreType.DMA
    vmem = pl.BlockSpec(memory_space=pltpu.VMEM)
    hbm = pl.BlockSpec(memory_space=pltpu.HBM)
    shapes = [((TOK, D), BF16)] * 2 + [((2, TOK), F32), ((32, FF), F32), ((D, 128), F32)]
    shapes += [((32, D), F32)] * 4 + [((128,), F32)] + [((32,), F32)] * 5
    shapes = [jax.ShapeDtypeStruct(*shape) for shape in shapes]
    scratch = [pltpu.VMEM(shape.shape, shape.dtype) for shape in shapes] + [dma((15,))]
    scratch += [
        v16(1024, 512), v16(1024, 512), v16(1024, 512), v16(1024, 1024),
        v16(1024, 2048), v16(2048, 1024),
        v16(512, 1024),
        v16(512, 512), v16(512, 512), v16(512, 512), v16(512, 512), v16(512, 512),
        v32(512, 512), v32(512, 512), v16(512, 512),
        v32(256, 1024), v32(256, 1024), v16(512, 1024),
        v16(512, 2048), v16(2048, 512),
        v16(256, 1024), v16(256, 1024), v32(256, 1024), v16(256, 1024),
        v16(1024, 512),
        v32(2, 32, 512), v32(8, 512), v32(2, 256, 128),
        v16(1024, 2048), v16(512, 2048), v16(256, 2048), v16(128, 2048), v16(64, 2048),
        v16(512, 1024), v16(256, 1024), v16(128, 1024), v16(512, 1024), v16(1024, 512),
        v16(512, 2048), v16(256, 2048), v16(128, 2048), v16(64, 2048),
        v32(1, 16, 1024), v32(5, 16, 1024),
        dma((6,)), dma((2,)), dma((2,)), dma((20,)), dma((20,)), dma((16,)), dma((16, 5)), dma((5,)), dma((5,)),
    ]
    results = pl.pallas_call(
        layer_kernel,
        out_shape=shapes,
        in_specs=[pl.BlockSpec(memory_space=pltpu.SMEM)]
        + [vmem] * 8
        + [pl.BlockSpec(memory_space=pl.ANY)] * 6,
        out_specs=[hbm] * 15,
        scratch_shapes=scratch,
        compiler_params=pltpu.CompilerParams(
            collective_id=0, has_side_effects=True, vmem_limit_bytes=VMEM_BYTES
        ),
    )(
        doc_lengths, tokens, cotangent,
        gain_pre_attn[None], gain_post_attn[None], gain_pre_mlp[None], gain_post_mlp[None],
        bias_up.reshape(32, 128), bias_down[None],
        w_query, w_key, w_value, w_out, w_up, w_down,
    )
    out, grad_tok, rms, gd, gu, go, gq, gk, gv, small_up, small_down, sa, sb, sc, sd = pl.pallas_call(
        finish_kernel,
        out_shape=shapes,
        in_specs=[hbm] * 15,
        out_specs=[hbm] * 15,
        scratch_shapes=[pltpu.VMEM(s.shape, s.dtype) for s in shapes] + [dma((15,))],
    )(*results)
    return (
        out, grad_tok, gq.T, gk.T, gv.T, go.T, gu, gd.T, small_up, small_down, sa, sb, sc, sd, rms
    )


def solution(mesh):
    placed = (
        P(("dp", "blk"), None),
        P("dp", None),
        P(),
        P(),
        P(),
        P(),
        P(),
        P(),
        P(),
        P(),
        P(),
        P(),
        P(),
        P(),
        P(("dp", "blk"), None),
    )
    paired = mesh.shape["blk"] == 2 and mesh.shape["dp"] == 16
    return jax.shard_map(
        layer_on_device if paired else on_device,
        mesh=mesh,
        in_specs=placed,
        out_specs=(
            P(("dp", "blk"), None),
            P(("dp", "blk"), None),
            P(None, ("dp", "blk")),
            P(None, ("dp", "blk")),
            P(None, ("dp", "blk")),
            P(None, ("dp", "blk")),
            P(None, ("dp", "blk")),
            P(None, ("dp", "blk")),
            P(("dp", "blk")),
            P(("dp", "blk")),
            P(("dp", "blk")),
            P(("dp", "blk")),
            P(("dp", "blk")),
            P(("dp", "blk")),
            P(None, ("dp", "blk")),
        ),
        check_vma=False,
    )
```
